32 devices in a mesh: wide: 8 (over y, x, core), narrow: 4 (over z).
Axes of the slice: x: 2, y: 2, z: 4, core: 2. Of those that a mesh axis runs over, the one named last changes fastest.
Arguments:
- tokens: bfloat16 [64, 1024, 512], P(('wide', 'narrow')), may hold values from -6 to 6
- out_grad: bfloat16 [64, 1024, 512], P(('wide', 'narrow')), may hold values from -6 to 6
- group_ids: int32 [64], P(('wide', 'narrow')), may hold values from 0 to 3
- domain_weight: float32 [4], replicated, may hold values from 0.5 to 2
- attn_w: float32 [5, 512, 512], P(None, 'narrow'), as said below
- ffn_w: float32 [2, 2048, 512], P(None, 'narrow'), as said below
- attn_mom: float32 [5, 512, 512], P(None, 'narrow'), as said below
- ffn_mom: float32 [2, 2048, 512], P(None, 'narrow'), as said below
- ln_params: float32 [4, 512], replicated, as said below
- ln_first: float32 [4, 512], P(None, 'narrow')
- ln_second: float32 [4, 512], P(None, 'narrow'), as said below
Outputs:
- output: bfloat16 [64, 1024, 512], P(('wide', 'narrow'))
- input_grad: float32 [64, 1024, 512], P(('wide', 'narrow'))
- attn_grad: float32 [5, 512, 512], P(None, 'narrow')
- ffn_grad: float32 [2, 2048, 512], P(None, 'narrow')
- ln_grad: float32 [4, 512], P(None, 'narrow')
- attn_mom_new: float32 [5, 512, 512], P(None, 'narrow')
- ffn_mom_new: float32 [2, 2048, 512], P(None, 'narrow')
- attn_new: float32 [5, 512, 512], P(None, 'narrow')
- ffn_new: float32 [2, 2048, 512], P(None, 'narrow')
- attn_copy: bfloat16 [5, 512, 512], P(None, 'narrow')
- ffn_copy: bfloat16 [2, 2048, 512], P(None, 'narrow')
- ln_first_new: float32 [4, 512], P(None, 'narrow')
- ln_second_new: float32 [4, 512], P(None, 'narrow')
- ln_new: float32 [4, 512], P(None, 'narrow')
The draws below stay inside these ranges and needn't reach their ends.
Inputs may be any that keep to these rules, and one draw needn't show every extreme that they name: `attn_mom`: independent entries; row scales of the momenta differ across rows. `ffn_mom`: independent entries. `attn_w`: independent entries. `ffn_w`: independent entries. `ln_params`: gains positive. `ln_second`: Positive.
All inputs are finite; a program needn't handle non-finite values.
Results may differ from the reference program's by a relative error of at most 0.014.
Values may be sent and summed in bfloat16 or wider, within the bound.
A program may use at most 256 MiB of HBM per device.

```python
import math
import jax
import jax.numpy as jnp
import numpy as np
from jax import lax

D = 512
HEADS = 8
SLOTS = 64
FF = 2048
HEAD_DIM = 64
SEQ_LEN = 1024
SEQS = 64
DOMAINS = 4
NS_ITERS = 2
STEP = 10


def clipped_normal(key, shape):
    return jnp.clip(jax.random.normal(key, shape, jnp.float32), -6.0, 6.0)


def gradient_size():
    return jnp.sqrt(jnp.float32(SEQ_LEN * SEQS))


def draw_attn_w(key, part):
    key = jax.random.fold_in(key, 1)
    fans = jnp.array([D // 2, D, D, D // 6, D // 2], jnp.float32)
    return clipped_normal(key, (5, D, D)) * jax.lax.rsqrt(fans)[:, None, None]


def draw_ffn_w(key, part):
    key = jax.random.fold_in(key, 2)
    fans = jnp.array([D, FF], jnp.float32)
    return clipped_normal(key, (2, FF, D)) * jax.lax.rsqrt(fans)[:, None, None]


def draw_attn_mom(key, part):
    key = jax.random.fold_in(key, 3)
    top = 10.0
    rising = jnp.exp(jnp.log(top) * jnp.arange(D, dtype=jnp.float32) / D)
    factors = jnp.array([0.15, 0.15, 0.3, 0.15, 0.5], jnp.float32)
    return clipped_normal(key, (5, D, D)) * factors[:, None, None] * gradient_size() * rising[None, :, None]


def draw_ffn_mom(key, part):
    key = jax.random.fold_in(key, 4)
    top = 10.0
    rising = jnp.exp(jnp.log(top) * jnp.arange(FF, dtype=jnp.float32) / FF)
    factors = jnp.array([0.25, 0.6], jnp.float32)
    return clipped_normal(key, (2, FF, D)) * factors[:, None, None] * gradient_size() * rising[None, :, None]


def draw_ln_params(key, part):
    key = jax.random.fold_in(key, 5)
    gain_key, shift_key = jax.random.split(key)
    gains = jax.random.uniform(gain_key, (2, D), jnp.float32, 0.6, 1.4)
    shifts = 0.2 * clipped_normal(shift_key, (2, D))
    return jnp.stack([gains[0], shifts[0], gains[1], shifts[1]])


def draw_ln_first(key, part):
    key = jax.random.fold_in(key, 6)
    return clipped_normal(key, (4, D)) * 0.055 * gradient_size()


def draw_ln_second(key, part):
    key = jax.random.fold_in(key, 7)
    level = 0.5 * gradient_size()
    return jax.random.uniform(key, (4, D), jnp.float32, 1.0, 4.0) * 0.001 * level * level


def plant(result, rng, low, largest):
    longest = result.shape.index(max(result.shape))
    spots = []
    for shift in (0, 1):
        where = [jax.random.randint(jax.random.fold_in(rng, axis), (), 0, length) for axis, length in enumerate(result.shape)]
        where[longest] = (where[longest] + shift) % result.shape[longest]
        spots.append(tuple(where))
    return result.at[spots[0]].set(low).at[spots[1]].set(largest)


def block_scale(key, dims, cuts, smallest, largest):
    def one(dim, blocks):
        heights = jax.random.uniform(jax.random.fold_in(jax.random.fold_in(key, 6), dim), (blocks,), jnp.float32, smallest / len(cuts), largest / len(cuts))
        return jnp.repeat(jnp.exp(heights), dims[dim] // blocks).reshape((-1,) + (1,) * (len(dims) - dim - 1))

    loudness = one(*cuts[0])
    for cut in cuts[1:]:
        loudness = loudness * one(*cut)
    return loudness


def rank_bounds(amount, lean):
    portions = [(1 << 20) // math.isqrt(grade ** lean) + 1 for grade in range(1, amount + 1)]
    scale = 1 + sum(portions) // (1 << 30)
    return np.cumsum(np.array([max(1, weight // scale) for weight in portions]))


def ranked(stream_key, extent, number_of, lean):
    table = rank_bounds(number_of, lean)
    ticket = jax.random.randint(jax.random.fold_in(stream_key, 1), extent, 0, int(table[number_of - 1]))
    rank = jnp.searchsorted(jnp.asarray(table, jnp.int32), ticket, side="right")
    return jax.random.permutation(jax.random.fold_in(stream_key, 2), number_of)[rank].astype(jnp.int32)


def centred(own_key, extent, scale, reach, shards=(), held_as=jnp.bfloat16):
    values = jax.random.normal(own_key, extent, jnp.float32) * scale
    if len(shards) > 0:
        values = block_scale(own_key, extent, shards, -0.22, 0.18) * values
    return jnp.clip(values, min=-reach, max=reach).astype(held_as)


def setup_inputs(seed: int = 0) -> dict:
    keys = jax.random.split(jax.random.key(seed), 12)
    return {
        "tokens": centred(keys[0], (SEQS, SEQ_LEN, D), 1.0, 6.0, ((0, 32),)),
        "out_grad": centred(keys[1], (SEQS, SEQ_LEN, D), 1.0, 6.0, ((0, 32),)),
        "group_ids": plant(ranked(keys[2], (SEQS,), DOMAINS, 2), jax.random.fold_in(keys[2], 3), 0, DOMAINS - 1).astype(jnp.int32),
        "domain_weight": jnp.clip(jnp.exp(jax.random.uniform(keys[3], (DOMAINS,), jnp.float32, math.log(0.5), math.log(2.0))), 0.5, 2.0),
        "attn_w": draw_attn_w(jax.random.fold_in(keys[11], 71), 0),
        "ffn_w": draw_ffn_w(jax.random.fold_in(keys[11], 71), 0),
        "attn_mom": draw_attn_mom(jax.random.fold_in(keys[11], 71), 0),
        "ffn_mom": draw_ffn_mom(jax.random.fold_in(keys[11], 71), 0),
        "ln_params": draw_ln_params(jax.random.fold_in(keys[11], 71), 0),
        "ln_first": draw_ln_first(jax.random.fold_in(keys[11], 71), 0),
        "ln_second": draw_ln_second(jax.random.fold_in(keys[11], 71), 0),
    }


@jax.custom_vjp
def low(v):
    return lax.optimization_barrier(v.astype(jnp.bfloat16)).astype(jnp.float32)

@jax.custom_vjp
def low_back(v):
    return v

def low_keep(v):
    return (low(v), None)

def low_pass(kept, grad):
    return (grad,)

def back_keep(v):
    return (v, None)

def back_low(kept, grad):
    return (low(grad),)
low.defvjp(low_keep, low_pass)
low_back.defvjp(back_keep, back_low)
norm_epsilon = 1e-05
momentum_keep = 0.5
quintic_lin = 3.4445
quintic_cube = -4.775
quintic_five = 2.0315
muon_rate = 0.7
muon_decay = 0.1
adam_rate = 0.2
beta_first = 0.9
beta_second = 0.999
adam_epsilon = 1e-08
highest = lax.Precision.HIGHEST

def both_round(values):
    return low(low_back(values))

def layer_norm(values, gain, shift):
    center = values - lax.optimization_barrier(jnp.mean(values, axis=-1, keepdims=True))
    spread = lax.optimization_barrier(jnp.mean(center * center, axis=-1, keepdims=True))
    return center * lax.rsqrt(spread + norm_epsilon) * gain + shift

def slot_attention(queries, key_rows, value_rows, slot_weight):
    length = queries.shape[0]
    places = jnp.arange(length)
    causal = (places[:, None] >= places[None, :]).astype(jnp.float32)
    scaling = queries.shape[-1] ** (-0.5)
    raw_scores = jnp.einsum('thd,shd->hts', queries, key_rows, precision=highest) * scaling * causal
    scores = both_round(raw_scores)
    numerator = low_back(jnp.einsum('hts,shm->thm', scores, slot_weight, precision=highest))
    totals = jnp.cumsum(slot_weight, axis=0)
    slot_prob = jax.nn.softmax(numerator / totals, axis=-1)
    shares = both_round(slot_prob / totals)
    mixing = both_round(jnp.einsum('thm,shm->hts', shares, slot_weight, precision=highest) * causal)
    return both_round(jnp.einsum('hts,shd->thd', mixing, value_rows, precision=highest))

def one_sequence(tokens_f, attn_in, ffn_in, ln_in):
    length, model_width = tokens_f.shape
    first_norm = low(layer_norm(tokens_f, ln_in[0], ln_in[1]))

    def project(number):
        return jnp.dot(first_norm, attn_in[number], precision=highest)
    queries = both_round(project(0)).reshape(length, HEADS, HEAD_DIM)
    key_rows = both_round(project(1)).reshape(length, HEADS, HEAD_DIM)
    value_rows = both_round(project(2)).reshape(length, HEADS, HEAD_DIM)
    slot_weight = both_round(jnp.exp(low_back(project(3)))).reshape(length, HEADS, SLOTS)
    attended = slot_attention(queries, key_rows, value_rows, slot_weight).reshape(length, model_width)
    mixed = tokens_f + low_back(jnp.dot(attended, attn_in[4], precision=highest))
    second_norm = low(layer_norm(mixed, ln_in[2], ln_in[3]))
    inner_act = low_back(jnp.dot(second_norm, ffn_in[0].T, precision=highest))
    hidden = both_round(jax.nn.gelu(inner_act))
    return mixed + low_back(jnp.dot(hidden, ffn_in[1], precision=highest))

def orthogonalize(moment):
    iterate = moment / (jnp.sqrt(jnp.sum(moment * moment)) + 1e-07)
    for newton_turn in range(NS_ITERS):
        gram = jnp.dot(iterate.T, iterate, precision=highest)
        poly = quintic_cube * gram + quintic_five * jnp.dot(gram, gram, precision=highest)
        iterate = quintic_lin * iterate + jnp.dot(iterate, poly, precision=highest)
    return iterate

def muon_update(weight, moment, grad_full):
    new_moment = momentum_keep * moment + grad_full
    ortho = jax.vmap(orthogonalize)(new_moment)
    scaling = muon_rate * 0.2 * math.sqrt(max(weight.shape[1], weight.shape[2]))
    new_weight = (1.0 - muon_rate * muon_decay) * weight - scaling * ortho
    return (new_moment, new_weight)

def reference(tokens, out_grad, group_ids, domain_weight, attn_w, ffn_w, attn_mom, ffn_mom, ln_params, ln_first, ln_second):
    member = (group_ids[:, None] == jnp.arange(DOMAINS)[None, :]).astype(jnp.int32)
    group_count = lax.optimization_barrier(jnp.sum(member, axis=0))
    weight_of = domain_weight[group_ids]
    count_of = group_count[group_ids].astype(jnp.float32)
    seq_weight = weight_of * SEQS / (DOMAINS * count_of)
    attn_low = attn_w.astype(jnp.bfloat16).astype(jnp.float32)
    ffn_low = ffn_w.astype(jnp.bfloat16).astype(jnp.float32)
    tokens_f = tokens.astype(jnp.float32)

    def forward(tokens_all, attn_in, ffn_in, ln_in):
        per_sequence = jax.checkpoint(lambda sequence: one_sequence(sequence, attn_in, ffn_in, ln_in))
        return lax.map(per_sequence, tokens_all)
    outputs, pullback = jax.vjp(forward, tokens_f, attn_low, ffn_low, ln_params)
    cotangent = out_grad.astype(jnp.float32) * seq_weight[:, None, None]
    input_grad, attn_grad, ffn_grad, ln_grad = pullback(cotangent)
    attn_mom_new, attn_new = muon_update(attn_w, attn_mom, attn_grad)
    ffn_mom_new, ffn_new = muon_update(ffn_w, ffn_mom, ffn_grad)
    first_new = beta_first * ln_first + (1.0 - beta_first) * ln_grad
    second_new = beta_second * ln_second + (1.0 - beta_second) * ln_grad * ln_grad
    first_fix = 1.0 - beta_first ** STEP
    second_fix = 1.0 - beta_second ** STEP
    ln_new = ln_params - adam_rate * (first_new / first_fix) / (jnp.sqrt(second_new / second_fix) + adam_epsilon)
    return (outputs.astype(jnp.bfloat16), input_grad, attn_grad, ffn_grad, ln_grad, attn_mom_new, ffn_mom_new, attn_new, ffn_new, attn_new.astype(jnp.bfloat16), ffn_new.astype(jnp.bfloat16), first_new, second_new, ln_new)
```

```python
import functools
import math

import jax
import jax.numpy as jnp
from jax import lax
from jax.experimental import pallas as pl
from jax.experimental.pallas import tpu as pltpu
from jax.sharding import PartitionSpec as P

D = 512
HEADS = 8
HEAD_DIM = 64
FF = 2048
STEP = 10

norm_epsilon = 1e-05
momentum_keep = 0.5
quintic_lin = 3.4445
quintic_cube = -4.775
quintic_five = 2.0315
muon_rate = 0.7
muon_decay = 0.1
adam_rate = 0.2
beta_first = 0.9
beta_second = 0.999
adam_epsilon = 1e-08

CHUNK = 128
PAIR = 2 * HEAD_DIM
PAIRS = HEADS // 2
VMEM_BYTES = 60 * 1024 * 1024
low_type = jnp.bfloat16
wide_type = jnp.float32


def dot_nn(left, right):
    return lax.dot_general(left, right, (((1,), (0,)), ((), ())), preferred_element_type=wide_type)


def dot_nt(left, right):
    return lax.dot_general(left, right, (((1,), (1,)), ((), ())), preferred_element_type=wide_type)


def dot_tn(left, right):
    return lax.dot_general(left, right, (((0,), (0,)), ((), ())), preferred_element_type=wide_type)


def normalize(rows):
    center = rows - jnp.mean(rows, axis=-1, keepdims=True)
    spread = jnp.mean(center * center, axis=-1, keepdims=True)
    inverse = lax.rsqrt(spread + norm_epsilon)
    return center * inverse, inverse


def norm_back(grad_rows, normed, inverse, gain):
    grad_normed = grad_rows * gain
    mean_grad = jnp.mean(grad_normed, axis=-1, keepdims=True)
    mean_cross = jnp.mean(grad_normed * normed, axis=-1, keepdims=True)
    return inverse * (grad_normed - mean_grad - normed * mean_cross)


def project_kernel(x_ref, w_ref, ln_ref, q_ref, k_ref, v_ref, a_ref):
    normed, _ = normalize(x_ref[...].astype(wide_type))
    first = (normed * ln_ref[0:1, :] + ln_ref[1:2, :]).astype(low_type)
    q_ref[...] = dot_nn(first, w_ref[0]).astype(low_type)
    k_ref[...] = dot_nn(first, w_ref[1]).astype(low_type)
    v_ref[...] = dot_nn(first, w_ref[2]).astype(low_type)
    a_ref[...] = jnp.exp(dot_nn(first, w_ref[3])).astype(low_type)


def project(rows, weights, ln_params):
    count = rows.shape[0]
    block = 512
    row_spec = pl.BlockSpec((block, D), lambda i: (i, 0))
    return pl.pallas_call(
        project_kernel,
        grid=(count // block,),
        in_specs=[
            row_spec,
            pl.BlockSpec((4, D, D), lambda i: (0, 0, 0)),
            pl.BlockSpec((4, D), lambda i: (0, 0)),
        ],
        out_specs=[row_spec] * 4,
        out_shape=[jax.ShapeDtypeStruct((count, D), low_type)] * 4,
        compiler_params=pltpu.CompilerParams(vmem_limit_bytes=VMEM_BYTES),
        name="project",
    )(rows, weights, ln_params)


def lane_of(shape):
    return lax.broadcasted_iota(jnp.int32, shape, 1)


def row_of(shape):
    return lax.broadcasted_iota(jnp.int32, shape, 0)


def split_pair(pair, first_head):
    zero = jnp.zeros_like(pair)
    return jnp.concatenate(
        [jnp.where(first_head, pair, zero), jnp.where(first_head, zero, pair)], axis=0
    )


def head_reduce(values, first_head, op, neutral):
    left = op(jnp.where(first_head, values, neutral), axis=-1, keepdims=True)
    right = op(jnp.where(first_head, neutral, values), axis=-1, keepdims=True)
    return jnp.where(first_head, left, right)


def attend_kernel(
    q_ref, k_ref, v_ref, a_ref, att_ref, share_ref, logit_ref, total_ref, state_ref, state, carry
):
    seqs = q_ref.shape[0]

    @pl.when(pl.program_id(0) == 0)
    def _():
        state[...] = jnp.zeros_like(state)
        carry[...] = jnp.zeros_like(carry)

    first_head = lane_of((CHUNK, PAIR)) < HEAD_DIM
    causal = row_of((CHUNK, 2 * CHUNK)) >= lane_of((CHUNK, 2 * CHUNK)) % CHUNK
    same_head = (row_of((PAIR, 2 * PAIR)) // HEAD_DIM) == (
        (lane_of((PAIR, 2 * PAIR)) // HEAD_DIM) % 2
    )
    lower = (row_of((CHUNK, CHUNK)) >= lane_of((CHUNK, CHUNK))).astype(low_type)
    for seq in range(seqs):
        slot_all = a_ref[seq]
        total_all = dot_nn(lower, slot_all) + carry[seq]
        total_ref[seq] = total_all
        carry[seq] = total_all[CHUNK - 1 :, :]
        inv_all = 1.0 / total_all
        for pair in range(PAIRS):
            lanes = slice(pair * PAIR, (pair + 1) * PAIR)
            q = q_ref[seq, :, lanes] * low_type(HEAD_DIM**-0.5)
            k = k_ref[seq, :, lanes]
            v = v_ref[seq, :, lanes]
            a = a_ref[seq, :, lanes]
            inv = inv_all[:, lanes]
            a_two = split_pair(a, first_head)
            now = jnp.where(same_head, state[seq, pair], 0.0).astype(low_type)
            state_ref[0, seq, pair] = now
            scores = jnp.where(causal, dot_nt(q, split_pair(k, first_head)), 0.0).astype(low_type)
            numer = dot_nn(scores, a_two) + dot_nt(q, now[:, :PAIR])
            logit = numer * inv
            logit_ref[seq, :, lanes] = logit
            expo = jnp.exp(logit - head_reduce(logit, first_head, jnp.max, -jnp.inf))
            share = expo * (inv / head_reduce(expo, first_head, jnp.sum, 0.0))
            share = share.astype(low_type)
            share_ref[seq, :, lanes] = share
            mix = jnp.where(causal, dot_nt(share, a_two), 0.0).astype(low_type)
            att = dot_nn(mix, split_pair(v, first_head)) + dot_nn(share, now[:, PAIR:])
            att_ref[seq, :, lanes] = att.astype(low_type)
            state[seq, pair] += dot_tn(a, jnp.concatenate([k, v], axis=1))


def attend(q, k, v, a):
    seqs, length, _ = q.shape
    chunks = length // CHUNK
    block = pl.BlockSpec((seqs, CHUNK, D), lambda i: (0, i, 0))
    low_out = jax.ShapeDtypeStruct(q.shape, low_type)
    wide_out = jax.ShapeDtypeStruct(q.shape, wide_type)
    return pl.pallas_call(
        attend_kernel,
        grid=(chunks,),
        in_specs=[block] * 4,
        out_specs=[
            block,
            block,
            block,
            block,
            pl.BlockSpec((1, seqs, PAIRS, PAIR, 2 * PAIR), lambda i: (i, 0, 0, 0, 0)),
        ],
        out_shape=[
            low_out,
            low_out,
            wide_out,
            wide_out,
            jax.ShapeDtypeStruct((chunks, seqs, PAIRS, PAIR, 2 * PAIR), low_type),
        ],
        scratch_shapes=[
            pltpu.VMEM((seqs, PAIRS, PAIR, 2 * PAIR), wide_type),
            pltpu.VMEM((seqs, 1, D), wide_type),
        ],
        compiler_params=pltpu.CompilerParams(vmem_limit_bytes=VMEM_BYTES),
        name="attend",
    )(q, k, v, a)


def attend_back_kernel(
    q_ref,
    k_ref,
    v_ref,
    a_ref,
    share_ref,
    logit_ref,
    total_ref,
    datt_ref,
    state_ref,
    dq_ref,
    dk_ref,
    dv_ref,
    de_ref,
    state,
    carry,
):
    seqs = q_ref.shape[0]

    @pl.when(pl.program_id(0) == 0)
    def _():
        state[...] = jnp.zeros_like(state)
        carry[...] = jnp.zeros_like(carry)

    scaling = HEAD_DIM**-0.5
    first_head = lane_of((CHUNK, PAIR)) < HEAD_DIM
    causal = row_of((CHUNK, 2 * CHUNK)) >= lane_of((CHUNK, 2 * CHUNK)) % CHUNK
    anti = row_of((CHUNK, 2 * CHUNK)) <= lane_of((CHUNK, 2 * CHUNK)) % CHUNK
    same_head = (row_of((PAIR, 2 * PAIR)) // HEAD_DIM) == (
        (lane_of((PAIR, 2 * PAIR)) // HEAD_DIM) % 2
    )
    upper = (row_of((CHUNK, CHUNK)) <= lane_of((CHUNK, CHUNK))).astype(low_type)
    for seq in range(seqs):
        for pair in range(PAIRS):
            lanes = slice(pair * PAIR, (pair + 1) * PAIR)
            q = q_ref[seq, :, lanes] * low_type(scaling)
            k = k_ref[seq, :, lanes]
            v = v_ref[seq, :, lanes]
            a = a_ref[seq, :, lanes]
            share = share_ref[seq, :, lanes]
            logit = logit_ref[seq, :, lanes]
            total = total_ref[seq, :, lanes]
            datt = datt_ref[seq, :, lanes]
            inv = 1.0 / total
            before = state_ref[0, seq, pair]
            after = jnp.where(same_head, state[seq, pair], 0.0).astype(low_type)
            q_two = split_pair(q, first_head)
            k_two = split_pair(k, first_head)
            v_two = split_pair(v, first_head)
            a_two = split_pair(a, first_head)
            share_two = split_pair(share, first_head)
            datt_two = split_pair(datt, first_head)

            dmix = jnp.where(causal, dot_nt(datt, v_two), 0.0).astype(low_type)
            dshare = dot_nn(dmix, a_two) + dot_nt(datt, before[:, PAIR:])
            prob = share.astype(wide_type) * total
            dprob = dshare * inv
            dlogit = prob * (dprob - head_reduce(dprob * prob, first_head, jnp.sum, 0.0))
            dnumer = (dlogit * inv).astype(low_type)
            dtotal = -(dprob * prob + dlogit * logit) * inv
            dnumer_two = split_pair(dnumer, first_head)
            dscores = jnp.where(causal, dot_nt(dnumer, a_two), 0.0).astype(low_type)
            dq = (dot_nn(dscores, k_two) + dot_nn(dnumer, before[:, :PAIR])) * scaling
            dq_ref[seq, :, lanes] = dq.astype(low_type)

            mix_t = jnp.where(anti, dot_nt(a, share_two), 0.0).astype(low_type)
            dscores_t = jnp.where(anti, dot_nt(a, dnumer_two), 0.0).astype(low_type)
            dmix_t = jnp.where(anti, dot_nt(v, datt_two), 0.0).astype(low_type)
            scores_t = jnp.where(anti, dot_nt(k, q_two), 0.0).astype(low_type)
            later = dot_nn(a, after)
            dv = dot_nn(mix_t, datt_two) + later[:, PAIR:]
            dv_ref[seq, :, lanes] = dv.astype(low_type)
            dk = dot_nn(dscores_t, q_two) + later[:, :PAIR]
            dk_ref[seq, :, lanes] = dk.astype(low_type)

            dtotal_high = dtotal.astype(low_type)
            dtotal_low = (dtotal - dtotal_high.astype(wide_type)).astype(low_type)
            tail = (
                dot_nn(upper, dtotal_high)
                + dot_nn(upper, dtotal_low)
                + carry[seq, :, lanes]
            )
            carry[seq, :, lanes] = tail[0:1, :]
            da = (
                dot_nn(dmix_t, share_two)
                + dot_nn(scores_t, dnumer_two)
                + dot_nt(jnp.concatenate([k, v], axis=1), after)
                + tail
            )
            de = da.astype(low_type).astype(wide_type) * a.astype(wide_type)
            de_ref[seq, :, lanes] = de.astype(low_type)
            state[seq, pair, :, :PAIR] += dot_tn(dnumer, q)
            state[seq, pair, :, PAIR:] += dot_tn(share, datt)


def attend_back(q, k, v, a, share, logit, total, datt, states):
    seqs, length, _ = q.shape
    chunks = length // CHUNK
    block = pl.BlockSpec((seqs, CHUNK, D), lambda i: (0, chunks - 1 - i, 0))
    return pl.pallas_call(
        attend_back_kernel,
        grid=(chunks,),
        in_specs=[block] * 8
        + [
            pl.BlockSpec(
                (1, seqs, PAIRS, PAIR, 2 * PAIR), lambda i: (chunks - 1 - i, 0, 0, 0, 0)
            )
        ],
        out_specs=[block] * 4,
        out_shape=[jax.ShapeDtypeStruct(q.shape, low_type)] * 4,
        scratch_shapes=[
            pltpu.VMEM((seqs, PAIRS, PAIR, 2 * PAIR), wide_type),
            pltpu.VMEM((seqs, 1, D), wide_type),
        ],
        compiler_params=pltpu.CompilerParams(vmem_limit_bytes=VMEM_BYTES),
        name="attend_back",
    )(q, k, v, a, share, logit, total, datt, states)


FF_BLOCK = 512
gelu_root = math.sqrt(2.0 / math.pi)
gelu_cube = 0.044715


def feed_kernel(
    weight_ref,
    x_ref,
    att_ref,
    og_ref,
    wo_ref,
    ffn_ref,
    ln_ref,
    out_ref,
    dx_ref,
    datt_ref,
    gup_ref,
    gdown_ref,
    go_ref,
    gln_ref,
    up_sum,
    down_sum,
    o_sum,
    *,
    per_seq,
):
    step = pl.program_id(0)

    @pl.when(step == 0)
    def _():
        up_sum[...] = jnp.zeros_like(up_sum)
        down_sum[...] = jnp.zeros_like(down_sum)
        o_sum[...] = jnp.zeros_like(o_sum)
        gln_ref[...] = jnp.zeros_like(gln_ref)

    att = att_ref[...]
    mixed = x_ref[...].astype(wide_type) + dot_nn(att, wo_ref[...])
    normed, inverse = normalize(mixed)
    second = (normed * ln_ref[2:3, :] + ln_ref[3:4, :]).astype(low_type)
    dout = og_ref[...].astype(wide_type) * weight_ref[step // per_seq]
    dy = dout.astype(low_type)
    second_t = second.T
    dy_t = dy.T
    result = mixed
    dsecond = jnp.zeros_like(mixed)
    for part in range(FF // FF_BLOCK):
        rows = slice(part * FF_BLOCK, (part + 1) * FF_BLOCK)
        up = ffn_ref[0, rows, :]
        down = ffn_ref[1, rows, :]
        inner = dot_nt(second, up)
        square = inner * inner
        bend = jnp.tanh(inner * (gelu_root + (gelu_root * gelu_cube) * square))
        half = 0.5 + 0.5 * bend
        hidden = (inner * half).astype(low_type)
        slope = half + (0.5 * inner) * (1.0 - bend * bend) * (
            gelu_root + (3.0 * gelu_root * gelu_cube) * square
        )
        result = result + dot_nn(hidden, down)
        down_sum[:, rows] += dot_nn(dy_t, hidden)
        dinner = (dot_nt(dy, down) * slope).astype(low_type)
        up_sum[:, rows] += dot_nn(second_t, dinner)
        dsecond = dsecond + dot_nn(dinner, up)
    out_ref[...] = result.astype(low_type)
    gln_ref[0:1, :] += jnp.sum(dsecond * normed, axis=0, keepdims=True)
    gln_ref[1:2, :] += jnp.sum(dsecond, axis=0, keepdims=True)
    dmixed = dout + norm_back(dsecond, normed, inverse, ln_ref[2:3, :])
    dx_ref[...] = dmixed
    datt = dmixed.astype(low_type)
    o_sum[...] += dot_tn(att, datt)
    datt_ref[...] = dot_nt(datt, wo_ref[...]).astype(low_type)

    @pl.when(step == pl.num_programs(0) - 1)
    def _():
        gup_ref[...] = up_sum[...].astype(low_type)
        gdown_ref[...] = down_sum[...].astype(low_type)
        go_ref[...] = o_sum[...].astype(low_type)


def feed(seq_weight, rows, att, grad, wo, ffn, ln_params, length):
    count = rows.shape[0]
    block = 256
    row_spec = pl.BlockSpec((block, D), lambda i: (i, 0))

    def whole(*shape):
        return pl.BlockSpec(shape, lambda i: (0,) * len(shape))

    return pl.pallas_call(
        functools.partial(feed_kernel, per_seq=length // block),
        grid=(count // block,),
        in_specs=[
            pl.BlockSpec(memory_space=pltpu.SMEM),
            row_spec,
            row_spec,
            row_spec,
            whole(D, D),
            whole(2, FF, D),
            whole(4, D),
        ],
        out_specs=[
            row_spec,
            row_spec,
            row_spec,
            whole(D, FF),
            whole(D, FF),
            whole(D, D),
            whole(2, D),
        ],
        out_shape=[
            jax.ShapeDtypeStruct((count, D), low_type),
            jax.ShapeDtypeStruct((count, D), wide_type),
            jax.ShapeDtypeStruct((count, D), low_type),
            jax.ShapeDtypeStruct((D, FF), low_type),
            jax.ShapeDtypeStruct((D, FF), low_type),
            jax.ShapeDtypeStruct((D, D), low_type),
            jax.ShapeDtypeStruct((2, D), wide_type),
        ],
        scratch_shapes=[
            pltpu.VMEM((D, FF), wide_type),
            pltpu.VMEM((D, FF), wide_type),
            pltpu.VMEM((D, D), wide_type),
        ],
        compiler_params=pltpu.CompilerParams(vmem_limit_bytes=VMEM_BYTES),
        name="feed",
    )(seq_weight, rows, att, grad, wo, ffn, ln_params)


def project_back_kernel(
    x_ref,
    dx_ref,
    dq_ref,
    dk_ref,
    dv_ref,
    de_ref,
    w_ref,
    ln_ref,
    grad_ref,
    gw_ref,
    gln_ref,
    w_sum,
):
    step = pl.program_id(0)

    @pl.when(step == 0)
    def _():
        w_sum[...] = jnp.zeros_like(w_sum)
        gln_ref[...] = jnp.zeros_like(gln_ref)

    normed, inverse = normalize(x_ref[...].astype(wide_type))
    first_t = (normed * ln_ref[0:1, :] + ln_ref[1:2, :]).astype(low_type).T
    dfirst = jnp.zeros(normed.shape, wide_type)
    for place, ref in enumerate((dq_ref, dk_ref, dv_ref, de_ref)):
        part = ref[...]
        w_sum[place] += dot_nn(first_t, part)
        dfirst = dfirst + dot_nt(part, w_ref[place])
    gln_ref[0:1, :] += jnp.sum(dfirst * normed, axis=0, keepdims=True)
    gln_ref[1:2, :] += jnp.sum(dfirst, axis=0, keepdims=True)
    grad_ref[...] = dx_ref[...] + norm_back(dfirst, normed, inverse, ln_ref[0:1, :])

    @pl.when(step == pl.num_programs(0) - 1)
    def _():
        gw_ref[...] = w_sum[...].astype(low_type)


def project_back(rows, dx, dq, dk, dv, de, weights, ln_params):
    count = rows.shape[0]
    block = 256
    row_spec = pl.BlockSpec((block, D), lambda i: (i, 0))

    def whole(*shape):
        return pl.BlockSpec(shape, lambda i: (0,) * len(shape))

    return pl.pallas_call(
        project_back_kernel,
        grid=(count // block,),
        in_specs=[row_spec] * 6 + [whole(4, D, D), whole(4, D)],
        out_specs=[row_spec, whole(4, D, D), whole(2, D)],
        out_shape=[
            jax.ShapeDtypeStruct((count, D), wide_type),
            jax.ShapeDtypeStruct((4, D, D), low_type),
            jax.ShapeDtypeStruct((2, D), wide_type),
        ],
        scratch_shapes=[pltpu.VMEM((4, D, D), wide_type)],
        compiler_params=pltpu.CompilerParams(vmem_limit_bytes=VMEM_BYTES),
        name="project_back",
    )(rows, dx, dq, dk, dv, de, weights, ln_params)


def newton_poly(gram):
    scale = jnp.sqrt(jnp.trace(gram)) + 1e-07
    eye = jnp.eye(D, dtype=wide_type)
    gram_one = gram * (1.0 / (scale * scale))
    poly_one = quintic_lin * eye + quintic_cube * gram_one + quintic_five * (gram_one @ gram_one)
    gram_two = (gram_one @ poly_one) @ poly_one
    poly_two = quintic_lin * eye + quintic_cube * gram_two + quintic_five * (gram_two @ gram_two)
    return (poly_one @ poly_two) * (1.0 / scale)


def sum_rows(stack, rows_at):
    wide = lax.axis_size("wide")
    narrow = lax.axis_size("narrow")
    mats = stack.shape[0]
    share = D // narrow // wide
    parts = stack.reshape(mats, narrow, wide, share, D)
    parts = lax.psum_scatter(parts, "wide", scatter_dimension=2, tiled=False)
    parts = lax.psum_scatter(parts, "narrow", scatter_dimension=1, tiled=False)
    return lax.all_gather(parts, "wide", axis=1, tiled=True)


def shards(
    tokens,
    out_grad,
    group_ids,
    domain_weight,
    attn_w,
    ffn_w,
    attn_mom,
    ffn_mom,
    ln_params,
    ln_first,
    ln_second,
):
    local_seqs, length, _ = tokens.shape
    token_count = local_seqs * length
    wide = lax.axis_size("wide")
    narrow = lax.axis_size("narrow")
    member = (group_ids[:, None] == jnp.arange(domain_weight.shape[0])[None, :]).astype(jnp.int32)
    group_count = lax.psum(jnp.sum(member, axis=0), ("wide", "narrow"))
    chosen = member.astype(wide_type)
    weight_of = jnp.sum(chosen * domain_weight[None, :], axis=1)
    count_of = jnp.sum(chosen * group_count[None, :].astype(wide_type), axis=1)
    total_seqs = local_seqs * wide * narrow
    seq_weight = weight_of * total_seqs / (domain_weight.shape[0] * count_of)

    attn_low = lax.all_gather(attn_w.astype(low_type), "narrow", axis=1, tiled=True)
    ffn_low = lax.all_gather(ffn_w.astype(low_type), "narrow", axis=1, tiled=True)
    rows = tokens.reshape(token_count, D)
    in_w, out_w = attn_low[:4], attn_low[4]
    q, k, v, a = project(rows, in_w, ln_params)
    head = (local_seqs, length, D)
    q, k, v, a = (item.reshape(head) for item in (q, k, v, a))
    att, share, logit, total, states = attend(q, k, v, a)
    output, dx, datt, gup, gdown, go, gln_two = feed(
        seq_weight,
        rows,
        att.reshape(token_count, D),
        out_grad.reshape(token_count, D),
        out_w,
        ffn_low,
        ln_params,
        length,
    )
    dq, dk, dv, de = attend_back(q, k, v, a, share, logit, total, datt.reshape(head), states)
    dq, dk, dv, de = (item.reshape(token_count, D) for item in (dq, dk, dv, de))
    input_grad, gw, gln_one = project_back(rows, dx, dq, dk, dv, de, in_w, ln_params)

    attn_grad = sum_rows(jnp.concatenate([gw, go[None]], axis=0), None).astype(wide_type)
    ffn_t = jnp.stack([gup, gdown])
    ffn_t = lax.psum_scatter(ffn_t, "wide", scatter_dimension=1, tiled=True)
    ffn_t = lax.psum_scatter(ffn_t, "narrow", scatter_dimension=2, tiled=True)
    ffn_t = lax.all_gather(ffn_t, "wide", axis=1, tiled=True)
    ffn_grad = jnp.swapaxes(ffn_t, 1, 2).astype(wide_type)
    ln_full = jnp.concatenate([gln_one, gln_two], axis=0)
    ln_sum = lax.psum(ln_full, ("wide", "narrow"))
    shard_width = ln_first.shape[1]
    ln_grad = lax.dynamic_slice_in_dim(
        ln_sum, lax.axis_index("narrow") * shard_width, shard_width, 1
    )

    attn_moment = momentum_keep * attn_mom + attn_grad
    ffn_moment = momentum_keep * ffn_mom + ffn_grad
    mats = attn_w.shape[0] + ffn_w.shape[0]
    attn_rows = attn_w.shape[1]
    ffn_rows = ffn_w.shape[1]
    padded = jnp.concatenate(
        [
            jnp.pad(attn_moment.astype(low_type), ((0, 0), (0, ffn_rows - attn_rows), (0, 0))),
            ffn_moment.astype(low_type),
        ],
        axis=0,
    )
    mine = lax.dynamic_index_in_dim(
        padded, jnp.minimum(lax.axis_index("wide"), mats - 1), 0, keepdims=False
    )
    gram = lax.psum(dot_tn(mine, mine), "narrow")
    poly = lax.all_gather(newton_poly(gram).astype(low_type), "wide", axis=0, tiled=False)[:mats]
    attn_ortho = jnp.einsum(
        "jrd,jde->jre",
        attn_moment.astype(low_type),
        poly[: attn_w.shape[0]],
        preferred_element_type=wide_type,
    )
    ffn_ortho = jnp.einsum(
        "jrd,jde->jre",
        ffn_moment.astype(low_type),
        poly[attn_w.shape[0] :],
        preferred_element_type=wide_type,
    )
    keep_factor = 1.0 - muon_rate * muon_decay
    attn_new = keep_factor * attn_w - muon_rate * 0.2 * math.sqrt(D) * attn_ortho
    ffn_new = keep_factor * ffn_w - muon_rate * 0.2 * math.sqrt(FF) * ffn_ortho
    own_params = lax.dynamic_slice_in_dim(
        ln_params, lax.axis_index("narrow") * shard_width, shard_width, 1
    )
    first_new = beta_first * ln_first + (1.0 - beta_first) * ln_grad
    second_new = beta_second * ln_second + (1.0 - beta_second) * ln_grad * ln_grad
    first_fix = 1.0 - beta_first**STEP
    second_fix = 1.0 - beta_second**STEP
    ln_new = own_params - adam_rate * (first_new / first_fix) / (
        jnp.sqrt(second_new / second_fix) + adam_epsilon
    )
    return (
        output.reshape(tokens.shape),
        input_grad.reshape(tokens.shape),
        attn_grad,
        ffn_grad,
        ln_grad,
        attn_moment,
        ffn_moment,
        attn_new,
        ffn_new,
        attn_new.astype(low_type),
        ffn_new.astype(low_type),
        first_new,
        second_new,
        ln_new,
    )


def solution(mesh):
    split = P(("wide", "narrow"), None, None)
    rows = P(None, "narrow", None)
    lanes = P(None, "narrow")
    inner = jax.shard_map(
        shards,
        mesh=mesh,
        in_specs=(
            split,
            split,
            P(("wide", "narrow")),
            P(),
            rows,
            rows,
            rows,
            rows,
            P(),
            lanes,
            lanes,
        ),
        out_specs=(
            split,
            split,
            rows,
            rows,
            lanes,
            rows,
            rows,
            rows,
            rows,
            rows,
            rows,
            lanes,
            lanes,
            lanes,
        ),
        check_vma=False,
    )
    return inner
```

```python
import functools
import math

import jax
import jax.numpy as jnp
from jax import lax
from jax.experimental import pallas as pl
from jax.experimental.pallas import tpu as pltpu
from jax.sharding import PartitionSpec as P

D = 512
HEADS = 8
HEAD_DIM = 64
FF = 2048
STEP = 10

norm_epsilon = 1e-05
momentum_keep = 0.5
quintic_lin = 3.4445
quintic_cube = -4.775
quintic_five = 2.0315
muon_rate = 0.7
muon_decay = 0.1
adam_rate = 0.2
beta_first = 0.9
beta_second = 0.999
adam_epsilon = 1e-08

CHUNK = 128
PAIR = 2 * HEAD_DIM
PAIRS = HEADS // 2
VMEM_BYTES = 60 * 1024 * 1024
low_type = jnp.bfloat16
wide_type = jnp.float32


def dot_nn(left, right):
    return lax.dot_general(left, right, (((1,), (0,)), ((), ())), preferred_element_type=wide_type)


def dot_nt(left, right):
    return lax.dot_general(left, right, (((1,), (1,)), ((), ())), preferred_element_type=wide_type)


def dot_tn(left, right):
    return lax.dot_general(left, right, (((0,), (0,)), ((), ())), preferred_element_type=wide_type)


def normalize(rows):
    center = rows - jnp.mean(rows, axis=-1, keepdims=True)
    spread = jnp.mean(center * center, axis=-1, keepdims=True)
    inverse = lax.rsqrt(spread + norm_epsilon)
    return center * inverse, inverse


def norm_back(grad_rows, normed, inverse, gain):
    grad_normed = grad_rows * gain
    mean_grad = jnp.mean(grad_normed, axis=-1, keepdims=True)
    mean_cross = jnp.mean(grad_normed * normed, axis=-1, keepdims=True)
    return inverse * (grad_normed - mean_grad - normed * mean_cross)


def lane_of(shape):
    return lax.broadcasted_iota(jnp.int32, shape, 1)


def row_of(shape):
    return lax.broadcasted_iota(jnp.int32, shape, 0)


def split_pair(pair, first_head):
    zero = jnp.zeros_like(pair)
    return jnp.concatenate(
        [jnp.where(first_head, pair, zero), jnp.where(first_head, zero, pair)], axis=0
    )


def head_reduce(values, first_head, op, neutral):
    left = op(jnp.where(first_head, values, neutral), axis=-1, keepdims=True)
    right = op(jnp.where(first_head, neutral, values), axis=-1, keepdims=True)
    return jnp.where(first_head, left, right)


def attend_back_kernel(
    q_ref,
    k_ref,
    v_ref,
    a_ref,
    share_ref,
    logit_ref,
    total_ref,
    datt_ref,
    state_ref,
    dq_ref,
    dk_ref,
    dv_ref,
    de_ref,
    state,
    carry,
):
    seqs = q_ref.shape[0]

    @pl.when(pl.program_id(0) == 0)
    def _():
        state[...] = jnp.zeros_like(state)
        carry[...] = jnp.zeros_like(carry)

    scaling = HEAD_DIM**-0.5
    first_head = lane_of((CHUNK, PAIR)) < HEAD_DIM
    causal = row_of((CHUNK, 2 * CHUNK)) >= lane_of((CHUNK, 2 * CHUNK)) % CHUNK
    anti = row_of((CHUNK, 2 * CHUNK)) <= lane_of((CHUNK, 2 * CHUNK)) % CHUNK
    same_head = (row_of((PAIR, 2 * PAIR)) // HEAD_DIM) == (
        (lane_of((PAIR, 2 * PAIR)) // HEAD_DIM) % 2
    )
    upper = (row_of((CHUNK, CHUNK)) <= lane_of((CHUNK, CHUNK))).astype(low_type)
    for seq in range(seqs):
        for pair in range(PAIRS):
            lanes = slice(pair * PAIR, (pair + 1) * PAIR)
            q = q_ref[seq, :, lanes] * low_type(scaling)
            k = k_ref[seq, :, lanes]
            v = v_ref[seq, :, lanes]
            a = a_ref[seq, :, lanes]
            share = share_ref[seq, :, lanes]
            logit = logit_ref[seq, :, lanes]
            total = total_ref[seq, :, lanes]
            datt = datt_ref[seq, :, lanes]
            inv = 1.0 / total
            before = state_ref[0, seq, pair]
            after = jnp.where(same_head, state[seq, pair], 0.0).astype(low_type)
            q_two = split_pair(q, first_head)
            k_two = split_pair(k, first_head)
            v_two = split_pair(v, first_head)
            a_two = split_pair(a, first_head)
            share_two = split_pair(share, first_head)
            datt_two = split_pair(datt, first_head)

            dmix = jnp.where(causal, dot_nt(datt, v_two), 0.0).astype(low_type)
            dshare = dot_nn(dmix, a_two) + dot_nt(datt, before[:, PAIR:])
            prob = share.astype(wide_type) * total
            dprob = dshare * inv
            dlogit = prob * (dprob - head_reduce(dprob * prob, first_head, jnp.sum, 0.0))
            dnumer = (dlogit * inv).astype(low_type)
            dtotal = -(dprob * prob + dlogit * logit) * inv
            dnumer_two = split_pair(dnumer, first_head)
            dscores = jnp.where(causal, dot_nt(dnumer, a_two), 0.0).astype(low_type)
            dq = (dot_nn(dscores, k_two) + dot_nn(dnumer, before[:, :PAIR])) * scaling
            dq_ref[seq, :, lanes] = dq.astype(low_type)

            mix_t = jnp.where(anti, dot_nt(a, share_two), 0.0).astype(low_type)
            dscores_t = jnp.where(anti, dot_nt(a, dnumer_two), 0.0).astype(low_type)
            dmix_t = jnp.where(anti, dot_nt(v, datt_two), 0.0).astype(low_type)
            scores_t = jnp.where(anti, dot_nt(k, q_two), 0.0).astype(low_type)
            later = dot_nn(a, after)
            dv = dot_nn(mix_t, datt_two) + later[:, PAIR:]
            dv_ref[seq, :, lanes] = dv.astype(low_type)
            dk = dot_nn(dscores_t, q_two) + later[:, :PAIR]
            dk_ref[seq, :, lanes] = dk.astype(low_type)

            dtotal_high = dtotal.astype(low_type)
            dtotal_low = (dtotal - dtotal_high.astype(wide_type)).astype(low_type)
            tail = (
                dot_nn(upper, dtotal_high)
                + dot_nn(upper, dtotal_low)
                + carry[seq, :, lanes]
            )
            carry[seq, :, lanes] = tail[0:1, :]
            da = (
                dot_nn(dmix_t, share_two)
                + dot_nn(scores_t, dnumer_two)
                + dot_nt(jnp.concatenate([k, v], axis=1), after)
                + tail
            )
            de = da.astype(low_type).astype(wide_type) * a.astype(wide_type)
            de_ref[seq, :, lanes] = de.astype(low_type)
            state[seq, pair, :, :PAIR] += dot_tn(dnumer, q)
            state[seq, pair, :, PAIR:] += dot_tn(share, datt)


def attend_back(q, k, v, a, share, logit, total, datt, states):
    seqs, length, _ = q.shape
    chunks = length // CHUNK
    block = pl.BlockSpec((seqs, CHUNK, D), lambda i: (0, chunks - 1 - i, 0))
    return pl.pallas_call(
        attend_back_kernel,
        grid=(chunks,),
        in_specs=[block] * 8
        + [
            pl.BlockSpec(
                (1, seqs, PAIRS, PAIR, 2 * PAIR), lambda i: (chunks - 1 - i, 0, 0, 0, 0)
            )
        ],
        out_specs=[block] * 4,
        out_shape=[jax.ShapeDtypeStruct(q.shape, low_type)] * 4,
        scratch_shapes=[
            pltpu.VMEM((seqs, PAIRS, PAIR, 2 * PAIR), wide_type),
            pltpu.VMEM((seqs, 1, D), wide_type),
        ],
        compiler_params=pltpu.CompilerParams(vmem_limit_bytes=VMEM_BYTES),
        name="attend_back",
    )(q, k, v, a, share, logit, total, datt, states)


FF_BLOCK = 512
gelu_root = math.sqrt(2.0 / math.pi)
gelu_cube = 0.044715


def feed_kernel(
    ids_ref,
    weight_ref,
    x_ref,
    att_ref,
    og_ref,
    wo_ref,
    ffn_ref,
    ln_ref,
    out_ref,
    dx_ref,
    datt_ref,
    gup_ref,
    gdown_ref,
    go_ref,
    gln_ref,
    up_sum,
    down_sum,
    o_sum,
    *,
    per_seq,
):
    step = pl.program_id(0)

    @pl.when(step == 0)
    def _():
        up_sum[...] = jnp.zeros_like(up_sum)
        down_sum[...] = jnp.zeros_like(down_sum)
        o_sum[...] = jnp.zeros_like(o_sum)
        gln_ref[...] = jnp.zeros_like(gln_ref)

    att = att_ref[...]
    mixed = x_ref[...].astype(wide_type) + dot_nn(att, wo_ref[...])
    normed, inverse = normalize(mixed)
    second = (normed * ln_ref[2:3, :] + ln_ref[3:4, :]).astype(low_type)
    mine = lane_of((1, LANES)) == ids_ref[step // per_seq]
    weight = jnp.sum(jnp.where(mine, weight_ref[0:1, :], 0.0), axis=1, keepdims=True)
    dout = og_ref[...].astype(wide_type) * weight
    dy = dout.astype(low_type)
    second_t = second.T
    dy_t = dy.T
    result = mixed
    dsecond = jnp.zeros_like(mixed)
    for part in range(FF // FF_BLOCK):
        rows = slice(part * FF_BLOCK, (part + 1) * FF_BLOCK)
        up = ffn_ref[0, rows, :]
        down = ffn_ref[1, rows, :]
        inner = dot_nt(second, up)
        square = inner * inner
        bend = jnp.tanh(inner * (gelu_root + (gelu_root * gelu_cube) * square))
        half = 0.5 + 0.5 * bend
        hidden = (inner * half).astype(low_type)
        slope = half + (0.5 * inner) * (1.0 - bend * bend) * (
            gelu_root + (3.0 * gelu_root * gelu_cube) * square
        )
        result = result + dot_nn(hidden, down)
        down_sum[:, rows] += dot_nn(dy_t, hidden)
        dinner = (dot_nt(dy, down) * slope).astype(low_type)
        up_sum[:, rows] += dot_nn(second_t, dinner)
        dsecond = dsecond + dot_nn(dinner, up)
    out_ref[...] = result.astype(low_type)
    gln_ref[0:1, :] += jnp.sum(dsecond * normed, axis=0, keepdims=True)
    gln_ref[1:2, :] += jnp.sum(dsecond, axis=0, keepdims=True)
    dmixed = dout + norm_back(dsecond, normed, inverse, ln_ref[2:3, :])
    dx_ref[...] = dmixed
    datt = dmixed.astype(low_type)
    o_sum[...] += dot_tn(att, datt)
    datt_ref[...] = dot_nt(datt, wo_ref[...]).astype(low_type)

    @pl.when(step == pl.num_programs(0) - 1)
    def _():
        gup_ref[...] = up_sum[...].astype(low_type)
        gdown_ref[...] = down_sum[...].astype(low_type)
        go_ref[...] = o_sum[...].astype(low_type)


def feed(ids, weights, rows, att, grad, wo, ffn, ln_params, length):
    count = rows.shape[0]
    block = 256
    row_spec = pl.BlockSpec((block, D), lambda i: (i, 0))

    def whole(*shape):
        return pl.BlockSpec(shape, lambda i: (0,) * len(shape))

    return pl.pallas_call(
        functools.partial(feed_kernel, per_seq=length // block),
        grid=(count // block,),
        in_specs=[
            pl.BlockSpec(memory_space=pltpu.SMEM),
            whole(8, LANES),
            row_spec,
            row_spec,
            row_spec,
            whole(D, D),
            whole(2, FF, D),
            whole(4, D),
        ],
        out_specs=[
            row_spec,
            row_spec,
            row_spec,
            whole(D, FF),
            whole(D, FF),
            whole(D, D),
            whole(2, D),
        ],
        out_shape=[
            jax.ShapeDtypeStruct((count, D), low_type),
            jax.ShapeDtypeStruct((count, D), wide_type),
            jax.ShapeDtypeStruct((count, D), low_type),
            jax.ShapeDtypeStruct((D, FF), low_type),
            jax.ShapeDtypeStruct((D, FF), low_type),
            jax.ShapeDtypeStruct((D, D), low_type),
            jax.ShapeDtypeStruct((2, D), wide_type),
        ],
        scratch_shapes=[
            pltpu.VMEM((D, FF), wide_type),
            pltpu.VMEM((D, FF), wide_type),
            pltpu.VMEM((D, D), wide_type),
        ],
        compiler_params=pltpu.CompilerParams(vmem_limit_bytes=VMEM_BYTES),
        name="feed",
    )(ids, weights, rows, att, grad, wo, ffn, ln_params)


def project_back_kernel(
    x_ref,
    dx_ref,
    dq_ref,
    dk_ref,
    dv_ref,
    de_ref,
    w_ref,
    ln_ref,
    grad_ref,
    gw_ref,
    gln_ref,
    w_sum,
):
    step = pl.program_id(0)

    @pl.when(step == 0)
    def _():
        w_sum[...] = jnp.zeros_like(w_sum)
        gln_ref[...] = jnp.zeros_like(gln_ref)

    normed, inverse = normalize(x_ref[...].astype(wide_type))
    first_t = (normed * ln_ref[0:1, :] + ln_ref[1:2, :]).astype(low_type).T
    dfirst = jnp.zeros(normed.shape, wide_type)
    for place, ref in enumerate((dq_ref, dk_ref, dv_ref, de_ref)):
        part = ref[...]
        w_sum[place] += dot_nn(first_t, part)
        dfirst = dfirst + dot_nt(part, w_ref[place])
    gln_ref[0:1, :] += jnp.sum(dfirst * normed, axis=0, keepdims=True)
    gln_ref[1:2, :] += jnp.sum(dfirst, axis=0, keepdims=True)
    grad_ref[...] = dx_ref[...] + norm_back(dfirst, normed, inverse, ln_ref[0:1, :])

    @pl.when(step == pl.num_programs(0) - 1)
    def _():
        gw_ref[...] = w_sum[...].astype(low_type)


def project_back(rows, dx, dq, dk, dv, de, weights, ln_params):
    count = rows.shape[0]
    block = 256
    row_spec = pl.BlockSpec((block, D), lambda i: (i, 0))

    def whole(*shape):
        return pl.BlockSpec(shape, lambda i: (0,) * len(shape))

    return pl.pallas_call(
        project_back_kernel,
        grid=(count // block,),
        in_specs=[row_spec] * 6 + [whole(4, D, D), whole(4, D)],
        out_specs=[row_spec, whole(4, D, D), whole(2, D)],
        out_shape=[
            jax.ShapeDtypeStruct((count, D), wide_type),
            jax.ShapeDtypeStruct((4, D, D), low_type),
            jax.ShapeDtypeStruct((2, D), wide_type),
        ],
        scratch_shapes=[pltpu.VMEM((4, D, D), wide_type)],
        compiler_params=pltpu.CompilerParams(vmem_limit_bytes=VMEM_BYTES),
        name="project_back",
    )(rows, dx, dq, dk, dv, de, weights, ln_params)


MESH = pl.DeviceIdType.MESH
LANES = 128


def remote(src, dst, send_sem, recv_sem, device):
    return pltpu.make_async_remote_copy(
        src_ref=src,
        dst_ref=dst,
        send_sem=send_sem,
        recv_sem=recv_sem,
        device_id=device,
        device_id_type=MESH,
    )


def greet(devices):
    barrier = pltpu.get_barrier_semaphore()
    for device in devices:
        pl.semaphore_signal(barrier, inc=1, device_id=device, device_id_type=MESH)
    pl.semaphore_wait(barrier, len(devices))


def attend_chunk(q_all, k_all, v_all, a_all, consts, refs, seq):
    first_head, causal, same_head, lower = consts
    att_ref, share_ref, logit_ref, total_ref, state_ref, state, carry = refs
    total_all = dot_nn(lower, a_all) + carry[seq]
    total_ref[seq] = total_all
    carry[seq] = total_all[CHUNK - 1 :, :]
    inv_all = 1.0 / total_all
    for pair in range(PAIRS):
        lanes = slice(pair * PAIR, (pair + 1) * PAIR)
        q = q_all[:, lanes] * low_type(HEAD_DIM**-0.5)
        k = k_all[:, lanes]
        v = v_all[:, lanes]
        a = a_all[:, lanes]
        inv = inv_all[:, lanes]
        a_two = split_pair(a, first_head)
        now = jnp.where(same_head, state[seq, pair], 0.0).astype(low_type)
        state_ref[0, seq, pair] = now
        scores = jnp.where(causal, dot_nt(q, split_pair(k, first_head)), 0.0).astype(low_type)
        numer = dot_nn(scores, a_two) + dot_nt(q, now[:, :PAIR])
        logit = numer * inv
        logit_ref[seq, :, lanes] = logit
        expo = jnp.exp(logit - head_reduce(logit, first_head, jnp.max, -jnp.inf))
        share = expo * (inv / head_reduce(expo, first_head, jnp.sum, 0.0))
        share = share.astype(low_type)
        share_ref[seq, :, lanes] = share
        mix = jnp.where(causal, dot_nt(share, a_two), 0.0).astype(low_type)
        att = dot_nn(mix, split_pair(v, first_head)) + dot_nn(share, now[:, PAIR:])
        att_ref[seq, :, lanes] = att.astype(low_type)
        state[seq, pair] += dot_tn(a, jnp.concatenate([k, v], axis=1))


def forward_kernel(
    ids_ref,
    dw_ref,
    x_ref,
    ln_ref,
    attn_ref,
    ffn_ref,
    q_ref,
    k_ref,
    v_ref,
    a_ref,
    att_ref,
    share_ref,
    logit_ref,
    total_ref,
    state_ref,
    weight_ref,
    in_hbm,
    out_hbm,
    ffn_hbm,
    state,
    carry,
    in_w,
    own,
    own_ffn,
    counts,
    counts_z,
    counts_w,
    in_send,
    in_recv,
    in_pass,
    in_got,
    ffn_send,
    ffn_recv,
    ffn_pass,
    ffn_got,
    out_send,
    out_recv,
    out_pass,
    out_got,
    cz_send,
    cz_recv,
    cw_send,
    cw_recv,
    local_sems,
    *,
    wide,
    narrow,
    total_seqs,
    groups,
):
    step = pl.program_id(0)
    steps = pl.num_programs(0)
    seqs = x_ref.shape[0]
    w = lax.axis_index("wide")
    z = lax.axis_index("narrow")
    core = lax.rem(w, 2)
    mate = (w + 1 - 2 * core, z)
    other = 1 - core
    rows = attn_ref.shape[1]
    ffn_rows = ffn_ref.shape[1]
    half = rows // 2
    hops = list(range(1, narrow))
    hops.sort(key=lambda hop: min(hop, narrow - hop))
    column = [(w, lax.rem(z + hop, narrow)) for hop in hops]
    plane = [(lax.rem(w + hop, wide), z) for hop in range(1, wide)]

    def at(owner, size):
        return pl.ds(pl.multiple_of(owner * size, size), size)

    def from_z(place):
        return lax.rem(z + narrow - hops[place], narrow)

    def half_at(owner, part):
        start = owner * rows + part * half
        return pl.ds(pl.multiple_of(start, half), half)

    def in_out(place):
        return remote(
            own.at[pl.ds(2 * core, 2)],
            in_w.at[pl.ds(2 * core, 2), at(z, rows)],
            in_send.at[place],
            in_recv.at[place],
            column[place],
        )

    def in_on(place):
        block = in_w.at[pl.ds(2 * core, 2), at(from_z(place), rows)]
        return remote(block, block, in_pass.at[place], in_got.at[place], mate)

    def ffn_out(place):
        return remote(
            own_ffn.at[core],
            ffn_hbm.at[core, at(z, ffn_rows)],
            ffn_send.at[place],
            ffn_recv.at[place],
            column[place],
        )

    def ffn_on(place):
        block = ffn_hbm.at[core, at(from_z(place), ffn_rows)]
        return remote(block, block, ffn_pass.at[place], ffn_got.at[place], mate)

    def out_out(place):
        return remote(
            own.at[4, pl.ds(pl.multiple_of(core * half, half), half)],
            out_hbm.at[half_at(z, core)],
            out_send.at[place],
            out_recv.at[place],
            column[place],
        )

    def out_on(place):
        block = out_hbm.at[half_at(from_z(place), core)]
        return remote(block, block, out_pass.at[place], out_got.at[place], mate)

    def count_z(place):
        return remote(
            counts, counts_z.at[place], cz_send.at[place], cz_recv.at[place], column[place]
        )

    def count_w(place):
        return remote(
            counts, counts_w.at[place], cw_send.at[place], cw_recv.at[place], plane[place]
        )

    keep_ffn = pltpu.make_async_copy(own_ffn, ffn_hbm.at[:, at(z, ffn_rows)], local_sems.at[0])
    keep_out = pltpu.make_async_copy(own.at[4], out_hbm.at[at(z, rows)], local_sems.at[1])
    keep_in = pltpu.make_async_copy(in_w, in_hbm, local_sems.at[2])

    @pl.when(step == 0)
    def _():
        state[...] = jnp.zeros_like(state)
        carry[...] = jnp.zeros_like(carry)
        own[...] = attn_ref[...].astype(low_type)
        greet(column + plane)
        for place in range(narrow - 1):
            in_out(place).start()
        for place in range(4):
            in_w[place, at(z, rows), :] = own[place]
        own_ffn[...] = ffn_ref[...].astype(low_type)
        lanes = lane_of((8, LANES))
        count = jnp.zeros((8, LANES), wide_type)
        for seq in range(seqs):
            count = count + (lanes == ids_ref[seq]).astype(wide_type)
        counts[...] = count
        for place in range(narrow - 1):
            in_out(place).wait_recv()
            in_on(place).start()
        for place in range(narrow - 1):
            count_z(place).start()
            ffn_out(place).start()
            out_out(place).start()
        keep_ffn.start()
        keep_out.start()
        for place in range(narrow - 1):
            in_on(place).wait_recv()
        keep_in.start()

    @pl.when(step == 1)
    def _():
        for place in range(narrow - 1):
            count_z(place).wait()
        total = counts[...]
        for place in range(narrow - 1):
            total = total + counts_z[place]
        counts[...] = total
        for place in range(wide - 1):
            count_w(place).start()

    @pl.when(step == 2)
    def _():
        for place in range(wide - 1):
            count_w(place).wait()
        total = counts[...]
        for place in range(wide - 1):
            total = total + counts_w[place]
        lanes = lane_of((8, LANES))
        values = jnp.zeros((8, LANES), wide_type)
        for group in range(groups):
            values = values + jnp.where(lanes == group, dw_ref[group], 0.0)
        weight_ref[...] = values * total_seqs / (groups * jnp.maximum(total, 1.0))

    @pl.when(step == steps - 3)
    def _():
        for place in range(narrow - 1):
            out_out(place).wait_recv()
            out_on(place).start()
            ffn_out(place).wait_recv()
            ffn_on(place).start()

    first_head = lane_of((CHUNK, PAIR)) < HEAD_DIM
    causal = row_of((CHUNK, 2 * CHUNK)) >= lane_of((CHUNK, 2 * CHUNK)) % CHUNK
    same_head = (row_of((PAIR, 2 * PAIR)) // HEAD_DIM) == (
        (lane_of((PAIR, 2 * PAIR)) // HEAD_DIM) % 2
    )
    lower = (row_of((CHUNK, CHUNK)) >= lane_of((CHUNK, CHUNK))).astype(low_type)
    normed, _ = normalize(x_ref[...].reshape(seqs * CHUNK, D).astype(wide_type))
    first = (normed * ln_ref[0:1, :] + ln_ref[1:2, :]).astype(low_type)
    q_all = dot_nn(first, in_w[0]).astype(low_type)
    k_all = dot_nn(first, in_w[1]).astype(low_type)
    v_all = dot_nn(first, in_w[2]).astype(low_type)
    a_all = jnp.exp(dot_nn(first, in_w[3])).astype(low_type)
    q_ref[...] = q_all.reshape(q_ref.shape)
    k_ref[...] = k_all.reshape(q_ref.shape)
    v_ref[...] = v_all.reshape(q_ref.shape)
    a_ref[...] = a_all.reshape(q_ref.shape)
    for seq in range(seqs):
        part = slice(seq * CHUNK, (seq + 1) * CHUNK)
        attend_chunk(
            q_all[part],
            k_all[part],
            v_all[part],
            a_all[part],
            (first_head, causal, same_head, lower),
            (att_ref, share_ref, logit_ref, total_ref, state_ref, state, carry),
            seq,
        )

    @pl.when(step == steps - 1)
    def _():
        keep_ffn.wait()
        keep_out.wait()
        keep_in.wait()
        for place in range(narrow - 1):
            in_out(place).wait_send()
            in_on(place).wait_send()
            out_out(place).wait_send()
            out_on(place).wait()
            ffn_out(place).wait_send()
            ffn_on(place).wait()


def forward(tokens, ids, dw, ln_params, attn_w, ffn_w):
    seqs, length, _ = tokens.shape
    chunks = length // CHUNK
    wide = lax.axis_size("wide")
    narrow = lax.axis_size("narrow")
    block = pl.BlockSpec((seqs, CHUNK, D), lambda i: (0, i, 0))
    low_out = jax.ShapeDtypeStruct(tokens.shape, low_type)
    wide_out = jax.ShapeDtypeStruct(tokens.shape, wide_type)
    any_spec = pl.BlockSpec(memory_space=pl.ANY)
    near, far = (narrow - 1,), (wide - 1,)

    def whole(*shape):
        return pl.BlockSpec(shape, lambda i: (0,) * len(shape))

    return pl.pallas_call(
        functools.partial(
            forward_kernel,
            wide=wide,
            narrow=narrow,
            total_seqs=seqs * wide * narrow,
            groups=dw.shape[0],
        ),
        grid=(chunks,),
        in_specs=[
            pl.BlockSpec(memory_space=pltpu.SMEM),
            pl.BlockSpec(memory_space=pltpu.SMEM),
            block,
            whole(4, D),
            whole(*attn_w.shape),
            whole(*ffn_w.shape),
        ],
        out_specs=[block] * 8
        + [
            pl.BlockSpec((1, seqs, PAIRS, PAIR, 2 * PAIR), lambda i: (i, 0, 0, 0, 0)),
            whole(8, LANES),
            any_spec,
            any_spec,
            any_spec,
        ],
        out_shape=[low_out] * 6
        + [
            wide_out,
            wide_out,
            jax.ShapeDtypeStruct((chunks, seqs, PAIRS, PAIR, 2 * PAIR), low_type),
            jax.ShapeDtypeStruct((8, LANES), wide_type),
            jax.ShapeDtypeStruct((4, D, D), low_type),
            jax.ShapeDtypeStruct((D, D), low_type),
            jax.ShapeDtypeStruct((2, FF, D), low_type),
        ],
        scratch_shapes=[
            pltpu.VMEM((seqs, PAIRS, PAIR, 2 * PAIR), wide_type),
            pltpu.VMEM((seqs, 1, D), wide_type),
            pltpu.VMEM((4, D, D), low_type),
            pltpu.VMEM(attn_w.shape, low_type),
            pltpu.VMEM(ffn_w.shape, low_type),
            pltpu.VMEM((8, LANES), wide_type),
            pltpu.VMEM((narrow - 1, 8, LANES), wide_type),
            pltpu.VMEM((wide - 1, 8, LANES), wide_type),
        ]
        + [pltpu.SemaphoreType.DMA(near)] * 14
        + [pltpu.SemaphoreType.DMA(far)] * 2
        + [pltpu.SemaphoreType.DMA((3,))],
        compiler_params=pltpu.CompilerParams(
            vmem_limit_bytes=VMEM_BYTES, collective_id=0, has_side_effects=True
        ),
        name="forward",
    )(ids, dw, tokens, ln_params, attn_w, ffn_w)


def newton_poly(gram):
    scale = jnp.sqrt(jnp.trace(gram)) + 1e-07
    eye = jnp.eye(D, dtype=wide_type)
    gram_one = gram * (1.0 / (scale * scale))
    poly_one = quintic_lin * eye + quintic_cube * gram_one + quintic_five * (gram_one @ gram_one)
    gram_two = (gram_one @ poly_one) @ poly_one
    poly_two = quintic_lin * eye + quintic_cube * gram_two + quintic_five * (gram_two @ gram_two)
    return (poly_one @ poly_two) * (1.0 / scale)


def sum_rows(stack, rows_at):
    wide = lax.axis_size("wide")
    narrow = lax.axis_size("narrow")
    mats = stack.shape[0]
    share = D // narrow // wide
    parts = stack.reshape(mats, narrow, wide, share, D)
    parts = lax.psum_scatter(parts, "wide", scatter_dimension=2, tiled=False)
    parts = lax.psum_scatter(parts, "narrow", scatter_dimension=1, tiled=False)
    return lax.all_gather(parts, "wide", axis=1, tiled=True)


def shards(
    tokens,
    out_grad,
    group_ids,
    domain_weight,
    attn_w,
    ffn_w,
    attn_mom,
    ffn_mom,
    ln_params,
    ln_first,
    ln_second,
):
    local_seqs, length, _ = tokens.shape
    token_count = local_seqs * length
    wide = lax.axis_size("wide")
    narrow = lax.axis_size("narrow")
    rows = tokens.reshape(token_count, D)
    head = (local_seqs, length, D)
    q, k, v, a, att, share, logit, total, states, weights, in_w, out_w, ffn_low = forward(
        tokens, group_ids, domain_weight, ln_params, attn_w, ffn_w
    )
    output, dx, datt, gup, gdown, go, gln_two = feed(
        group_ids,
        weights,
        rows,
        att.reshape(token_count, D),
        out_grad.reshape(token_count, D),
        out_w,
        ffn_low,
        ln_params,
        length,
    )
    dq, dk, dv, de = attend_back(q, k, v, a, share, logit, total, datt.reshape(head), states)
    dq, dk, dv, de = (item.reshape(token_count, D) for item in (dq, dk, dv, de))
    input_grad, gw, gln_one = project_back(rows, dx, dq, dk, dv, de, in_w, ln_params)

    attn_grad = sum_rows(jnp.concatenate([gw, go[None]], axis=0), None).astype(wide_type)
    ffn_t = jnp.stack([gup, gdown])
    ffn_t = lax.psum_scatter(ffn_t, "wide", scatter_dimension=1, tiled=True)
    ffn_t = lax.psum_scatter(ffn_t, "narrow", scatter_dimension=2, tiled=True)
    ffn_t = lax.all_gather(ffn_t, "wide", axis=1, tiled=True)
    ffn_grad = jnp.swapaxes(ffn_t, 1, 2).astype(wide_type)
    ln_full = jnp.concatenate([gln_one, gln_two], axis=0)
    ln_sum = lax.psum(ln_full, ("wide", "narrow"))
    shard_width = ln_first.shape[1]
    ln_grad = lax.dynamic_slice_in_dim(
        ln_sum, lax.axis_index("narrow") * shard_width, shard_width, 1
    )

    attn_moment = momentum_keep * attn_mom + attn_grad
    ffn_moment = momentum_keep * ffn_mom + ffn_grad
    mats = attn_w.shape[0] + ffn_w.shape[0]
    attn_rows = attn_w.shape[1]
    ffn_rows = ffn_w.shape[1]
    padded = jnp.concatenate(
        [
            jnp.pad(attn_moment.astype(low_type), ((0, 0), (0, ffn_rows - attn_rows), (0, 0))),
            ffn_moment.astype(low_type),
        ],
        axis=0,
    )
    mine = lax.dynamic_index_in_dim(
        padded, jnp.minimum(lax.axis_index("wide"), mats - 1), 0, keepdims=False
    )
    gram = lax.psum(dot_tn(mine, mine), "narrow")
    poly = lax.all_gather(newton_poly(gram).astype(low_type), "wide", axis=0, tiled=False)[:mats]
    attn_ortho = jnp.einsum(
        "jrd,jde->jre",
        attn_moment.astype(low_type),
        poly[: attn_w.shape[0]],
        preferred_element_type=wide_type,
    )
    ffn_ortho = jnp.einsum(
        "jrd,jde->jre",
        ffn_moment.astype(low_type),
        poly[attn_w.shape[0] :],
        preferred_element_type=wide_type,
    )
    keep_factor = 1.0 - muon_rate * muon_decay
    attn_new = keep_factor * attn_w - muon_rate * 0.2 * math.sqrt(D) * attn_ortho
    ffn_new = keep_factor * ffn_w - muon_rate * 0.2 * math.sqrt(FF) * ffn_ortho
    own_params = lax.dynamic_slice_in_dim(
        ln_params, lax.axis_index("narrow") * shard_width, shard_width, 1
    )
    first_new = beta_first * ln_first + (1.0 - beta_first) * ln_grad
    second_new = beta_second * ln_second + (1.0 - beta_second) * ln_grad * ln_grad
    first_fix = 1.0 - beta_first**STEP
    second_fix = 1.0 - beta_second**STEP
    ln_new = own_params - adam_rate * (first_new / first_fix) / (
        jnp.sqrt(second_new / second_fix) + adam_epsilon
    )
    return (
        output.reshape(tokens.shape),
        input_grad.reshape(tokens.shape),
        attn_grad,
        ffn_grad,
        ln_grad,
        attn_moment,
        ffn_moment,
        attn_new,
        ffn_new,
        attn_new.astype(low_type),
        ffn_new.astype(low_type),
        first_new,
        second_new,
        ln_new,
    )


def solution(mesh):
    split = P(("wide", "narrow"), None, None)
    rows = P(None, "narrow", None)
    lanes = P(None, "narrow")
    inner = jax.shard_map(
        shards,
        mesh=mesh,
        in_specs=(
            split,
            split,
            P(("wide", "narrow")),
            P(),
            rows,
            rows,
            rows,
            rows,
            P(),
            lanes,
            lanes,
        ),
        out_specs=(
            split,
            split,
            rows,
            rows,
            lanes,
            rows,
            rows,
            rows,
            rows,
            rows,
            rows,
            lanes,
            lanes,
            lanes,
        ),
        check_vma=False,
    )
    return inner
```

```python
import functools
import math

import jax
import jax.numpy as jnp
from jax import lax
from jax.experimental import pallas as pl
from jax.experimental.pallas import tpu as pltpu
from jax.sharding import PartitionSpec as P

D = 512
HEADS = 8
HEAD_DIM = 64
FF = 2048
STEP = 10

norm_epsilon = 1e-05
momentum_keep = 0.5
quintic_lin = 3.4445
quintic_cube = -4.775
quintic_five = 2.0315
muon_rate = 0.7
muon_decay = 0.1
adam_rate = 0.2
beta_first = 0.9
beta_second = 0.999
adam_epsilon = 1e-08

CHUNK = 128
PAIR = 2 * HEAD_DIM
PAIRS = HEADS // 2
VMEM_BYTES = 60 * 1024 * 1024
low_type = jnp.bfloat16
wide_type = jnp.float32


def dot_nn(left, right):
    return lax.dot_general(left, right, (((1,), (0,)), ((), ())), preferred_element_type=wide_type)


def dot_nt(left, right):
    return lax.dot_general(left, right, (((1,), (1,)), ((), ())), preferred_element_type=wide_type)


def dot_tn(left, right):
    return lax.dot_general(left, right, (((0,), (0,)), ((), ())), preferred_element_type=wide_type)


def normalize(rows):
    center = rows - jnp.mean(rows, axis=-1, keepdims=True)
    spread = jnp.mean(center * center, axis=-1, keepdims=True)
    inverse = lax.rsqrt(spread + norm_epsilon)
    return center * inverse, inverse


def norm_back(grad_rows, normed, inverse, gain):
    grad_normed = grad_rows * gain
    mean_grad = jnp.mean(grad_normed, axis=-1, keepdims=True)
    mean_cross = jnp.mean(grad_normed * normed, axis=-1, keepdims=True)
    return inverse * (grad_normed - mean_grad - normed * mean_cross)


def lane_of(shape):
    return lax.broadcasted_iota(jnp.int32, shape, 1)


def row_of(shape):
    return lax.broadcasted_iota(jnp.int32, shape, 0)


def split_pair(pair, first_head):
    zero = jnp.zeros_like(pair)
    return jnp.concatenate(
        [jnp.where(first_head, pair, zero), jnp.where(first_head, zero, pair)], axis=0
    )


def head_reduce(values, first_head, op, neutral):
    left = op(jnp.where(first_head, values, neutral), axis=-1, keepdims=True)
    right = op(jnp.where(first_head, neutral, values), axis=-1, keepdims=True)
    return jnp.where(first_head, left, right)


def attend_back_chunk(refs, state, carry):
    (
        q_ref,
        k_ref,
        v_ref,
        a_ref,
        share_ref,
        logit_ref,
        before_ref,
        datt_ref,
        state_ref,
        dq_ref,
        dk_ref,
        dv_ref,
        de_ref,
    ) = refs
    scaling = HEAD_DIM**-0.5
    first_head = lane_of((CHUNK, PAIR)) < HEAD_DIM
    causal = row_of((CHUNK, 2 * CHUNK)) >= lane_of((CHUNK, 2 * CHUNK)) % CHUNK
    anti = row_of((CHUNK, 2 * CHUNK)) <= lane_of((CHUNK, 2 * CHUNK)) % CHUNK
    same_head = (row_of((PAIR, 2 * PAIR)) // HEAD_DIM) == (
        (lane_of((PAIR, 2 * PAIR)) // HEAD_DIM) % 2
    )
    lower = (row_of((CHUNK, CHUNK)) >= lane_of((CHUNK, CHUNK))).astype(low_type)
    upper = (row_of((CHUNK, CHUNK)) <= lane_of((CHUNK, CHUNK))).astype(low_type)

    def masked(mask, raw):
        return jnp.where(mask, raw, 0.0).astype(low_type)

    items = []
    for seq in range(q_ref.shape[0]):
        total = dot_nn(lower, a_ref[seq]) + before_ref[0, seq]
        inv = 1.0 / total
        for pair in range(PAIRS):
            lanes = slice(pair * PAIR, (pair + 1) * PAIR)
            items.append(
                dict(seq=seq, pair=pair, lanes=lanes, total=total[:, lanes], inv=inv[:, lanes])
            )

    def load(t):
        seq, lanes = t["seq"], t["lanes"]
        t["k"] = k_ref[seq, :, lanes]
        t["v"] = v_ref[seq, :, lanes]
        t["a"] = a_ref[seq, :, lanes]
        t["share"] = share_ref[seq, :, lanes]
        t["datt"] = datt_ref[seq, :, lanes]
        t["q"] = q_ref[seq, :, lanes] * low_type(scaling)
        t["before"] = state_ref[0, seq, t["pair"]]
        t["after"] = jnp.where(same_head, state[seq, t["pair"]], 0.0).astype(low_type)
        t["v_two"] = split_pair(t["v"], first_head)
        t["a_two"] = split_pair(t["a"], first_head)
        t["dmix"] = masked(causal, dot_nt(t["datt"], t["v_two"]))

    def gather(t):
        t["share_two"] = split_pair(t["share"], first_head)
        t["datt_two"] = split_pair(t["datt"], first_head)
        t["dshare"] = dot_nn(t["dmix"], t["a_two"]) + dot_nt(t["datt"], t["before"][:, PAIR:])

    def soften(t):
        logit = logit_ref[t["seq"], :, t["lanes"]].astype(wide_type)
        prob = t["share"].astype(wide_type) * t["total"]
        cross = t["dshare"] * t["inv"] * prob
        dlogit = cross - prob * head_reduce(cross, first_head, jnp.sum, 0.0)
        t["dnumer"] = (dlogit * t["inv"]).astype(low_type)
        t["dtotal"] = -(cross + dlogit * logit) * t["inv"]
        t["mix_t"] = masked(anti, dot_nt(t["a"], t["share_two"]))
        t["dmix_t"] = masked(anti, dot_nt(t["v"], t["datt_two"]))

    def blend(t):
        t["dnumer_two"] = split_pair(t["dnumer"], first_head)
        t["dscores"] = masked(causal, dot_nt(t["dnumer"], t["a_two"]))
        t["dscores_t"] = masked(anti, dot_nt(t["a"], t["dnumer_two"]))
        t["k_two"] = split_pair(t["k"], first_head)
        t["q_two"] = split_pair(t["q"], first_head)
        t["scores_t"] = masked(anti, dot_nt(t["k"], t["q_two"]))
        t["later"] = dot_nn(t["a"], t["after"])

    def finish(t):
        seq, lanes = t["seq"], t["lanes"]
        dq = dot_nn(t["dscores"], t["k_two"]) + dot_nn(t["dnumer"], t["before"][:, :PAIR])
        dq_ref[seq, :, lanes] = (dq * scaling).astype(low_type)
        dv = dot_nn(t["mix_t"], t["datt_two"]) + t["later"][:, PAIR:]
        dv_ref[seq, :, lanes] = dv.astype(low_type)
        dk = dot_nn(t["dscores_t"], t["q_two"]) + t["later"][:, :PAIR]
        dk_ref[seq, :, lanes] = dk.astype(low_type)
        high = t["dtotal"].astype(low_type)
        rest = (t["dtotal"] - high.astype(wide_type)).astype(low_type)
        tail = dot_nn(upper, high) + dot_nn(upper, rest) + carry[seq, :, lanes]
        carry[seq, :, lanes] = tail[0:1, :]
        da = dot_nn(t["dmix_t"], t["share_two"]) + dot_nn(t["scores_t"], t["dnumer_two"])
        da = da + dot_nt(jnp.concatenate([t["k"], t["v"]], axis=1), t["after"]) + tail
        de = da.astype(low_type).astype(wide_type) * t["a"].astype(wide_type)
        de_ref[seq, :, lanes] = de.astype(low_type)
        state[seq, t["pair"], :, :PAIR] += dot_tn(t["dnumer"], t["q"])
        state[seq, t["pair"], :, PAIR:] += dot_tn(t["share"], t["datt"])

    for stage in (load, gather, soften, blend, finish):
        for item in items:
            stage(item)


def attend_back_kernel(*refs):
    *blocks, state, carry = refs

    @pl.when(pl.program_id(0) == 0)
    def _():
        state[...] = jnp.zeros_like(state)
        carry[...] = jnp.zeros_like(carry)

    attend_back_chunk(blocks, state, carry)


def attend_back(q, k, v, a, share, logit, before, datt, states):
    seqs, length, _ = q.shape
    chunks = length // CHUNK
    block = pl.BlockSpec((seqs, CHUNK, D), lambda i: (0, chunks - 1 - i, 0))
    return pl.pallas_call(
        attend_back_kernel,
        grid=(chunks,),
        in_specs=[block] * 6
        + [
            pl.BlockSpec((1, seqs, 1, D), lambda i: (chunks - 1 - i, 0, 0, 0)),
            block,
            pl.BlockSpec(
                (1, seqs, PAIRS, PAIR, 2 * PAIR), lambda i: (chunks - 1 - i, 0, 0, 0, 0)
            ),
        ],
        out_specs=[block] * 4,
        out_shape=[jax.ShapeDtypeStruct(q.shape, low_type)] * 4,
        scratch_shapes=[
            pltpu.VMEM((seqs, PAIRS, PAIR, 2 * PAIR), wide_type),
            pltpu.VMEM((seqs, 1, D), wide_type),
        ],
        compiler_params=pltpu.CompilerParams(vmem_limit_bytes=VMEM_BYTES),
        name="attend_back",
    )(q, k, v, a, share, logit, before, datt, states)


FF_BLOCK = 512
gelu_root = math.sqrt(2.0 / math.pi)
gelu_cube = 0.044715


def feed_kernel(
    ids_ref,
    weight_ref,
    x_ref,
    att_ref,
    og_ref,
    wo_ref,
    ffn_ref,
    ln_ref,
    out_ref,
    dx_ref,
    datt_ref,
    gup_ref,
    gdown_ref,
    go_ref,
    gln_ref,
    up_sum,
    down_sum,
    o_sum,
    *,
    per_seq,
):
    step = pl.program_id(0)

    @pl.when(step == 0)
    def _():
        up_sum[...] = jnp.zeros_like(up_sum)
        down_sum[...] = jnp.zeros_like(down_sum)
        o_sum[...] = jnp.zeros_like(o_sum)
        gln_ref[...] = jnp.zeros_like(gln_ref)

    att = att_ref[...]
    mixed = x_ref[...].astype(wide_type) + dot_nn(att, wo_ref[...])
    normed, inverse = normalize(mixed)
    second = (normed * ln_ref[2:3, :] + ln_ref[3:4, :]).astype(low_type)
    mine = lane_of((1, LANES)) == ids_ref[step // per_seq]
    weight = jnp.sum(jnp.where(mine, weight_ref[0:1, :], 0.0), axis=1, keepdims=True)
    dout = og_ref[...].astype(wide_type) * weight
    dy = dout.astype(low_type)
    second_t = second.T
    dy_t = dy.T
    parts = [dict(rows=slice(part * FF_BLOCK, (part + 1) * FF_BLOCK)) for part in range(FF // FF_BLOCK)]

    def open_part(t):
        t["up"] = ffn_ref[0, t["rows"], :]
        t["down"] = ffn_ref[1, t["rows"], :]
        t["inner"] = dot_nt(second, t["up"])
        t["dhidden"] = dot_nt(dy, t["down"])

    result, dsecond = mixed, 0.0
    open_part(parts[0])
    for place, t in enumerate(parts):
        if place + 1 < len(parts):
            open_part(parts[place + 1])
        inner = t["inner"]
        square = inner * inner
        bend = jnp.tanh(inner * (gelu_root + (gelu_root * gelu_cube) * square))
        half = 0.5 + 0.5 * bend
        hidden = (inner * half).astype(low_type)
        slope = half + (0.5 * inner) * (1.0 - bend * bend) * (
            gelu_root + (3.0 * gelu_root * gelu_cube) * square
        )
        dinner = (t["dhidden"] * slope).astype(low_type)
        result = result + dot_nn(hidden, t["down"])
        down_sum[:, t["rows"]] += dot_nn(dy_t, hidden)
        up_sum[:, t["rows"]] += dot_nn(second_t, dinner)
        dsecond = dsecond + dot_nn(dinner, t["up"])
    out_ref[...] = result.astype(low_type)
    gln_ref[0:1, :] += jnp.sum(dsecond * normed, axis=0, keepdims=True)
    gln_ref[1:2, :] += jnp.sum(dsecond, axis=0, keepdims=True)
    dmixed = dout + norm_back(dsecond, normed, inverse, ln_ref[2:3, :])
    dx_ref[...] = dmixed
    datt = dmixed.astype(low_type)
    o_sum[...] += dot_tn(att, datt)
    datt_ref[...] = dot_nt(datt, wo_ref[...]).astype(low_type)

    @pl.when(step == pl.num_programs(0) - 1)
    def _():
        gup_ref[...] = up_sum[...].astype(low_type)
        gdown_ref[...] = down_sum[...].astype(low_type)
        go_ref[...] = o_sum[...].astype(low_type)


def feed(ids, weights, rows, att, grad, wo, ffn, ln_params, length):
    count = rows.shape[0]
    block = 512
    row_spec = pl.BlockSpec((block, D), lambda i: (i, 0))

    def whole(*shape):
        return pl.BlockSpec(shape, lambda i: (0,) * len(shape))

    return pl.pallas_call(
        functools.partial(feed_kernel, per_seq=length // block),
        grid=(count // block,),
        in_specs=[
            pl.BlockSpec(memory_space=pltpu.SMEM),
            whole(8, LANES),
            row_spec,
            row_spec,
            row_spec,
            whole(D, D),
            whole(2, FF, D),
            whole(4, D),
        ],
        out_specs=[
            row_spec,
            row_spec,
            row_spec,
            whole(D, FF),
            whole(D, FF),
            whole(D, D),
            whole(2, D),
        ],
        out_shape=[
            jax.ShapeDtypeStruct((count, D), low_type),
            jax.ShapeDtypeStruct((count, D), wide_type),
            jax.ShapeDtypeStruct((count, D), low_type),
            jax.ShapeDtypeStruct((D, FF), low_type),
            jax.ShapeDtypeStruct((D, FF), low_type),
            jax.ShapeDtypeStruct((D, D), low_type),
            jax.ShapeDtypeStruct((2, D), wide_type),
        ],
        scratch_shapes=[
            pltpu.VMEM((D, FF), wide_type),
            pltpu.VMEM((D, FF), wide_type),
            pltpu.VMEM((D, D), wide_type),
        ],
        compiler_params=pltpu.CompilerParams(vmem_limit_bytes=VMEM_BYTES),
        name="feed",
    )(ids, weights, rows, att, grad, wo, ffn, ln_params)


def project_back_kernel(
    x_ref,
    dx_ref,
    dq_ref,
    dk_ref,
    dv_ref,
    de_ref,
    w_ref,
    ln_ref,
    grad_ref,
    gw_ref,
    gln_ref,
    w_sum,
):
    step = pl.program_id(0)

    @pl.when(step == 0)
    def _():
        w_sum[...] = jnp.zeros_like(w_sum)
        gln_ref[...] = jnp.zeros_like(gln_ref)

    parts = (dq_ref, dk_ref, dv_ref, de_ref)
    dfirst = dot_nt(dq_ref[...], w_ref[0])
    for place in range(1, 4):
        dfirst = dfirst + dot_nt(parts[place][...], w_ref[place])
    normed, inverse = normalize(x_ref[...].astype(wide_type))
    first_t = (normed * ln_ref[0:1, :] + ln_ref[1:2, :]).astype(low_type).T
    for place in range(4):
        w_sum[place] += dot_nn(first_t, parts[place][...])
    gln_ref[0:1, :] += jnp.sum(dfirst * normed, axis=0, keepdims=True)
    gln_ref[1:2, :] += jnp.sum(dfirst, axis=0, keepdims=True)
    grad_ref[...] = dx_ref[...] + norm_back(dfirst, normed, inverse, ln_ref[0:1, :])

    @pl.when(step == pl.num_programs(0) - 1)
    def _():
        gw_ref[...] = w_sum[...].astype(low_type)


def project_back(rows, dx, dq, dk, dv, de, weights, ln_params):
    count = rows.shape[0]
    block = 512
    row_spec = pl.BlockSpec((block, D), lambda i: (i, 0))

    def whole(*shape):
        return pl.BlockSpec(shape, lambda i: (0,) * len(shape))

    return pl.pallas_call(
        project_back_kernel,
        grid=(count // block,),
        in_specs=[row_spec] * 6 + [whole(4, D, D), whole(4, D)],
        out_specs=[row_spec, whole(4, D, D), whole(2, D)],
        out_shape=[
            jax.ShapeDtypeStruct((count, D), wide_type),
            jax.ShapeDtypeStruct((4, D, D), low_type),
            jax.ShapeDtypeStruct((2, D), wide_type),
        ],
        scratch_shapes=[pltpu.VMEM((4, D, D), wide_type)],
        compiler_params=pltpu.CompilerParams(vmem_limit_bytes=VMEM_BYTES),
        name="project_back",
    )(rows, dx, dq, dk, dv, de, weights, ln_params)


MESH = pl.DeviceIdType.MESH
LANES = 128


def remote(src, dst, send_sem, recv_sem, device):
    return pltpu.make_async_remote_copy(
        src_ref=src,
        dst_ref=dst,
        send_sem=send_sem,
        recv_sem=recv_sem,
        device_id=device,
        device_id_type=MESH,
    )


def greet(devices):
    barrier = pltpu.get_barrier_semaphore()
    for device in devices:
        pl.semaphore_signal(barrier, inc=1, device_id=device, device_id_type=MESH)
    pl.semaphore_wait(barrier, len(devices))


def attend_chunks(q_all, k_all, v_all, a_all, refs, seqs):
    att_ref, share_ref, logit_ref, before_ref, state_ref, state, carry = refs
    first_head = lane_of((CHUNK, PAIR)) < HEAD_DIM
    causal = row_of((CHUNK, 2 * CHUNK)) >= lane_of((CHUNK, 2 * CHUNK)) % CHUNK
    same_head = (row_of((PAIR, 2 * PAIR)) // HEAD_DIM) == (
        (lane_of((PAIR, 2 * PAIR)) // HEAD_DIM) % 2
    )
    lower = (row_of((CHUNK, CHUNK)) >= lane_of((CHUNK, CHUNK))).astype(low_type)
    items = []
    for seq in range(seqs):
        part = slice(seq * CHUNK, (seq + 1) * CHUNK)
        before = carry[seq]
        before_ref[0, seq] = before
        total = dot_nn(lower, a_all[part]) + before
        carry[seq] = total[CHUNK - 1 :, :]
        inv = 1.0 / total
        for pair in range(PAIRS):
            lanes = slice(pair * PAIR, (pair + 1) * PAIR)
            items.append(
                dict(
                    seq=seq,
                    pair=pair,
                    lanes=lanes,
                    q=q_all[part, lanes] * low_type(HEAD_DIM**-0.5),
                    k=k_all[part, lanes],
                    v=v_all[part, lanes],
                    a=a_all[part, lanes],
                    inv=inv[:, lanes],
                )
            )

    def score(t):
        t["a_two"] = split_pair(t["a"], first_head)
        t["now"] = jnp.where(same_head, state[t["seq"], t["pair"]], 0.0).astype(low_type)
        state_ref[0, t["seq"], t["pair"]] = t["now"]
        raw = dot_nt(t["q"], split_pair(t["k"], first_head))
        t["scores"] = jnp.where(causal, raw, 0.0).astype(low_type)

    def gather(t):
        numer = dot_nn(t["scores"], t["a_two"]) + dot_nt(t["q"], t["now"][:, :PAIR])
        t["logit"] = numer * t["inv"]
        logit_ref[t["seq"], :, t["lanes"]] = t["logit"].astype(low_type)

    def soften(t):
        expo = jnp.exp(t["logit"] - head_reduce(t["logit"], first_head, jnp.max, -jnp.inf))
        share = expo * (t["inv"] / head_reduce(expo, first_head, jnp.sum, 0.0))
        t["share"] = share.astype(low_type)
        share_ref[t["seq"], :, t["lanes"]] = t["share"]

    def blend(t):
        raw = dot_nt(t["share"], t["a_two"])
        t["mix"] = jnp.where(causal, raw, 0.0).astype(low_type)

    def finish(t):
        att = dot_nn(t["mix"], split_pair(t["v"], first_head))
        att = att + dot_nn(t["share"], t["now"][:, PAIR:])
        att_ref[t["seq"], :, t["lanes"]] = att.astype(low_type)
        state[t["seq"], t["pair"]] += dot_tn(t["a"], jnp.concatenate([t["k"], t["v"]], axis=1))

    for stage in (score, gather, soften, blend, finish):
        for item in items:
            stage(item)


def forward_kernel(
    ids_ref,
    dw_ref,
    x_ref,
    ln_ref,
    attn_ref,
    ffn_ref,
    q_ref,
    k_ref,
    v_ref,
    a_ref,
    att_ref,
    share_ref,
    logit_ref,
    before_ref,
    state_ref,
    weight_ref,
    in_hbm,
    out_hbm,
    ffn_hbm,
    state,
    carry,
    in_w,
    own,
    own_ffn,
    counts,
    counts_z,
    counts_w,
    in_sems,
    in_far,
    ffn_sems,
    ffn_far,
    out_sems,
    cz_send,
    cz_recv,
    cw_send,
    cw_recv,
    local_sems,
    *,
    wide,
    narrow,
    total_seqs,
    groups,
):
    step = pl.program_id(0)
    steps = pl.num_programs(0)
    seqs = x_ref.shape[0]
    w = lax.axis_index("wide")
    z = lax.axis_index("narrow")
    core = lax.rem(w, 2)
    mate = (w + 1 - 2 * core, z)
    other = 1 - core
    rows = attn_ref.shape[1]
    ffn_rows = ffn_ref.shape[1]
    half = rows // 2
    quarter = ffn_rows // 4
    chip = lax.rem(w // 2, 4)
    hops = list(range(1, narrow))
    column = [(w, lax.rem(z + hop, narrow)) for hop in hops]
    plane = [(lax.rem(w + hop, wide), z) for hop in range(1, wide)]
    chips = [(w - 2 * chip + 2 * lax.rem(chip + hop, 4), z) for hop in range(1, 4)]

    def at(owner, size):
        return pl.ds(pl.multiple_of(owner * size, size), size)

    def from_z(place):
        return lax.rem(z + narrow - hops[place], narrow)

    def in_part(owner, matrix):
        return in_w.at[matrix, at(2 * owner + core, half)]

    def in_z(place):
        return remote(
            own.at[chip, at(core, half)],
            in_part(z, chip),
            in_sems.at[0, place],
            in_sems.at[1, place],
            column[place],
        )

    def in_chip(place, hop):
        block = in_part(from_z(place), chip)
        return remote(
            block, block, in_far.at[0, place, hop], in_far.at[1, place, hop], chips[hop]
        )

    def in_core(place):
        block = in_w.at[:, at(2 * from_z(place) + core, half)]
        return remote(block, block, in_sems.at[2, place], in_sems.at[3, place], mate)

    def ffn_z(place):
        return remote(
            own_ffn.at[core, at(chip, quarter)],
            ffn_hbm.at[core, at(4 * z + chip, quarter)],
            ffn_sems.at[0, place],
            ffn_sems.at[1, place],
            column[place],
        )

    def ffn_chip(place, hop):
        block = ffn_hbm.at[core, at(4 * from_z(place) + chip, quarter)]
        return remote(
            block, block, ffn_far.at[0, place, hop], ffn_far.at[1, place, hop], chips[hop]
        )

    def ffn_core(place):
        block = ffn_hbm.at[core, at(from_z(place), ffn_rows)]
        return remote(block, block, ffn_sems.at[2, place], ffn_sems.at[3, place], mate)

    def out_z(place):
        return remote(
            own.at[4, at(core, half)],
            out_hbm.at[at(2 * z + core, half)],
            out_sems.at[0, place],
            out_sems.at[1, place],
            column[place],
        )

    def out_core(place):
        block = out_hbm.at[at(2 * from_z(place) + core, half)]
        return remote(block, block, out_sems.at[2, place], out_sems.at[3, place], mate)

    def count_z(place):
        return remote(
            counts, counts_z.at[place], cz_send.at[place], cz_recv.at[place], column[place]
        )

    def count_w(place):
        return remote(
            counts, counts_w.at[place], cw_send.at[place], cw_recv.at[place], plane[place]
        )

    keep_ffn = pltpu.make_async_copy(own_ffn, ffn_hbm.at[:, at(z, ffn_rows)], local_sems.at[0])
    keep_out = pltpu.make_async_copy(own.at[4], out_hbm.at[at(z, rows)], local_sems.at[1])
    keep_in = pltpu.make_async_copy(in_w, in_hbm, local_sems.at[2])

    @pl.when(step == 0)
    def _():
        state[...] = jnp.zeros_like(state)
        carry[...] = jnp.zeros_like(carry)
        own[...] = attn_ref[...].astype(low_type)
        greet(column + plane)
        for place in range(narrow - 1):
            in_z(place).start()
        for place in range(4):
            in_w[place, at(z, rows), :] = own[place]
        own_ffn[...] = ffn_ref[...].astype(low_type)
        lanes = lane_of((8, LANES))
        count = jnp.zeros((8, LANES), wide_type)
        for seq in range(seqs):
            count = count + (lanes == ids_ref[seq]).astype(wide_type)
        counts[...] = count
        for place in range(narrow - 1):
            in_z(place).wait_recv()
            for hop in range(3):
                in_chip(place, hop).start()
        for place in range(narrow - 1):
            for hop in range(3):
                in_chip(place, hop).wait_recv()
            in_core(place).start()
        keep_ffn.start()
        keep_out.start()
        for place in range(narrow - 1):
            count_z(place).start()
            out_z(place).start()
            ffn_z(place).start()
        for place in range(narrow - 1):
            in_core(place).wait_recv()
        keep_in.start()

    @pl.when(step == 1)
    def _():
        for place in range(narrow - 1):
            count_z(place).wait()
        total = counts[...]
        for place in range(narrow - 1):
            total = total + counts_z[place]
        counts[...] = total
        for place in range(wide - 1):
            count_w(place).start()

    @pl.when(step == 2)
    def _():
        for place in range(wide - 1):
            count_w(place).wait()
        total = counts[...]
        for place in range(wide - 1):
            total = total + counts_w[place]
        lanes = lane_of((8, LANES))
        values = jnp.zeros((8, LANES), wide_type)
        for group in range(groups):
            values = values + jnp.where(lanes == group, dw_ref[group], 0.0)
        weight_ref[...] = values * total_seqs / (groups * jnp.maximum(total, 1.0))

    @pl.when(step == steps // 2 - 1)
    def _():
        for place in range(narrow - 1):
            out_z(place).wait_recv()
            out_core(place).start()
            ffn_z(place).wait_recv()
            for hop in range(3):
                ffn_chip(place, hop).start()

    @pl.when(step == steps - 2)
    def _():
        for place in range(narrow - 1):
            for hop in range(3):
                ffn_chip(place, hop).wait_recv()
            ffn_core(place).start()

    normed, _ = normalize(x_ref[...].reshape(seqs * CHUNK, D).astype(wide_type))
    first = (normed * ln_ref[0:1, :] + ln_ref[1:2, :]).astype(low_type)
    q_all = dot_nn(first, in_w[0]).astype(low_type)
    k_all = dot_nn(first, in_w[1]).astype(low_type)
    v_all = dot_nn(first, in_w[2]).astype(low_type)
    a_all = jnp.exp(dot_nn(first, in_w[3])).astype(low_type)
    q_ref[...] = q_all.reshape(q_ref.shape)
    k_ref[...] = k_all.reshape(q_ref.shape)
    v_ref[...] = v_all.reshape(q_ref.shape)
    a_ref[...] = a_all.reshape(q_ref.shape)
    attend_chunks(
        q_all,
        k_all,
        v_all,
        a_all,
        (att_ref, share_ref, logit_ref, before_ref, state_ref, state, carry),
        seqs,
    )

    @pl.when(step == steps - 1)
    def _():
        keep_ffn.wait()
        keep_out.wait()
        keep_in.wait()
        for place in range(narrow - 1):
            in_z(place).wait_send()
            in_core(place).wait_send()
            out_z(place).wait_send()
            out_core(place).wait()
            ffn_z(place).wait_send()
            for hop in range(3):
                in_chip(place, hop).wait_send()
                ffn_chip(place, hop).wait_send()
            ffn_core(place).wait()


def forward(tokens, ids, dw, ln_params, attn_w, ffn_w):
    seqs, length, _ = tokens.shape
    chunks = length // CHUNK
    wide = lax.axis_size("wide")
    narrow = lax.axis_size("narrow")
    block = pl.BlockSpec((seqs, CHUNK, D), lambda i: (0, i, 0))
    low_out = jax.ShapeDtypeStruct(tokens.shape, low_type)
    any_spec = pl.BlockSpec(memory_space=pl.ANY)

    def whole(*shape):
        return pl.BlockSpec(shape, lambda i: (0,) * len(shape))

    return pl.pallas_call(
        functools.partial(
            forward_kernel,
            wide=wide,
            narrow=narrow,
            total_seqs=seqs * wide * narrow,
            groups=dw.shape[0],
        ),
        grid=(chunks,),
        in_specs=[
            pl.BlockSpec(memory_space=pltpu.SMEM),
            pl.BlockSpec(memory_space=pltpu.SMEM),
            block,
            whole(4, D),
            whole(*attn_w.shape),
            whole(*ffn_w.shape),
        ],
        out_specs=[block] * 7
        + [
            pl.BlockSpec((1, seqs, 1, D), lambda i: (i, 0, 0, 0)),
            pl.BlockSpec((1, seqs, PAIRS, PAIR, 2 * PAIR), lambda i: (i, 0, 0, 0, 0)),
            whole(8, LANES),
            any_spec,
            any_spec,
            any_spec,
        ],
        out_shape=[low_out] * 7
        + [
            jax.ShapeDtypeStruct((chunks, seqs, 1, D), wide_type),
            jax.ShapeDtypeStruct((chunks, seqs, PAIRS, PAIR, 2 * PAIR), low_type),
            jax.ShapeDtypeStruct((8, LANES), wide_type),
            jax.ShapeDtypeStruct((4, D, D), low_type),
            jax.ShapeDtypeStruct((D, D), low_type),
            jax.ShapeDtypeStruct((2, FF, D), low_type),
        ],
        scratch_shapes=[
            pltpu.VMEM((seqs, PAIRS, PAIR, 2 * PAIR), wide_type),
            pltpu.VMEM((seqs, 1, D), wide_type),
            pltpu.VMEM((4, D, D), low_type),
            pltpu.VMEM(attn_w.shape, low_type),
            pltpu.VMEM(ffn_w.shape, low_type),
            pltpu.VMEM((8, LANES), wide_type),
            pltpu.VMEM((narrow - 1, 8, LANES), wide_type),
            pltpu.VMEM((wide - 1, 8, LANES), wide_type),
        ]
        + [
            pltpu.SemaphoreType.DMA((4, narrow - 1)),
            pltpu.SemaphoreType.DMA((2, narrow - 1, 3)),
            pltpu.SemaphoreType.DMA((4, narrow - 1)),
            pltpu.SemaphoreType.DMA((2, narrow - 1, 3)),
            pltpu.SemaphoreType.DMA((4, narrow - 1)),
            pltpu.SemaphoreType.DMA((narrow - 1,)),
            pltpu.SemaphoreType.DMA((narrow - 1,)),
            pltpu.SemaphoreType.DMA((wide - 1,)),
            pltpu.SemaphoreType.DMA((wide - 1,)),
        ]
        + [pltpu.SemaphoreType.DMA((3,))],
        compiler_params=pltpu.CompilerParams(
            vmem_limit_bytes=VMEM_BYTES, collective_id=0, has_side_effects=True
        ),
        name="forward",
    )(ids, dw, tokens, ln_params, attn_w, ffn_w)


def newton_poly(gram):
    scale = jnp.sqrt(jnp.trace(gram)) + 1e-07
    eye = jnp.eye(D, dtype=wide_type)
    gram_one = gram * (1.0 / (scale * scale))
    poly_one = quintic_lin * eye + quintic_cube * gram_one + quintic_five * (gram_one @ gram_one)
    gram_two = (gram_one @ poly_one) @ poly_one
    poly_two = quintic_lin * eye + quintic_cube * gram_two + quintic_five * (gram_two @ gram_two)
    return (poly_one @ poly_two) * (1.0 / scale)


def sum_rows(stack, rows_at):
    wide = lax.axis_size("wide")
    narrow = lax.axis_size("narrow")
    mats = stack.shape[0]
    share = D // narrow // wide
    parts = stack.reshape(mats, narrow, wide, share, D)
    parts = lax.psum_scatter(parts, "wide", scatter_dimension=2, tiled=False)
    parts = lax.psum_scatter(parts, "narrow", scatter_dimension=1, tiled=False)
    return lax.all_gather(parts, "wide", axis=1, tiled=True)


def shards(
    tokens,
    out_grad,
    group_ids,
    domain_weight,
    attn_w,
    ffn_w,
    attn_mom,
    ffn_mom,
    ln_params,
    ln_first,
    ln_second,
):
    local_seqs, length, _ = tokens.shape
    token_count = local_seqs * length
    wide = lax.axis_size("wide")
    narrow = lax.axis_size("narrow")
    rows = tokens.reshape(token_count, D)
    head = (local_seqs, length, D)
    q, k, v, a, att, share, logit, before, states, weights, in_w, out_w, ffn_low = forward(
        tokens, group_ids, domain_weight, ln_params, attn_w, ffn_w
    )
    output, dx, datt, gup, gdown, go, gln_two = feed(
        group_ids,
        weights,
        rows,
        att.reshape(token_count, D),
        out_grad.reshape(token_count, D),
        out_w,
        ffn_low,
        ln_params,
        length,
    )
    dq, dk, dv, de = attend_back(q, k, v, a, share, logit, before, datt.reshape(head), states)
    dq, dk, dv, de = (item.reshape(token_count, D) for item in (dq, dk, dv, de))
    input_grad, gw, gln_one = project_back(rows, dx, dq, dk, dv, de, in_w, ln_params)

    attn_grad = sum_rows(jnp.concatenate([gw, go[None]], axis=0), None).astype(wide_type)
    ffn_t = jnp.stack([gup, gdown])
    ffn_t = lax.psum_scatter(ffn_t, "wide", scatter_dimension=1, tiled=True)
    ffn_t = lax.psum_scatter(ffn_t, "narrow", scatter_dimension=2, tiled=True)
    ffn_t = lax.all_gather(ffn_t, "wide", axis=1, tiled=True)
    ffn_grad = jnp.swapaxes(ffn_t, 1, 2).astype(wide_type)
    ln_full = jnp.concatenate([gln_one, gln_two], axis=0)
    ln_sum = lax.psum(ln_full, ("wide", "narrow"))
    shard_width = ln_first.shape[1]
    ln_grad = lax.dynamic_slice_in_dim(
        ln_sum, lax.axis_index("narrow") * shard_width, shard_width, 1
    )

    attn_moment = momentum_keep * attn_mom + attn_grad
    ffn_moment = momentum_keep * ffn_mom + ffn_grad
    mats = attn_w.shape[0] + ffn_w.shape[0]
    attn_rows = attn_w.shape[1]
    ffn_rows = ffn_w.shape[1]
    padded = jnp.concatenate(
        [
            jnp.pad(attn_moment.astype(low_type), ((0, 0), (0, ffn_rows - attn_rows), (0, 0))),
            ffn_moment.astype(low_type),
        ],
        axis=0,
    )
    mine = lax.dynamic_index_in_dim(
        padded, jnp.minimum(lax.axis_index("wide"), mats - 1), 0, keepdims=False
    )
    gram = lax.psum(dot_tn(mine, mine), "narrow")
    poly = lax.all_gather(newton_poly(gram).astype(low_type), "wide", axis=0, tiled=False)[:mats]
    attn_ortho = jnp.einsum(
        "jrd,jde->jre",
        attn_moment.astype(low_type),
        poly[: attn_w.shape[0]],
        preferred_element_type=wide_type,
    )
    ffn_ortho = jnp.einsum(
        "jrd,jde->jre",
        ffn_moment.astype(low_type),
        poly[attn_w.shape[0] :],
        preferred_element_type=wide_type,
    )
    keep_factor = 1.0 - muon_rate * muon_decay
    attn_new = keep_factor * attn_w - muon_rate * 0.2 * math.sqrt(D) * attn_ortho
    ffn_new = keep_factor * ffn_w - muon_rate * 0.2 * math.sqrt(FF) * ffn_ortho
    own_params = lax.dynamic_slice_in_dim(
        ln_params, lax.axis_index("narrow") * shard_width, shard_width, 1
    )
    first_new = beta_first * ln_first + (1.0 - beta_first) * ln_grad
    second_new = beta_second * ln_second + (1.0 - beta_second) * ln_grad * ln_grad
    first_fix = 1.0 - beta_first**STEP
    second_fix = 1.0 - beta_second**STEP
    ln_new = own_params - adam_rate * (first_new / first_fix) / (
        jnp.sqrt(second_new / second_fix) + adam_epsilon
    )
    return (
        output.reshape(tokens.shape),
        input_grad.reshape(tokens.shape),
        attn_grad,
        ffn_grad,
        ln_grad,
        attn_moment,
        ffn_moment,
        attn_new,
        ffn_new,
        attn_new.astype(low_type),
        ffn_new.astype(low_type),
        first_new,
        second_new,
        ln_new,
    )


def solution(mesh):
    split = P(("wide", "narrow"), None, None)
    rows = P(None, "narrow", None)
    lanes = P(None, "narrow")
    inner = jax.shard_map(
        shards,
        mesh=mesh,
        in_specs=(
            split,
            split,
            P(("wide", "narrow")),
            P(),
            rows,
            rows,
            rows,
            rows,
            P(),
            lanes,
            lanes,
        ),
        out_specs=(
            split,
            split,
            rows,
            rows,
            lanes,
            rows,
            rows,
            rows,
            rows,
            rows,
            rows,
            lanes,
            lanes,
            lanes,
        ),
        check_vma=False,
    )
    return inner
```

```python
import functools
import math

import jax
import jax.numpy as jnp
from jax import lax
from jax.experimental import pallas as pl
from jax.experimental.pallas import tpu as pltpu
from jax.sharding import PartitionSpec as P

D = 512
HEADS = 8
HEAD_DIM = 64
FF = 2048
STEP = 10

norm_epsilon = 1e-05
momentum_keep = 0.5
quintic_lin = 3.4445
quintic_cube = -4.775
quintic_five = 2.0315
muon_rate = 0.7
muon_decay = 0.1
adam_rate = 0.2
beta_first = 0.9
beta_second = 0.999
adam_epsilon = 1e-08

CHUNK = 128
PAIR = 2 * HEAD_DIM
PAIRS = HEADS // 2
VMEM_BYTES = 60 * 1024 * 1024
low_type = jnp.bfloat16
wide_type = jnp.float32


def dot_nn(left, right):
    return lax.dot_general(left, right, (((1,), (0,)), ((), ())), preferred_element_type=wide_type)


def dot_nt(left, right):
    return lax.dot_general(left, right, (((1,), (1,)), ((), ())), preferred_element_type=wide_type)


def dot_tn(left, right):
    return lax.dot_general(left, right, (((0,), (0,)), ((), ())), preferred_element_type=wide_type)


def normalize(rows):
    center = rows - jnp.mean(rows, axis=-1, keepdims=True)
    spread = jnp.mean(center * center, axis=-1, keepdims=True)
    inverse = lax.rsqrt(spread + norm_epsilon)
    return center * inverse, inverse


def norm_back(grad_rows, normed, inverse, gain):
    grad_normed = grad_rows * gain
    mean_grad = jnp.mean(grad_normed, axis=-1, keepdims=True)
    mean_cross = jnp.mean(grad_normed * normed, axis=-1, keepdims=True)
    return inverse * (grad_normed - mean_grad - normed * mean_cross)


def lane_of(shape):
    return lax.broadcasted_iota(jnp.int32, shape, 1)


def row_of(shape):
    return lax.broadcasted_iota(jnp.int32, shape, 0)


def split_pair(pair, first_head):
    zero = jnp.zeros_like(pair)
    return jnp.concatenate(
        [jnp.where(first_head, pair, zero), jnp.where(first_head, zero, pair)], axis=0
    )


def head_reduce(values, first_head, op, neutral):
    left = op(jnp.where(first_head, values, neutral), axis=-1, keepdims=True)
    right = op(jnp.where(first_head, neutral, values), axis=-1, keepdims=True)
    return jnp.where(first_head, left, right)


def attend_back_chunk(refs, state, carry):
    (
        q_ref,
        k_ref,
        v_ref,
        a_ref,
        share_ref,
        logit_ref,
        before_ref,
        datt_ref,
        state_ref,
        dq_ref,
        dk_ref,
        dv_ref,
        de_ref,
    ) = refs
    scaling = HEAD_DIM**-0.5
    first_head = lane_of((CHUNK, PAIR)) < HEAD_DIM
    causal = row_of((CHUNK, 2 * CHUNK)) >= lane_of((CHUNK, 2 * CHUNK)) % CHUNK
    anti = row_of((CHUNK, 2 * CHUNK)) <= lane_of((CHUNK, 2 * CHUNK)) % CHUNK
    same_head = (row_of((PAIR, 2 * PAIR)) // HEAD_DIM) == (
        (lane_of((PAIR, 2 * PAIR)) // HEAD_DIM) % 2
    )
    lower = (row_of((CHUNK, CHUNK)) >= lane_of((CHUNK, CHUNK))).astype(low_type)
    upper = (row_of((CHUNK, CHUNK)) <= lane_of((CHUNK, CHUNK))).astype(low_type)

    def masked(mask, raw):
        return jnp.where(mask, raw, 0.0).astype(low_type)

    items = []
    for seq in range(q_ref.shape[0]):
        total = dot_nn(lower, a_ref[seq]) + before_ref[0, seq]
        inv = 1.0 / total
        for pair in range(PAIRS):
            lanes = slice(pair * PAIR, (pair + 1) * PAIR)
            items.append(
                dict(seq=seq, pair=pair, lanes=lanes, total=total[:, lanes], inv=inv[:, lanes])
            )

    def load(t):
        seq, lanes = t["seq"], t["lanes"]
        t["k"] = k_ref[seq, :, lanes]
        t["v"] = v_ref[seq, :, lanes]
        t["a"] = a_ref[seq, :, lanes]
        t["share"] = share_ref[seq, :, lanes]
        t["datt"] = datt_ref[seq, :, lanes]
        t["q"] = q_ref[seq, :, lanes] * low_type(scaling)
        t["before"] = state_ref[0, seq, t["pair"]]
        t["after"] = jnp.where(same_head, state[seq, t["pair"]], 0.0).astype(low_type)
        t["v_two"] = split_pair(t["v"], first_head)
        t["a_two"] = split_pair(t["a"], first_head)
        t["dmix"] = masked(causal, dot_nt(t["datt"], t["v_two"]))

    def gather(t):
        t["share_two"] = split_pair(t["share"], first_head)
        t["datt_two"] = split_pair(t["datt"], first_head)
        t["dshare"] = dot_nn(t["dmix"], t["a_two"]) + dot_nt(t["datt"], t["before"][:, PAIR:])

    def soften(t):
        logit = logit_ref[t["seq"], :, t["lanes"]].astype(wide_type)
        prob = t["share"].astype(wide_type) * t["total"]
        cross = t["dshare"] * t["inv"] * prob
        dlogit = cross - prob * head_reduce(cross, first_head, jnp.sum, 0.0)
        t["dnumer"] = (dlogit * t["inv"]).astype(low_type)
        t["dtotal"] = -(cross + dlogit * logit) * t["inv"]
        t["mix_t"] = masked(anti, dot_nt(t["a"], t["share_two"]))
        t["dmix_t"] = masked(anti, dot_nt(t["v"], t["datt_two"]))

    def blend(t):
        t["dnumer_two"] = split_pair(t["dnumer"], first_head)
        t["dscores"] = masked(causal, dot_nt(t["dnumer"], t["a_two"]))
        t["dscores_t"] = masked(anti, dot_nt(t["a"], t["dnumer_two"]))
        t["k_two"] = split_pair(t["k"], first_head)
        t["q_two"] = split_pair(t["q"], first_head)
        t["scores_t"] = masked(anti, dot_nt(t["k"], t["q_two"]))
        t["later"] = dot_nn(t["a"], t["after"])

    def finish(t):
        seq, lanes = t["seq"], t["lanes"]
        dq = dot_nn(t["dscores"], t["k_two"]) + dot_nn(t["dnumer"], t["before"][:, :PAIR])
        dq_ref[seq, :, lanes] = (dq * scaling).astype(low_type)
        dv = dot_nn(t["mix_t"], t["datt_two"]) + t["later"][:, PAIR:]
        dv_ref[seq, :, lanes] = dv.astype(low_type)
        dk = dot_nn(t["dscores_t"], t["q_two"]) + t["later"][:, :PAIR]
        dk_ref[seq, :, lanes] = dk.astype(low_type)
        high = t["dtotal"].astype(low_type)
        rest = (t["dtotal"] - high.astype(wide_type)).astype(low_type)
        tail = dot_nn(upper, high) + dot_nn(upper, rest) + carry[seq, :, lanes]
        carry[seq, :, lanes] = tail[0:1, :]
        da = dot_nn(t["dmix_t"], t["share_two"]) + dot_nn(t["scores_t"], t["dnumer_two"])
        da = da + dot_nt(jnp.concatenate([t["k"], t["v"]], axis=1), t["after"]) + tail
        de = da.astype(low_type).astype(wide_type) * t["a"].astype(wide_type)
        de_ref[seq, :, lanes] = de.astype(low_type)
        state[seq, t["pair"], :, :PAIR] += dot_tn(t["dnumer"], t["q"])
        state[seq, t["pair"], :, PAIR:] += dot_tn(t["share"], t["datt"])

    for stage in (load, gather, soften, blend, finish):
        for item in items:
            stage(item)


FF_BLOCK = 512
gelu_root = math.sqrt(2.0 / math.pi)
gelu_cube = 0.044715


def feed_kernel(
    ids_ref,
    weight_ref,
    x_ref,
    att_ref,
    og_ref,
    wo_ref,
    ffn_ref,
    ln_ref,
    out_ref,
    dx_ref,
    datt_ref,
    gffn_ref,
    go_ref,
    gln_ref,
    up_sum,
    down_sum,
    o_sum,
    *,
    per_seq,
):
    step = pl.program_id(0)

    @pl.when(step == 0)
    def _():
        up_sum[...] = jnp.zeros_like(up_sum)
        down_sum[...] = jnp.zeros_like(down_sum)
        o_sum[...] = jnp.zeros_like(o_sum)
        gln_ref[...] = jnp.zeros_like(gln_ref)

    att = att_ref[...]
    mixed = x_ref[...].astype(wide_type) + dot_nn(att, wo_ref[...])
    normed, inverse = normalize(mixed)
    second = (normed * ln_ref[2:3, :] + ln_ref[3:4, :]).astype(low_type)
    mine = lane_of((1, LANES)) == ids_ref[step // per_seq]
    weight = jnp.sum(jnp.where(mine, weight_ref[0:1, :], 0.0), axis=1, keepdims=True)
    dout = og_ref[...].astype(wide_type) * weight
    dy = dout.astype(low_type)
    second_t = second.T
    dy_t = dy.T
    parts = [dict(rows=slice(part * FF_BLOCK, (part + 1) * FF_BLOCK)) for part in range(FF // FF_BLOCK)]

    def open_part(t):
        t["up"] = ffn_ref[0, t["rows"], :]
        t["down"] = ffn_ref[1, t["rows"], :]
        t["inner"] = dot_nt(second, t["up"])
        t["dhidden"] = dot_nt(dy, t["down"])

    result, dsecond = mixed, 0.0
    open_part(parts[0])
    for place, t in enumerate(parts):
        if place + 1 < len(parts):
            open_part(parts[place + 1])
        inner = t["inner"]
        square = inner * inner
        bend = jnp.tanh(inner * (gelu_root + (gelu_root * gelu_cube) * square))
        half = 0.5 + 0.5 * bend
        hidden = (inner * half).astype(low_type)
        slope = half + (0.5 * inner) * (1.0 - bend * bend) * (
            gelu_root + (3.0 * gelu_root * gelu_cube) * square
        )
        dinner = (t["dhidden"] * slope).astype(low_type)
        result = result + dot_nn(hidden, t["down"])
        down_sum[:, t["rows"]] += dot_nn(dy_t, hidden)
        up_sum[:, t["rows"]] += dot_nn(second_t, dinner)
        dsecond = dsecond + dot_nn(dinner, t["up"])
    out_ref[...] = result.astype(low_type)
    gln_ref[0:1, :] += jnp.sum(dsecond * normed, axis=0, keepdims=True)
    gln_ref[1:2, :] += jnp.sum(dsecond, axis=0, keepdims=True)
    dmixed = dout + norm_back(dsecond, normed, inverse, ln_ref[2:3, :])
    dx_ref[...] = dmixed
    datt = dmixed.astype(low_type)
    o_sum[...] += dot_tn(att, datt)
    datt_ref[...] = dot_nt(datt, wo_ref[...]).astype(low_type)

    @pl.when(step == pl.num_programs(0) - 1)
    def _():
        gffn_ref[0] = up_sum[...].astype(low_type)
        gffn_ref[1] = down_sum[...].astype(low_type)
        go_ref[...] = o_sum[...].astype(low_type)


def feed(ids, weights, rows, att, grad, wo, ffn, ln_params, length):
    count = rows.shape[0]
    block = 512
    row_spec = pl.BlockSpec((block, D), lambda i: (i, 0))

    def whole(*shape):
        return pl.BlockSpec(shape, lambda i: (0,) * len(shape))

    return pl.pallas_call(
        functools.partial(feed_kernel, per_seq=length // block),
        grid=(count // block,),
        in_specs=[
            pl.BlockSpec(memory_space=pltpu.SMEM),
            whole(8, LANES),
            row_spec,
            row_spec,
            row_spec,
            whole(D, D),
            whole(2, FF, D),
            whole(4, D),
        ],
        out_specs=[
            row_spec,
            row_spec,
            row_spec,
            whole(2, D, FF),
            whole(D, D),
            whole(2, D),
        ],
        out_shape=[
            jax.ShapeDtypeStruct((count, D), low_type),
            jax.ShapeDtypeStruct((count, D), wide_type),
            jax.ShapeDtypeStruct((count, D), low_type),
            jax.ShapeDtypeStruct((2, D, FF), low_type),
            jax.ShapeDtypeStruct((D, D), low_type),
            jax.ShapeDtypeStruct((2, D), wide_type),
        ],
        scratch_shapes=[
            pltpu.VMEM((D, FF), wide_type),
            pltpu.VMEM((D, FF), wide_type),
            pltpu.VMEM((D, D), wide_type),
        ],
        compiler_params=pltpu.CompilerParams(vmem_limit_bytes=VMEM_BYTES),
        name="feed",
    )(ids, weights, rows, att, grad, wo, ffn, ln_params)


def project_back_kernel(
    x_ref,
    dx_ref,
    dq_ref,
    dk_ref,
    dv_ref,
    de_ref,
    w_ref,
    ln_ref,
    grad_ref,
    gw_ref,
    gln_ref,
    w_sum,
):
    step = pl.program_id(0)

    @pl.when(step == 0)
    def _():
        w_sum[...] = jnp.zeros_like(w_sum)
        gln_ref[...] = jnp.zeros_like(gln_ref)

    parts = (dq_ref, dk_ref, dv_ref, de_ref)
    dfirst = dot_nt(dq_ref[...], w_ref[0])
    for place in range(1, 4):
        dfirst = dfirst + dot_nt(parts[place][...], w_ref[place])
    normed, inverse = normalize(x_ref[...].astype(wide_type))
    first_t = (normed * ln_ref[0:1, :] + ln_ref[1:2, :]).astype(low_type).T
    for place in range(4):
        w_sum[place] += dot_nn(first_t, parts[place][...])
    gln_ref[0:1, :] += jnp.sum(dfirst * normed, axis=0, keepdims=True)
    gln_ref[1:2, :] += jnp.sum(dfirst, axis=0, keepdims=True)
    grad_ref[...] = dx_ref[...] + norm_back(dfirst, normed, inverse, ln_ref[0:1, :])

    @pl.when(step == pl.num_programs(0) - 1)
    def _():
        gw_ref[...] = w_sum[...].astype(low_type)


def project_back(rows, dx, dq, dk, dv, de, weights, ln_params):
    count = rows.shape[0]
    block = 512
    row_spec = pl.BlockSpec((block, D), lambda i: (i, 0))

    def whole(*shape):
        return pl.BlockSpec(shape, lambda i: (0,) * len(shape))

    return pl.pallas_call(
        project_back_kernel,
        grid=(count // block,),
        in_specs=[row_spec] * 6 + [whole(4, D, D), whole(4, D)],
        out_specs=[row_spec, whole(4, D, D), whole(2, D)],
        out_shape=[
            jax.ShapeDtypeStruct((count, D), wide_type),
            jax.ShapeDtypeStruct((4, D, D), low_type),
            jax.ShapeDtypeStruct((2, D), wide_type),
        ],
        scratch_shapes=[pltpu.VMEM((4, D, D), wide_type)],
        compiler_params=pltpu.CompilerParams(vmem_limit_bytes=VMEM_BYTES),
        name="project_back",
    )(rows, dx, dq, dk, dv, de, weights, ln_params)


MESH = pl.DeviceIdType.MESH
LANES = 128


def remote(src, dst, send_sem, recv_sem, device):
    return pltpu.make_async_remote_copy(
        src_ref=src,
        dst_ref=dst,
        send_sem=send_sem,
        recv_sem=recv_sem,
        device_id=device,
        device_id_type=MESH,
    )


def greet(devices):
    barrier = pltpu.get_barrier_semaphore()
    for device in devices:
        pl.semaphore_signal(barrier, inc=1, device_id=device, device_id_type=MESH)
    pl.semaphore_wait(barrier, len(devices))


def attend_chunks(q_all, k_all, v_all, a_all, refs, seqs):
    att_ref, share_ref, logit_ref, before_ref, state_ref, state, carry = refs
    first_head = lane_of((CHUNK, PAIR)) < HEAD_DIM
    causal = row_of((CHUNK, 2 * CHUNK)) >= lane_of((CHUNK, 2 * CHUNK)) % CHUNK
    same_head = (row_of((PAIR, 2 * PAIR)) // HEAD_DIM) == (
        (lane_of((PAIR, 2 * PAIR)) // HEAD_DIM) % 2
    )
    lower = (row_of((CHUNK, CHUNK)) >= lane_of((CHUNK, CHUNK))).astype(low_type)
    items = []
    for seq in range(seqs):
        part = slice(seq * CHUNK, (seq + 1) * CHUNK)
        before = carry[seq]
        before_ref[0, seq] = before
        total = dot_nn(lower, a_all[part]) + before
        carry[seq] = total[CHUNK - 1 :, :]
        inv = 1.0 / total
        for pair in range(PAIRS):
            lanes = slice(pair * PAIR, (pair + 1) * PAIR)
            items.append(
                dict(
                    seq=seq,
                    pair=pair,
                    lanes=lanes,
                    q=q_all[part, lanes] * low_type(HEAD_DIM**-0.5),
                    k=k_all[part, lanes],
                    v=v_all[part, lanes],
                    a=a_all[part, lanes],
                    inv=inv[:, lanes],
                )
            )

    def score(t):
        t["a_two"] = split_pair(t["a"], first_head)
        t["now"] = jnp.where(same_head, state[t["seq"], t["pair"]], 0.0).astype(low_type)
        state_ref[0, t["seq"], t["pair"]] = t["now"]
        raw = dot_nt(t["q"], split_pair(t["k"], first_head))
        t["scores"] = jnp.where(causal, raw, 0.0).astype(low_type)

    def gather(t):
        numer = dot_nn(t["scores"], t["a_two"]) + dot_nt(t["q"], t["now"][:, :PAIR])
        t["logit"] = numer * t["inv"]
        logit_ref[t["seq"], :, t["lanes"]] = t["logit"].astype(low_type)

    def soften(t):
        expo = jnp.exp(t["logit"] - head_reduce(t["logit"], first_head, jnp.max, -jnp.inf))
        share = expo * (t["inv"] / head_reduce(expo, first_head, jnp.sum, 0.0))
        t["share"] = share.astype(low_type)
        share_ref[t["seq"], :, t["lanes"]] = t["share"]

    def blend(t):
        raw = dot_nt(t["share"], t["a_two"])
        t["mix"] = jnp.where(causal, raw, 0.0).astype(low_type)

    def finish(t):
        att = dot_nn(t["mix"], split_pair(t["v"], first_head))
        att = att + dot_nn(t["share"], t["now"][:, PAIR:])
        att_ref[t["seq"], :, t["lanes"]] = att.astype(low_type)
        state[t["seq"], t["pair"]] += dot_tn(t["a"], jnp.concatenate([t["k"], t["v"]], axis=1))

    for stage in (score, gather, soften, blend, finish):
        for item in items:
            stage(item)


def forward_kernel(
    ids_ref,
    dw_ref,
    x_ref,
    ln_ref,
    attn_ref,
    ffn_ref,
    q_ref,
    k_ref,
    v_ref,
    a_ref,
    att_ref,
    share_ref,
    logit_ref,
    before_ref,
    state_ref,
    weight_ref,
    in_hbm,
    out_hbm,
    ffn_hbm,
    state,
    carry,
    in_w,
    own,
    own_ffn,
    counts,
    counts_z,
    counts_w,
    in_sems,
    in_far,
    ffn_sems,
    ffn_far,
    out_sems,
    out_far,
    cz_send,
    cz_recv,
    cw_send,
    cw_recv,
    local_sems,
    *,
    wide,
    narrow,
    total_seqs,
    groups,
):
    step = pl.program_id(0)
    steps = pl.num_programs(0)
    seqs = x_ref.shape[0]
    w = lax.axis_index("wide")
    z = lax.axis_index("narrow")
    core = lax.rem(w, 2)
    mate = (w + 1 - 2 * core, z)
    other = 1 - core
    rows = attn_ref.shape[1]
    ffn_rows = ffn_ref.shape[1]
    half = rows // 2
    quarter = ffn_rows // 4
    chip = lax.rem(w // 2, 4)
    hops = list(range(1, narrow))
    column = [(w, lax.rem(z + hop, narrow)) for hop in hops]
    plane = [(lax.rem(w + hop, wide), z) for hop in range(1, wide)]
    chips = [(w - 2 * chip + 2 * lax.rem(chip + hop, 4), z) for hop in range(1, 4)]

    def at(owner, size):
        return pl.ds(pl.multiple_of(owner * size, size), size)

    def from_z(place):
        return lax.rem(z + narrow - hops[place], narrow)

    def in_part(owner, matrix):
        return in_w.at[matrix, at(2 * owner + core, half)]

    def in_z(place):
        return remote(
            own.at[chip, at(core, half)],
            in_part(z, chip),
            in_sems.at[0, place],
            in_sems.at[1, place],
            column[place],
        )

    def in_chip(place, hop):
        block = in_part(from_z(place), chip)
        return remote(
            block, block, in_far.at[0, place, hop], in_far.at[1, place, hop], chips[hop]
        )

    def in_core(place):
        block = in_w.at[:, at(2 * from_z(place) + core, half)]
        return remote(block, block, in_sems.at[2, place], in_sems.at[3, place], mate)

    def ffn_z(place):
        return remote(
            own_ffn.at[core, at(chip, quarter)],
            ffn_hbm.at[core, at(4 * z + chip, quarter)],
            ffn_sems.at[0, place],
            ffn_sems.at[1, place],
            column[place],
        )

    def ffn_chip(place, hop):
        block = ffn_hbm.at[core, at(4 * from_z(place) + chip, quarter)]
        return remote(
            block, block, ffn_far.at[0, place, hop], ffn_far.at[1, place, hop], chips[hop]
        )

    def ffn_core(place):
        block = ffn_hbm.at[core, at(from_z(place), ffn_rows)]
        return remote(block, block, ffn_sems.at[2, place], ffn_sems.at[3, place], mate)

    def out_block(owner, part):
        return out_hbm.at[at(4 * owner + part, rows // 4), at(core, D // 2)]

    def out_z(place):
        return remote(
            own.at[4, at(chip, rows // 4), at(core, D // 2)],
            out_block(z, chip),
            out_sems.at[0, place],
            out_sems.at[1, place],
            column[place],
        )

    def out_chip(place, hop):
        block = out_block(from_z(place), chip)
        return remote(
            block, block, out_far.at[0, place, hop], out_far.at[1, place, hop], chips[hop]
        )

    def out_core(place):
        block = out_hbm.at[at(from_z(place), rows), at(core, D // 2)]
        return remote(block, block, out_sems.at[2, place], out_sems.at[3, place], mate)

    def count_z(place):
        return remote(
            counts, counts_z.at[place], cz_send.at[place], cz_recv.at[place], column[place]
        )

    def count_w(place):
        return remote(
            counts, counts_w.at[place], cw_send.at[place], cw_recv.at[place], plane[place]
        )

    keep_ffn = pltpu.make_async_copy(own_ffn, ffn_hbm.at[:, at(z, ffn_rows)], local_sems.at[0])
    keep_out = pltpu.make_async_copy(own.at[4], out_hbm.at[at(z, rows)], local_sems.at[1])
    keep_in = pltpu.make_async_copy(in_w, in_hbm, local_sems.at[2])

    @pl.when(step == 0)
    def _():
        state[...] = jnp.zeros_like(state)
        carry[...] = jnp.zeros_like(carry)
        own[...] = attn_ref[...].astype(low_type)
        greet(column + plane)
        for place in range(narrow - 1):
            in_z(place).start()
        for place in range(4):
            in_w[place, at(z, rows), :] = own[place]
        own_ffn[...] = ffn_ref[...].astype(low_type)
        lanes = lane_of((8, LANES))
        count = jnp.zeros((8, LANES), wide_type)
        for seq in range(seqs):
            count = count + (lanes == ids_ref[seq]).astype(wide_type)
        counts[...] = count
        for place in range(narrow - 1):
            in_z(place).wait_recv()
            for hop in range(3):
                in_chip(place, hop).start()
        for place in range(narrow - 1):
            ffn_z(place).start()
            out_z(place).start()
            count_z(place).start()
        keep_ffn.start()
        keep_out.start()
        for place in range(narrow - 1):
            for hop in range(3):
                in_chip(place, hop).wait_recv()
            in_core(place).start()
        for place in range(narrow - 1):
            in_core(place).wait_recv()
        keep_in.start()

    @pl.when(step == 1)
    def _():
        for place in range(narrow - 1):
            count_z(place).wait()
        total = counts[...]
        for place in range(narrow - 1):
            total = total + counts_z[place]
        counts[...] = total
        for place in range(wide - 1):
            count_w(place).start()

    @pl.when(step == 2)
    def _():
        for place in range(wide - 1):
            count_w(place).wait()
        total = counts[...]
        for place in range(wide - 1):
            total = total + counts_w[place]
        lanes = lane_of((8, LANES))
        values = jnp.zeros((8, LANES), wide_type)
        for group in range(groups):
            values = values + jnp.where(lanes == group, dw_ref[group], 0.0)
        weight_ref[...] = values * total_seqs / (groups * jnp.maximum(total, 1.0))

    @pl.when(step == 1)
    def _():
        for place in range(narrow - 1):
            ffn_z(place).wait_recv()
            out_z(place).wait_recv()
            for hop in range(3):
                ffn_chip(place, hop).start()
                out_chip(place, hop).start()

    @pl.when(step == steps - 2)
    def _():
        for place in range(narrow - 1):
            for hop in range(3):
                ffn_chip(place, hop).wait_recv()
                out_chip(place, hop).wait_recv()
            ffn_core(place).start()
            out_core(place).start()

    normed, _ = normalize(x_ref[...].reshape(seqs * CHUNK, D).astype(wide_type))
    first = (normed * ln_ref[0:1, :] + ln_ref[1:2, :]).astype(low_type)
    q_all = dot_nn(first, in_w[0]).astype(low_type)
    k_all = dot_nn(first, in_w[1]).astype(low_type)
    v_all = dot_nn(first, in_w[2]).astype(low_type)
    a_all = jnp.exp(dot_nn(first, in_w[3])).astype(low_type)
    q_ref[...] = q_all.reshape(q_ref.shape)
    k_ref[...] = k_all.reshape(q_ref.shape)
    v_ref[...] = v_all.reshape(q_ref.shape)
    a_ref[...] = a_all.reshape(q_ref.shape)
    attend_chunks(
        q_all,
        k_all,
        v_all,
        a_all,
        (att_ref, share_ref, logit_ref, before_ref, state_ref, state, carry),
        seqs,
    )

    @pl.when(step == steps - 1)
    def _():
        keep_ffn.wait()
        keep_out.wait()
        keep_in.wait()
        for place in range(narrow - 1):
            in_z(place).wait_send()
            in_core(place).wait_send()
            out_z(place).wait_send()
            out_core(place).wait()
            ffn_z(place).wait_send()
            for hop in range(3):
                in_chip(place, hop).wait_send()
                ffn_chip(place, hop).wait_send()
                out_chip(place, hop).wait_send()
            ffn_core(place).wait()


def forward(tokens, ids, dw, ln_params, attn_w, ffn_w):
    seqs, length, _ = tokens.shape
    chunks = length // CHUNK
    wide = lax.axis_size("wide")
    narrow = lax.axis_size("narrow")
    block = pl.BlockSpec((seqs, CHUNK, D), lambda i: (0, i, 0))
    low_out = jax.ShapeDtypeStruct(tokens.shape, low_type)
    any_spec = pl.BlockSpec(memory_space=pl.ANY)

    def whole(*shape):
        return pl.BlockSpec(shape, lambda i: (0,) * len(shape))

    return pl.pallas_call(
        functools.partial(
            forward_kernel,
            wide=wide,
            narrow=narrow,
            total_seqs=seqs * wide * narrow,
            groups=dw.shape[0],
        ),
        grid=(chunks,),
        in_specs=[
            pl.BlockSpec(memory_space=pltpu.SMEM),
            pl.BlockSpec(memory_space=pltpu.SMEM),
            block,
            whole(4, D),
            whole(*attn_w.shape),
            whole(*ffn_w.shape),
        ],
        out_specs=[block] * 7
        + [
            pl.BlockSpec((1, seqs, 1, D), lambda i: (i, 0, 0, 0)),
            pl.BlockSpec((1, seqs, PAIRS, PAIR, 2 * PAIR), lambda i: (i, 0, 0, 0, 0)),
            whole(8, LANES),
            any_spec,
            any_spec,
            any_spec,
        ],
        out_shape=[low_out] * 7
        + [
            jax.ShapeDtypeStruct((chunks, seqs, 1, D), wide_type),
            jax.ShapeDtypeStruct((chunks, seqs, PAIRS, PAIR, 2 * PAIR), low_type),
            jax.ShapeDtypeStruct((8, LANES), wide_type),
            jax.ShapeDtypeStruct((4, D, D), low_type),
            jax.ShapeDtypeStruct((D, D), low_type),
            jax.ShapeDtypeStruct((2, FF, D), low_type),
        ],
        scratch_shapes=[
            pltpu.VMEM((seqs, PAIRS, PAIR, 2 * PAIR), wide_type),
            pltpu.VMEM((seqs, 1, D), wide_type),
            pltpu.VMEM((4, D, D), low_type),
            pltpu.VMEM(attn_w.shape, low_type),
            pltpu.VMEM(ffn_w.shape, low_type),
            pltpu.VMEM((8, LANES), wide_type),
            pltpu.VMEM((narrow - 1, 8, LANES), wide_type),
            pltpu.VMEM((wide - 1, 8, LANES), wide_type),
        ]
        + [
            pltpu.SemaphoreType.DMA((4, narrow - 1)),
            pltpu.SemaphoreType.DMA((2, narrow - 1, 3)),
            pltpu.SemaphoreType.DMA((4, narrow - 1)),
            pltpu.SemaphoreType.DMA((2, narrow - 1, 3)),
            pltpu.SemaphoreType.DMA((4, narrow - 1)),
            pltpu.SemaphoreType.DMA((2, narrow - 1, 3)),
            pltpu.SemaphoreType.DMA((narrow - 1,)),
            pltpu.SemaphoreType.DMA((narrow - 1,)),
            pltpu.SemaphoreType.DMA((wide - 1,)),
            pltpu.SemaphoreType.DMA((wide - 1,)),
        ]
        + [pltpu.SemaphoreType.DMA((3,))],
        compiler_params=pltpu.CompilerParams(
            vmem_limit_bytes=VMEM_BYTES, collective_id=0, has_side_effects=True
        ),
        name="forward",
    )(ids, dw, tokens, ln_params, attn_w, ffn_w)


class Place:
    def __init__(self, narrow):
        self.narrow = narrow
        w = lax.axis_index("wide")
        self.z = lax.axis_index("narrow")
        self.core = lax.rem(w, 2)
        self.chip = lax.rem(w // 2, 4)
        self.other = 1 - self.core
        self.hops = list(range(1, narrow))
        self.column_z = [lax.rem(self.z + hop, narrow) for hop in self.hops]
        self.column = [(w, place) for place in self.column_z]
        self.chip_at = [lax.rem(self.chip + hop, 4) for hop in range(1, 4)]
        self.chips = [(w - 2 * self.chip + 2 * chip, self.z) for chip in self.chip_at]
        self.mate = (w + 1 - 2 * self.core, self.z)


class Copies:
    def __init__(self, sems):
        self.sems = sems
        self.used = 0

    def remote(self, src, dst, device):
        at = self.used
        self.used += 2
        return remote(src, dst, self.sems.at[at], self.sems.at[at + 1], device)

    def local(self, src, dst):
        at = self.used
        self.used += 1
        return pltpu.make_async_copy(src, dst, self.sems.at[at])


def blocks_at(owner, size):
    return pl.ds(pl.multiple_of(owner * size, size), size)


def wide_sum(parts):
    total = parts[0].astype(wide_type)
    for part in parts[1:]:
        total = total + part.astype(wide_type)
    return total


def newton_poly(gram):
    size = gram.shape[0]
    eye = row_of((size, size)) == lane_of((size, size))
    trace = jnp.sum(jnp.where(eye, gram, 0.0), axis=1, keepdims=True)
    trace = jnp.sum(trace, axis=0, keepdims=True)
    scale = 1.0 / (jnp.sqrt(trace) + 1e-07)

    def low_dot(left, right):
        return dot_nn(left.astype(low_type), right.astype(low_type))

    def polynomial(one):
        poly = quintic_cube * one + quintic_five * low_dot(one, one)
        return poly + jnp.where(eye, quintic_lin, 0.0)

    gram_one = gram * (scale * scale)
    poly_one = polynomial(gram_one)
    gram_two = low_dot(low_dot(gram_one, poly_one), poly_one)
    poly_two = polynomial(gram_two)
    return low_dot(poly_one, poly_two) * scale


def back_kernel(*refs, narrow):
    blocks = list(refs[:9])
    gffn_hbm, go_hbm = refs[9:11]
    outs = list(refs[11:15])
    fsum_ref, osum_ref = refs[15:17]
    (state, carry, own_f, got_f, far_f, own_o, got_o, cut_o, far_o, sems) = refs[17:]
    step = pl.program_id(0)
    steps = pl.num_programs(0)
    here = Place(narrow)
    copies = Copies(sems)
    half = D // 2
    part = D // 4
    rows = cut_o.shape[2]

    keep_f = copies.local(gffn_hbm.at[here.core], own_f)
    keep_o = copies.local(go_hbm.at[:, blocks_at(here.core, half)], own_o)
    core_f = copies.remote(gffn_hbm.at[here.other], got_f, here.mate)
    core_o = copies.remote(go_hbm.at[:, blocks_at(here.other, half)], got_o, here.mate)
    plane_f, plane_o = [], []
    for hop in range(3):
        there = here.chip_at[hop]
        plane_f.append(
            copies.remote(own_f.at[blocks_at(there, part)], far_f.at[hop], here.chips[hop])
        )
        plane_o.append(copies.remote(cut_o.at[:, there], far_o.at[hop], here.chips[hop]))

    @pl.when(step == 0)
    def _():
        state[...] = jnp.zeros_like(state)
        carry[...] = jnp.zeros_like(carry)
        greet(here.chips + [here.mate])
        for copy in (core_f, core_o, keep_f, keep_o):
            copy.start()

    @pl.when(step == steps // 4)
    def _():
        for copy in (core_f, core_o, keep_f, keep_o):
            copy.wait()
        own_f[...] = wide_sum([own_f[...], got_f[...]]).astype(low_type)
        cut_o[...] = wide_sum([own_o[...], got_o[...]]).astype(low_type).reshape(cut_o.shape)
        for copy in plane_f + plane_o:
            copy.start()

    attend_back_chunk(blocks + outs, state, carry)

    @pl.when(step == steps - 1)
    def _():
        for copy in plane_f + plane_o:
            copy.wait()
        mine = own_f[blocks_at(here.chip, part), :]
        fsum_ref[...] = wide_sum([mine] + [far_f[hop] for hop in range(3)]).astype(low_type)
        mine = cut_o[:, here.chip]
        osum_ref[...] = wide_sum([mine] + [far_o[hop] for hop in range(3)]).astype(low_type)


def back(q, k, v, a, share, logit, before, datt, states, gffn, go):
    seqs, length, _ = q.shape
    chunks = length // CHUNK
    narrow = lax.axis_size("narrow")
    rows = D // narrow // 4
    block = pl.BlockSpec((seqs, CHUNK, D), lambda i: (0, chunks - 1 - i, 0))
    any_spec = pl.BlockSpec(memory_space=pl.ANY)
    f_shape, o_shape = (D // 4, FF), (narrow, rows, D // 2)
    return pl.pallas_call(
        functools.partial(back_kernel, narrow=narrow),
        grid=(chunks,),
        in_specs=[block] * 6
        + [
            pl.BlockSpec((1, seqs, 1, D), lambda i: (chunks - 1 - i, 0, 0, 0)),
            block,
            pl.BlockSpec(
                (1, seqs, PAIRS, PAIR, 2 * PAIR), lambda i: (chunks - 1 - i, 0, 0, 0, 0)
            ),
            any_spec,
            any_spec,
        ],
        out_specs=[block] * 4
        + [pl.BlockSpec(f_shape, lambda i: (0, 0)), pl.BlockSpec(o_shape, lambda i: (0, 0, 0))],
        out_shape=[jax.ShapeDtypeStruct(q.shape, low_type)] * 4
        + [jax.ShapeDtypeStruct(f_shape, low_type), jax.ShapeDtypeStruct(o_shape, low_type)],
        scratch_shapes=[
            pltpu.VMEM((seqs, PAIRS, PAIR, 2 * PAIR), wide_type),
            pltpu.VMEM((seqs, 1, D), wide_type),
            pltpu.VMEM((D, FF), low_type),
            pltpu.VMEM((D, FF), low_type),
            pltpu.VMEM((3,) + f_shape, low_type),
            pltpu.VMEM((D, D // 2), low_type),
            pltpu.VMEM((D, D // 2), low_type),
            pltpu.VMEM((narrow, 4, rows, D // 2), low_type),
            pltpu.VMEM((3,) + o_shape, low_type),
            pltpu.SemaphoreType.DMA((24,)),
        ],
        compiler_params=pltpu.CompilerParams(
            vmem_limit_bytes=VMEM_BYTES, collective_id=1, has_side_effects=True
        ),
        name="back",
    )(q, k, v, a, share, logit, before, datt, states, gffn, go)


def update_kernel(
    gw_hbm,
    fsum_ref,
    osum_ref,
    mom_in_hbm,
    mom_o_ref,
    mom_f_hbm,
    ln_one_ref,
    ln_two_ref,
    grad_attn,
    step_attn,
    grad_ffn,
    step_ffn,
    ln_ref,
    ln_now,
    ln_mate,
    ln_chips,
    ln_column,
    half_w,
    half_got,
    far_w,
    cut_w,
    col_w,
    grad_w,
    mom_w,
    moment_w,
    poly_w,
    send_w,
    all_w,
    col_f,
    all_f,
    mom_f,
    moment_f,
    out_f,
    col_o,
    all_o,
    moment_o,
    step_o,
    cut_gf,
    col_gf,
    strips_gf,
    gram_f,
    cut_go,
    col_go,
    strips_go,
    gram_o,
    sems,
    *,
    narrow,
):
    here = Place(narrow)
    copies = Copies(sems)
    z, core, chip = here.z, here.core, here.chip
    half = D // 2
    quarter = D // 4
    rows = D // narrow
    small = rows // 4
    ffn_rows = FF // narrow
    strip = quarter // narrow
    column = range(narrow - 1)
    planes = range(3)
    own_cols = blocks_at(core, half)
    mate_cols = blocks_at(here.other, half)
    own_quarter = blocks_at(chip, quarter)
    own_small = blocks_at(chip, small)
    matrix = lax.rem(z, 4)

    def to_plane(src, dst):
        return [copies.remote(src(i), dst(i), here.chips[i]) for i in planes]

    def to_column(src, dst):
        return [copies.remote(src(i), dst(i), here.column[i]) for i in column]

    def same(block):
        return lambda i: block

    keep_w = copies.local(gw_hbm.at[:, :, own_cols], half_w)
    keep_mom = copies.local(mom_in_hbm.at[matrix], mom_w)
    keep_f = copies.local(mom_f_hbm.at[core], mom_f)
    mate_sum = [
        copies.remote(gw_hbm.at[:, :, mate_cols], half_got, here.mate),
        copies.remote(ln_now, ln_mate, here.mate),
    ]
    z_sum_f = to_column(
        lambda i: fsum_ref.at[:, blocks_at(here.column_z[i], ffn_rows)], lambda i: col_f.at[i]
    ) + to_column(lambda i: osum_ref.at[here.column_z[i]], lambda i: col_o.at[i])
    plane_sum = to_plane(
        lambda i: half_w.at[:, blocks_at(here.chip_at[i], quarter)], lambda i: far_w.at[i]
    )
    plane_ln = to_plane(same(ln_now), lambda i: ln_chips.at[i])
    block = all_f.at[own_quarter]
    plane_f = to_plane(same(block), same(block))
    block = all_o.at[own_small, own_cols]
    plane_f = plane_f + to_plane(same(block), same(block))
    z_sum = to_column(lambda i: cut_w.at[lax.rem(here.column_z[i], 4)], lambda i: col_w.at[i])
    z_ln = to_column(same(ln_now), lambda i: ln_column.at[i])
    block = out_f.at[0, core]
    mate_f = copies.remote(block, block, here.mate)
    block = all_o.at[:, own_cols]
    mate_o = copies.remote(block, block, here.mate)
    z_gf = to_column(
        lambda i: cut_gf.at[blocks_at(here.column_z[i], strip)], lambda i: col_gf.at[i]
    )
    block = grad_w.at[own_quarter, own_cols]
    plane_w = to_plane(same(block), same(block))
    z_go = to_column(
        lambda i: cut_go.at[blocks_at(here.column_z[i], strip)], lambda i: col_go.at[i]
    )
    block = grad_w.at[:, own_cols]
    mate_w = copies.remote(block, block, here.mate)
    block = strips_gf.at[blocks_at(z, strip)]
    z_back_f = to_column(same(block), same(block))
    block = strips_go.at[blocks_at(z, strip)]
    z_back_o = to_column(same(block), same(block))
    block = gram_f.at[own_quarter]
    plane_gf = to_plane(same(block), same(block))
    block = gram_o.at[own_quarter, own_cols]
    plane_go = to_plane(same(block), same(block))
    spread = []
    for hop in range(1, 4):
        there = z - matrix + lax.rem(matrix + hop, 4)
        spread.append(
            copies.remote(
                send_w.at[there],
                all_w.at[matrix, :, own_small, own_cols],
                (lax.axis_index("wide"), there),
            )
        )
    block = gram_o.at[:, own_cols]
    mate_go = copies.remote(block, block, here.mate)
    block = out_f.at[1, core]
    mate_x = copies.remote(block, block, here.mate)
    block = all_w.at[:, :, own_small, own_cols]
    plane_all = to_plane(same(block), same(block))
    block = all_w.at[:, :, :, own_cols]
    mate_all = copies.remote(block, block, here.mate)
    write_f = [copies.local(out_f.at[0], grad_ffn), copies.local(out_f.at[1], step_ffn)]
    write_o = [copies.local(all_o, grad_attn.at[4]), copies.local(step_o, step_attn.at[4])]
    write_w = [
        copies.local(all_w.at[:, 0], grad_attn.at[pl.ds(0, 4)]),
        copies.local(all_w.at[:, 1], step_attn.at[pl.ds(0, 4)]),
    ]
    sent = []

    def start(group):
        for copy in group:
            copy.start()
        sent.extend(group)

    def arrive(group):
        for copy in group:
            copy.wait_recv()

    def begin(group):
        for copy in group:
            copy.start()

    greet(here.column + here.chips + [here.mate])
    keep_w.start()
    ln_now[...] = jnp.zeros_like(ln_now)
    ln_now[0:2, :] = ln_one_ref[...]
    ln_now[2:4, :] = ln_two_ref[...]
    start(mate_sum)
    start(z_sum_f)
    begin([keep_f, keep_mom])

    keep_w.wait()
    arrive(mate_sum)
    half_w[...] = wide_sum([half_w[...], half_got[...]]).astype(low_type)
    start(plane_sum)
    mate_sum[1].wait_send()
    ln_now[...] = ln_now[...] + ln_mate[...]
    start(plane_ln)

    arrive(z_sum_f)
    total = wide_sum([fsum_ref[:, blocks_at(z, ffn_rows)]] + [col_f[i] for i in column])
    all_f[own_quarter, :] = total.astype(low_type)
    total = wide_sum([osum_ref[z]] + [col_o[i] for i in column])
    all_o[own_small, own_cols] = total.astype(low_type)
    start(plane_f)

    arrive(plane_sum)
    mine = half_w[:, own_quarter, :]
    cut_w[...] = wide_sum([mine] + [far_w[i] for i in planes]).astype(low_type)
    start(z_sum)
    arrive(plane_ln)
    for copy in plane_ln:
        copy.wait_send()
    ln_now[...] = ln_now[...] + ln_chips[0] + ln_chips[1] + ln_chips[2]
    start(z_ln)

    keep_f.wait()
    arrive(plane_f)
    start([mate_o])
    grad = all_f[...].T
    out_f[0, core] = grad
    start([mate_f])
    moment_f[...] = (momentum_keep * mom_f[...] + grad.astype(wide_type)).astype(low_type)
    cut_gf[...] = dot_tn(moment_f[:, own_quarter], moment_f[...]).astype(low_type)
    start(z_gf)

    arrive(z_sum)
    total = wide_sum([cut_w[matrix]] + [col_w[i] for i in column])
    grad_w[own_quarter, own_cols] = total.astype(low_type)
    start(plane_w)

    arrive([mate_o])
    moment = momentum_keep * mom_o_ref[...] + all_o[...].astype(wide_type)
    moment_o[...] = moment.astype(low_type)
    cut_go[...] = dot_tn(moment_o[:, own_quarter], moment_o[:, own_cols]).astype(low_type)
    start(z_go)

    arrive(plane_w)
    start([mate_w])

    arrive(z_gf)
    total = wide_sum([cut_gf[blocks_at(z, strip), :]] + [col_gf[i] for i in column])
    strips_gf[blocks_at(z, strip), :] = total.astype(low_type)
    start(z_back_f)
    arrive(z_go)
    total = wide_sum([cut_go[blocks_at(z, strip), :]] + [col_go[i] for i in column])
    strips_go[blocks_at(z, strip), :] = total.astype(low_type)
    start(z_back_o)

    keep_mom.wait()
    arrive([mate_w])
    moment = momentum_keep * mom_w[...].astype(wide_type) + grad_w[...].astype(wide_type)
    moment_w[...] = moment.astype(low_type)
    gram = dot_tn(moment_w[...], moment_w[...])

    arrive(z_back_f)
    gram_f[own_quarter, :] = strips_gf[...]
    start(plane_gf)
    arrive(z_back_o)
    gram_o[own_quarter, own_cols] = strips_go[...]
    start(plane_go)

    poly_w[...] = newton_poly(gram).astype(low_type)
    picked = [moment_w[pl.ds(pl.multiple_of(there * rows + chip * small, small), small), :] for there in range(narrow)]
    ortho = dot_nn(jnp.concatenate(picked, axis=0), poly_w[:, own_cols]).astype(low_type)
    for there in range(narrow):
        place = pl.ds(pl.multiple_of(there * rows + chip * small, small), small)
        send_w[there, 0] = grad_w[place, own_cols]
        send_w[there, 1] = ortho[there * small : (there + 1) * small, :]
    start(spread)
    all_w[matrix, :, own_small, own_cols] = send_w[z]

    arrive(plane_go)
    start([mate_go])
    arrive(plane_gf)
    poly = newton_poly(gram_f[...].astype(wide_type)).astype(low_type)
    out_f[1, core] = dot_nn(moment_f[...], poly).astype(low_type)
    start([mate_x])

    arrive(spread)
    start(plane_all)

    arrive([mate_go])
    poly = newton_poly(gram_o[...].astype(wide_type)).astype(low_type)
    step_o[...] = dot_nn(moment_o[...], poly).astype(low_type)
    begin(write_o)
    arrive([mate_f, mate_x])
    begin(write_f)
    arrive(z_ln)
    total = ln_now[...]
    for i in column:
        total = total + ln_column[i]
    ln_ref[...] = total

    arrive(plane_all)
    start([mate_all])
    arrive([mate_all])
    begin(write_w)
    for copy in write_o + write_f + write_w:
        copy.wait()
    settled = [id(copy) for copy in [mate_sum[1]] + plane_ln]
    for copy in sent:
        if id(copy) not in settled:
            copy.wait_send()


def update(gw, fsum, osum, mom_in, mom_o, mom_f, ln_one, ln_two):
    narrow = lax.axis_size("narrow")
    rows, ffn_rows = D // narrow, FF // narrow
    small, half, quarter = rows // 4, D // 2, D // 4
    strip = quarter // narrow
    column = narrow - 1
    any_spec = pl.BlockSpec(memory_space=pl.ANY)
    vmem = pl.BlockSpec(memory_space=pltpu.VMEM)

    def low(*shape):
        return pltpu.VMEM(shape, low_type)

    def full(*shape):
        return pltpu.VMEM(shape, wide_type)

    scratch = [
        full(8, D),
        full(8, D),
        full(3, 8, D),
        full(column, 8, D),
        low(4, D, half),
        low(4, D, half),
        low(3, 4, quarter, half),
        low(4, quarter, half),
        low(column, quarter, half),
        low(D, D),
        low(D, D),
        low(D, D),
        low(D, D),
        low(narrow, 2, small, half),
        low(4, 2, rows, D),
        low(column, quarter, ffn_rows),
        low(D, ffn_rows),
        full(ffn_rows, D),
        low(ffn_rows, D),
        low(2, 2, ffn_rows, D),
        low(column, small, half),
        low(rows, D),
        low(rows, D),
        low(rows, D),
        low(quarter, D),
        low(column, strip, D),
        low(quarter, D),
        low(D, D),
        low(quarter, half),
        low(column, strip, half),
        low(quarter, half),
        low(D, D),
        pltpu.SemaphoreType.DMA((9 + 2 * (10 + 27 + 9 * column),)),
    ]
    return pl.pallas_call(
        functools.partial(update_kernel, narrow=narrow),
        in_specs=[any_spec, vmem, vmem, any_spec, vmem, any_spec, vmem, vmem],
        out_specs=[any_spec, any_spec, any_spec, any_spec, vmem],
        out_shape=[
            jax.ShapeDtypeStruct((5, rows, D), low_type),
            jax.ShapeDtypeStruct((5, rows, D), low_type),
            jax.ShapeDtypeStruct((2, ffn_rows, D), low_type),
            jax.ShapeDtypeStruct((2, ffn_rows, D), low_type),
            jax.ShapeDtypeStruct((8, D), wide_type),
        ],
        scratch_shapes=scratch,
        compiler_params=pltpu.CompilerParams(
            vmem_limit_bytes=VMEM_BYTES, collective_id=2, has_side_effects=True
        ),
        name="update",
    )(gw, fsum, osum, mom_in, mom_o, mom_f, ln_one, ln_two)


def group_sum(values):
    wide = lax.axis_size("wide")
    if wide == 8:
        return values
    groups = [[place + 8 * group for group in range(wide // 8)] for place in range(8)]
    return lax.psum(values, "wide", axis_index_groups=groups)


def shards(
    tokens,
    out_grad,
    group_ids,
    domain_weight,
    attn_w,
    ffn_w,
    attn_mom,
    ffn_mom,
    ln_params,
    ln_first,
    ln_second,
):
    local_seqs, length, _ = tokens.shape
    token_count = local_seqs * length
    rows = tokens.reshape(token_count, D)
    head = (local_seqs, length, D)
    q, k, v, a, att, share, logit, before, states, weights, in_w, out_w, ffn_low = forward(
        tokens, group_ids, domain_weight, ln_params, attn_w, ffn_w
    )
    moms = attn_mom[:4].astype(low_type)
    moms, weights = lax.optimization_barrier((moms, weights))
    mom_in = lax.all_gather(moms, "narrow", axis=1, tiled=True)
    output, dx, datt, gffn, go, ln_two = feed(
        group_ids,
        weights,
        rows,
        att.reshape(token_count, D),
        out_grad.reshape(token_count, D),
        out_w,
        ffn_low,
        ln_params,
        length,
    )
    gffn, go, ln_two = group_sum((gffn, go, ln_two))
    dq, dk, dv, de, fsum, osum = back(
        q, k, v, a, share, logit, before, datt.reshape(head), states, gffn, go
    )
    dq, dk, dv, de = (item.reshape(token_count, D) for item in (dq, dk, dv, de))
    input_grad, gw, ln_one = project_back(rows, dx, dq, dk, dv, de, in_w, ln_params)
    gw, ln_one = group_sum((gw, ln_one))
    attn_low, attn_ortho, ffn_low_grad, ffn_ortho, ln_sum = update(
        gw, fsum, osum, mom_in, attn_mom[4], ffn_mom, ln_one, ln_two
    )
    attn_grad = attn_low.astype(wide_type)
    ffn_grad = ffn_low_grad.astype(wide_type)
    attn_ortho = attn_ortho.astype(wide_type)
    ffn_ortho = ffn_ortho.astype(wide_type)
    shard_width = ln_first.shape[1]
    ln_grad = lax.dynamic_slice_in_dim(
        ln_sum[:4], lax.axis_index("narrow") * shard_width, shard_width, 1
    )

    attn_moment = momentum_keep * attn_mom + attn_grad
    ffn_moment = momentum_keep * ffn_mom + ffn_grad
    keep_factor = 1.0 - muon_rate * muon_decay
    attn_new = keep_factor * attn_w - muon_rate * 0.2 * math.sqrt(D) * attn_ortho
    ffn_new = keep_factor * ffn_w - muon_rate * 0.2 * math.sqrt(FF) * ffn_ortho
    own_params = lax.dynamic_slice_in_dim(
        ln_params, lax.axis_index("narrow") * shard_width, shard_width, 1
    )
    first_new = beta_first * ln_first + (1.0 - beta_first) * ln_grad
    second_new = beta_second * ln_second + (1.0 - beta_second) * ln_grad * ln_grad
    first_fix = 1.0 - beta_first**STEP
    second_fix = 1.0 - beta_second**STEP
    ln_new = own_params - adam_rate * (first_new / first_fix) / (
        jnp.sqrt(second_new / second_fix) + adam_epsilon
    )
    return (
        output.reshape(tokens.shape),
        input_grad.reshape(tokens.shape),
        attn_grad,
        ffn_grad,
        ln_grad,
        attn_moment,
        ffn_moment,
        attn_new,
        ffn_new,
        attn_new.astype(low_type),
        ffn_new.astype(low_type),
        first_new,
        second_new,
        ln_new,
    )


def solution(mesh):
    split = P(("wide", "narrow"), None, None)
    rows = P(None, "narrow", None)
    lanes = P(None, "narrow")
    inner = jax.shard_map(
        shards,
        mesh=mesh,
        in_specs=(
            split,
            split,
            P(("wide", "narrow")),
            P(),
            rows,
            rows,
            rows,
            rows,
            P(),
            lanes,
            lanes,
        ),
        out_specs=(
            split,
            split,
            rows,
            rows,
            lanes,
            rows,
            rows,
            rows,
            rows,
            rows,
            rows,
            lanes,
            lanes,
            lanes,
        ),
        check_vma=False,
    )
    return inner
```

```python
import functools
import math

import jax
import jax.numpy as jnp
from jax import lax
from jax.experimental import pallas as pl
from jax.experimental.pallas import tpu as pltpu
from jax.sharding import PartitionSpec as P

D = 512
HEADS = 8
HEAD_DIM = 64
FF = 2048
STEP = 10

norm_epsilon = 1e-05
momentum_keep = 0.5
quintic_lin = 3.4445
quintic_cube = -4.775
quintic_five = 2.0315
muon_rate = 0.7
muon_decay = 0.1
adam_rate = 0.2
beta_first = 0.9
beta_second = 0.999
adam_epsilon = 1e-08

CHUNK = 128
PAIR = 2 * HEAD_DIM
PAIRS = HEADS // 2
VMEM_BYTES = 60 * 1024 * 1024
low_type = jnp.bfloat16
wide_type = jnp.float32


def dot_nn(left, right):
    return lax.dot_general(left, right, (((1,), (0,)), ((), ())), preferred_element_type=wide_type)


def dot_nt(left, right):
    return lax.dot_general(left, right, (((1,), (1,)), ((), ())), preferred_element_type=wide_type)


def dot_tn(left, right):
    return lax.dot_general(left, right, (((0,), (0,)), ((), ())), preferred_element_type=wide_type)


def normalize(rows):
    center = rows - jnp.mean(rows, axis=-1, keepdims=True)
    spread = jnp.mean(center * center, axis=-1, keepdims=True)
    inverse = lax.rsqrt(spread + norm_epsilon)
    return center * inverse, inverse


def norm_back(grad_rows, normed, inverse, gain):
    grad_normed = grad_rows * gain
    mean_grad = jnp.mean(grad_normed, axis=-1, keepdims=True)
    mean_cross = jnp.mean(grad_normed * normed, axis=-1, keepdims=True)
    return inverse * (grad_normed - mean_grad - normed * mean_cross)


def lane_of(shape):
    return lax.broadcasted_iota(jnp.int32, shape, 1)


def row_of(shape):
    return lax.broadcasted_iota(jnp.int32, shape, 0)


def split_pair(pair, first_head):
    zero = jnp.zeros_like(pair)
    return jnp.concatenate(
        [jnp.where(first_head, pair, zero), jnp.where(first_head, zero, pair)], axis=0
    )


def head_reduce(values, first_head, op, neutral):
    left = op(jnp.where(first_head, values, neutral), axis=-1, keepdims=True)
    right = op(jnp.where(first_head, neutral, values), axis=-1, keepdims=True)
    return jnp.where(first_head, left, right)


def attend_back_chunk(refs, state, carry):
    (
        q_ref,
        k_ref,
        v_ref,
        a_ref,
        share_ref,
        logit_ref,
        before_ref,
        datt_ref,
        state_ref,
        dq_ref,
        dk_ref,
        dv_ref,
        de_ref,
    ) = refs
    scaling = HEAD_DIM**-0.5
    first_head = lane_of((CHUNK, PAIR)) < HEAD_DIM
    causal = row_of((CHUNK, 2 * CHUNK)) >= lane_of((CHUNK, 2 * CHUNK)) % CHUNK
    anti = row_of((CHUNK, 2 * CHUNK)) <= lane_of((CHUNK, 2 * CHUNK)) % CHUNK
    same_head = (row_of((PAIR, 2 * PAIR)) // HEAD_DIM) == (
        (lane_of((PAIR, 2 * PAIR)) // HEAD_DIM) % 2
    )
    lower = (row_of((CHUNK, CHUNK)) >= lane_of((CHUNK, CHUNK))).astype(low_type)
    upper = (row_of((CHUNK, CHUNK)) <= lane_of((CHUNK, CHUNK))).astype(low_type)

    def masked(mask, raw):
        return jnp.where(mask, raw, 0.0).astype(low_type)

    items = []
    for seq in range(q_ref.shape[0]):
        total = dot_nn(lower, a_ref[seq]) + before_ref[0, seq]
        inv = 1.0 / total
        for pair in range(PAIRS):
            lanes = slice(pair * PAIR, (pair + 1) * PAIR)
            items.append(
                dict(seq=seq, pair=pair, lanes=lanes, total=total[:, lanes], inv=inv[:, lanes])
            )

    def load(t):
        seq, lanes = t["seq"], t["lanes"]
        t["k"] = k_ref[seq, :, lanes]
        t["v"] = v_ref[seq, :, lanes]
        t["a"] = a_ref[seq, :, lanes]
        t["share"] = share_ref[seq, :, lanes]
        t["datt"] = datt_ref[seq, :, lanes]
        t["q"] = q_ref[seq, :, lanes] * low_type(scaling)
        t["before"] = state_ref[0, seq, t["pair"]]
        t["after"] = jnp.where(same_head, state[seq, t["pair"]], 0.0).astype(low_type)
        t["v_two"] = split_pair(t["v"], first_head)
        t["a_two"] = split_pair(t["a"], first_head)
        t["dmix"] = masked(causal, dot_nt(t["datt"], t["v_two"]))

    def gather(t):
        t["share_two"] = split_pair(t["share"], first_head)
        t["datt_two"] = split_pair(t["datt"], first_head)
        t["dshare"] = dot_nn(t["dmix"], t["a_two"]) + dot_nt(t["datt"], t["before"][:, PAIR:])

    def soften(t):
        logit = logit_ref[t["seq"], :, t["lanes"]].astype(wide_type)
        prob = t["share"].astype(wide_type) * t["total"]
        cross = t["dshare"] * t["inv"] * prob
        dlogit = cross - prob * head_reduce(cross, first_head, jnp.sum, 0.0)
        t["dnumer"] = (dlogit * t["inv"]).astype(low_type)
        t["dtotal"] = -(cross + dlogit * logit) * t["inv"]
        t["mix_t"] = masked(anti, dot_nt(t["a"], t["share_two"]))
        t["dmix_t"] = masked(anti, dot_nt(t["v"], t["datt_two"]))

    def blend(t):
        t["dnumer_two"] = split_pair(t["dnumer"], first_head)
        t["dscores"] = masked(causal, dot_nt(t["dnumer"], t["a_two"]))
        t["dscores_t"] = masked(anti, dot_nt(t["a"], t["dnumer_two"]))
        t["k_two"] = split_pair(t["k"], first_head)
        t["q_two"] = split_pair(t["q"], first_head)
        t["scores_t"] = masked(anti, dot_nt(t["k"], t["q_two"]))
        t["later"] = dot_nn(t["a"], t["after"])

    def finish(t):
        seq, lanes = t["seq"], t["lanes"]
        dq = dot_nn(t["dscores"], t["k_two"]) + dot_nn(t["dnumer"], t["before"][:, :PAIR])
        dq_ref[seq, :, lanes] = (dq * scaling).astype(low_type)
        dv = dot_nn(t["mix_t"], t["datt_two"]) + t["later"][:, PAIR:]
        dv_ref[seq, :, lanes] = dv.astype(low_type)
        dk = dot_nn(t["dscores_t"], t["q_two"]) + t["later"][:, :PAIR]
        dk_ref[seq, :, lanes] = dk.astype(low_type)
        high = t["dtotal"].astype(low_type)
        rest = (t["dtotal"] - high.astype(wide_type)).astype(low_type)
        tail = dot_nn(upper, high) + dot_nn(upper, rest) + carry[seq, :, lanes]
        carry[seq, :, lanes] = tail[0:1, :]
        da = dot_nn(t["dmix_t"], t["share_two"]) + dot_nn(t["scores_t"], t["dnumer_two"])
        da = da + dot_nt(jnp.concatenate([t["k"], t["v"]], axis=1), t["after"]) + tail
        de = da.astype(low_type).astype(wide_type) * t["a"].astype(wide_type)
        de_ref[seq, :, lanes] = de.astype(low_type)
        state[seq, t["pair"], :, :PAIR] += dot_tn(t["dnumer"], t["q"])
        state[seq, t["pair"], :, PAIR:] += dot_tn(t["share"], t["datt"])

    for stage in (load, gather, soften, blend, finish):
        for item in items:
            stage(item)


FF_BLOCK = 512
gelu_root = math.sqrt(2.0 / math.pi)
gelu_cube = 0.044715


def feed_kernel(
    ids_ref,
    weight_ref,
    x_ref,
    att_ref,
    og_ref,
    wo_ref,
    ffn_ref,
    ln_ref,
    out_ref,
    dx_ref,
    datt_ref,
    gffn_ref,
    go_ref,
    gln_ref,
    up_sum,
    down_sum,
    o_sum,
    *,
    per_seq,
):
    step = pl.program_id(0)

    @pl.when(step == 0)
    def _():
        up_sum[...] = jnp.zeros_like(up_sum)
        down_sum[...] = jnp.zeros_like(down_sum)
        o_sum[...] = jnp.zeros_like(o_sum)
        gln_ref[...] = jnp.zeros_like(gln_ref)

    att = att_ref[...]
    mixed = x_ref[...].astype(wide_type) + dot_nn(att, wo_ref[...])
    normed, inverse = normalize(mixed)
    second = (normed * ln_ref[2:3, :] + ln_ref[3:4, :]).astype(low_type)
    mine = lane_of((1, LANES)) == ids_ref[step // per_seq]
    weight = jnp.sum(jnp.where(mine, weight_ref[0:1, :], 0.0), axis=1, keepdims=True)
    dout = og_ref[...].astype(wide_type) * weight
    dy = dout.astype(low_type)
    second_t = second.T
    dy_t = dy.T
    parts = [dict(rows=slice(part * FF_BLOCK, (part + 1) * FF_BLOCK)) for part in range(FF // FF_BLOCK)]

    def open_part(t):
        t["up"] = ffn_ref[0, t["rows"], :]
        t["down"] = ffn_ref[1, t["rows"], :]
        t["inner"] = dot_nt(second, t["up"])
        t["dhidden"] = dot_nt(dy, t["down"])

    result, dsecond = mixed, 0.0
    open_part(parts[0])
    for place, t in enumerate(parts):
        if place + 1 < len(parts):
            open_part(parts[place + 1])
        inner = t["inner"]
        square = inner * inner
        bend = jnp.tanh(inner * (gelu_root + (gelu_root * gelu_cube) * square))
        half = 0.5 + 0.5 * bend
        hidden = (inner * half).astype(low_type)
        slope = half + (0.5 * inner) * (1.0 - bend * bend) * (
            gelu_root + (3.0 * gelu_root * gelu_cube) * square
        )
        dinner = (t["dhidden"] * slope).astype(low_type)
        result = result + dot_nn(hidden, t["down"])
        down_sum[:, t["rows"]] += dot_nn(dy_t, hidden)
        up_sum[:, t["rows"]] += dot_nn(second_t, dinner)
        dsecond = dsecond + dot_nn(dinner, t["up"])
    out_ref[...] = result.astype(low_type)
    gln_ref[0:1, :] += jnp.sum(dsecond * normed, axis=0, keepdims=True)
    gln_ref[1:2, :] += jnp.sum(dsecond, axis=0, keepdims=True)
    dmixed = dout + norm_back(dsecond, normed, inverse, ln_ref[2:3, :])
    datt = dmixed.astype(low_type)
    dx_ref[...] = datt
    o_sum[...] += dot_tn(att, datt)
    datt_ref[...] = dot_nt(datt, wo_ref[...]).astype(low_type)

    @pl.when(step == pl.num_programs(0) - 1)
    def _():
        gffn_ref[0] = up_sum[...].astype(low_type)
        gffn_ref[1] = down_sum[...].astype(low_type)
        go_ref[...] = o_sum[...].astype(low_type)


def feed(ids, weights, rows, att, grad, wo, ffn, ln_params, length):
    count = rows.shape[0]
    block = 512
    row_spec = pl.BlockSpec((block, D), lambda i: (i, 0))

    def whole(*shape):
        return pl.BlockSpec(shape, lambda i: (0,) * len(shape))

    return pl.pallas_call(
        functools.partial(feed_kernel, per_seq=length // block),
        grid=(count // block,),
        in_specs=[
            pl.BlockSpec(memory_space=pltpu.SMEM),
            whole(8, LANES),
            row_spec,
            row_spec,
            row_spec,
            whole(D, D),
            whole(2, FF, D),
            whole(4, D),
        ],
        out_specs=[
            row_spec,
            row_spec,
            row_spec,
            whole(2, D, FF),
            whole(D, D),
            whole(2, D),
        ],
        out_shape=[
            jax.ShapeDtypeStruct((count, D), low_type),
            jax.ShapeDtypeStruct((count, D), low_type),
            jax.ShapeDtypeStruct((count, D), low_type),
            jax.ShapeDtypeStruct((2, D, FF), low_type),
            jax.ShapeDtypeStruct((D, D), low_type),
            jax.ShapeDtypeStruct((2, D), wide_type),
        ],
        scratch_shapes=[
            pltpu.VMEM((D, FF), wide_type),
            pltpu.VMEM((D, FF), wide_type),
            pltpu.VMEM((D, D), wide_type),
        ],
        compiler_params=pltpu.CompilerParams(vmem_limit_bytes=VMEM_BYTES),
        name="feed",
    )(ids, weights, rows, att, grad, wo, ffn, ln_params)


def finish_kernel(
    dx_ref,
    dz_ref,
    ga_ref,
    sa_ref,
    wa_ref,
    ma_ref,
    gf_ref,
    sf_ref,
    wf_ref,
    mf_ref,
    ln_ref,
    first_ref,
    second_ref,
    sum_ref,
    grad_ref,
    ga_out,
    ma_out,
    wa_out,
    ca_out,
    gf_out,
    mf_out,
    wf_out,
    cf_out,
    gl_out,
    first_out,
    second_out,
    ln_out,
):
    grad_ref[...] = dx_ref[...].astype(wide_type) + dz_ref[...].astype(wide_type)
    keep = 1.0 - muon_rate * muon_decay
    for refs, size in (
        ((ga_ref, sa_ref, wa_ref, ma_ref, ga_out, ma_out, wa_out, ca_out), D),
        ((gf_ref, sf_ref, wf_ref, mf_ref, gf_out, mf_out, wf_out, cf_out), FF),
    ):
        grad, ortho, weight, moment, grad_out, moment_out, weight_out, copy_out = refs
        grad = grad[...].astype(wide_type)
        grad_out[...] = grad
        moment_out[...] = momentum_keep * moment[...] + grad
        rate = muon_rate * 0.2 * math.sqrt(size)
        new = keep * weight[...] - rate * ortho[...].astype(wide_type)
        weight_out[...] = new
        copy_out[...] = new.astype(low_type)
    width = first_ref.shape[1]
    place = lax.axis_index("narrow")

    def own(ref):
        picked = jnp.zeros((4, width), wide_type)
        for at in range(D // width):
            picked = picked + jnp.where(place == at, ref[0:4, at * width : (at + 1) * width], 0.0)
        return picked

    grad = own(sum_ref)
    first = beta_first * first_ref[...] + (1.0 - beta_first) * grad
    second = beta_second * second_ref[...] + (1.0 - beta_second) * grad * grad
    gl_out[...] = grad
    first_out[...] = first
    second_out[...] = second
    first_fix = 1.0 - beta_first**STEP
    second_fix = 1.0 - beta_second**STEP
    ln_out[...] = own(ln_ref) - adam_rate * (first / first_fix) / (
        jnp.sqrt(second / second_fix) + adam_epsilon
    )


def finish(dx, dz, attn, ffn, ln):
    steps = 8

    def rows(item):
        block = item.shape[0] // steps
        return pl.BlockSpec((block, item.shape[1]), lambda i: (i, 0))

    def whole(item):
        return pl.BlockSpec(item.shape, lambda i: (0, 0))

    def outs(group):
        shape = group[0].shape
        return [jax.ShapeDtypeStruct(shape, wide_type)] * 3 + [
            jax.ShapeDtypeStruct(shape, low_type)
        ]

    row_items = [dx, dz] + list(attn) + list(ffn)
    row_outs = [jax.ShapeDtypeStruct(dx.shape, wide_type)] + outs(attn) + outs(ffn)
    ln_outs = [jax.ShapeDtypeStruct(ln[1].shape, wide_type)] * 4
    return pl.pallas_call(
        finish_kernel,
        grid=(steps,),
        in_specs=[rows(item) for item in row_items] + [whole(item) for item in ln],
        out_specs=[rows(item) for item in row_outs] + [whole(item) for item in ln_outs],
        out_shape=row_outs + ln_outs,
        compiler_params=pltpu.CompilerParams(vmem_limit_bytes=VMEM_BYTES),
        name="finish",
    )(*row_items, *ln)


MESH = pl.DeviceIdType.MESH
LANES = 128


def remote(src, dst, send_sem, recv_sem, device):
    return pltpu.make_async_remote_copy(
        src_ref=src,
        dst_ref=dst,
        send_sem=send_sem,
        recv_sem=recv_sem,
        device_id=device,
        device_id_type=MESH,
    )


def greet(devices):
    barrier = pltpu.get_barrier_semaphore()
    for device in devices:
        pl.semaphore_signal(barrier, inc=1, device_id=device, device_id_type=MESH)
    pl.semaphore_wait(barrier, len(devices))


def attend_chunks(q_all, k_all, v_all, a_all, refs, seqs):
    att_ref, share_ref, logit_ref, before_ref, state_ref, state, carry = refs
    first_head = lane_of((CHUNK, PAIR)) < HEAD_DIM
    causal = row_of((CHUNK, 2 * CHUNK)) >= lane_of((CHUNK, 2 * CHUNK)) % CHUNK
    same_head = (row_of((PAIR, 2 * PAIR)) // HEAD_DIM) == (
        (lane_of((PAIR, 2 * PAIR)) // HEAD_DIM) % 2
    )
    lower = (row_of((CHUNK, CHUNK)) >= lane_of((CHUNK, CHUNK))).astype(low_type)
    items = []
    for seq in range(seqs):
        part = slice(seq * CHUNK, (seq + 1) * CHUNK)
        before = carry[seq]
        before_ref[0, seq] = before
        total = dot_nn(lower, a_all[part]) + before
        carry[seq] = total[CHUNK - 1 :, :]
        inv = 1.0 / total
        for pair in range(PAIRS):
            lanes = slice(pair * PAIR, (pair + 1) * PAIR)
            items.append(
                dict(
                    seq=seq,
                    pair=pair,
                    lanes=lanes,
                    q=q_all[part, lanes] * low_type(HEAD_DIM**-0.5),
                    k=k_all[part, lanes],
                    v=v_all[part, lanes],
                    a=a_all[part, lanes],
                    inv=inv[:, lanes],
                )
            )

    def score(t):
        t["a_two"] = split_pair(t["a"], first_head)
        t["now"] = jnp.where(same_head, state[t["seq"], t["pair"]], 0.0).astype(low_type)
        state_ref[0, t["seq"], t["pair"]] = t["now"]
        raw = dot_nt(t["q"], split_pair(t["k"], first_head))
        t["scores"] = jnp.where(causal, raw, 0.0).astype(low_type)

    def gather(t):
        numer = dot_nn(t["scores"], t["a_two"]) + dot_nt(t["q"], t["now"][:, :PAIR])
        t["logit"] = numer * t["inv"]
        logit_ref[t["seq"], :, t["lanes"]] = t["logit"].astype(low_type)

    def soften(t):
        expo = jnp.exp(t["logit"] - head_reduce(t["logit"], first_head, jnp.max, -jnp.inf))
        share = expo * (t["inv"] / head_reduce(expo, first_head, jnp.sum, 0.0))
        t["share"] = share.astype(low_type)
        share_ref[t["seq"], :, t["lanes"]] = t["share"]

    def blend(t):
        raw = dot_nt(t["share"], t["a_two"])
        t["mix"] = jnp.where(causal, raw, 0.0).astype(low_type)

    def finish(t):
        att = dot_nn(t["mix"], split_pair(t["v"], first_head))
        att = att + dot_nn(t["share"], t["now"][:, PAIR:])
        att_ref[t["seq"], :, t["lanes"]] = att.astype(low_type)
        state[t["seq"], t["pair"]] += dot_tn(t["a"], jnp.concatenate([t["k"], t["v"]], axis=1))

    for stage in (score, gather, soften, blend, finish):
        for item in items:
            stage(item)


def forward_kernel(
    ids_ref,
    dw_ref,
    x_ref,
    ln_ref,
    attn_ref,
    ffn_ref,
    q_ref,
    k_ref,
    v_ref,
    a_ref,
    att_ref,
    share_ref,
    logit_ref,
    before_ref,
    state_ref,
    weight_ref,
    in_hbm,
    out_hbm,
    ffn_hbm,
    state,
    carry,
    in_w,
    own,
    own_ffn,
    counts,
    counts_z,
    counts_w,
    in_sems,
    in_far,
    ffn_sems,
    ffn_far,
    out_sems,
    out_far,
    cz_send,
    cz_recv,
    cw_send,
    cw_recv,
    local_sems,
    *,
    wide,
    narrow,
    total_seqs,
    groups,
):
    step = pl.program_id(0)
    steps = pl.num_programs(0)
    seqs = x_ref.shape[0]
    w = lax.axis_index("wide")
    z = lax.axis_index("narrow")
    core = lax.rem(w, 2)
    mate = (w + 1 - 2 * core, z)
    other = 1 - core
    rows = attn_ref.shape[1]
    ffn_rows = ffn_ref.shape[1]
    half = rows // 2
    quarter = ffn_rows // 4
    chip = lax.rem(w // 2, 4)
    hops = list(range(1, narrow))
    column = [(w, lax.rem(z + hop, narrow)) for hop in hops]
    plane = [(lax.rem(w + hop, wide), z) for hop in range(1, wide)]
    chips = [(w - 2 * chip + 2 * lax.rem(chip + hop, 4), z) for hop in range(1, 4)]

    def at(owner, size):
        return pl.ds(pl.multiple_of(owner * size, size), size)

    def from_z(place):
        return lax.rem(z + narrow - hops[place], narrow)

    def in_part(owner, matrix):
        return in_w.at[matrix, at(2 * owner + core, half)]

    def in_z(place):
        return remote(
            own.at[chip, at(core, half)],
            in_part(z, chip),
            in_sems.at[0, place],
            in_sems.at[1, place],
            column[place],
        )

    def in_chip(place, hop):
        block = in_part(from_z(place), chip)
        return remote(
            block, block, in_far.at[0, place, hop], in_far.at[1, place, hop], chips[hop]
        )

    def in_core(place):
        block = in_w.at[:, at(2 * from_z(place) + core, half)]
        return remote(block, block, in_sems.at[2, place], in_sems.at[3, place], mate)

    def ffn_z(place):
        return remote(
            own_ffn.at[core, at(chip, quarter)],
            ffn_hbm.at[core, at(4 * z + chip, quarter)],
            ffn_sems.at[0, place],
            ffn_sems.at[1, place],
            column[place],
        )

    def ffn_chip(place, hop):
        block = ffn_hbm.at[core, at(4 * from_z(place) + chip, quarter)]
        return remote(
            block, block, ffn_far.at[0, place, hop], ffn_far.at[1, place, hop], chips[hop]
        )

    def ffn_core(place):
        block = ffn_hbm.at[core, at(from_z(place), ffn_rows)]
        return remote(block, block, ffn_sems.at[2, place], ffn_sems.at[3, place], mate)

    def out_block(owner, part):
        return out_hbm.at[at(4 * owner + part, rows // 4), at(core, D // 2)]

    def out_z(place):
        return remote(
            own.at[4, at(chip, rows // 4), at(core, D // 2)],
            out_block(z, chip),
            out_sems.at[0, place],
            out_sems.at[1, place],
            column[place],
        )

    def out_chip(place, hop):
        block = out_block(from_z(place), chip)
        return remote(
            block, block, out_far.at[0, place, hop], out_far.at[1, place, hop], chips[hop]
        )

    def out_core(place):
        block = out_hbm.at[at(from_z(place), rows), at(core, D // 2)]
        return remote(block, block, out_sems.at[2, place], out_sems.at[3, place], mate)

    def count_z(place):
        return remote(
            counts, counts_z.at[place], cz_send.at[place], cz_recv.at[place], column[place]
        )

    def count_w(place):
        return remote(
            counts, counts_w.at[place], cw_send.at[place], cw_recv.at[place], plane[place]
        )

    keep_ffn = pltpu.make_async_copy(own_ffn, ffn_hbm.at[:, at(z, ffn_rows)], local_sems.at[0])
    keep_out = pltpu.make_async_copy(own.at[4], out_hbm.at[at(z, rows)], local_sems.at[1])
    keep_in = pltpu.make_async_copy(in_w, in_hbm, local_sems.at[2])

    @pl.when(step == 0)
    def _():
        state[...] = jnp.zeros_like(state)
        carry[...] = jnp.zeros_like(carry)
        own[chip, at(core, half), :] = attn_ref[chip, at(core, half), :].astype(low_type)
        greet(column + plane)
        for place in range(narrow - 1):
            in_z(place).start()
        own[4] = attn_ref[4].astype(low_type)
        for place in range(4):
            in_w[place, at(z, rows), :] = attn_ref[place].astype(low_type)
        own_ffn[...] = ffn_ref[...].astype(low_type)
        lanes = lane_of((8, LANES))
        count = jnp.zeros((8, LANES), wide_type)
        for seq in range(seqs):
            count = count + (lanes == ids_ref[seq]).astype(wide_type)
        counts[...] = count
        for place in range(narrow - 1):
            in_z(place).wait_recv()
            for hop in range(3):
                in_chip(place, hop).start()
        for place in range(narrow - 1):
            ffn_z(place).start()
            out_z(place).start()
            count_z(place).start()
        keep_ffn.start()
        keep_out.start()
        for place in range(narrow - 1):
            for hop in range(3):
                in_chip(place, hop).wait_recv()
            in_core(place).start()
        for place in range(narrow - 1):
            in_core(place).wait_recv()
        keep_in.start()

    @pl.when(step == 1)
    def _():
        for place in range(narrow - 1):
            count_z(place).wait()
        total = counts[...]
        for place in range(narrow - 1):
            total = total + counts_z[place]
        counts[...] = total
        for place in range(wide - 1):
            count_w(place).start()

    @pl.when(step == 2)
    def _():
        for place in range(wide - 1):
            count_w(place).wait()
        total = counts[...]
        for place in range(wide - 1):
            total = total + counts_w[place]
        lanes = lane_of((8, LANES))
        values = jnp.zeros((8, LANES), wide_type)
        for group in range(groups):
            values = values + jnp.where(lanes == group, dw_ref[group], 0.0)
        weight_ref[...] = values * total_seqs / (groups * jnp.maximum(total, 1.0))

    @pl.when(step == 1)
    def _():
        for place in range(narrow - 1):
            ffn_z(place).wait_recv()
            out_z(place).wait_recv()
            for hop in range(3):
                ffn_chip(place, hop).start()
                out_chip(place, hop).start()

    @pl.when(step == steps - 2)
    def _():
        for place in range(narrow - 1):
            for hop in range(3):
                ffn_chip(place, hop).wait_recv()
                out_chip(place, hop).wait_recv()
            ffn_core(place).start()
            out_core(place).start()

    normed, _ = normalize(x_ref[...].reshape(seqs * CHUNK, D).astype(wide_type))
    first = (normed * ln_ref[0:1, :] + ln_ref[1:2, :]).astype(low_type)
    q_all = dot_nn(first, in_w[0]).astype(low_type)
    k_all = dot_nn(first, in_w[1]).astype(low_type)
    v_all = dot_nn(first, in_w[2]).astype(low_type)
    a_all = jnp.exp(dot_nn(first, in_w[3])).astype(low_type)
    q_ref[...] = q_all.reshape(q_ref.shape)
    k_ref[...] = k_all.reshape(q_ref.shape)
    v_ref[...] = v_all.reshape(q_ref.shape)
    a_ref[...] = a_all.reshape(q_ref.shape)
    attend_chunks(
        q_all,
        k_all,
        v_all,
        a_all,
        (att_ref, share_ref, logit_ref, before_ref, state_ref, state, carry),
        seqs,
    )

    @pl.when(step == steps - 1)
    def _():
        keep_ffn.wait()
        keep_out.wait()
        keep_in.wait()
        for place in range(narrow - 1):
            in_z(place).wait_send()
            in_core(place).wait_send()
            out_z(place).wait_send()
            out_core(place).wait()
            ffn_z(place).wait_send()
            for hop in range(3):
                in_chip(place, hop).wait_send()
                ffn_chip(place, hop).wait_send()
                out_chip(place, hop).wait_send()
            ffn_core(place).wait()


def forward(tokens, ids, dw, ln_params, attn_w, ffn_w):
    seqs, length, _ = tokens.shape
    chunks = length // CHUNK
    wide = lax.axis_size("wide")
    narrow = lax.axis_size("narrow")
    block = pl.BlockSpec((seqs, CHUNK, D), lambda i: (0, i, 0))
    low_out = jax.ShapeDtypeStruct(tokens.shape, low_type)
    any_spec = pl.BlockSpec(memory_space=pl.ANY)

    def whole(*shape):
        return pl.BlockSpec(shape, lambda i: (0,) * len(shape))

    return pl.pallas_call(
        functools.partial(
            forward_kernel,
            wide=wide,
            narrow=narrow,
            total_seqs=seqs * wide * narrow,
            groups=dw.shape[0],
        ),
        grid=(chunks,),
        in_specs=[
            pl.BlockSpec(memory_space=pltpu.SMEM),
            pl.BlockSpec(memory_space=pltpu.SMEM),
            block,
            whole(4, D),
            whole(*attn_w.shape),
            whole(*ffn_w.shape),
        ],
        out_specs=[block] * 7
        + [
            pl.BlockSpec((1, seqs, 1, D), lambda i: (i, 0, 0, 0)),
            pl.BlockSpec((1, seqs, PAIRS, PAIR, 2 * PAIR), lambda i: (i, 0, 0, 0, 0)),
            whole(8, LANES),
            any_spec,
            any_spec,
            any_spec,
        ],
        out_shape=[low_out] * 7
        + [
            jax.ShapeDtypeStruct((chunks, seqs, 1, D), wide_type),
            jax.ShapeDtypeStruct((chunks, seqs, PAIRS, PAIR, 2 * PAIR), low_type),
            jax.ShapeDtypeStruct((8, LANES), wide_type),
            jax.ShapeDtypeStruct((4, D, D), low_type),
            jax.ShapeDtypeStruct((D, D), low_type),
            jax.ShapeDtypeStruct((2, FF, D), low_type),
        ],
        scratch_shapes=[
            pltpu.VMEM((seqs, PAIRS, PAIR, 2 * PAIR), wide_type),
            pltpu.VMEM((seqs, 1, D), wide_type),
            pltpu.VMEM((4, D, D), low_type),
            pltpu.VMEM(attn_w.shape, low_type),
            pltpu.VMEM(ffn_w.shape, low_type),
            pltpu.VMEM((8, LANES), wide_type),
            pltpu.VMEM((narrow - 1, 8, LANES), wide_type),
            pltpu.VMEM((wide - 1, 8, LANES), wide_type),
        ]
        + [
            pltpu.SemaphoreType.DMA((4, narrow - 1)),
            pltpu.SemaphoreType.DMA((2, narrow - 1, 3)),
            pltpu.SemaphoreType.DMA((4, narrow - 1)),
            pltpu.SemaphoreType.DMA((2, narrow - 1, 3)),
            pltpu.SemaphoreType.DMA((4, narrow - 1)),
            pltpu.SemaphoreType.DMA((2, narrow - 1, 3)),
            pltpu.SemaphoreType.DMA((narrow - 1,)),
            pltpu.SemaphoreType.DMA((narrow - 1,)),
            pltpu.SemaphoreType.DMA((wide - 1,)),
            pltpu.SemaphoreType.DMA((wide - 1,)),
        ]
        + [pltpu.SemaphoreType.DMA((3,))],
        compiler_params=pltpu.CompilerParams(
            vmem_limit_bytes=VMEM_BYTES, collective_id=0, has_side_effects=True
        ),
        name="forward",
    )(ids, dw, tokens, ln_params, attn_w, ffn_w)


class Place:
    def __init__(self, narrow):
        self.narrow = narrow
        w = lax.axis_index("wide")
        self.z = lax.axis_index("narrow")
        self.core = lax.rem(w, 2)
        self.chip = lax.rem(w // 2, 4)
        self.other = 1 - self.core
        self.hops = list(range(1, narrow))
        self.column_z = [lax.rem(self.z + hop, narrow) for hop in self.hops]
        self.column = [(w, place) for place in self.column_z]
        self.chip_at = [lax.rem(self.chip + hop, 4) for hop in range(1, 4)]
        self.chips = [(w - 2 * self.chip + 2 * chip, self.z) for chip in self.chip_at]
        self.mate = (w + 1 - 2 * self.core, self.z)


class Copies:
    def __init__(self, sems):
        self.sems = sems
        self.used = 0

    def remote(self, src, dst, device):
        at = self.used
        self.used += 2
        return remote(src, dst, self.sems.at[at], self.sems.at[at + 1], device)

    def local(self, src, dst):
        at = self.used
        self.used += 1
        return pltpu.make_async_copy(src, dst, self.sems.at[at])


def blocks_at(owner, size):
    return pl.ds(pl.multiple_of(owner * size, size), size)


def wide_sum(parts):
    total = parts[0].astype(wide_type)
    for part in parts[1:]:
        total = total + part.astype(wide_type)
    return total


def newton_poly(gram):
    size = gram.shape[0]
    eye = row_of((size, size)) == lane_of((size, size))
    trace = jnp.sum(jnp.where(eye, gram, 0.0), axis=1, keepdims=True)
    trace = jnp.sum(trace, axis=0, keepdims=True)
    scale = 1.0 / (jnp.sqrt(trace) + 1e-07)

    def low_dot(left, right):
        return dot_nn(left.astype(low_type), right.astype(low_type))

    def polynomial(one):
        poly = quintic_cube * one + quintic_five * low_dot(one, one)
        return poly + jnp.where(eye, quintic_lin, 0.0)

    gram_one = gram * (scale * scale)
    poly_one = polynomial(gram_one)
    gram_two = low_dot(low_dot(gram_one, poly_one), poly_one)
    poly_two = polynomial(gram_two)
    return low_dot(poly_one, poly_two) * scale


def back_kernel(*refs, narrow, chunks):
    blocks = list(refs[:9])
    xc_ref, x_ref, w_ref, ln_ref, gffn_hbm, go_hbm, mom_hbm = refs[9:16]
    dz_ref, gln_ref, wsum_ref, fsum_ref, osum_ref, mom_ref = refs[16:22]
    state, carry, dq_all, dk_all, dv_all, de_all, first_t = refs[22:29]
    own_f, got_f, far_f, col_f, own_o, got_o, cut_o, far_o, col_o = refs[29:38]
    low_f, low_o, mom_own, mom_low, mom_all = refs[38:43]
    grad_w, got_w, half_w, far_w, staged, sems = refs[43:]
    step = pl.program_id(0)
    steps = pl.num_programs(0)
    here = Place(narrow)
    copies = Copies(sems)
    half = D // 2
    part = D // 4
    rows = D // narrow
    ffn_rows = FF // narrow
    column = range(narrow - 1)
    own_cols = blocks_at(here.core, half)
    mate_cols = blocks_at(here.other, half)
    grads = (dq_all, dk_all, dv_all, de_all)

    keep_f = copies.local(gffn_hbm.at[here.core], own_f)
    keep_o = copies.local(go_hbm.at[:, own_cols], own_o)
    keep_mom = copies.local(mom_hbm.at[pl.ds(0, 4)], mom_own)
    mate_sum = [
        copies.remote(gffn_hbm.at[here.other], got_f, here.mate),
        copies.remote(go_hbm.at[:, mate_cols], got_o, here.mate),
    ]
    plane_sum = []
    for hop in range(3):
        there = here.chip_at[hop]
        plane_sum.append(
            copies.remote(own_f.at[blocks_at(there, part)], far_f.at[hop], here.chips[hop])
        )
        plane_sum.append(copies.remote(cut_o.at[:, there], far_o.at[hop], here.chips[hop]))
    z_sum = []
    for i in column:
        there = here.column_z[i]
        z_sum.append(
            copies.remote(low_f.at[:, blocks_at(there, ffn_rows)], col_f.at[i], here.column[i])
        )
        z_sum.append(copies.remote(low_o.at[there], col_o.at[i], here.column[i]))
    z_mom = [
        copies.remote(
            mom_low.at[lax.rem(here.column_z[i], 4), :, own_cols],
            mom_all.at[blocks_at(here.z, rows), own_cols],
            here.column[i],
        )
        for i in column
    ]
    mate_mom = copies.remote(mom_all.at[:, own_cols], mom_all.at[:, own_cols], here.mate)
    mate_w = [
        copies.remote(grad_w.at[m, :, mate_cols], got_w.at[m], here.mate) for m in range(4)
    ]
    plane_w = [
        [
            copies.remote(
                half_w.at[m, blocks_at(here.chip_at[hop], part)],
                far_w.at[hop, m],
                here.chips[hop],
            )
            for hop in range(3)
        ]
        for m in range(4)
    ]

    def gradient(m):
        total = dot_nn(first_t[...], grads[m][...].reshape(-1, D))
        grad_w[m] = total.astype(low_type)
        mate_w[m].start()

    def over_cores(m):
        mate_w[m].wait()
        half_w[m] = wide_sum([grad_w[m, :, own_cols], got_w[m]]).astype(low_type)
        for copy in plane_w[m]:
            copy.start()

    def over_chips(m):
        for copy in plane_w[m]:
            copy.wait()
        mine = half_w[m, blocks_at(here.chip, part), :]
        wsum_ref[m] = wide_sum([mine] + [far_w[hop, m] for hop in range(3)]).astype(low_type)

    @pl.when(step == 0)
    def _():
        state[...] = jnp.zeros_like(state)
        carry[...] = jnp.zeros_like(carry)
        gln_ref[...] = jnp.zeros_like(gln_ref)
        greet(here.column + here.chips + [here.mate])
        for copy in mate_sum + [keep_f, keep_o, keep_mom]:
            copy.start()

    @pl.when(step == 1)
    def _():
        keep_mom.wait()
        mom_low[...] = mom_own[...].astype(low_type)
        for copy in z_mom:
            copy.start()
        mom_all[blocks_at(here.z, rows), own_cols] = mom_low[lax.rem(here.z, 4), :, own_cols]

    @pl.when(step == chunks // 4)
    def _():
        for copy in mate_sum + [keep_f, keep_o]:
            copy.wait()
        own_f[...] = wide_sum([own_f[...], got_f[...]]).astype(low_type)
        cut_o[...] = wide_sum([own_o[...], got_o[...]]).astype(low_type).reshape(cut_o.shape)
        for copy in plane_sum:
            copy.start()

    @pl.when(step < chunks)
    def _():
        chunk = chunks - 1 - step
        seqs = xc_ref.shape[0]
        for seq in range(seqs):
            normed, _ = normalize(xc_ref[seq].astype(wide_type))
            first = (normed * ln_ref[0:1, :] + ln_ref[1:2, :]).astype(low_type)
            first_t[:, blocks_at(chunk * seqs + seq, CHUNK)] = first.T
        attend_back_chunk(blocks + [staged.at[place] for place in range(4)], state, carry)
        for place in range(4):
            grads[place][chunk] = staged[place]

    @pl.when(step == chunks)
    def _():
        gradient(0)
        gradient(1)
        for copy in z_mom:
            copy.wait_recv()
        mate_mom.start()

    @pl.when(step == chunks + 1)
    def _():
        over_cores(0)
        over_cores(1)
        for copy in plane_sum:
            copy.wait()
        mine = own_f[blocks_at(here.chip, part), :]
        low_f[...] = wide_sum([mine] + [far_f[hop] for hop in range(3)]).astype(low_type)
        mine = cut_o[:, here.chip]
        low_o[...] = wide_sum([mine] + [far_o[hop] for hop in range(3)]).astype(low_type)
        for copy in z_sum:
            copy.start()
        gradient(2)
        gradient(3)

    @pl.when(step == chunks + 2)
    def _():
        over_cores(2)
        over_cores(3)

    @pl.when(step >= chunks)
    def _():
        per = chunks // 4
        seqs = x_ref.shape[0]
        parts = [item[pl.ds((step - chunks) * per, per)].reshape(-1, D) for item in grads]
        dfirst = dot_nt(parts[0], w_ref[0])
        for place in range(1, 4):
            dfirst = dfirst + dot_nt(parts[place], w_ref[place])
        spans = [slice(at * CHUNK, (at + 1) * CHUNK) for at in range(per)]
        rows_in = [x_ref[:, span, :].reshape(-1, D) for span in spans]
        normed, inverse = normalize(jnp.concatenate(rows_in, axis=0).astype(wide_type))
        gln_ref[0:1, :] += jnp.sum(dfirst * normed, axis=0, keepdims=True)
        gln_ref[1:2, :] += jnp.sum(dfirst, axis=0, keepdims=True)
        dz = norm_back(dfirst, normed, inverse, ln_ref[0:1, :]).astype(low_type)
        for at, span in enumerate(spans):
            size = seqs * CHUNK
            dz_ref[:, span, :] = dz[at * size : (at + 1) * size].reshape(seqs, CHUNK, D)

    @pl.when(step == steps - 1)
    def _():
        mate_mom.wait()
        mom_ref[...] = mom_all[...]
        for m in range(4):
            over_chips(m)
        for copy in z_sum:
            copy.wait()
        mine = low_f[:, blocks_at(here.z, ffn_rows)]
        fsum_ref[...] = wide_sum([mine] + [col_f[i] for i in column]).astype(low_type)
        osum_ref[...] = wide_sum([low_o[here.z]] + [col_o[i] for i in column]).astype(low_type)
        for copy in z_mom:
            copy.wait_send()


def back(q, k, v, a, share, logit, before, datt, states, tokens, in_w, ln_params, gffn, go, mom):
    seqs, length, _ = q.shape
    chunks = length // CHUNK
    narrow = lax.axis_size("narrow")
    small, half, part = D // narrow // 4, D // 2, D // 4
    ffn_rows = FF // narrow

    def chunk_at(i):
        return jnp.maximum(chunks - 1 - i, 0)

    def rows_at(i):
        return (0, jnp.maximum(i - chunks, 0), 0)

    def whole(*shape):
        return pl.BlockSpec(shape, lambda i: (0,) * len(shape))

    block = pl.BlockSpec((seqs, CHUNK, D), lambda i: (0, chunk_at(i), 0))
    row_spec = pl.BlockSpec((seqs, length // 4, D), rows_at)
    any_spec = pl.BlockSpec(memory_space=pl.ANY)
    outs = [(4, part, half), (part, ffn_rows), (small, half), (D, D)]

    def low(*shape):
        return pltpu.VMEM(shape, low_type)

    return pl.pallas_call(
        functools.partial(back_kernel, narrow=narrow, chunks=chunks),
        grid=(chunks + 4,),
        in_specs=[block] * 6
        + [
            pl.BlockSpec((1, seqs, 1, D), lambda i: (chunk_at(i), 0, 0, 0)),
            block,
            pl.BlockSpec((1, seqs, PAIRS, PAIR, 2 * PAIR), lambda i: (chunk_at(i), 0, 0, 0, 0)),
            block,
            row_spec,
            whole(4, D, D),
            whole(4, D),
            any_spec,
            any_spec,
            any_spec,
        ],
        out_specs=[row_spec, whole(2, D)] + [whole(*shape) for shape in outs],
        out_shape=[
            jax.ShapeDtypeStruct(q.shape, low_type),
            jax.ShapeDtypeStruct((2, D), wide_type),
        ]
        + [jax.ShapeDtypeStruct(shape, low_type) for shape in outs],
        scratch_shapes=[
            pltpu.VMEM((seqs, PAIRS, PAIR, 2 * PAIR), wide_type),
            pltpu.VMEM((seqs, 1, D), wide_type),
            low(chunks, seqs, CHUNK, D),
            low(chunks, seqs, CHUNK, D),
            low(chunks, seqs, CHUNK, D),
            low(chunks, seqs, CHUNK, D),
            low(D, seqs * length),
            low(D, FF),
            low(D, FF),
            low(3, part, FF),
            low(narrow - 1, part, ffn_rows),
            low(D, half),
            low(D, half),
            low(narrow, 4, small, half),
            low(3, narrow, small, half),
            low(narrow - 1, small, half),
            low(part, FF),
            low(narrow, small, half),
            pltpu.VMEM((4, D // narrow, D), wide_type),
            low(4, D // narrow, D),
            low(D, D),
            low(4, D, D),
            low(4, D, half),
            low(4, D, half),
            low(3, 4, part, half),
            low(4, seqs, CHUNK, D),
            pltpu.SemaphoreType.DMA((3 + 2 * (2 + 6 + 3 * (narrow - 1) + 1 + 4 + 12),)),
        ],
        compiler_params=pltpu.CompilerParams(
            vmem_limit_bytes=VMEM_BYTES, collective_id=1, has_side_effects=True
        ),
        name="back",
    )(
        q,
        k,
        v,
        a,
        share,
        logit,
        before,
        datt,
        states,
        tokens,
        tokens,
        in_w,
        ln_params,
        gffn,
        go,
        mom,
    )


def update_kernel(
    wsum_ref,
    fsum_ref,
    osum_ref,
    mom_w_ref,
    mom_hbm,
    mom_f_hbm,
    ln_one_ref,
    ln_two_ref,
    grad_attn,
    step_attn,
    grad_ffn,
    step_ffn,
    ln_ref,
    ln_now,
    ln_mate,
    ln_chips,
    ln_column,
    col_w,
    grad_w,
    moment_w,
    poly_w,
    send_w,
    all_w,
    all_f,
    mom_f,
    mom_o,
    moment_f,
    out_f,
    all_o,
    moment_o,
    step_o,
    cut_gf,
    col_gf,
    strips_gf,
    gram_f,
    cut_go,
    col_go,
    strips_go,
    gram_o,
    sems,
    *,
    narrow,
):
    here = Place(narrow)
    copies = Copies(sems)
    z, core, chip = here.z, here.core, here.chip
    half = D // 2
    quarter = D // 4
    rows = D // narrow
    small = rows // 4
    ffn_rows = FF // narrow
    strip = quarter // narrow
    column = range(narrow - 1)
    planes = range(3)
    own_cols = blocks_at(core, half)
    own_quarter = blocks_at(chip, quarter)
    own_small = blocks_at(chip, small)
    matrix = lax.rem(z, 4)

    def to_plane(src, dst):
        return [copies.remote(src(i), dst(i), here.chips[i]) for i in planes]

    def to_column(src, dst):
        return [copies.remote(src(i), dst(i), here.column[i]) for i in column]

    def same(block):
        return lambda i: block

    keep_f = copies.local(mom_f_hbm.at[core], mom_f)
    keep_o = copies.local(mom_hbm.at[4], mom_o)
    mate_ln = [copies.remote(ln_now, ln_mate, here.mate)]
    plane_ln = to_plane(same(ln_now), lambda i: ln_chips.at[i])
    block = all_f.at[own_quarter]
    plane_f = to_plane(same(block), same(block))
    block = all_o.at[own_small, own_cols]
    plane_f = plane_f + to_plane(same(block), same(block))
    z_sum = to_column(lambda i: wsum_ref.at[lax.rem(here.column_z[i], 4)], lambda i: col_w.at[i])
    z_ln = to_column(same(ln_now), lambda i: ln_column.at[i])
    block = out_f.at[0, core]
    mate_f = [copies.remote(block, block, here.mate)]
    block = all_o.at[:, own_cols]
    mate_o = [copies.remote(block, block, here.mate)]
    z_gf = to_column(
        lambda i: cut_gf.at[blocks_at(here.column_z[i], strip)], lambda i: col_gf.at[i]
    )
    block = grad_w.at[own_quarter, own_cols]
    plane_w = to_plane(same(block), same(block))
    z_go = to_column(
        lambda i: cut_go.at[blocks_at(here.column_z[i], strip)], lambda i: col_go.at[i]
    )
    block = grad_w.at[:, own_cols]
    mate_w = [copies.remote(block, block, here.mate)]
    block = strips_gf.at[blocks_at(z, strip)]
    z_back_f = to_column(same(block), same(block))
    block = strips_go.at[blocks_at(z, strip)]
    z_back_o = to_column(same(block), same(block))
    block = gram_f.at[own_quarter]
    plane_gf = to_plane(same(block), same(block))
    block = gram_o.at[own_quarter, own_cols]
    plane_go = to_plane(same(block), same(block))
    quad = [z - matrix + lax.rem(matrix + hop, 4) for hop in range(1, 4)]

    def hand_back(kind):
        spread = [
            copies.remote(
                send_w.at[kind, there],
                all_w.at[kind, matrix, own_small, own_cols],
                (lax.axis_index("wide"), there),
            )
            for there in quad
        ]
        block = all_w.at[kind, :, own_small, own_cols]
        plane = to_plane(same(block), same(block))
        block = all_w.at[kind, :, :, own_cols]
        return spread, plane, [copies.remote(block, block, here.mate)]

    spread_g, plane_g, mate_g = hand_back(0)
    spread_s, plane_s, mate_s = hand_back(1)
    block = gram_o.at[:, own_cols]
    mate_go = [copies.remote(block, block, here.mate)]
    block = out_f.at[1, core]
    mate_x = [copies.remote(block, block, here.mate)]
    write_f = [copies.local(out_f.at[0], grad_ffn), copies.local(out_f.at[1], step_ffn)]
    write_o = [copies.local(all_o, grad_attn.at[4]), copies.local(step_o, step_attn.at[4])]
    write_w = [
        copies.local(all_w.at[0], grad_attn.at[pl.ds(0, 4)]),
        copies.local(all_w.at[1], step_attn.at[pl.ds(0, 4)]),
    ]
    sent = []

    def start(group):
        for copy in group:
            copy.start()
        sent.extend(group)

    def arrive(group):
        for copy in group:
            copy.wait_recv()

    def begin(group):
        for copy in group:
            copy.start()

    greet(here.column + here.chips + [here.mate])
    start(z_sum)
    all_f[own_quarter, :] = fsum_ref[...]
    all_o[own_small, own_cols] = osum_ref[...]
    start(plane_f)
    begin([keep_f, keep_o])
    ln_now[...] = jnp.zeros_like(ln_now)
    ln_now[0:2, :] = ln_one_ref[...]
    ln_now[2:4, :] = ln_two_ref[...]
    start(mate_ln)

    arrive(z_sum)
    total = wide_sum([wsum_ref[matrix]] + [col_w[i] for i in column])
    grad_w[own_quarter, own_cols] = total.astype(low_type)
    start(plane_w)
    arrive(mate_ln)
    mate_ln[0].wait_send()
    ln_now[...] = ln_now[...] + ln_mate[...]
    start(plane_ln)

    keep_f.wait()
    arrive(plane_f)
    start(mate_o)
    grad = all_f[...].T
    out_f[0, core] = grad
    start(mate_f)
    moment_f[...] = (momentum_keep * mom_f[...] + grad.astype(wide_type)).astype(low_type)
    cut_gf[...] = dot_tn(moment_f[:, own_quarter], moment_f[...]).astype(low_type)
    start(z_gf)

    arrive(plane_w)
    start(mate_w)
    arrive(plane_ln)
    for copy in plane_ln:
        copy.wait_send()
    ln_now[...] = ln_now[...] + ln_chips[0] + ln_chips[1] + ln_chips[2]
    start(z_ln)

    arrive(mate_o)
    keep_o.wait()
    moment = momentum_keep * mom_o[...] + all_o[...].astype(wide_type)
    moment_o[...] = moment.astype(low_type)
    cut_go[...] = dot_tn(moment_o[:, own_quarter], moment_o[:, own_cols]).astype(low_type)
    start(z_go)

    def small_rows(there):
        return pl.ds(pl.multiple_of(there * rows + chip * small, small), small)

    arrive(mate_w)
    for there in range(narrow):
        send_w[0, there] = grad_w[small_rows(there), own_cols]
    start(spread_g)
    all_w[0, matrix, own_small, own_cols] = send_w[0, z]
    moment = momentum_keep * mom_w_ref[...].astype(wide_type) + grad_w[...].astype(wide_type)
    moment_w[...] = moment.astype(low_type)
    gram = dot_tn(moment_w[...], moment_w[...])
    arrive(z_gf)
    total = wide_sum([cut_gf[blocks_at(z, strip), :]] + [col_gf[i] for i in column])
    strips_gf[blocks_at(z, strip), :] = total.astype(low_type)
    start(z_back_f)
    poly_w[...] = newton_poly(gram).astype(low_type)
    picked = jnp.concatenate([moment_w[small_rows(there), :] for there in range(narrow)], axis=0)
    ortho = dot_nn(picked, poly_w[:, own_cols]).astype(low_type)
    for there in range(narrow):
        send_w[1, there] = ortho[there * small : (there + 1) * small, :]
    start(spread_s)
    all_w[1, matrix, own_small, own_cols] = send_w[1, z]

    arrive(z_go)
    total = wide_sum([cut_go[blocks_at(z, strip), :]] + [col_go[i] for i in column])
    strips_go[blocks_at(z, strip), :] = total.astype(low_type)
    start(z_back_o)
    arrive(z_back_f)
    gram_f[own_quarter, :] = strips_gf[...]
    start(plane_gf)
    arrive(spread_g)
    start(plane_g)
    arrive(z_back_o)
    gram_o[own_quarter, own_cols] = strips_go[...]
    start(plane_go)
    arrive(spread_s)
    start(plane_s)
    arrive(plane_gf)
    poly = newton_poly(gram_f[...].astype(wide_type)).astype(low_type)
    out_f[1, core] = dot_nn(moment_f[...], poly).astype(low_type)
    start(mate_x)
    arrive(plane_g)
    start(mate_g)
    arrive(plane_go)
    start(mate_go)
    arrive(plane_s)
    start(mate_s)
    arrive(mate_go)
    poly = newton_poly(gram_o[...].astype(wide_type)).astype(low_type)
    step_o[...] = dot_nn(moment_o[...], poly).astype(low_type)
    begin(write_o)
    arrive(mate_f)
    arrive(mate_x)
    begin(write_f)
    arrive(z_ln)
    total = ln_now[...]
    for i in column:
        total = total + ln_column[i]
    ln_ref[...] = total
    arrive(mate_g)
    begin(write_w[:1])
    arrive(mate_s)
    begin(write_w[1:])
    for copy in write_o + write_f + write_w:
        copy.wait()
    settled = [id(copy) for copy in mate_ln + plane_ln]
    for copy in sent:
        if id(copy) not in settled:
            copy.wait_send()


def update(wsum, fsum, osum, mom_in, mom, mom_f, ln_one, ln_two):
    narrow = lax.axis_size("narrow")
    rows, ffn_rows = D // narrow, FF // narrow
    small, half, quarter = rows // 4, D // 2, D // 4
    strip = quarter // narrow
    column = narrow - 1
    any_spec = pl.BlockSpec(memory_space=pl.ANY)
    vmem = pl.BlockSpec(memory_space=pltpu.VMEM)

    def low(*shape):
        return pltpu.VMEM(shape, low_type)

    def full(*shape):
        return pltpu.VMEM(shape, wide_type)

    scratch = [
        full(8, D),
        full(8, D),
        full(3, 8, D),
        full(column, 8, D),
        low(column, quarter, half),
        low(D, D),
        low(D, D),
        low(D, D),
        low(2, narrow, small, half),
        low(2, 4, rows, D),
        low(D, ffn_rows),
        full(ffn_rows, D),
        full(rows, D),
        low(ffn_rows, D),
        low(2, 2, ffn_rows, D),
        low(rows, D),
        low(rows, D),
        low(rows, D),
        low(quarter, D),
        low(column, strip, D),
        low(quarter, D),
        low(D, D),
        low(quarter, half),
        low(column, strip, half),
        low(quarter, half),
        low(D, D),
        pltpu.SemaphoreType.DMA((8 + 2 * (38 + 6 * column),)),
    ]
    return pl.pallas_call(
        functools.partial(update_kernel, narrow=narrow),
        in_specs=[vmem, vmem, vmem, vmem, any_spec, any_spec, vmem, vmem],
        out_specs=[any_spec, any_spec, any_spec, any_spec, vmem],
        out_shape=[
            jax.ShapeDtypeStruct((5, rows, D), low_type),
            jax.ShapeDtypeStruct((5, rows, D), low_type),
            jax.ShapeDtypeStruct((2, ffn_rows, D), low_type),
            jax.ShapeDtypeStruct((2, ffn_rows, D), low_type),
            jax.ShapeDtypeStruct((8, D), wide_type),
        ],
        scratch_shapes=scratch,
        compiler_params=pltpu.CompilerParams(
            vmem_limit_bytes=VMEM_BYTES, collective_id=2, has_side_effects=True
        ),
        name="update",
    )(wsum, fsum, osum, mom_in, mom, mom_f, ln_one, ln_two)


def group_sum(values):
    wide = lax.axis_size("wide")
    if wide == 8:
        return values
    groups = [[place + 8 * group for group in range(wide // 8)] for place in range(8)]
    return lax.psum(values, "wide", axis_index_groups=groups)


def shards(
    tokens,
    out_grad,
    group_ids,
    domain_weight,
    attn_w,
    ffn_w,
    attn_mom,
    ffn_mom,
    ln_params,
    ln_first,
    ln_second,
):
    local_seqs, length, _ = tokens.shape
    token_count = local_seqs * length
    rows = tokens.reshape(token_count, D)
    head = (local_seqs, length, D)
    q, k, v, a, att, share, logit, before, states, weights, in_w, out_w, ffn_low = forward(
        tokens, group_ids, domain_weight, ln_params, attn_w, ffn_w
    )
    output, dx, datt, gffn, go, ln_two = feed(
        group_ids,
        weights,
        rows,
        att.reshape(token_count, D),
        out_grad.reshape(token_count, D),
        out_w,
        ffn_low,
        ln_params,
        length,
    )
    dz, ln_one, wsum, fsum, osum, mom_in = back(
        q,
        k,
        v,
        a,
        share,
        logit,
        before,
        datt.reshape(head),
        states,
        tokens,
        in_w,
        ln_params,
        gffn,
        go,
        attn_mom,
    )
    wsum, fsum, osum, ln_one, ln_two = group_sum((wsum, fsum, osum, ln_one, ln_two))
    attn_grad, attn_step, ffn_grad, ffn_step, ln_sum = update(
        wsum, fsum, osum, mom_in, attn_mom, ffn_mom, ln_one, ln_two
    )
    def flat(*items):
        return [item.reshape(-1, D) for item in items]

    results = finish(
        dx,
        dz.reshape(token_count, D),
        flat(attn_grad, attn_step, attn_w, attn_mom),
        flat(ffn_grad, ffn_step, ffn_w, ffn_mom),
        (ln_params, ln_first, ln_second, ln_sum),
    )
    input_grad, ga, ma, wa, ca, gf, mf, wf, cf, ln_grad, first_new, second_new, ln_new = results
    attn, ffn = attn_w.shape, ffn_w.shape
    return (
        output.reshape(tokens.shape),
        input_grad.reshape(tokens.shape),
        ga.reshape(attn),
        gf.reshape(ffn),
        ln_grad,
        ma.reshape(attn),
        mf.reshape(ffn),
        wa.reshape(attn),
        wf.reshape(ffn),
        ca.reshape(attn),
        cf.reshape(ffn),
        first_new,
        second_new,
        ln_new,
    )


def solution(mesh):
    split = P(("wide", "narrow"), None, None)
    rows = P(None, "narrow", None)
    lanes = P(None, "narrow")
    inner = jax.shard_map(
        shards,
        mesh=mesh,
        in_specs=(
            split,
            split,
            P(("wide", "narrow")),
            P(),
            rows,
            rows,
            rows,
            rows,
            P(),
            lanes,
            lanes,
        ),
        out_specs=(
            split,
            split,
            rows,
            rows,
            lanes,
            rows,
            rows,
            rows,
            rows,
            rows,
            rows,
            lanes,
            lanes,
            lanes,
        ),
        check_vma=False,
    )
    return inner
```

```python
import functools
import math

import jax
import jax.numpy as jnp
from jax import lax
from jax.experimental import pallas as pl
from jax.experimental.pallas import tpu as pltpu
from jax.sharding import PartitionSpec as P

D = 512
HEADS = 8
HEAD_DIM = 64
FF = 2048
STEP = 10

norm_epsilon = 1e-05
momentum_keep = 0.5
quintic_lin = 3.4445
quintic_cube = -4.775
quintic_five = 2.0315
muon_rate = 0.7
muon_decay = 0.1
adam_rate = 0.2
beta_first = 0.9
beta_second = 0.999
adam_epsilon = 1e-08

CHUNK = 128
PAIR = 2 * HEAD_DIM
PAIRS = HEADS // 2
VMEM_BYTES = 60 * 1024 * 1024
low_type = jnp.bfloat16
wide_type = jnp.float32


def dot_nn(left, right):
    return lax.dot_general(left, right, (((1,), (0,)), ((), ())), preferred_element_type=wide_type)


def dot_nt(left, right):
    return lax.dot_general(left, right, (((1,), (1,)), ((), ())), preferred_element_type=wide_type)


def dot_tn(left, right):
    return lax.dot_general(left, right, (((0,), (0,)), ((), ())), preferred_element_type=wide_type)


def normalize(rows):
    center = rows - jnp.mean(rows, axis=-1, keepdims=True)
    spread = jnp.mean(center * center, axis=-1, keepdims=True)
    inverse = lax.rsqrt(spread + norm_epsilon)
    return center * inverse, inverse


def norm_back(grad_rows, normed, inverse, gain):
    grad_normed = grad_rows * gain
    mean_grad = jnp.mean(grad_normed, axis=-1, keepdims=True)
    mean_cross = jnp.mean(grad_normed * normed, axis=-1, keepdims=True)
    return inverse * (grad_normed - mean_grad - normed * mean_cross)


def lane_of(shape):
    return lax.broadcasted_iota(jnp.int32, shape, 1)


def row_of(shape):
    return lax.broadcasted_iota(jnp.int32, shape, 0)


def split_pair(pair, first_head):
    zero = jnp.zeros_like(pair)
    return jnp.concatenate(
        [jnp.where(first_head, pair, zero), jnp.where(first_head, zero, pair)], axis=0
    )


def head_reduce(values, first_head, op, neutral):
    left = op(jnp.where(first_head, values, neutral), axis=-1, keepdims=True)
    right = op(jnp.where(first_head, neutral, values), axis=-1, keepdims=True)
    return jnp.where(first_head, left, right)


def attend_back_chunk(refs, state, carry):
    (
        q_ref,
        k_ref,
        v_ref,
        a_ref,
        share_ref,
        logit_ref,
        before_ref,
        datt_ref,
        state_ref,
        dq_ref,
        dk_ref,
        dv_ref,
        de_ref,
    ) = refs
    scaling = HEAD_DIM**-0.5
    first_head = lane_of((CHUNK, PAIR)) < HEAD_DIM
    causal = row_of((CHUNK, 2 * CHUNK)) >= lane_of((CHUNK, 2 * CHUNK)) % CHUNK
    anti = row_of((CHUNK, 2 * CHUNK)) <= lane_of((CHUNK, 2 * CHUNK)) % CHUNK
    same_head = (row_of((PAIR, 2 * PAIR)) // HEAD_DIM) == (
        (lane_of((PAIR, 2 * PAIR)) // HEAD_DIM) % 2
    )
    lower = (row_of((CHUNK, CHUNK)) >= lane_of((CHUNK, CHUNK))).astype(low_type)
    upper = (row_of((CHUNK, CHUNK)) <= lane_of((CHUNK, CHUNK))).astype(low_type)

    def masked(mask, raw):
        return jnp.where(mask, raw, 0.0).astype(low_type)

    items = []
    for seq in range(q_ref.shape[0]):
        total = dot_nn(lower, a_ref[seq]) + before_ref[0, seq]
        inv = 1.0 / total
        for pair in range(PAIRS):
            lanes = slice(pair * PAIR, (pair + 1) * PAIR)
            items.append(
                dict(seq=seq, pair=pair, lanes=lanes, total=total[:, lanes], inv=inv[:, lanes])
            )

    def load(t):
        seq, lanes = t["seq"], t["lanes"]
        t["k"] = k_ref[seq, :, lanes]
        t["v"] = v_ref[seq, :, lanes]
        t["a"] = a_ref[seq, :, lanes]
        t["share"] = share_ref[seq, :, lanes]
        t["datt"] = datt_ref[seq, :, lanes]
        t["q"] = q_ref[seq, :, lanes] * low_type(scaling)
        t["before"] = state_ref[0, seq, t["pair"]]
        t["after"] = jnp.where(same_head, state[seq, t["pair"]], 0.0).astype(low_type)
        t["v_two"] = split_pair(t["v"], first_head)
        t["a_two"] = split_pair(t["a"], first_head)
        t["dmix"] = masked(causal, dot_nt(t["datt"], t["v_two"]))

    def gather(t):
        t["share_two"] = split_pair(t["share"], first_head)
        t["datt_two"] = split_pair(t["datt"], first_head)
        t["dshare"] = dot_nn(t["dmix"], t["a_two"]) + dot_nt(t["datt"], t["before"][:, PAIR:])

    def soften(t):
        logit = logit_ref[t["seq"], :, t["lanes"]].astype(wide_type)
        prob = t["share"].astype(wide_type) * t["total"]
        cross = t["dshare"] * t["inv"] * prob
        dlogit = cross - prob * head_reduce(cross, first_head, jnp.sum, 0.0)
        t["dnumer"] = (dlogit * t["inv"]).astype(low_type)
        t["dtotal"] = -(cross + dlogit * logit) * t["inv"]
        t["mix_t"] = masked(anti, dot_nt(t["a"], t["share_two"]))
        t["dmix_t"] = masked(anti, dot_nt(t["v"], t["datt_two"]))

    def blend(t):
        t["dnumer_two"] = split_pair(t["dnumer"], first_head)
        t["dscores"] = masked(causal, dot_nt(t["dnumer"], t["a_two"]))
        t["dscores_t"] = masked(anti, dot_nt(t["a"], t["dnumer_two"]))
        t["k_two"] = split_pair(t["k"], first_head)
        t["q_two"] = split_pair(t["q"], first_head)
        t["scores_t"] = masked(anti, dot_nt(t["k"], t["q_two"]))
        t["later"] = dot_nn(t["a"], t["after"])

    def finish(t):
        seq, lanes = t["seq"], t["lanes"]
        dq = dot_nn(t["dscores"], t["k_two"]) + dot_nn(t["dnumer"], t["before"][:, :PAIR])
        dq_ref[seq, :, lanes] = (dq * scaling).astype(low_type)
        dv = dot_nn(t["mix_t"], t["datt_two"]) + t["later"][:, PAIR:]
        dv_ref[seq, :, lanes] = dv.astype(low_type)
        dk = dot_nn(t["dscores_t"], t["q_two"]) + t["later"][:, :PAIR]
        dk_ref[seq, :, lanes] = dk.astype(low_type)
        high = t["dtotal"].astype(low_type)
        rest = (t["dtotal"] - high.astype(wide_type)).astype(low_type)
        tail = dot_nn(upper, high) + dot_nn(upper, rest) + carry[seq, :, lanes]
        carry[seq, :, lanes] = tail[0:1, :]
        da = dot_nn(t["dmix_t"], t["share_two"]) + dot_nn(t["scores_t"], t["dnumer_two"])
        da = da + dot_nt(jnp.concatenate([t["k"], t["v"]], axis=1), t["after"]) + tail
        de = da.astype(low_type).astype(wide_type) * t["a"].astype(wide_type)
        de_ref[seq, :, lanes] = de.astype(low_type)
        state[seq, t["pair"], :, :PAIR] += dot_tn(t["dnumer"], t["q"])
        state[seq, t["pair"], :, PAIR:] += dot_tn(t["share"], t["datt"])

    for stage in (load, gather, soften, blend, finish):
        for item in items:
            stage(item)


FF_BLOCK = 512
gelu_root = math.sqrt(2.0 / math.pi)
gelu_cube = 0.044715


def feed_kernel(
    ids_ref,
    weight_ref,
    x_ref,
    att_ref,
    og_ref,
    wo_ref,
    ffn_ref,
    ln_ref,
    out_ref,
    dx_ref,
    datt_ref,
    gffn_ref,
    go_ref,
    gln_ref,
    up_sum,
    down_sum,
    o_sum,
    *,
    per_seq,
):
    step = pl.program_id(0)

    @pl.when(step == 0)
    def _():
        up_sum[...] = jnp.zeros_like(up_sum)
        down_sum[...] = jnp.zeros_like(down_sum)
        o_sum[...] = jnp.zeros_like(o_sum)
        gln_ref[...] = jnp.zeros_like(gln_ref)

    att = att_ref[...]
    mixed = x_ref[...].astype(wide_type) + dot_nn(att, wo_ref[...])
    normed, inverse = normalize(mixed)
    second = (normed * ln_ref[2:3, :] + ln_ref[3:4, :]).astype(low_type)
    mine = lane_of((1, LANES)) == ids_ref[step // per_seq]
    weight = jnp.sum(jnp.where(mine, weight_ref[0:1, :], 0.0), axis=1, keepdims=True)
    dout = og_ref[...].astype(wide_type) * weight
    dy = dout.astype(low_type)
    second_t = second.T
    dy_t = dy.T
    parts = [dict(rows=slice(part * FF_BLOCK, (part + 1) * FF_BLOCK)) for part in range(FF // FF_BLOCK)]

    def open_part(t):
        t["up"] = ffn_ref[0, t["rows"], :]
        t["down"] = ffn_ref[1, t["rows"], :]
        t["inner"] = dot_nt(second, t["up"])
        t["dhidden"] = dot_nt(dy, t["down"])

    result, dsecond = mixed, 0.0
    open_part(parts[0])
    for place, t in enumerate(parts):
        if place + 1 < len(parts):
            open_part(parts[place + 1])
        inner = t["inner"]
        square = inner * inner
        bend = jnp.tanh(inner * (gelu_root + (gelu_root * gelu_cube) * square))
        half = 0.5 + 0.5 * bend
        hidden = (inner * half).astype(low_type)
        slope = half + (0.5 * inner) * (1.0 - bend * bend) * (
            gelu_root + (3.0 * gelu_root * gelu_cube) * square
        )
        dinner = (t["dhidden"] * slope).astype(low_type)
        result = result + dot_nn(hidden, t["down"])
        down_sum[:, t["rows"]] += dot_nn(dy_t, hidden)
        up_sum[:, t["rows"]] += dot_nn(second_t, dinner)
        dsecond = dsecond + dot_nn(dinner, t["up"])
    out_ref[...] = result.astype(low_type)
    gln_ref[0:1, :] += jnp.sum(dsecond * normed, axis=0, keepdims=True)
    gln_ref[1:2, :] += jnp.sum(dsecond, axis=0, keepdims=True)
    dmixed = dout + norm_back(dsecond, normed, inverse, ln_ref[2:3, :])
    datt = dmixed.astype(low_type)
    dx_ref[...] = datt
    o_sum[...] += dot_tn(att, datt)
    datt_ref[...] = dot_nt(datt, wo_ref[...]).astype(low_type)

    @pl.when(step == pl.num_programs(0) - 1)
    def _():
        gffn_ref[0] = up_sum[...].astype(low_type)
        gffn_ref[1] = down_sum[...].astype(low_type)
        go_ref[...] = o_sum[...].astype(low_type)


def feed(ids, weights, rows, att, grad, wo, ffn, ln_params, length):
    count = rows.shape[0]
    block = 512
    row_spec = pl.BlockSpec((block, D), lambda i: (i, 0))

    def whole(*shape):
        return pl.BlockSpec(shape, lambda i: (0,) * len(shape))

    return pl.pallas_call(
        functools.partial(feed_kernel, per_seq=length // block),
        grid=(count // block,),
        in_specs=[
            pl.BlockSpec(memory_space=pltpu.SMEM),
            whole(8, LANES),
            row_spec,
            row_spec,
            row_spec,
            whole(D, D),
            whole(2, FF, D),
            whole(4, D),
        ],
        out_specs=[
            row_spec,
            row_spec,
            row_spec,
            whole(2, D, FF),
            whole(D, D),
            whole(2, D),
        ],
        out_shape=[
            jax.ShapeDtypeStruct((count, D), low_type),
            jax.ShapeDtypeStruct((count, D), low_type),
            jax.ShapeDtypeStruct((count, D), low_type),
            jax.ShapeDtypeStruct((2, D, FF), low_type),
            jax.ShapeDtypeStruct((D, D), low_type),
            jax.ShapeDtypeStruct((2, D), wide_type),
        ],
        scratch_shapes=[
            pltpu.VMEM((D, FF), wide_type),
            pltpu.VMEM((D, FF), wide_type),
            pltpu.VMEM((D, D), wide_type),
        ],
        compiler_params=pltpu.CompilerParams(vmem_limit_bytes=VMEM_BYTES),
        name="feed",
    )(ids, weights, rows, att, grad, wo, ffn, ln_params)


def finish_kernel(
    dx_ref,
    dz_ref,
    ga_ref,
    sa_ref,
    wa_ref,
    ma_ref,
    gf_ref,
    sf_ref,
    wf_ref,
    mf_ref,
    ln_ref,
    first_ref,
    second_ref,
    sum_ref,
    grad_ref,
    ga_out,
    ma_out,
    wa_out,
    ca_out,
    gf_out,
    mf_out,
    wf_out,
    cf_out,
    gl_out,
    first_out,
    second_out,
    ln_out,
):
    grad_ref[...] = dx_ref[...].astype(wide_type) + dz_ref[...].astype(wide_type)
    keep = 1.0 - muon_rate * muon_decay
    for refs, size in (
        ((ga_ref, sa_ref, wa_ref, ma_ref, ga_out, ma_out, wa_out, ca_out), D),
        ((gf_ref, sf_ref, wf_ref, mf_ref, gf_out, mf_out, wf_out, cf_out), FF),
    ):
        grad, ortho, weight, moment, grad_out, moment_out, weight_out, copy_out = refs
        grad = grad[...].astype(wide_type)
        grad_out[...] = grad
        moment_out[...] = momentum_keep * moment[...] + grad
        rate = muon_rate * 0.2 * math.sqrt(size)
        new = keep * weight[...] - rate * ortho[...].astype(wide_type)
        weight_out[...] = new
        copy_out[...] = new.astype(low_type)
    width = first_ref.shape[1]
    place = lax.axis_index("narrow")

    def own(ref):
        picked = jnp.zeros((4, width), wide_type)
        for at in range(D // width):
            picked = picked + jnp.where(place == at, ref[0:4, at * width : (at + 1) * width], 0.0)
        return picked

    grad = own(sum_ref)
    first = beta_first * first_ref[...] + (1.0 - beta_first) * grad
    second = beta_second * second_ref[...] + (1.0 - beta_second) * grad * grad
    gl_out[...] = grad
    first_out[...] = first
    second_out[...] = second
    first_fix = 1.0 - beta_first**STEP
    second_fix = 1.0 - beta_second**STEP
    ln_out[...] = own(ln_ref) - adam_rate * (first / first_fix) / (
        jnp.sqrt(second / second_fix) + adam_epsilon
    )


def finish(dx, dz, attn, ffn, ln):
    steps = 4

    def rows(item):
        block = item.shape[0] // steps
        return pl.BlockSpec((block, item.shape[1]), lambda i: (i, 0))

    def whole(item):
        return pl.BlockSpec(item.shape, lambda i: (0, 0))

    def outs(group):
        shape = group[0].shape
        return [jax.ShapeDtypeStruct(shape, wide_type)] * 3 + [
            jax.ShapeDtypeStruct(shape, low_type)
        ]

    row_items = [dx, dz] + list(attn) + list(ffn)
    row_outs = [jax.ShapeDtypeStruct(dx.shape, wide_type)] + outs(attn) + outs(ffn)
    ln_outs = [jax.ShapeDtypeStruct(ln[1].shape, wide_type)] * 4
    return pl.pallas_call(
        finish_kernel,
        grid=(steps,),
        in_specs=[rows(item) for item in row_items] + [whole(item) for item in ln],
        out_specs=[rows(item) for item in row_outs] + [whole(item) for item in ln_outs],
        out_shape=row_outs + ln_outs,
        compiler_params=pltpu.CompilerParams(vmem_limit_bytes=VMEM_BYTES),
        name="finish",
    )(*row_items, *ln)


MESH = pl.DeviceIdType.MESH
LANES = 128


def remote(src, dst, send_sem, recv_sem, device):
    return pltpu.make_async_remote_copy(
        src_ref=src,
        dst_ref=dst,
        send_sem=send_sem,
        recv_sem=recv_sem,
        device_id=device,
        device_id_type=MESH,
    )


def greet(devices):
    barrier = pltpu.get_barrier_semaphore()
    for device in devices:
        pl.semaphore_signal(barrier, inc=1, device_id=device, device_id_type=MESH)
    pl.semaphore_wait(barrier, len(devices))


def attend_chunks(source, refs, seqs, asides):
    att_ref, share_ref, logit_ref, before_ref, state_ref, state, carry = refs
    q_in, k_in, v_in, a_in = source
    first_head = lane_of((CHUNK, PAIR)) < HEAD_DIM
    causal = row_of((CHUNK, 2 * CHUNK)) >= lane_of((CHUNK, 2 * CHUNK)) % CHUNK
    same_head = (row_of((PAIR, 2 * PAIR)) // HEAD_DIM) == (
        (lane_of((PAIR, 2 * PAIR)) // HEAD_DIM) % 2
    )
    lower = (row_of((CHUNK, CHUNK)) >= lane_of((CHUNK, CHUNK))).astype(low_type)
    items = []
    for seq in range(seqs):
        part = slice(seq * CHUNK, (seq + 1) * CHUNK)
        before = carry[seq]
        before_ref[0, seq] = before
        total = dot_nn(lower, a_in[part, :]) + before
        carry[seq] = total[CHUNK - 1 :, :]
        inv = 1.0 / total
        for pair in range(PAIRS):
            lanes = slice(pair * PAIR, (pair + 1) * PAIR)
            items.append(
                dict(
                    seq=seq,
                    pair=pair,
                    lanes=lanes,
                    q=q_in[part, lanes] * low_type(HEAD_DIM**-0.5),
                    k=k_in[part, lanes],
                    v=v_in[part, lanes],
                    a=a_in[part, lanes],
                    inv=inv[:, lanes],
                )
            )

    def score(t):
        t["a_two"] = split_pair(t["a"], first_head)
        t["now"] = jnp.where(same_head, state[t["seq"], t["pair"]], 0.0).astype(low_type)
        state_ref[0, t["seq"], t["pair"]] = t["now"]
        raw = dot_nt(t["q"], split_pair(t["k"], first_head))
        t["scores"] = jnp.where(causal, raw, 0.0).astype(low_type)

    def gather(t):
        numer = dot_nn(t["scores"], t["a_two"]) + dot_nt(t["q"], t["now"][:, :PAIR])
        t["logit"] = numer * t["inv"]
        logit_ref[t["seq"], :, t["lanes"]] = t["logit"].astype(low_type)

    def soften(t):
        expo = jnp.exp(t["logit"] - head_reduce(t["logit"], first_head, jnp.max, -jnp.inf))
        share = expo * (t["inv"] / head_reduce(expo, first_head, jnp.sum, 0.0))
        t["share"] = share.astype(low_type)
        share_ref[t["seq"], :, t["lanes"]] = t["share"]

    def blend(t):
        raw = dot_nt(t["share"], t["a_two"])
        t["mix"] = jnp.where(causal, raw, 0.0).astype(low_type)

    def finish_item(t):
        att = dot_nn(t["mix"], split_pair(t["v"], first_head))
        att = att + dot_nn(t["share"], t["now"][:, PAIR:])
        att_ref[t["seq"], :, t["lanes"]] = att.astype(low_type)
        state[t["seq"], t["pair"]] += dot_tn(t["a"], jnp.concatenate([t["k"], t["v"]], axis=1))

    for stage, aside in zip((score, gather, soften, blend, finish_item), asides):
        for place, item in enumerate(items):
            stage(item)
            if place == len(items) // 2 - 1 and aside is not None:
                aside()


def forward_kernel(
    ids_ref,
    dw_ref,
    x_first_ref,
    x_ref,
    ln_ref,
    attn_hbm,
    ffn_w_hbm,
    q_ref,
    k_ref,
    v_ref,
    a_ref,
    att_ref,
    share_ref,
    logit_ref,
    before_ref,
    state_ref,
    weight_ref,
    in_hbm,
    out_hbm,
    ffn_hbm,
    state,
    carry,
    held,
    in_w,
    piece_ref,
    attn_ref,
    ffn_ref,
    own,
    own_ffn,
    counts,
    counts_z,
    counts_chip,
    counts_mate,
    sems,
    *,
    narrow,
    total_seqs,
    groups,
):
    step = pl.program_id(0)
    steps = pl.num_programs(0)
    seqs = x_ref.shape[0]
    here = Place(narrow)
    copies = Copies(sems)
    z, core, chip = here.z, here.core, here.chip
    rows = attn_ref.shape[1]
    ffn_rows = ffn_ref.shape[1]
    half = rows // 2
    bit = half // 2
    quarter = ffn_rows // 4
    small = rows // 4
    w = lax.axis_index("wide")
    column = range(narrow - 1)
    planes = range(3)
    rounds = range(1, narrow)
    cols = blocks_at(core, D // 2)

    def inside(shard):
        return jnp.clip(shard, 0, narrow - 1)

    def from_z(place):
        return lax.rem(z + narrow - here.hops[place], narrow)

    def in_rows(owner, part):
        return blocks_at(4 * owner + 2 * core + part, bit)

    in_z, in_chip, in_core = [], [], []
    for part in range(2):
        in_z.append(
            [
                copies.remote(
                    own.at[chip, blocks_at(2 * core + part, bit)],
                    in_w.at[chip, in_rows(z, part)],
                    here.column[i],
                )
                for i in column
            ]
        )
        blocks = [in_w.at[chip, in_rows(from_z(i), part)] for i in column]
        in_chip.append(
            [[copies.remote(block, block, here.chips[p]) for p in planes] for block in blocks]
        )
        blocks = [in_w.at[:, in_rows(from_z(i), part)] for i in column]
        in_core.append([copies.remote(block, block, here.mate) for block in blocks])

    def ffn_block(shard):
        return ffn_hbm.at[core, blocks_at(4 * shard + chip, quarter)]

    def out_block(shard):
        return out_hbm.at[blocks_at(4 * shard + chip, small), cols]

    def sends(way, turn):
        if way == 0:
            return jnp.logical_and(z < narrow - 1, z + 1 - turn >= 0)
        return jnp.logical_and(z > 0, z - 1 + turn <= narrow - 1)

    def gets(way, turn):
        return z - turn >= 0 if way == 0 else z + turn <= narrow - 1

    relay, spread, passed = {}, {}, {}
    for turn in rounds:
        for way in range(2):
            sign = 1 if way == 0 else -1
            there = (w, inside(z + sign))
            shard = inside(z + sign * (1 - turn))
            if turn == 1:
                sources = [
                    own_ffn.at[core, blocks_at(chip, quarter)],
                    own.at[4, blocks_at(chip, small), cols],
                ]
            else:
                sources = [ffn_block(shard), out_block(shard)]
            targets = [ffn_block(shard), out_block(shard)]
            relay[way, turn] = [
                copies.remote(src, dst, there) for src, dst in zip(sources, targets)
            ]
            got = inside(z - sign * turn)
            spread[way, turn] = [
                copies.remote(block, block, here.chips[p])
                for block in (ffn_block(got), out_block(got))
                for p in planes
            ]
            passed[way, turn] = [
                copies.remote(block, block, here.mate)
                for block in (
                    ffn_hbm.at[core, blocks_at(got, ffn_rows)],
                    out_hbm.at[blocks_at(got, rows), cols],
                )
            ]

    def relay_send(turn):
        for way in range(2):

            @pl.when(sends(way, turn))
            def _():
                for copy in relay[way, turn]:
                    copy.start()

    def relay_get(turn):
        for way in range(2):

            @pl.when(gets(way, turn))
            def _():
                for copy in relay[way, turn]:
                    copy.wait_recv()
                for copy in spread[way, turn]:
                    copy.start()

        if turn + 1 < narrow:
            relay_send(turn + 1)

    def pass_on(turn):
        for way in range(2):

            @pl.when(gets(way, turn))
            def _():
                for copy in spread[way, turn]:
                    copy.wait_recv()
                for copy in passed[way, turn]:
                    copy.start()

    count_z = [copies.remote(counts, counts_z.at[i], here.column[i]) for i in column]
    count_chip = [copies.remote(counts, counts_chip.at[p], here.chips[p]) for p in planes]
    count_mate = copies.remote(counts, counts_mate, here.mate)
    load_piece = copies.local(attn_hbm.at[chip, blocks_at(core, half)], piece_ref)
    load_attn = copies.local(attn_hbm, attn_ref)
    load_ffn = copies.local(ffn_w_hbm, ffn_ref)
    keep_ffn = copies.local(own_ffn, ffn_hbm.at[:, blocks_at(z, ffn_rows)])
    keep_out = copies.local(own.at[4], out_hbm.at[blocks_at(z, rows)])
    keep_in = copies.local(in_w, in_hbm)

    def normal(ref):
        normed, _ = normalize(ref[...].reshape(seqs * CHUNK, D).astype(wide_type))
        return (normed * ln_ref[0:1, :] + ln_ref[1:2, :]).astype(low_type)

    def product(first, place):
        out = dot_nn(first, in_w[place])
        held[place] = (jnp.exp(out) if place == 3 else out).astype(low_type)

    @pl.when(step == 0)
    def _():
        for copy in (load_piece, load_attn, load_ffn):
            copy.start()
        state[...] = jnp.zeros_like(state)
        carry[...] = jnp.zeros_like(carry)
        greet(here.column + here.chips + [here.mate])
        load_piece.wait()
        own[chip, blocks_at(core, half), :] = piece_ref[...].astype(low_type)
        for part in range(2):
            for i in column:
                in_z[part][i].start()
        load_attn.wait()
        load_ffn.wait()
        for place in range(4):
            in_w[place, blocks_at(z, rows), :] = attn_ref[place].astype(low_type)
        own[4] = attn_ref[4].astype(low_type)
        own_ffn[...] = ffn_ref[...].astype(low_type)
        lanes = lane_of((8, LANES))
        count = jnp.zeros((8, LANES), wide_type)
        for seq in range(ids_ref.shape[0]):
            count = count + (lanes == ids_ref[seq]).astype(wide_type)
        counts[...] = count
        for part in range(2):
            for i in column:
                in_z[part][i].wait_recv()
                for p in planes:
                    in_chip[part][i][p].start()
        relay_send(1)
        for copy in count_z:
            copy.start()
        keep_ffn.start()
        keep_out.start()
        for part in range(2):
            for i in column:
                for p in planes:
                    in_chip[part][i][p].wait_recv()
                in_core[part][i].start()
        relay_get(1)
        for part in range(2):
            for i in column:
                in_core[part][i].wait_recv()
        keep_in.start()
        first = normal(x_first_ref)
        for place in range(4):
            product(first, place)
        if narrow > 2:
            relay_get(2)

    for turn in range(3, narrow):

        @pl.when(step == turn - 1)
        def _():
            relay_get(turn)

    @pl.when(step == 1)
    def _():
        for copy in count_z:
            copy.wait()
        counts[...] = counts[...] + sum(counts_z[i] for i in column)
        for copy in count_chip:
            copy.start()

    @pl.when(step == 2)
    def _():
        for copy in count_chip:
            copy.wait()
        counts[...] = counts[...] + sum(counts_chip[p] for p in planes)
        count_mate.start()

    @pl.when(step == 3)
    def _():
        count_mate.wait()
        total = counts[...] + counts_mate[...]
        lanes = lane_of((8, LANES))
        values = jnp.zeros((8, LANES), wide_type)
        for group in range(groups):
            values = values + jnp.where(lanes == group, dw_ref[group], 0.0)
        weight_ref[...] = values * total_seqs / (groups * jnp.maximum(total, 1.0))

    for turn in rounds:

        @pl.when(step == jnp.minimum(steps - 1, turn + 4))
        def _():
            pass_on(turn)

    source = [held[place] for place in range(4)]
    for ref, item in zip((q_ref, k_ref, v_ref, a_ref), source):
        ref[...] = item.reshape(ref.shape)
    later = {}

    def aside_norm():
        later["first"] = normal(x_ref)

    attend_chunks(
        source,
        (att_ref, share_ref, logit_ref, before_ref, state_ref, state, carry),
        seqs,
        (
            aside_norm,
            lambda: product(later["first"], 0),
            lambda: product(later["first"], 1),
            lambda: product(later["first"], 2),
            lambda: product(later["first"], 3),
        ),
    )

    @pl.when(step == steps - 1)
    def _():
        keep_ffn.wait()
        keep_out.wait()
        keep_in.wait()
        for part in range(2):
            for i in column:
                in_z[part][i].wait_send()
                for p in planes:
                    in_chip[part][i][p].wait_send()
                in_core[part][i].wait_send()
        for turn in rounds:
            for way in range(2):

                @pl.when(sends(way, turn))
                def _():
                    for copy in relay[way, turn]:
                        copy.wait_send()

                @pl.when(gets(way, turn))
                def _():
                    for copy in spread[way, turn]:
                        copy.wait_send()
                    for copy in passed[way, turn]:
                        copy.wait()


def forward(tokens, ids, dw, ln_params, attn_w, ffn_w):
    seqs, length, _ = tokens.shape
    chunks = length // CHUNK
    wide = lax.axis_size("wide")
    narrow = lax.axis_size("narrow")
    if wide > 8:
        sets = [[place + 8 * group for group in range(wide // 8)] for place in range(8)]
        ids = lax.all_gather(ids, "wide", axis_index_groups=sets, tiled=True)
    block = pl.BlockSpec((seqs, CHUNK, D), lambda i: (0, i, 0))
    ahead = pl.BlockSpec((seqs, CHUNK, D), lambda i: (0, jnp.minimum(i + 1, chunks - 1), 0))
    low_out = jax.ShapeDtypeStruct(tokens.shape, low_type)
    any_spec = pl.BlockSpec(memory_space=pl.ANY)

    def whole(*shape):
        return pl.BlockSpec(shape, lambda i: (0,) * len(shape))

    column = narrow - 1
    sems = 6 + 2 * (10 * column + 2 * column * 10 + column + 4)
    return pl.pallas_call(
        functools.partial(
            forward_kernel,
            narrow=narrow,
            total_seqs=seqs * wide * narrow,
            groups=dw.shape[0],
        ),
        grid=(chunks,),
        in_specs=[
            pl.BlockSpec(memory_space=pltpu.SMEM),
            pl.BlockSpec(memory_space=pltpu.SMEM),
            whole(seqs, CHUNK, D),
            ahead,
            whole(4, D),
            any_spec,
            any_spec,
        ],
        out_specs=[block] * 7
        + [
            pl.BlockSpec((1, seqs, 1, D), lambda i: (i, 0, 0, 0)),
            pl.BlockSpec((1, seqs, PAIRS, PAIR, 2 * PAIR), lambda i: (i, 0, 0, 0, 0)),
            whole(8, LANES),
            any_spec,
            any_spec,
            any_spec,
        ],
        out_shape=[low_out] * 7
        + [
            jax.ShapeDtypeStruct((chunks, seqs, 1, D), wide_type),
            jax.ShapeDtypeStruct((chunks, seqs, PAIRS, PAIR, 2 * PAIR), low_type),
            jax.ShapeDtypeStruct((8, LANES), wide_type),
            jax.ShapeDtypeStruct((4, D, D), low_type),
            jax.ShapeDtypeStruct((D, D), low_type),
            jax.ShapeDtypeStruct((2, FF, D), low_type),
        ],
        scratch_shapes=[
            pltpu.VMEM((seqs, PAIRS, PAIR, 2 * PAIR), wide_type),
            pltpu.VMEM((seqs, 1, D), wide_type),
            pltpu.VMEM((4, seqs * CHUNK, D), low_type),
            pltpu.VMEM((4, D, D), low_type),
            pltpu.VMEM((attn_w.shape[1] // 2, D), wide_type),
            pltpu.VMEM(attn_w.shape, wide_type),
            pltpu.VMEM(ffn_w.shape, wide_type),
            pltpu.VMEM(attn_w.shape, low_type),
            pltpu.VMEM(ffn_w.shape, low_type),
            pltpu.VMEM((8, LANES), wide_type),
            pltpu.VMEM((column, 8, LANES), wide_type),
            pltpu.VMEM((3, 8, LANES), wide_type),
            pltpu.VMEM((8, LANES), wide_type),
            pltpu.SemaphoreType.DMA((sems,)),
        ],
        compiler_params=pltpu.CompilerParams(
            vmem_limit_bytes=VMEM_BYTES, collective_id=0, has_side_effects=True
        ),
        name="forward",
    )(ids, dw, tokens, tokens, ln_params, attn_w, ffn_w)


class Place:
    def __init__(self, narrow):
        self.narrow = narrow
        w = lax.axis_index("wide")
        self.z = lax.axis_index("narrow")
        self.core = lax.rem(w, 2)
        self.chip = lax.rem(w // 2, 4)
        self.other = 1 - self.core
        self.hops = list(range(1, narrow))
        self.column_z = [lax.rem(self.z + hop, narrow) for hop in self.hops]
        self.column = [(w, place) for place in self.column_z]
        self.chip_at = [lax.rem(self.chip + hop, 4) for hop in range(1, 4)]
        self.chips = [(w - 2 * self.chip + 2 * chip, self.z) for chip in self.chip_at]
        self.mate = (w + 1 - 2 * self.core, self.z)


class Copies:
    def __init__(self, sems):
        self.sems = sems
        self.used = 0

    def remote(self, src, dst, device):
        at = self.used
        self.used += 2
        return remote(src, dst, self.sems.at[at], self.sems.at[at + 1], device)

    def local(self, src, dst):
        at = self.used
        self.used += 1
        return pltpu.make_async_copy(src, dst, self.sems.at[at])


def blocks_at(owner, size):
    return pl.ds(pl.multiple_of(owner * size, size), size)


def wide_sum(parts):
    total = parts[0].astype(wide_type)
    for part in parts[1:]:
        total = total + part.astype(wide_type)
    return total


def newton_poly(gram):
    size = gram.shape[0]
    eye = row_of((size, size)) == lane_of((size, size))
    trace = jnp.sum(jnp.where(eye, gram, 0.0), axis=1, keepdims=True)
    trace = jnp.sum(trace, axis=0, keepdims=True)
    scale = 1.0 / (jnp.sqrt(trace) + 1e-07)

    def low_dot(left, right):
        return dot_nn(left.astype(low_type), right.astype(low_type))

    def polynomial(one):
        poly = quintic_cube * one + quintic_five * low_dot(one, one)
        return poly + jnp.where(eye, quintic_lin, 0.0)

    gram_one = gram * (scale * scale)
    poly_one = polynomial(gram_one)
    gram_two = low_dot(low_dot(gram_one, poly_one), poly_one)
    poly_two = polynomial(gram_two)
    return low_dot(poly_one, poly_two) * scale


def update_body(
    wsum_ref,
    take_f,
    mom_w_ref,
    mom_hbm,
    mom_f_hbm,
    ln_one_ref,
    ln_two_ref,
    grad_attn,
    step_attn,
    grad_ffn,
    step_ffn,
    ln_ref,
    ln_now,
    ln_mate,
    ln_chips,
    ln_column,
    col_w,
    grad_w,
    moment_w,
    poly_w,
    send_w,
    all_w,
    all_f,
    mom_f,
    mom_o,
    moment_f,
    out_f,
    all_o,
    moment_o,
    step_o,
    cut_gf,
    col_gf,
    strips_gf,
    gram_f,
    cut_go,
    col_go,
    strips_go,
    gram_o,
    *,
    narrow,
    here,
    copies,
    over_groups,
):
    z, core, chip = here.z, here.core, here.chip
    half = D // 2
    quarter = D // 4
    rows = D // narrow
    small = rows // 4
    ffn_rows = FF // narrow
    strip = quarter // narrow
    column = range(narrow - 1)
    planes = range(3)
    own_cols = blocks_at(core, half)
    own_quarter = blocks_at(chip, quarter)
    own_small = blocks_at(chip, small)
    matrix = lax.rem(z, 4)

    def to_plane(src, dst):
        return [copies.remote(src(i), dst(i), here.chips[i]) for i in planes]

    def to_column(src, dst):
        return [copies.remote(src(i), dst(i), here.column[i]) for i in column]

    def same(block):
        return lambda i: block

    keep_f = copies.local(mom_f_hbm.at[core], mom_f)
    keep_o = copies.local(mom_hbm.at[4], mom_o)
    mate_ln = [copies.remote(ln_now, ln_mate, here.mate)]
    plane_ln = to_plane(same(ln_now), lambda i: ln_chips.at[i])
    block = all_f.at[own_quarter]
    plane_f = to_plane(same(block), same(block))
    block = all_o.at[own_small, own_cols]
    plane_f = plane_f + to_plane(same(block), same(block))
    z_sum = to_column(lambda i: wsum_ref.at[lax.rem(here.column_z[i], 4)], lambda i: col_w.at[i])
    z_ln = to_column(same(ln_now), lambda i: ln_column.at[i])
    block = out_f.at[0, core]
    mate_f = [copies.remote(block, block, here.mate)]
    block = all_o.at[:, own_cols]
    mate_o = [copies.remote(block, block, here.mate)]
    z_gf = to_column(
        lambda i: cut_gf.at[blocks_at(here.column_z[i], strip)], lambda i: col_gf.at[i]
    )
    block = grad_w.at[own_quarter, own_cols]
    plane_w = to_plane(same(block), same(block))
    z_go = to_column(
        lambda i: cut_go.at[blocks_at(here.column_z[i], strip)], lambda i: col_go.at[i]
    )
    block = grad_w.at[:, own_cols]
    mate_w = [copies.remote(block, block, here.mate)]
    block = strips_gf.at[blocks_at(z, strip)]
    z_back_f = to_column(same(block), same(block))
    block = strips_go.at[blocks_at(z, strip)]
    z_back_o = to_column(same(block), same(block))
    block = gram_f.at[own_quarter]
    plane_gf = to_plane(same(block), same(block))
    block = gram_o.at[own_quarter, own_cols]
    plane_go = to_plane(same(block), same(block))
    quad = [z - matrix + lax.rem(matrix + hop, 4) for hop in range(1, 4)]

    def hand_back(kind):
        spread = [
            copies.remote(
                send_w.at[kind, there],
                all_w.at[kind, matrix, own_small, own_cols],
                (lax.axis_index("wide"), there),
            )
            for there in quad
        ]
        block = all_w.at[kind, :, own_small, own_cols]
        plane = to_plane(same(block), same(block))
        block = all_w.at[kind, :, :, own_cols]
        return spread, plane, [copies.remote(block, block, here.mate)]

    spread_g, plane_g, mate_g = hand_back(0)
    spread_s, plane_s, mate_s = hand_back(1)
    block = gram_o.at[:, own_cols]
    mate_go = [copies.remote(block, block, here.mate)]
    block = out_f.at[1, core]
    mate_x = [copies.remote(block, block, here.mate)]
    write_f = [copies.local(out_f.at[0], grad_ffn), copies.local(out_f.at[1], step_ffn)]
    write_o = [copies.local(all_o, grad_attn.at[4]), copies.local(step_o, step_attn.at[4])]
    write_w = [
        copies.local(all_w.at[0], grad_attn.at[pl.ds(0, 4)]),
        copies.local(all_w.at[1], step_attn.at[pl.ds(0, 4)]),
    ]
    sent = []

    def start(group):
        for copy in group:
            copy.start()
        sent.extend(group)

    def arrive(group):
        for copy in group:
            copy.wait_recv()

    def begin(group):
        for copy in group:
            copy.start()

    start(z_sum)
    begin([keep_f, keep_o])
    ln_now[...] = jnp.zeros_like(ln_now)
    ln_now[0:2, :] = ln_one_ref[...]
    ln_now[2:4, :] = ln_two_ref[...]
    over_groups(ln_now, 2)
    start(mate_ln)
    grad_f, grad_o = take_f()
    all_f[own_quarter, :] = grad_f
    all_o[own_small, own_cols] = grad_o
    start(plane_f)

    arrive(z_sum)
    total = wide_sum([wsum_ref[matrix]] + [col_w[i] for i in column])
    grad_w[own_quarter, own_cols] = total.astype(low_type)
    start(plane_w)
    arrive(mate_ln)
    mate_ln[0].wait_send()
    ln_now[...] = ln_now[...] + ln_mate[...]
    start(plane_ln)

    keep_f.wait()
    arrive(plane_f)
    start(mate_o)
    grad = all_f[...].T
    out_f[0, core] = grad
    start(mate_f)
    moment_f[...] = (momentum_keep * mom_f[...] + grad.astype(wide_type)).astype(low_type)
    cut_gf[...] = dot_tn(moment_f[:, own_quarter], moment_f[...]).astype(low_type)
    start(z_gf)

    arrive(plane_w)
    start(mate_w)
    arrive(plane_ln)
    for copy in plane_ln:
        copy.wait_send()
    ln_now[...] = ln_now[...] + ln_chips[0] + ln_chips[1] + ln_chips[2]
    start(z_ln)

    arrive(mate_o)
    keep_o.wait()
    moment = momentum_keep * mom_o[...] + all_o[...].astype(wide_type)
    moment_o[...] = moment.astype(low_type)
    cut_go[...] = dot_tn(moment_o[:, own_quarter], moment_o[:, own_cols]).astype(low_type)
    start(z_go)

    def small_rows(there):
        return pl.ds(pl.multiple_of(there * rows + chip * small, small), small)

    arrive(mate_w)
    for there in range(narrow):
        send_w[0, there] = grad_w[small_rows(there), own_cols]
    start(spread_g)
    all_w[0, matrix, own_small, own_cols] = send_w[0, z]
    moment = momentum_keep * mom_w_ref[...].astype(wide_type) + grad_w[...].astype(wide_type)
    moment_w[...] = moment.astype(low_type)
    gram = dot_tn(moment_w[...], moment_w[...])
    arrive(z_gf)
    total = wide_sum([cut_gf[blocks_at(z, strip), :]] + [col_gf[i] for i in column])
    strips_gf[blocks_at(z, strip), :] = total.astype(low_type)
    start(z_back_f)
    arrive(z_go)
    total = wide_sum([cut_go[blocks_at(z, strip), :]] + [col_go[i] for i in column])
    strips_go[blocks_at(z, strip), :] = total.astype(low_type)
    start(z_back_o)
    poly_w[...] = newton_poly(gram).astype(low_type)
    picked = jnp.concatenate([moment_w[small_rows(there), :] for there in range(narrow)], axis=0)
    ortho = dot_nn(picked, poly_w[:, own_cols]).astype(low_type)
    for there in range(narrow):
        send_w[1, there] = ortho[there * small : (there + 1) * small, :]
    start(spread_s)
    all_w[1, matrix, own_small, own_cols] = send_w[1, z]

    arrive(z_back_f)
    gram_f[own_quarter, :] = strips_gf[...]
    start(plane_gf)
    arrive(spread_g)
    start(plane_g)
    arrive(spread_s)
    start(plane_s)
    arrive(z_back_o)
    gram_o[own_quarter, own_cols] = strips_go[...]
    start(plane_go)
    arrive(plane_gf)
    poly = newton_poly(gram_f[...].astype(wide_type)).astype(low_type)
    out_f[1, core] = dot_nn(moment_f[...], poly).astype(low_type)
    start(mate_x)
    arrive(plane_g)
    start(mate_g)
    arrive(plane_s)
    start(mate_s)
    arrive(plane_go)
    start(mate_go)
    arrive(mate_go)
    poly = newton_poly(gram_o[...].astype(wide_type)).astype(low_type)
    step_o[...] = dot_nn(moment_o[...], poly).astype(low_type)
    begin(write_o)
    arrive(mate_f)
    arrive(mate_x)
    begin(write_f)
    arrive(z_ln)
    total = ln_now[...]
    for i in column:
        total = total + ln_column[i]
    ln_ref[...] = total
    arrive(mate_g)
    begin(write_w[:1])
    arrive(mate_s)
    begin(write_w[1:])
    for copy in write_o + write_f + write_w:
        copy.wait()
    settled = [id(copy) for copy in mate_ln + plane_ln]
    for copy in sent:
        if id(copy) not in settled:
            copy.wait_send()


def back_kernel(*refs, narrow, chunks, sets):
    blocks = list(refs[:9])
    xc_ref, x_ref, w_ref, ln_ref, gffn_hbm, go_hbm, mom_hbm, mom_f_hbm, ln_two_ref = refs[9:18]
    dz_ref, grad_attn, step_attn, grad_ffn, step_ffn, ln_sum_ref = refs[18:24]
    state, carry, dq_all, dk_all, dv_all, de_all, first_t = refs[24:31]
    own_f, got_f, far_f, col_f, own_o, got_o, cut_o, far_o, col_o = refs[31:40]
    low_f, low_o, mom_own, mom_low, mom_all = refs[40:45]
    grad_w, got_w, half_w, far_w, staged, gln_ref, wsum_ref = refs[45:52]
    sums = refs[52:54]
    group_w, group_f, group_o, group_ln = refs[54:58]
    *update_refs, sems = refs[58:]
    step = pl.program_id(0)
    steps = pl.num_programs(0)
    here = Place(narrow)
    copies = Copies(sems)
    half = D // 2
    part = D // 4
    rows = D // narrow
    ffn_rows = FF // narrow
    column = range(narrow - 1)
    own_cols = blocks_at(here.core, half)
    mate_cols = blocks_at(here.other, half)
    grads = (dq_all, dk_all, dv_all, de_all)
    w = lax.axis_index("wide")
    peers = [(lax.rem(w + 8 * at, 8 * sets), here.z) for at in range(1, sets)]

    keep_f = copies.local(gffn_hbm.at[here.core], own_f)
    keep_o = copies.local(go_hbm.at[:, own_cols], own_o)
    keep_mom = copies.local(mom_hbm.at[pl.ds(0, 4)], mom_own)
    pieces = [blocks_at(there, part) for there in here.chip_at + [here.chip]]
    mate_f = [
        copies.remote(gffn_hbm.at[here.other, piece], got_f.at[piece], here.mate)
        for piece in pieces
    ]
    mate_o = copies.remote(go_hbm.at[:, mate_cols], got_o, here.mate)
    plane_f = [
        copies.remote(own_f.at[pieces[hop]], far_f.at[hop], here.chips[hop]) for hop in range(3)
    ]
    plane_o = [
        copies.remote(cut_o.at[:, here.chip_at[hop]], far_o.at[hop], here.chips[hop])
        for hop in range(3)
    ]
    z_sum = []
    for i in column:
        there = here.column_z[i]
        z_sum.append(
            copies.remote(low_f.at[:, blocks_at(there, ffn_rows)], col_f.at[i], here.column[i])
        )
        z_sum.append(copies.remote(low_o.at[there], col_o.at[i], here.column[i]))
    z_mom = [
        copies.remote(
            mom_low.at[lax.rem(here.column_z[i], 4), :, own_cols],
            mom_all.at[blocks_at(here.z, rows), own_cols],
            here.column[i],
        )
        for i in column
    ]
    mate_mom = copies.remote(mom_all.at[:, own_cols], mom_all.at[:, own_cols], here.mate)
    mate_w = [
        copies.remote(grad_w.at[m, :, mate_cols], got_w.at[m], here.mate) for m in range(4)
    ]
    plane_w = [
        [
            copies.remote(
                half_w.at[m, blocks_at(here.chip_at[hop], part)],
                far_w.at[hop, m],
                here.chips[hop],
            )
            for hop in range(3)
        ]
        for m in range(4)
    ]

    def gradient(m):
        total = dot_nn(first_t[...], grads[m][...].reshape(-1, D))
        grad_w[m] = total.astype(low_type)
        mate_w[m].start()

    def over_cores(m):
        mate_w[m].wait()
        half_w[m] = wide_sum([grad_w[m, :, own_cols], got_w[m]]).astype(low_type)
        for copy in plane_w[m]:
            copy.start()

    def over_chips(m):
        for copy in plane_w[m]:
            copy.wait()
        mine = half_w[m, blocks_at(here.chip, part), :]
        wsum_ref[m] = wide_sum([mine] + [far_w[hop, m] for hop in range(3)]).astype(low_type)

    @pl.when(step == 0)
    def _():
        state[...] = jnp.zeros_like(state)
        carry[...] = jnp.zeros_like(carry)
        gln_ref[...] = jnp.zeros_like(gln_ref)
        greet(here.column + here.chips + [here.mate] + peers)
        for copy in [keep_f] + mate_f + [keep_o, mate_o, keep_mom]:
            copy.start()

    @pl.when(step == 1)
    def _():
        keep_mom.wait()
        mom_low[...] = mom_own[...].astype(low_type)
        for copy in z_mom:
            copy.start()
        mom_all[blocks_at(here.z, rows), own_cols] = mom_low[lax.rem(here.z, 4), :, own_cols]

    def piece_sum(at):
        mate_f[at].wait()
        piece = pieces[at]
        own_f[piece, :] = wide_sum([own_f[piece, :], got_f[piece, :]]).astype(low_type)
        if at < 3:
            plane_f[at].start()

    @pl.when(step == 1)
    def _():
        keep_f.wait()
        for at in range(2):
            piece_sum(at)

    @pl.when(step == 2)
    def _():
        for at in range(2, 4):
            piece_sum(at)
        keep_o.wait()
        mate_o.wait()
        cut_o[...] = wide_sum([own_o[...], got_o[...]]).astype(low_type).reshape(cut_o.shape)
        for copy in plane_o:
            copy.start()

    @pl.when(step < chunks)
    def _():
        chunk = chunks - 1 - step
        seqs = xc_ref.shape[0]

        for seq in range(seqs):
            normed, _ = normalize(xc_ref[seq].astype(wide_type))
            first = (normed * ln_ref[0:1, :] + ln_ref[1:2, :]).astype(low_type)
            first_t[:, blocks_at(chunk * seqs + seq, CHUNK)] = first.T
        attend_back_chunk(blocks + [staged.at[place] for place in range(4)], state, carry)
        for place in range(4):
            grads[place][chunk] = staged[place]

    @pl.when(step == chunks)
    def _():
        for copy in plane_f + plane_o:
            copy.wait()
        mine = own_f[blocks_at(here.chip, part), :]
        low_f[...] = wide_sum([mine] + [far_f[hop] for hop in range(3)]).astype(low_type)
        mine = cut_o[:, here.chip]
        low_o[...] = wide_sum([mine] + [far_o[hop] for hop in range(3)]).astype(low_type)
        for copy in z_sum:
            copy.start()
        gradient(0)
        gradient(1)
        over_cores(0)
        gradient(2)
        over_cores(1)
        gradient(3)
        for copy in z_mom:
            copy.wait_recv()
        mate_mom.start()

    @pl.when(step == chunks + 1)
    def _():
        over_cores(2)
        over_cores(3)

    @pl.when(step >= chunks)
    def _():
        per = chunks // 4
        seqs = x_ref.shape[0]
        parts = [item[pl.ds((step - chunks) * per, per)].reshape(-1, D) for item in grads]
        dfirst = dot_nt(parts[0], w_ref[0])
        for place in range(1, 4):
            dfirst = dfirst + dot_nt(parts[place], w_ref[place])
        spans = [slice(at * CHUNK, (at + 1) * CHUNK) for at in range(per)]
        rows_in = [x_ref[:, span, :].reshape(-1, D) for span in spans]
        normed, inverse = normalize(jnp.concatenate(rows_in, axis=0).astype(wide_type))
        gln_ref[0:1, :] += jnp.sum(dfirst * normed, axis=0, keepdims=True)
        gln_ref[1:2, :] += jnp.sum(dfirst, axis=0, keepdims=True)
        dz = norm_back(dfirst, normed, inverse, ln_ref[0:1, :]).astype(low_type)
        for at, span in enumerate(spans):
            size = seqs * CHUNK
            dz_ref[:, span, :] = dz[at * size : (at + 1) * size].reshape(seqs, CHUNK, D)

    def over_groups(ref, number):
        if sets == 1:
            return
        slots = (group_w, group_f, group_ln, group_o)[number]
        exchange = [
            copies.remote(ref, slots.at[at], peer) for at, peer in enumerate(peers)
        ]
        for copy in exchange:
            copy.start()
        for copy in exchange:
            copy.wait()
        total = wide_sum([ref[...]] + [slots[at] for at in range(len(peers))])
        ref[...] = total.astype(ref.dtype)

    def take_f():
        for copy in z_sum:
            copy.wait()
        sum_f, sum_o = sums
        mine = low_f[:, blocks_at(here.z, ffn_rows)]
        sum_f[...] = wide_sum([mine] + [col_f[i] for i in column]).astype(low_type)
        sum_o[...] = wide_sum([low_o[here.z]] + [col_o[i] for i in column]).astype(low_type)
        over_groups(sum_f, 1)
        over_groups(sum_o, 3)
        return sum_f[...], sum_o[...]

    @pl.when(step == steps - 1)
    def _():
        for m in range(4):
            over_chips(m)
        over_groups(wsum_ref, 0)
        mate_mom.wait()
        for copy in z_mom:
            copy.wait_send()
        update_body(
            wsum_ref,
            take_f,
            mom_all,
            mom_hbm,
            mom_f_hbm,
            gln_ref,
            ln_two_ref,
            grad_attn,
            step_attn,
            grad_ffn,
            step_ffn,
            ln_sum_ref,
            *update_refs,
            narrow=narrow,
            here=here,
            copies=copies,
            over_groups=over_groups,
        )


def back(q, k, v, a, share, logit, before, datt, states, tokens, in_w, ln_params, gffn, go, mom, mom_f, ln_two):
    seqs, length, _ = q.shape
    chunks = length // CHUNK
    narrow = lax.axis_size("narrow")
    small, half, part = D // narrow // 4, D // 2, D // 4
    ffn_rows = FF // narrow

    def chunk_at(i):
        return jnp.maximum(chunks - 1 - i, 0)

    def rows_at(i):
        return (0, jnp.maximum(i - chunks, 0), 0)

    def whole(*shape):
        return pl.BlockSpec(shape, lambda i: (0,) * len(shape))

    block = pl.BlockSpec((seqs, CHUNK, D), lambda i: (0, chunk_at(i), 0))
    row_spec = pl.BlockSpec((seqs, length // 4, D), rows_at)
    any_spec = pl.BlockSpec(memory_space=pl.ANY)
    rows, strip, column = D // narrow, part // narrow, narrow - 1
    sets = lax.axis_size("wide") // 8
    spare = max(sets - 1, 1)
    outs = [(5, rows, D), (5, rows, D), (2, ffn_rows, D), (2, ffn_rows, D)]

    def full(*shape):
        return pltpu.VMEM(shape, wide_type)

    def low(*shape):
        return pltpu.VMEM(shape, low_type)

    return pl.pallas_call(
        functools.partial(back_kernel, narrow=narrow, chunks=chunks, sets=sets),
        grid=(chunks + 4,),
        in_specs=[block] * 6
        + [
            pl.BlockSpec((1, seqs, 1, D), lambda i: (chunk_at(i), 0, 0, 0)),
            block,
            pl.BlockSpec((1, seqs, PAIRS, PAIR, 2 * PAIR), lambda i: (chunk_at(i), 0, 0, 0, 0)),
            block,
            row_spec,
            whole(4, D, D),
            whole(4, D),
            any_spec,
            any_spec,
            any_spec,
            any_spec,
            whole(2, D),
        ],
        out_specs=[row_spec] + [any_spec] * 4 + [whole(8, D)],
        out_shape=[jax.ShapeDtypeStruct(q.shape, low_type)]
        + [jax.ShapeDtypeStruct(shape, low_type) for shape in outs]
        + [jax.ShapeDtypeStruct((8, D), wide_type)],
        scratch_shapes=[
            pltpu.VMEM((seqs, PAIRS, PAIR, 2 * PAIR), wide_type),
            pltpu.VMEM((seqs, 1, D), wide_type),
            low(chunks, seqs, CHUNK, D),
            low(chunks, seqs, CHUNK, D),
            low(chunks, seqs, CHUNK, D),
            low(chunks, seqs, CHUNK, D),
            low(D, seqs * length),
            low(D, FF),
            low(D, FF),
            low(3, part, FF),
            low(narrow - 1, part, ffn_rows),
            low(D, half),
            low(D, half),
            low(narrow, 4, small, half),
            low(3, narrow, small, half),
            low(narrow - 1, small, half),
            low(part, FF),
            low(narrow, small, half),
            pltpu.VMEM((4, D // narrow, D), wide_type),
            low(4, D // narrow, D),
            low(D, D),
            low(4, D, D),
            low(4, D, half),
            low(4, D, half),
            low(3, 4, part, half),
            low(4, seqs, CHUNK, D),
            full(2, D),
            low(4, part, half),
            low(part, ffn_rows),
            low(small, half),
            low(spare, 4, part, half),
            low(spare, part, ffn_rows),
            low(spare, small, half),
            full(spare, 8, D),
            full(8, D),
            full(8, D),
            full(3, 8, D),
            full(column, 8, D),
            low(column, part, half),
            low(D, D),
            low(D, D),
            low(D, D),
            low(2, narrow, small, half),
            low(2, 4, rows, D),
            low(D, ffn_rows),
            full(ffn_rows, D),
            full(rows, D),
            low(ffn_rows, D),
            low(2, 2, ffn_rows, D),
            low(rows, D),
            low(rows, D),
            low(rows, D),
            low(part, D),
            low(column, strip, D),
            low(part, D),
            low(D, D),
            low(part, half),
            low(column, strip, half),
            low(part, half),
            low(D, D),
            pltpu.SemaphoreType.DMA((11 + 2 * (65 + 9 * column + 4 * spare),)),
        ],
        compiler_params=pltpu.CompilerParams(
            vmem_limit_bytes=VMEM_BYTES, collective_id=1, has_side_effects=True
        ),
        name="back",
    )(
        q,
        k,
        v,
        a,
        share,
        logit,
        before,
        datt,
        states,
        tokens,
        tokens,
        in_w,
        ln_params,
        gffn,
        go,
        mom,
        mom_f,
        ln_two,
    )


def shards(
    tokens,
    out_grad,
    group_ids,
    domain_weight,
    attn_w,
    ffn_w,
    attn_mom,
    ffn_mom,
    ln_params,
    ln_first,
    ln_second,
):
    local_seqs, length, _ = tokens.shape
    token_count = local_seqs * length
    rows = tokens.reshape(token_count, D)
    head = (local_seqs, length, D)
    q, k, v, a, att, share, logit, before, states, weights, in_w, out_w, ffn_low = forward(
        tokens, group_ids, domain_weight, ln_params, attn_w, ffn_w
    )
    output, dx, datt, gffn, go, ln_two = feed(
        group_ids,
        weights,
        rows,
        att.reshape(token_count, D),
        out_grad.reshape(token_count, D),
        out_w,
        ffn_low,
        ln_params,
        length,
    )
    dz, attn_grad, attn_step, ffn_grad, ffn_step, ln_sum = back(
        q,
        k,
        v,
        a,
        share,
        logit,
        before,
        datt.reshape(head),
        states,
        tokens,
        in_w,
        ln_params,
        gffn,
        go,
        attn_mom,
        ffn_mom,
        ln_two,
    )

    def flat(*items):
        return [item.reshape(-1, D) for item in items]

    results = finish(
        dx,
        dz.reshape(token_count, D),
        flat(attn_grad, attn_step, attn_w, attn_mom),
        flat(ffn_grad, ffn_step, ffn_w, ffn_mom),
        (ln_params, ln_first, ln_second, ln_sum),
    )
    input_grad, ga, ma, wa, ca, gf, mf, wf, cf, ln_grad, first_new, second_new, ln_new = results
    attn, ffn = attn_w.shape, ffn_w.shape
    return (
        output.reshape(tokens.shape),
        input_grad.reshape(tokens.shape),
        ga.reshape(attn),
        gf.reshape(ffn),
        ln_grad,
        ma.reshape(attn),
        mf.reshape(ffn),
        wa.reshape(attn),
        wf.reshape(ffn),
        ca.reshape(attn),
        cf.reshape(ffn),
        first_new,
        second_new,
        ln_new,
    )


def solution(mesh):
    split = P(("wide", "narrow"), None, None)
    rows = P(None, "narrow", None)
    lanes = P(None, "narrow")
    inner = jax.shard_map(
        shards,
        mesh=mesh,
        in_specs=(
            split,
            split,
            P(("wide", "narrow")),
            P(),
            rows,
            rows,
            rows,
            rows,
            P(),
            lanes,
            lanes,
        ),
        out_specs=(
            split,
            split,
            rows,
            rows,
            lanes,
            rows,
            rows,
            rows,
            rows,
            rows,
            rows,
            lanes,
            lanes,
            lanes,
        ),
        check_vma=False,
    )
    return inner
```

```python
import functools
import math

import jax
import jax.numpy as jnp
from jax import lax
from jax.experimental import pallas as pl
from jax.experimental.pallas import tpu as pltpu
from jax.sharding import PartitionSpec as P

D = 512
HEADS = 8
HEAD_DIM = 64
FF = 2048
STEP = 10

norm_epsilon = 1e-05
momentum_keep = 0.5
quintic_lin = 3.4445
quintic_cube = -4.775
quintic_five = 2.0315
muon_rate = 0.7
muon_decay = 0.1
adam_rate = 0.2
beta_first = 0.9
beta_second = 0.999
adam_epsilon = 1e-08

CHUNK = 128
PAIR = 2 * HEAD_DIM
PAIRS = HEADS // 2
VMEM_BYTES = 60 * 1024 * 1024
low_type = jnp.bfloat16
wide_type = jnp.float32


def dot_nn(left, right):
    return lax.dot_general(left, right, (((1,), (0,)), ((), ())), preferred_element_type=wide_type)


def dot_nt(left, right):
    return lax.dot_general(left, right, (((1,), (1,)), ((), ())), preferred_element_type=wide_type)


def dot_tn(left, right):
    return lax.dot_general(left, right, (((0,), (0,)), ((), ())), preferred_element_type=wide_type)


def normalize(rows):
    center = rows - jnp.mean(rows, axis=-1, keepdims=True)
    spread = jnp.mean(center * center, axis=-1, keepdims=True)
    inverse = lax.rsqrt(spread + norm_epsilon)
    return center * inverse, inverse


def norm_back(grad_rows, normed, inverse, gain):
    grad_normed = grad_rows * gain
    mean_grad = jnp.mean(grad_normed, axis=-1, keepdims=True)
    mean_cross = jnp.mean(grad_normed * normed, axis=-1, keepdims=True)
    return inverse * (grad_normed - mean_grad - normed * mean_cross)


def lane_of(shape):
    return lax.broadcasted_iota(jnp.int32, shape, 1)


def row_of(shape):
    return lax.broadcasted_iota(jnp.int32, shape, 0)


def split_pair(pair, first_head):
    zero = jnp.zeros_like(pair)
    return jnp.concatenate(
        [jnp.where(first_head, pair, zero), jnp.where(first_head, zero, pair)], axis=0
    )


def head_reduce(values, first_head, op, neutral):
    left = op(jnp.where(first_head, values, neutral), axis=-1, keepdims=True)
    right = op(jnp.where(first_head, neutral, values), axis=-1, keepdims=True)
    return jnp.where(first_head, left, right)


def attend_back_chunk(refs, state, carry):
    (
        q_ref,
        k_ref,
        v_ref,
        a_ref,
        share_ref,
        logit_ref,
        before_ref,
        datt_ref,
        state_ref,
        dq_ref,
        dk_ref,
        dv_ref,
        de_ref,
    ) = refs
    scaling = HEAD_DIM**-0.5
    first_head = lane_of((CHUNK, PAIR)) < HEAD_DIM
    causal = row_of((CHUNK, 2 * CHUNK)) >= lane_of((CHUNK, 2 * CHUNK)) % CHUNK
    anti = row_of((CHUNK, 2 * CHUNK)) <= lane_of((CHUNK, 2 * CHUNK)) % CHUNK
    same_head = (row_of((PAIR, 2 * PAIR)) // HEAD_DIM) == (
        (lane_of((PAIR, 2 * PAIR)) // HEAD_DIM) % 2
    )
    lower = (row_of((CHUNK, CHUNK)) >= lane_of((CHUNK, CHUNK))).astype(low_type)
    upper = (row_of((CHUNK, CHUNK)) <= lane_of((CHUNK, CHUNK))).astype(low_type)

    def masked(mask, raw):
        return jnp.where(mask, raw, 0.0).astype(low_type)

    items = []
    for seq in range(q_ref.shape[0]):
        total = dot_nn(lower, a_ref[seq]) + before_ref[0, seq]
        inv = 1.0 / total
        for pair in range(PAIRS):
            lanes = slice(pair * PAIR, (pair + 1) * PAIR)
            items.append(
                dict(seq=seq, pair=pair, lanes=lanes, total=total[:, lanes], inv=inv[:, lanes])
            )

    def load(t):
        seq, lanes = t["seq"], t["lanes"]
        t["k"] = k_ref[seq, :, lanes]
        t["v"] = v_ref[seq, :, lanes]
        t["a"] = a_ref[seq, :, lanes]
        t["share"] = share_ref[seq, :, lanes]
        t["datt"] = datt_ref[seq, :, lanes]
        t["q"] = q_ref[seq, :, lanes] * low_type(scaling)
        t["before"] = state_ref[0, seq, t["pair"]]
        t["after"] = jnp.where(same_head, state[seq, t["pair"]], 0.0).astype(low_type)
        t["v_two"] = split_pair(t["v"], first_head)
        t["a_two"] = split_pair(t["a"], first_head)
        t["dmix"] = masked(causal, dot_nt(t["datt"], t["v_two"]))

    def gather(t):
        t["share_two"] = split_pair(t["share"], first_head)
        t["datt_two"] = split_pair(t["datt"], first_head)
        t["dshare"] = dot_nn(t["dmix"], t["a_two"]) + dot_nt(t["datt"], t["before"][:, PAIR:])

    def soften(t):
        logit = logit_ref[t["seq"], :, t["lanes"]].astype(wide_type)
        prob = t["share"].astype(wide_type) * t["total"]
        cross = t["dshare"] * t["inv"] * prob
        dlogit = cross - prob * head_reduce(cross, first_head, jnp.sum, 0.0)
        t["dnumer"] = (dlogit * t["inv"]).astype(low_type)
        t["dtotal"] = -(cross + dlogit * logit) * t["inv"]
        t["mix_t"] = masked(anti, dot_nt(t["a"], t["share_two"]))
        t["dmix_t"] = masked(anti, dot_nt(t["v"], t["datt_two"]))

    def blend(t):
        t["dnumer_two"] = split_pair(t["dnumer"], first_head)
        t["dscores"] = masked(causal, dot_nt(t["dnumer"], t["a_two"]))
        t["dscores_t"] = masked(anti, dot_nt(t["a"], t["dnumer_two"]))
        t["k_two"] = split_pair(t["k"], first_head)
        t["q_two"] = split_pair(t["q"], first_head)
        t["scores_t"] = masked(anti, dot_nt(t["k"], t["q_two"]))
        t["later"] = dot_nn(t["a"], t["after"])

    def finish(t):
        seq, lanes = t["seq"], t["lanes"]
        dq = dot_nn(t["dscores"], t["k_two"]) + dot_nn(t["dnumer"], t["before"][:, :PAIR])
        dq_ref[seq, :, lanes] = (dq * scaling).astype(low_type)
        dv = dot_nn(t["mix_t"], t["datt_two"]) + t["later"][:, PAIR:]
        dv_ref[seq, :, lanes] = dv.astype(low_type)
        dk = dot_nn(t["dscores_t"], t["q_two"]) + t["later"][:, :PAIR]
        dk_ref[seq, :, lanes] = dk.astype(low_type)
        high = t["dtotal"].astype(low_type)
        rest = (t["dtotal"] - high.astype(wide_type)).astype(low_type)
        tail = dot_nn(upper, high) + dot_nn(upper, rest) + carry[seq, :, lanes]
        carry[seq, :, lanes] = tail[0:1, :]
        da = dot_nn(t["dmix_t"], t["share_two"]) + dot_nn(t["scores_t"], t["dnumer_two"])
        da = da + dot_nt(jnp.concatenate([t["k"], t["v"]], axis=1), t["after"]) + tail
        de = da.astype(low_type).astype(wide_type) * t["a"].astype(wide_type)
        de_ref[seq, :, lanes] = de.astype(low_type)
        state[seq, t["pair"], :, :PAIR] += dot_tn(t["dnumer"], t["q"])
        state[seq, t["pair"], :, PAIR:] += dot_tn(t["share"], t["datt"])

    for stage in (load, gather, soften, blend, finish):
        for item in items:
            stage(item)


FF_BLOCK = 256
gelu_root = math.sqrt(2.0 / math.pi)
gelu_cube = 0.044715


def feed_kernel(
    ids_ref,
    weight_ref,
    x_ref,
    att_ref,
    og_ref,
    wo_ref,
    ffn_ref,
    ln_ref,
    out_ref,
    dx_ref,
    datt_ref,
    gffn_ref,
    go_ref,
    gln_ref,
    up_sum,
    down_sum,
    o_sum,
    hidden,
    dinner,
    *,
    per_seq,
):
    step = pl.program_id(0)

    @pl.when(step == 0)
    def _():
        up_sum[...] = jnp.zeros_like(up_sum)
        down_sum[...] = jnp.zeros_like(down_sum)
        o_sum[...] = jnp.zeros_like(o_sum)
        gln_ref[...] = jnp.zeros_like(gln_ref)

    att = att_ref[...]
    mixed = x_ref[...].astype(wide_type) + dot_nn(att, wo_ref[...])
    normed, inverse = normalize(mixed)
    second = (normed * ln_ref[2:3, :] + ln_ref[3:4, :]).astype(low_type)
    mine = lane_of((1, LANES)) == ids_ref[step // per_seq]
    weight = jnp.sum(jnp.where(mine, weight_ref[0:1, :], 0.0), axis=1, keepdims=True)
    dout = og_ref[...].astype(wide_type) * weight
    dy = dout.astype(low_type)
    second_t = second.T
    dy_t = dy.T
    parts = [slice(part * FF_BLOCK, (part + 1) * FF_BLOCK) for part in range(FF // FF_BLOCK)]

    def open_part(part):
        return dot_nt(second, ffn_ref[0, part, :]), dot_nt(dy, ffn_ref[1, part, :])

    ahead = open_part(parts[0])
    for place, part in enumerate(parts):
        inner, dhidden = ahead
        if place + 1 < len(parts):
            ahead = open_part(parts[place + 1])
        square = inner * inner
        bend = jnp.tanh(inner * (gelu_root + (gelu_root * gelu_cube) * square))
        half = 0.5 + 0.5 * bend
        hidden[:, part] = (inner * half).astype(low_type)
        slope = half + (0.5 * inner) * (1.0 - bend * bend) * (
            gelu_root + (3.0 * gelu_root * gelu_cube) * square
        )
        dinner[:, part] = (dhidden * slope).astype(low_type)
    result = mixed + dot_nn(hidden[...], ffn_ref[1])
    dsecond = dot_nn(dinner[...], ffn_ref[0])
    for part in parts:
        down_sum[:, part] += dot_nn(dy_t, hidden[:, part])
        up_sum[:, part] += dot_nn(second_t, dinner[:, part])
    out_ref[...] = result.astype(low_type)
    gln_ref[0:1, :] += jnp.sum(dsecond * normed, axis=0, keepdims=True)
    gln_ref[1:2, :] += jnp.sum(dsecond, axis=0, keepdims=True)
    dmixed = dout + norm_back(dsecond, normed, inverse, ln_ref[2:3, :])
    datt = dmixed.astype(low_type)
    dx_ref[...] = datt
    o_sum[...] += dot_tn(att, datt)
    datt_ref[...] = dot_nt(datt, wo_ref[...]).astype(low_type)

    @pl.when(step == pl.num_programs(0) - 1)
    def _():
        gffn_ref[0] = up_sum[...].astype(low_type)
        gffn_ref[1] = down_sum[...].astype(low_type)
        go_ref[...] = o_sum[...].astype(low_type)


def feed(ids, weights, rows, att, grad, wo, ffn, ln_params, length):
    count = rows.shape[0]
    block = 512
    row_spec = pl.BlockSpec((block, D), lambda i: (i, 0))

    def whole(*shape):
        return pl.BlockSpec(shape, lambda i: (0,) * len(shape))

    return pl.pallas_call(
        functools.partial(feed_kernel, per_seq=length // block),
        grid=(count // block,),
        in_specs=[
            pl.BlockSpec(memory_space=pltpu.SMEM),
            whole(8, LANES),
            row_spec,
            row_spec,
            row_spec,
            whole(D, D),
            whole(2, FF, D),
            whole(4, D),
        ],
        out_specs=[
            row_spec,
            row_spec,
            row_spec,
            whole(2, D, FF),
            whole(D, D),
            whole(2, D),
        ],
        out_shape=[
            jax.ShapeDtypeStruct((count, D), low_type),
            jax.ShapeDtypeStruct((count, D), low_type),
            jax.ShapeDtypeStruct((count, D), low_type),
            jax.ShapeDtypeStruct((2, D, FF), low_type),
            jax.ShapeDtypeStruct((D, D), low_type),
            jax.ShapeDtypeStruct((2, D), wide_type),
        ],
        scratch_shapes=[
            pltpu.VMEM((D, FF), wide_type),
            pltpu.VMEM((D, FF), wide_type),
            pltpu.VMEM((D, D), wide_type),
            pltpu.VMEM((block, FF), low_type),
            pltpu.VMEM((block, FF), low_type),
        ],
        compiler_params=pltpu.CompilerParams(vmem_limit_bytes=VMEM_BYTES),
        name="feed",
    )(ids, weights, rows, att, grad, wo, ffn, ln_params)


def finish_kernel(
    dx_ref,
    dz_ref,
    ga_ref,
    sa_ref,
    wa_ref,
    ma_ref,
    gf_ref,
    sf_ref,
    wf_ref,
    mf_ref,
    ln_ref,
    first_ref,
    second_ref,
    sum_ref,
    grad_ref,
    ga_out,
    ma_out,
    wa_out,
    ca_out,
    gf_out,
    mf_out,
    wf_out,
    cf_out,
    gl_out,
    first_out,
    second_out,
    ln_out,
):
    grad_ref[...] = dx_ref[...].astype(wide_type) + dz_ref[...].astype(wide_type)
    keep = 1.0 - muon_rate * muon_decay
    for refs, size in (
        ((ga_ref, sa_ref, wa_ref, ma_ref, ga_out, ma_out, wa_out, ca_out), D),
        ((gf_ref, sf_ref, wf_ref, mf_ref, gf_out, mf_out, wf_out, cf_out), FF),
    ):
        grad, ortho, weight, moment, grad_out, moment_out, weight_out, copy_out = refs
        grad = grad[...].astype(wide_type)
        grad_out[...] = grad
        moment_out[...] = momentum_keep * moment[...] + grad
        rate = muon_rate * 0.2 * math.sqrt(size)
        new = keep * weight[...] - rate * ortho[...].astype(wide_type)
        weight_out[...] = new
        copy_out[...] = new.astype(low_type)
    width = first_ref.shape[1]
    place = lax.axis_index("narrow")

    def own(ref):
        picked = jnp.zeros((4, width), wide_type)
        for at in range(D // width):
            picked = picked + jnp.where(place == at, ref[0:4, at * width : (at + 1) * width], 0.0)
        return picked

    grad = own(sum_ref)
    first = beta_first * first_ref[...] + (1.0 - beta_first) * grad
    second = beta_second * second_ref[...] + (1.0 - beta_second) * grad * grad
    gl_out[...] = grad
    first_out[...] = first
    second_out[...] = second
    first_fix = 1.0 - beta_first**STEP
    second_fix = 1.0 - beta_second**STEP
    ln_out[...] = own(ln_ref) - adam_rate * (first / first_fix) / (
        jnp.sqrt(second / second_fix) + adam_epsilon
    )


def finish(dx, dz, attn, ffn, ln):
    steps = 4

    def rows(item):
        block = item.shape[0] // steps
        return pl.BlockSpec((block, item.shape[1]), lambda i: (i, 0))

    def whole(item):
        return pl.BlockSpec(item.shape, lambda i: (0, 0))

    def outs(group):
        shape = group[0].shape
        return [jax.ShapeDtypeStruct(shape, wide_type)] * 3 + [
            jax.ShapeDtypeStruct(shape, low_type)
        ]

    row_items = [dx, dz] + list(attn) + list(ffn)
    row_outs = [jax.ShapeDtypeStruct(dx.shape, wide_type)] + outs(attn) + outs(ffn)
    ln_outs = [jax.ShapeDtypeStruct(ln[1].shape, wide_type)] * 4
    return pl.pallas_call(
        finish_kernel,
        grid=(steps,),
        in_specs=[rows(item) for item in row_items] + [whole(item) for item in ln],
        out_specs=[rows(item) for item in row_outs] + [whole(item) for item in ln_outs],
        out_shape=row_outs + ln_outs,
        compiler_params=pltpu.CompilerParams(vmem_limit_bytes=VMEM_BYTES),
        name="finish",
    )(*row_items, *ln)


MESH = pl.DeviceIdType.MESH
LANES = 128


def remote(src, dst, send_sem, recv_sem, device):
    return pltpu.make_async_remote_copy(
        src_ref=src,
        dst_ref=dst,
        send_sem=send_sem,
        recv_sem=recv_sem,
        device_id=device,
        device_id_type=MESH,
    )


def greet(devices):
    barrier = pltpu.get_barrier_semaphore()
    for device in devices:
        pl.semaphore_signal(barrier, inc=1, device_id=device, device_id_type=MESH)
    pl.semaphore_wait(barrier, len(devices))


def attend_chunks(source, refs, seqs, asides):
    att_ref, share_ref, logit_ref, before_ref, state_ref, state, carry = refs
    q_in, k_in, v_in, a_in = source
    first_head = lane_of((CHUNK, PAIR)) < HEAD_DIM
    causal = row_of((CHUNK, 2 * CHUNK)) >= lane_of((CHUNK, 2 * CHUNK)) % CHUNK
    same_head = (row_of((PAIR, 2 * PAIR)) // HEAD_DIM) == (
        (lane_of((PAIR, 2 * PAIR)) // HEAD_DIM) % 2
    )
    lower = (row_of((CHUNK, CHUNK)) >= lane_of((CHUNK, CHUNK))).astype(low_type)
    items = []
    for seq in range(seqs):
        part = slice(seq * CHUNK, (seq + 1) * CHUNK)
        before = carry[seq]
        before_ref[0, seq] = before
        total = dot_nn(lower, a_in[part, :]) + before
        carry[seq] = total[CHUNK - 1 :, :]
        inv = 1.0 / total
        for pair in range(PAIRS):
            lanes = slice(pair * PAIR, (pair + 1) * PAIR)
            items.append(
                dict(
                    seq=seq,
                    pair=pair,
                    lanes=lanes,
                    q=q_in[part, lanes] * low_type(HEAD_DIM**-0.5),
                    k=k_in[part, lanes],
                    v=v_in[part, lanes],
                    a=a_in[part, lanes],
                    inv=inv[:, lanes],
                )
            )

    def score(t):
        t["a_two"] = split_pair(t["a"], first_head)
        t["now"] = jnp.where(same_head, state[t["seq"], t["pair"]], 0.0).astype(low_type)
        state_ref[0, t["seq"], t["pair"]] = t["now"]
        raw = dot_nt(t["q"], split_pair(t["k"], first_head))
        t["scores"] = jnp.where(causal, raw, 0.0).astype(low_type)

    def gather(t):
        numer = dot_nn(t["scores"], t["a_two"]) + dot_nt(t["q"], t["now"][:, :PAIR])
        t["logit"] = numer * t["inv"]
        logit_ref[t["seq"], :, t["lanes"]] = t["logit"].astype(low_type)

    def soften(t):
        expo = jnp.exp(t["logit"] - head_reduce(t["logit"], first_head, jnp.max, -jnp.inf))
        share = expo * (t["inv"] / head_reduce(expo, first_head, jnp.sum, 0.0))
        t["share"] = share.astype(low_type)
        share_ref[t["seq"], :, t["lanes"]] = t["share"]

    def blend(t):
        raw = dot_nt(t["share"], t["a_two"])
        t["mix"] = jnp.where(causal, raw, 0.0).astype(low_type)

    def finish_item(t):
        att = dot_nn(t["mix"], split_pair(t["v"], first_head))
        att = att + dot_nn(t["share"], t["now"][:, PAIR:])
        att_ref[t["seq"], :, t["lanes"]] = att.astype(low_type)
        state[t["seq"], t["pair"]] += dot_tn(t["a"], jnp.concatenate([t["k"], t["v"]], axis=1))

    for stage, aside in zip((score, gather, soften, blend, finish_item), asides):
        for place, item in enumerate(items):
            stage(item)
            if place == len(items) // 2 - 1 and aside is not None:
                aside()


def forward_kernel(
    ids_ref,
    dw_ref,
    x_first_ref,
    x_ref,
    ln_ref,
    attn_hbm,
    ffn_w_hbm,
    q_ref,
    k_ref,
    v_ref,
    a_ref,
    att_ref,
    share_ref,
    logit_ref,
    before_ref,
    state_ref,
    weight_ref,
    in_hbm,
    out_hbm,
    ffn_hbm,
    state,
    carry,
    held,
    in_w,
    piece_ref,
    attn_ref,
    ffn_ref,
    own,
    own_ffn,
    counts,
    counts_z,
    counts_chip,
    counts_mate,
    sems,
    *,
    narrow,
    total_seqs,
    groups,
):
    step = pl.program_id(0)
    steps = pl.num_programs(0)
    seqs = x_ref.shape[0]
    here = Place(narrow)
    copies = Copies(sems)
    z, core, chip = here.z, here.core, here.chip
    rows = attn_ref.shape[1]
    ffn_rows = ffn_ref.shape[1]
    half = rows // 2
    bit = half // 2
    quarter = ffn_rows // 4
    small = rows // 4
    w = lax.axis_index("wide")
    column = range(narrow - 1)
    planes = range(3)
    rounds = range(1, narrow)
    cols = blocks_at(core, D // 2)

    def inside(shard):
        return jnp.clip(shard, 0, narrow - 1)

    def from_z(place):
        return lax.rem(z + narrow - here.hops[place], narrow)

    def in_rows(owner, part):
        return blocks_at(4 * owner + 2 * core + part, bit)

    in_z, in_chip, in_core = [], [], []
    for part in range(2):
        in_z.append(
            [
                copies.remote(
                    own.at[chip, blocks_at(2 * core + part, bit)],
                    in_w.at[chip, in_rows(z, part)],
                    here.column[i],
                )
                for i in column
            ]
        )
        blocks = [in_w.at[chip, in_rows(from_z(i), part)] for i in column]
        in_chip.append(
            [[copies.remote(block, block, here.chips[p]) for p in planes] for block in blocks]
        )
        blocks = [in_w.at[:, in_rows(from_z(i), part)] for i in column]
        in_core.append([copies.remote(block, block, here.mate) for block in blocks])

    def ffn_block(shard):
        return ffn_hbm.at[core, blocks_at(4 * shard + chip, quarter)]

    def out_block(shard):
        return out_hbm.at[blocks_at(4 * shard + chip, small), cols]

    def sends(way, turn):
        if way == 0:
            return jnp.logical_and(z < narrow - 1, z + 1 - turn >= 0)
        return jnp.logical_and(z > 0, z - 1 + turn <= narrow - 1)

    def gets(way, turn):
        return z - turn >= 0 if way == 0 else z + turn <= narrow - 1

    relay, spread, passed = {}, {}, {}
    for turn in rounds:
        for way in range(2):
            sign = 1 if way == 0 else -1
            there = (w, inside(z + sign))
            shard = inside(z + sign * (1 - turn))
            if turn == 1:
                sources = [
                    own_ffn.at[core, blocks_at(chip, quarter)],
                    own.at[4, blocks_at(chip, small), cols],
                ]
            else:
                sources = [ffn_block(shard), out_block(shard)]
            targets = [ffn_block(shard), out_block(shard)]
            relay[way, turn] = [
                copies.remote(src, dst, there) for src, dst in zip(sources, targets)
            ]
            got = inside(z - sign * turn)
            spread[way, turn] = [
                copies.remote(block, block, here.chips[p])
                for block in (ffn_block(got), out_block(got))
                for p in planes
            ]
            passed[way, turn] = [
                copies.remote(block, block, here.mate)
                for block in (
                    ffn_hbm.at[core, blocks_at(got, ffn_rows)],
                    out_hbm.at[blocks_at(got, rows), cols],
                )
            ]

    def relay_send(turn):
        for way in range(2):

            @pl.when(sends(way, turn))
            def _():
                for copy in relay[way, turn]:
                    copy.start()

    def relay_get(turn):
        for way in range(2):

            @pl.when(gets(way, turn))
            def _():
                for copy in relay[way, turn]:
                    copy.wait_recv()
                for copy in spread[way, turn]:
                    copy.start()

        if turn + 1 < narrow:
            relay_send(turn + 1)

    def pass_on(turn):
        for way in range(2):

            @pl.when(gets(way, turn))
            def _():
                for copy in spread[way, turn]:
                    copy.wait_recv()
                for copy in passed[way, turn]:
                    copy.start()

    count_z = [copies.remote(counts, counts_z.at[i], here.column[i]) for i in column]
    count_chip = [copies.remote(counts, counts_chip.at[p], here.chips[p]) for p in planes]
    count_mate = copies.remote(counts, counts_mate, here.mate)
    load_piece = copies.local(attn_hbm.at[chip, blocks_at(core, half)], piece_ref)
    load_attn = copies.local(attn_hbm, attn_ref)
    load_ffn = copies.local(ffn_w_hbm, ffn_ref)
    keep_ffn = copies.local(own_ffn, ffn_hbm.at[:, blocks_at(z, ffn_rows)])
    keep_out = copies.local(own.at[4], out_hbm.at[blocks_at(z, rows)])
    keep_in = copies.local(in_w, in_hbm)

    def normal(ref):
        normed, _ = normalize(ref[...].reshape(seqs * CHUNK, D).astype(wide_type))
        return (normed * ln_ref[0:1, :] + ln_ref[1:2, :]).astype(low_type)

    def product(first, place):
        out = dot_nn(first, in_w[place])
        held[place] = (jnp.exp(out) if place == 3 else out).astype(low_type)

    @pl.when(step == 0)
    def _():
        for copy in (load_piece, load_attn, load_ffn):
            copy.start()
        state[...] = jnp.zeros_like(state)
        carry[...] = jnp.zeros_like(carry)
        greet(here.column + here.chips + [here.mate])
        load_piece.wait()
        own[chip, blocks_at(core, half), :] = piece_ref[...].astype(low_type)
        for part in range(2):
            for i in column:
                in_z[part][i].start()
        load_attn.wait()
        load_ffn.wait()
        for place in range(4):
            in_w[place, blocks_at(z, rows), :] = attn_ref[place].astype(low_type)
        own[4] = attn_ref[4].astype(low_type)
        own_ffn[...] = ffn_ref[...].astype(low_type)
        lanes = lane_of((8, LANES))
        count = jnp.zeros((8, LANES), wide_type)
        for seq in range(ids_ref.shape[0]):
            count = count + (lanes == ids_ref[seq]).astype(wide_type)
        counts[...] = count
        for part in range(2):
            for i in column:
                in_z[part][i].wait_recv()
                for p in planes:
                    in_chip[part][i][p].start()
        relay_send(1)
        for copy in count_z:
            copy.start()
        keep_ffn.start()
        keep_out.start()
        for part in range(2):
            for i in column:
                for p in planes:
                    in_chip[part][i][p].wait_recv()
                in_core[part][i].start()
        relay_get(1)
        for part in range(2):
            for i in column:
                in_core[part][i].wait_recv()
        keep_in.start()
        first = normal(x_first_ref)
        for place in range(4):
            product(first, place)
        if narrow > 2:
            relay_get(2)

    for turn in range(3, narrow):

        @pl.when(step == turn - 1)
        def _():
            relay_get(turn)

    @pl.when(step == 1)
    def _():
        for copy in count_z:
            copy.wait()
        counts[...] = counts[...] + sum(counts_z[i] for i in column)
        for copy in count_chip:
            copy.start()

    @pl.when(step == 2)
    def _():
        for copy in count_chip:
            copy.wait()
        counts[...] = counts[...] + sum(counts_chip[p] for p in planes)
        count_mate.start()

    @pl.when(step == 3)
    def _():
        count_mate.wait()
        total = counts[...] + counts_mate[...]
        lanes = lane_of((8, LANES))
        values = jnp.zeros((8, LANES), wide_type)
        for group in range(groups):
            values = values + jnp.where(lanes == group, dw_ref[group], 0.0)
        weight_ref[...] = values * total_seqs / (groups * jnp.maximum(total, 1.0))

    for turn in rounds:

        @pl.when(step == jnp.minimum(steps - 1, turn + 4))
        def _():
            pass_on(turn)

    source = [held[place] for place in range(4)]
    for ref, item in zip((q_ref, k_ref, v_ref, a_ref), source):
        ref[...] = item.reshape(ref.shape)
    later = {}

    def aside_norm():
        later["first"] = normal(x_ref)

    attend_chunks(
        source,
        (att_ref, share_ref, logit_ref, before_ref, state_ref, state, carry),
        seqs,
        (
            aside_norm,
            lambda: product(later["first"], 0),
            lambda: product(later["first"], 1),
            lambda: product(later["first"], 2),
            lambda: product(later["first"], 3),
        ),
    )

    @pl.when(step == steps - 1)
    def _():
        keep_ffn.wait()
        keep_out.wait()
        keep_in.wait()
        for part in range(2):
            for i in column:
                in_z[part][i].wait_send()
                for p in planes:
                    in_chip[part][i][p].wait_send()
                in_core[part][i].wait_send()
        for turn in rounds:
            for way in range(2):

                @pl.when(sends(way, turn))
                def _():
                    for copy in relay[way, turn]:
                        copy.wait_send()

                @pl.when(gets(way, turn))
                def _():
                    for copy in spread[way, turn]:
                        copy.wait_send()
                    for copy in passed[way, turn]:
                        copy.wait()


def forward(tokens, ids, dw, ln_params, attn_w, ffn_w):
    seqs, length, _ = tokens.shape
    chunks = length // CHUNK
    wide = lax.axis_size("wide")
    narrow = lax.axis_size("narrow")
    if wide > 8:
        sets = [[place + 8 * group for group in range(wide // 8)] for place in range(8)]
        ids = lax.all_gather(ids, "wide", axis_index_groups=sets, tiled=True)
    block = pl.BlockSpec((seqs, CHUNK, D), lambda i: (0, i, 0))
    ahead = pl.BlockSpec((seqs, CHUNK, D), lambda i: (0, jnp.minimum(i + 1, chunks - 1), 0))
    low_out = jax.ShapeDtypeStruct(tokens.shape, low_type)
    any_spec = pl.BlockSpec(memory_space=pl.ANY)

    def whole(*shape):
        return pl.BlockSpec(shape, lambda i: (0,) * len(shape))

    column = narrow - 1
    sems = 6 + 2 * (10 * column + 2 * column * 10 + column + 4)
    return pl.pallas_call(
        functools.partial(
            forward_kernel,
            narrow=narrow,
            total_seqs=seqs * wide * narrow,
            groups=dw.shape[0],
        ),
        grid=(chunks,),
        in_specs=[
            pl.BlockSpec(memory_space=pltpu.SMEM),
            pl.BlockSpec(memory_space=pltpu.SMEM),
            whole(seqs, CHUNK, D),
            ahead,
            whole(4, D),
            any_spec,
            any_spec,
        ],
        out_specs=[block] * 7
        + [
            pl.BlockSpec((1, seqs, 1, D), lambda i: (i, 0, 0, 0)),
            pl.BlockSpec((1, seqs, PAIRS, PAIR, 2 * PAIR), lambda i: (i, 0, 0, 0, 0)),
            whole(8, LANES),
            any_spec,
            any_spec,
            any_spec,
        ],
        out_shape=[low_out] * 7
        + [
            jax.ShapeDtypeStruct((chunks, seqs, 1, D), wide_type),
            jax.ShapeDtypeStruct((chunks, seqs, PAIRS, PAIR, 2 * PAIR), low_type),
            jax.ShapeDtypeStruct((8, LANES), wide_type),
            jax.ShapeDtypeStruct((4, D, D), low_type),
            jax.ShapeDtypeStruct((D, D), low_type),
            jax.ShapeDtypeStruct((2, FF, D), low_type),
        ],
        scratch_shapes=[
            pltpu.VMEM((seqs, PAIRS, PAIR, 2 * PAIR), wide_type),
            pltpu.VMEM((seqs, 1, D), wide_type),
            pltpu.VMEM((4, seqs * CHUNK, D), low_type),
            pltpu.VMEM((4, D, D), low_type),
            pltpu.VMEM((attn_w.shape[1] // 2, D), wide_type),
            pltpu.VMEM(attn_w.shape, wide_type),
            pltpu.VMEM(ffn_w.shape, wide_type),
            pltpu.VMEM(attn_w.shape, low_type),
            pltpu.VMEM(ffn_w.shape, low_type),
            pltpu.VMEM((8, LANES), wide_type),
            pltpu.VMEM((column, 8, LANES), wide_type),
            pltpu.VMEM((3, 8, LANES), wide_type),
            pltpu.VMEM((8, LANES), wide_type),
            pltpu.SemaphoreType.DMA((sems,)),
        ],
        compiler_params=pltpu.CompilerParams(
            vmem_limit_bytes=VMEM_BYTES, collective_id=0, has_side_effects=True
        ),
        name="forward",
    )(ids, dw, tokens, tokens, ln_params, attn_w, ffn_w)


class Place:
    def __init__(self, narrow):
        self.narrow = narrow
        w = lax.axis_index("wide")
        self.z = lax.axis_index("narrow")
        self.core = lax.rem(w, 2)
        self.chip = lax.rem(w // 2, 4)
        self.other = 1 - self.core
        self.hops = list(range(1, narrow))
        self.column_z = [lax.rem(self.z + hop, narrow) for hop in self.hops]
        self.column = [(w, place) for place in self.column_z]
        self.chip_at = [lax.rem(self.chip + hop, 4) for hop in range(1, 4)]
        self.chips = [(w - 2 * self.chip + 2 * chip, self.z) for chip in self.chip_at]
        self.mate = (w + 1 - 2 * self.core, self.z)


class Copies:
    def __init__(self, sems):
        self.sems = sems
        self.used = 0

    def remote(self, src, dst, device):
        at = self.used
        self.used += 2
        return remote(src, dst, self.sems.at[at], self.sems.at[at + 1], device)

    def local(self, src, dst):
        at = self.used
        self.used += 1
        return pltpu.make_async_copy(src, dst, self.sems.at[at])


def blocks_at(owner, size):
    return pl.ds(pl.multiple_of(owner * size, size), size)


def wide_sum(parts):
    total = parts[0].astype(wide_type)
    for part in parts[1:]:
        total = total + part.astype(wide_type)
    return total


def newton_poly(gram):
    size = gram.shape[0]
    eye = row_of((size, size)) == lane_of((size, size))
    trace = jnp.sum(jnp.where(eye, gram, 0.0), axis=1, keepdims=True)
    trace = jnp.sum(trace, axis=0, keepdims=True)
    scale = 1.0 / (jnp.sqrt(trace) + 1e-07)

    def low_dot(left, right):
        return dot_nn(left.astype(low_type), right.astype(low_type))

    def polynomial(one):
        poly = quintic_cube * one + quintic_five * low_dot(one, one)
        return poly + jnp.where(eye, quintic_lin, 0.0)

    gram_one = gram * (scale * scale)
    poly_one = polynomial(gram_one)
    gram_two = low_dot(low_dot(gram_one, poly_one), poly_one)
    poly_two = polynomial(gram_two)
    return low_dot(poly_one, poly_two) * scale


def update_body(
    wsum_ref,
    take_f,
    mom_w_ref,
    mom_hbm,
    mom_f_hbm,
    ln_one_ref,
    ln_two_ref,
    grad_attn,
    step_attn,
    grad_ffn,
    step_ffn,
    ln_ref,
    ln_now,
    ln_mate,
    ln_chips,
    ln_column,
    col_w,
    grad_w,
    moment_w,
    poly_w,
    send_w,
    all_w,
    all_f,
    mom_f,
    mom_o,
    moment_f,
    out_f,
    all_o,
    moment_o,
    step_o,
    cut_gf,
    col_gf,
    strips_gf,
    gram_f,
    cut_go,
    col_go,
    strips_go,
    gram_o,
    *,
    narrow,
    here,
    copies,
    over_groups,
):
    z, core, chip = here.z, here.core, here.chip
    half = D // 2
    quarter = D // 4
    rows = D // narrow
    small = rows // 4
    ffn_rows = FF // narrow
    strip = quarter // narrow
    column = range(narrow - 1)
    planes = range(3)
    own_cols = blocks_at(core, half)
    own_quarter = blocks_at(chip, quarter)
    own_small = blocks_at(chip, small)
    matrix = lax.rem(z, 4)

    def to_plane(src, dst):
        return [copies.remote(src(i), dst(i), here.chips[i]) for i in planes]

    def to_column(src, dst):
        return [copies.remote(src(i), dst(i), here.column[i]) for i in column]

    def same(block):
        return lambda i: block

    keep_f = copies.local(mom_f_hbm.at[core], mom_f)
    keep_o = copies.local(mom_hbm.at[4], mom_o)
    mate_ln = [copies.remote(ln_now, ln_mate, here.mate)]
    plane_ln = to_plane(same(ln_now), lambda i: ln_chips.at[i])
    block = all_f.at[own_quarter]
    plane_f = to_plane(same(block), same(block))
    block = all_o.at[own_small, own_cols]
    plane_f = plane_f + to_plane(same(block), same(block))
    z_sum = to_column(lambda i: wsum_ref.at[lax.rem(here.column_z[i], 4)], lambda i: col_w.at[i])
    z_ln = to_column(same(ln_now), lambda i: ln_column.at[i])
    block = out_f.at[0, core]
    mate_f = [copies.remote(block, block, here.mate)]
    block = all_o.at[:, own_cols]
    mate_o = [copies.remote(block, block, here.mate)]
    z_gf = to_column(
        lambda i: cut_gf.at[blocks_at(here.column_z[i], strip)], lambda i: col_gf.at[i]
    )
    block = grad_w.at[own_quarter, own_cols]
    plane_w = to_plane(same(block), same(block))
    z_go = to_column(
        lambda i: cut_go.at[blocks_at(here.column_z[i], strip)], lambda i: col_go.at[i]
    )
    block = grad_w.at[:, own_cols]
    mate_w = [copies.remote(block, block, here.mate)]
    block = strips_gf.at[blocks_at(z, strip)]
    z_back_f = to_column(same(block), same(block))
    block = strips_go.at[blocks_at(z, strip)]
    z_back_o = to_column(same(block), same(block))
    block = gram_f.at[own_quarter]
    plane_gf = to_plane(same(block), same(block))
    block = gram_o.at[own_quarter, own_cols]
    plane_go = to_plane(same(block), same(block))
    quad = [z - matrix + lax.rem(matrix + hop, 4) for hop in range(1, 4)]

    def hand_back(kind):
        spread = [
            copies.remote(
                send_w.at[kind, there],
                all_w.at[kind, matrix, own_small, own_cols],
                (lax.axis_index("wide"), there),
            )
            for there in quad
        ]
        block = all_w.at[kind, :, own_small, own_cols]
        plane = to_plane(same(block), same(block))
        block = all_w.at[kind, :, :, own_cols]
        return spread, plane, [copies.remote(block, block, here.mate)]

    spread_g, plane_g, mate_g = hand_back(0)
    spread_s, plane_s, mate_s = hand_back(1)
    block = gram_o.at[:, own_cols]
    mate_go = [copies.remote(block, block, here.mate)]
    block = out_f.at[1, core]
    mate_x = [copies.remote(block, block, here.mate)]
    write_f = [copies.local(out_f.at[0], grad_ffn), copies.local(out_f.at[1], step_ffn)]
    write_o = [copies.local(all_o, grad_attn.at[4]), copies.local(step_o, step_attn.at[4])]
    write_w = [
        copies.local(all_w.at[0], grad_attn.at[pl.ds(0, 4)]),
        copies.local(all_w.at[1], step_attn.at[pl.ds(0, 4)]),
    ]
    sent = []

    def start(group):
        for copy in group:
            copy.start()
        sent.extend(group)

    def arrive(group):
        for copy in group:
            copy.wait_recv()

    def begin(group):
        for copy in group:
            copy.start()

    start(z_sum)
    begin([keep_f, keep_o])
    ln_now[...] = jnp.zeros_like(ln_now)
    ln_now[0:2, :] = ln_one_ref[...]
    ln_now[2:4, :] = ln_two_ref[...]
    over_groups(ln_now, 2)
    start(mate_ln)
    grad_f, grad_o = take_f()
    all_f[own_quarter, :] = grad_f
    all_o[own_small, own_cols] = grad_o
    start(plane_f)

    keep_f.wait()
    arrive(plane_f)
    start(mate_o)
    grad = all_f[...].T
    out_f[0, core] = grad
    start(mate_f)
    moment_f[...] = (momentum_keep * mom_f[...] + grad.astype(wide_type)).astype(low_type)
    cut_gf[...] = dot_tn(moment_f[:, own_quarter], moment_f[...]).astype(low_type)
    start(z_gf)

    keep_o.wait()
    arrive(mate_o)
    moment = momentum_keep * mom_o[...] + all_o[...].astype(wide_type)
    moment_o[...] = moment.astype(low_type)
    cut_go[...] = dot_tn(moment_o[:, own_quarter], moment_o[:, own_cols]).astype(low_type)
    start(z_go)

    arrive(z_sum)
    total = wide_sum([wsum_ref[matrix]] + [col_w[i] for i in column])
    grad_w[own_quarter, own_cols] = total.astype(low_type)
    start(plane_w)
    arrive(mate_ln)
    mate_ln[0].wait_send()
    ln_now[...] = ln_now[...] + ln_mate[...]
    start(plane_ln)

    arrive(z_gf)
    total = wide_sum([cut_gf[blocks_at(z, strip), :]] + [col_gf[i] for i in column])
    strips_gf[blocks_at(z, strip), :] = total.astype(low_type)
    start(z_back_f)
    arrive(z_go)
    total = wide_sum([cut_go[blocks_at(z, strip), :]] + [col_go[i] for i in column])
    strips_go[blocks_at(z, strip), :] = total.astype(low_type)
    start(z_back_o)

    arrive(plane_w)
    start(mate_w)
    arrive(plane_ln)
    for copy in plane_ln:
        copy.wait_send()
    ln_now[...] = ln_now[...] + ln_chips[0] + ln_chips[1] + ln_chips[2]
    start(z_ln)

    def small_rows(there):
        return pl.ds(pl.multiple_of(there * rows + chip * small, small), small)

    arrive(mate_w)
    for there in range(narrow):
        send_w[0, there] = grad_w[small_rows(there), own_cols]
    start(spread_g)
    all_w[0, matrix, own_small, own_cols] = send_w[0, z]
    moment = momentum_keep * mom_w_ref[...].astype(wide_type) + grad_w[...].astype(wide_type)
    moment_w[...] = moment.astype(low_type)
    gram = dot_tn(moment_w[...], moment_w[...])
    arrive(z_back_f)
    gram_f[own_quarter, :] = strips_gf[...]
    start(plane_gf)
    arrive(z_back_o)
    gram_o[own_quarter, own_cols] = strips_go[...]
    start(plane_go)

    poly_w[...] = newton_poly(gram).astype(low_type)
    picked = jnp.concatenate([moment_w[small_rows(there), :] for there in range(narrow)], axis=0)
    ortho = dot_nn(picked, poly_w[:, own_cols]).astype(low_type)
    for there in range(narrow):
        send_w[1, there] = ortho[there * small : (there + 1) * small, :]
    start(spread_s)
    all_w[1, matrix, own_small, own_cols] = send_w[1, z]
    arrive(spread_g)
    start(plane_g)

    arrive(plane_gf)
    poly = newton_poly(gram_f[...].astype(wide_type)).astype(low_type)
    out_f[1, core] = dot_nn(moment_f[...], poly).astype(low_type)
    start(mate_x)
    arrive(spread_s)
    start(plane_s)
    arrive(plane_go)
    start(mate_go)
    arrive(plane_g)
    start(mate_g)
    arrive(mate_go)
    poly = newton_poly(gram_o[...].astype(wide_type)).astype(low_type)
    step_o[...] = dot_nn(moment_o[...], poly).astype(low_type)
    arrive(plane_s)
    start(mate_s)
    begin(write_o)
    arrive(mate_f)
    arrive(mate_x)
    begin(write_f)
    arrive(z_ln)
    total = ln_now[...]
    for i in column:
        total = total + ln_column[i]
    ln_ref[...] = total
    arrive(mate_g)
    begin(write_w[:1])
    arrive(mate_s)
    begin(write_w[1:])
    for copy in write_o + write_f + write_w:
        copy.wait()
    settled = [id(copy) for copy in mate_ln + plane_ln]
    for copy in sent:
        if id(copy) not in settled:
            copy.wait_send()


def back_kernel(*refs, narrow, chunks, sets):
    blocks = list(refs[:9])
    xc_ref, x_ref, w_ref, ln_ref, gffn_hbm, go_hbm, mom_hbm, mom_f_hbm, ln_two_ref = refs[9:18]
    dz_ref, grad_attn, step_attn, grad_ffn, step_ffn, ln_sum_ref = refs[18:24]
    state, carry, dq_all, dk_all, dv_all, de_all, first_t = refs[24:31]
    own_f, got_f, far_f, col_f, own_o, got_o, cut_o, far_o, col_o = refs[31:40]
    low_f, low_o, mom_own, mom_low, mom_all = refs[40:45]
    grad_w, got_w, half_w, far_w, staged, gln_ref, wsum_ref = refs[45:52]
    sums = refs[52:54]
    group_w, group_f, group_o, group_ln = refs[54:58]
    *update_refs, sems = refs[58:]
    step = pl.program_id(0)
    steps = pl.num_programs(0)
    here = Place(narrow)
    copies = Copies(sems)
    half = D // 2
    part = D // 4
    rows = D // narrow
    ffn_rows = FF // narrow
    column = range(narrow - 1)
    own_cols = blocks_at(here.core, half)
    mate_cols = blocks_at(here.other, half)
    grads = (dq_all, dk_all, dv_all, de_all)
    w = lax.axis_index("wide")
    peers = [(lax.rem(w + 8 * at, 8 * sets), here.z) for at in range(1, sets)]

    keep_f = copies.local(gffn_hbm.at[here.core], own_f)
    keep_o = copies.local(go_hbm.at[:, own_cols], own_o)
    keep_mom = copies.local(mom_hbm.at[pl.ds(0, 4)], mom_own)
    pieces = [blocks_at(there, part) for there in here.chip_at + [here.chip]]
    mate_f = [
        copies.remote(gffn_hbm.at[here.other, piece], got_f.at[piece], here.mate)
        for piece in pieces
    ]
    mate_o = copies.remote(go_hbm.at[:, mate_cols], got_o, here.mate)
    plane_f = [
        copies.remote(own_f.at[pieces[hop]], far_f.at[hop], here.chips[hop]) for hop in range(3)
    ]
    plane_o = [
        copies.remote(cut_o.at[:, here.chip_at[hop]], far_o.at[hop], here.chips[hop])
        for hop in range(3)
    ]
    z_sum = []
    for i in column:
        there = here.column_z[i]
        z_sum.append(
            copies.remote(low_f.at[:, blocks_at(there, ffn_rows)], col_f.at[i], here.column[i])
        )
        z_sum.append(copies.remote(low_o.at[there], col_o.at[i], here.column[i]))
    z_mom = [
        copies.remote(
            mom_low.at[lax.rem(here.column_z[i], 4), :, own_cols],
            mom_all.at[blocks_at(here.z, rows), own_cols],
            here.column[i],
        )
        for i in column
    ]
    mate_mom = copies.remote(mom_all.at[:, own_cols], mom_all.at[:, own_cols], here.mate)
    mate_w = [
        copies.remote(grad_w.at[m, :, mate_cols], got_w.at[m], here.mate) for m in range(4)
    ]
    plane_w = [
        [
            copies.remote(
                half_w.at[m, blocks_at(here.chip_at[hop], part)],
                far_w.at[hop, m],
                here.chips[hop],
            )
            for hop in range(3)
        ]
        for m in range(4)
    ]

    def gradient(m):
        total = dot_nn(first_t[...], grads[m][...].reshape(-1, D))
        grad_w[m] = total.astype(low_type)
        mate_w[m].start()

    def over_cores(m):
        mate_w[m].wait()
        half_w[m] = wide_sum([grad_w[m, :, own_cols], got_w[m]]).astype(low_type)
        for copy in plane_w[m]:
            copy.start()

    def over_chips(m):
        for copy in plane_w[m]:
            copy.wait()
        mine = half_w[m, blocks_at(here.chip, part), :]
        wsum_ref[m] = wide_sum([mine] + [far_w[hop, m] for hop in range(3)]).astype(low_type)

    @pl.when(step == 0)
    def _():
        state[...] = jnp.zeros_like(state)
        carry[...] = jnp.zeros_like(carry)
        gln_ref[...] = jnp.zeros_like(gln_ref)
        greet(here.column + here.chips + [here.mate] + peers)
        for copy in [keep_f] + mate_f + [keep_o, mate_o, keep_mom]:
            copy.start()

    @pl.when(step == 1)
    def _():
        keep_mom.wait()
        mom_low[...] = mom_own[...].astype(low_type)
        for copy in z_mom:
            copy.start()
        mom_all[blocks_at(here.z, rows), own_cols] = mom_low[lax.rem(here.z, 4), :, own_cols]

    def piece_sum(at):
        mate_f[at].wait()
        piece = pieces[at]
        own_f[piece, :] = wide_sum([own_f[piece, :], got_f[piece, :]]).astype(low_type)
        if at < 3:
            plane_f[at].start()

    @pl.when(step == 1)
    def _():
        keep_f.wait()
        for at in range(2):
            piece_sum(at)

    @pl.when(step == 2)
    def _():
        for at in range(2, 4):
            piece_sum(at)
        keep_o.wait()
        mate_o.wait()
        cut_o[...] = wide_sum([own_o[...], got_o[...]]).astype(low_type).reshape(cut_o.shape)
        for copy in plane_o:
            copy.start()

    @pl.when(step < chunks)
    def _():
        chunk = chunks - 1 - step
        seqs = xc_ref.shape[0]

        for seq in range(seqs):
            normed, _ = normalize(xc_ref[seq].astype(wide_type))
            first = (normed * ln_ref[0:1, :] + ln_ref[1:2, :]).astype(low_type)
            first_t[:, blocks_at(chunk * seqs + seq, CHUNK)] = first.T
        attend_back_chunk(blocks + [staged.at[place] for place in range(4)], state, carry)
        for place in range(4):
            grads[place][chunk] = staged[place]

    @pl.when(step == chunks)
    def _():
        gradient(0)
        gradient(1)
        gradient(2)
        over_cores(0)
        over_cores(1)
        for copy in plane_f + plane_o:
            copy.wait()
        mine = own_f[blocks_at(here.chip, part), :]
        low_f[...] = wide_sum([mine] + [far_f[hop] for hop in range(3)]).astype(low_type)
        mine = cut_o[:, here.chip]
        low_o[...] = wide_sum([mine] + [far_o[hop] for hop in range(3)]).astype(low_type)
        for copy in z_sum:
            copy.start()
        gradient(3)
        over_cores(2)
        over_cores(3)
        for copy in z_mom:
            copy.wait_recv()
        mate_mom.start()

    @pl.when(step >= chunks)
    def _():
        per = chunks // 4
        seqs = x_ref.shape[0]
        parts = [item[pl.ds((step - chunks) * per, per)].reshape(-1, D) for item in grads]
        dfirst = dot_nt(parts[0], w_ref[0])
        for place in range(1, 4):
            dfirst = dfirst + dot_nt(parts[place], w_ref[place])
        spans = [slice(at * CHUNK, (at + 1) * CHUNK) for at in range(per)]
        rows_in = [x_ref[:, span, :].reshape(-1, D) for span in spans]
        normed, inverse = normalize(jnp.concatenate(rows_in, axis=0).astype(wide_type))
        gln_ref[0:1, :] += jnp.sum(dfirst * normed, axis=0, keepdims=True)
        gln_ref[1:2, :] += jnp.sum(dfirst, axis=0, keepdims=True)
        dz = norm_back(dfirst, normed, inverse, ln_ref[0:1, :]).astype(low_type)
        for at, span in enumerate(spans):
            size = seqs * CHUNK
            dz_ref[:, span, :] = dz[at * size : (at + 1) * size].reshape(seqs, CHUNK, D)

    def over_groups(ref, number):
        if sets == 1:
            return
        slots = (group_w, group_f, group_ln, group_o)[number]
        exchange = [
            copies.remote(ref, slots.at[at], peer) for at, peer in enumerate(peers)
        ]
        for copy in exchange:
            copy.start()
        for copy in exchange:
            copy.wait()
        total = wide_sum([ref[...]] + [slots[at] for at in range(len(peers))])
        ref[...] = total.astype(ref.dtype)

    def take_f():
        for copy in z_sum:
            copy.wait()
        sum_f, sum_o = sums
        mine = low_f[:, blocks_at(here.z, ffn_rows)]
        sum_f[...] = wide_sum([mine] + [col_f[i] for i in column]).astype(low_type)
        sum_o[...] = wide_sum([low_o[here.z]] + [col_o[i] for i in column]).astype(low_type)
        over_groups(sum_f, 1)
        over_groups(sum_o, 3)
        return sum_f[...], sum_o[...]

    @pl.when(step == steps - 1)
    def _():
        for m in range(4):
            over_chips(m)
        over_groups(wsum_ref, 0)
        mate_mom.wait()
        for copy in z_mom:
            copy.wait_send()
        update_body(
            wsum_ref,
            take_f,
            mom_all,
            mom_hbm,
            mom_f_hbm,
            gln_ref,
            ln_two_ref,
            grad_attn,
            step_attn,
            grad_ffn,
            step_ffn,
            ln_sum_ref,
            *update_refs,
            narrow=narrow,
            here=here,
            copies=copies,
            over_groups=over_groups,
        )


def back(q, k, v, a, share, logit, before, datt, states, tokens, in_w, ln_params, gffn, go, mom, mom_f, ln_two):
    seqs, length, _ = q.shape
    chunks = length // CHUNK
    narrow = lax.axis_size("narrow")
    small, half, part = D // narrow // 4, D // 2, D // 4
    ffn_rows = FF // narrow

    def chunk_at(i):
        return jnp.maximum(chunks - 1 - i, 0)

    def rows_at(i):
        return (0, jnp.maximum(i - chunks, 0), 0)

    def whole(*shape):
        return pl.BlockSpec(shape, lambda i: (0,) * len(shape))

    block = pl.BlockSpec((seqs, CHUNK, D), lambda i: (0, chunk_at(i), 0))
    row_spec = pl.BlockSpec((seqs, length // 4, D), rows_at)
    any_spec = pl.BlockSpec(memory_space=pl.ANY)
    rows, strip, column = D // narrow, part // narrow, narrow - 1
    sets = lax.axis_size("wide") // 8
    spare = max(sets - 1, 1)
    outs = [(5, rows, D), (5, rows, D), (2, ffn_rows, D), (2, ffn_rows, D)]

    def full(*shape):
        return pltpu.VMEM(shape, wide_type)

    def low(*shape):
        return pltpu.VMEM(shape, low_type)

    return pl.pallas_call(
        functools.partial(back_kernel, narrow=narrow, chunks=chunks, sets=sets),
        grid=(chunks + 4,),
        in_specs=[block] * 6
        + [
            pl.BlockSpec((1, seqs, 1, D), lambda i: (chunk_at(i), 0, 0, 0)),
            block,
            pl.BlockSpec((1, seqs, PAIRS, PAIR, 2 * PAIR), lambda i: (chunk_at(i), 0, 0, 0, 0)),
            block,
            row_spec,
            whole(4, D, D),
            whole(4, D),
            any_spec,
            any_spec,
            any_spec,
            any_spec,
            whole(2, D),
        ],
        out_specs=[row_spec] + [any_spec] * 4 + [whole(8, D)],
        out_shape=[jax.ShapeDtypeStruct(q.shape, low_type)]
        + [jax.ShapeDtypeStruct(shape, low_type) for shape in outs]
        + [jax.ShapeDtypeStruct((8, D), wide_type)],
        scratch_shapes=[
            pltpu.VMEM((seqs, PAIRS, PAIR, 2 * PAIR), wide_type),
            pltpu.VMEM((seqs, 1, D), wide_type),
            low(chunks, seqs, CHUNK, D),
            low(chunks, seqs, CHUNK, D),
            low(chunks, seqs, CHUNK, D),
            low(chunks, seqs, CHUNK, D),
            low(D, seqs * length),
            low(D, FF),
            low(D, FF),
            low(3, part, FF),
            low(narrow - 1, part, ffn_rows),
            low(D, half),
            low(D, half),
            low(narrow, 4, small, half),
            low(3, narrow, small, half),
            low(narrow - 1, small, half),
            low(part, FF),
            low(narrow, small, half),
            pltpu.VMEM((4, D // narrow, D), wide_type),
            low(4, D // narrow, D),
            low(D, D),
            low(4, D, D),
            low(4, D, half),
            low(4, D, half),
            low(3, 4, part, half),
            low(4, seqs, CHUNK, D),
            full(2, D),
            low(4, part, half),
            low(part, ffn_rows),
            low(small, half),
            low(spare, 4, part, half),
            low(spare, part, ffn_rows),
            low(spare, small, half),
            full(spare, 8, D),
            full(8, D),
            full(8, D),
            full(3, 8, D),
            full(column, 8, D),
            low(column, part, half),
            low(D, D),
            low(D, D),
            low(D, D),
            low(2, narrow, small, half),
            low(2, 4, rows, D),
            low(D, ffn_rows),
            full(ffn_rows, D),
            full(rows, D),
            low(ffn_rows, D),
            low(2, 2, ffn_rows, D),
            low(rows, D),
            low(rows, D),
            low(rows, D),
            low(part, D),
            low(column, strip, D),
            low(part, D),
            low(D, D),
            low(part, half),
            low(column, strip, half),
            low(part, half),
            low(D, D),
            pltpu.SemaphoreType.DMA((11 + 2 * (65 + 9 * column + 4 * spare),)),
        ],
        compiler_params=pltpu.CompilerParams(
            vmem_limit_bytes=VMEM_BYTES, collective_id=1, has_side_effects=True
        ),
        name="back",
    )(
        q,
        k,
        v,
        a,
        share,
        logit,
        before,
        datt,
        states,
        tokens,
        tokens,
        in_w,
        ln_params,
        gffn,
        go,
        mom,
        mom_f,
        ln_two,
    )


def shards(
    tokens,
    out_grad,
    group_ids,
    domain_weight,
    attn_w,
    ffn_w,
    attn_mom,
    ffn_mom,
    ln_params,
    ln_first,
    ln_second,
):
    local_seqs, length, _ = tokens.shape
    token_count = local_seqs * length
    rows = tokens.reshape(token_count, D)
    head = (local_seqs, length, D)
    q, k, v, a, att, share, logit, before, states, weights, in_w, out_w, ffn_low = forward(
        tokens, group_ids, domain_weight, ln_params, attn_w, ffn_w
    )
    output, dx, datt, gffn, go, ln_two = feed(
        group_ids,
        weights,
        rows,
        att.reshape(token_count, D),
        out_grad.reshape(token_count, D),
        out_w,
        ffn_low,
        ln_params,
        length,
    )
    dz, attn_grad, attn_step, ffn_grad, ffn_step, ln_sum = back(
        q,
        k,
        v,
        a,
        share,
        logit,
        before,
        datt.reshape(head),
        states,
        tokens,
        in_w,
        ln_params,
        gffn,
        go,
        attn_mom,
        ffn_mom,
        ln_two,
    )

    def flat(*items):
        return [item.reshape(-1, D) for item in items]

    results = finish(
        dx,
        dz.reshape(token_count, D),
        flat(attn_grad, attn_step, attn_w, attn_mom),
        flat(ffn_grad, ffn_step, ffn_w, ffn_mom),
        (ln_params, ln_first, ln_second, ln_sum),
    )
    input_grad, ga, ma, wa, ca, gf, mf, wf, cf, ln_grad, first_new, second_new, ln_new = results
    attn, ffn = attn_w.shape, ffn_w.shape
    return (
        output.reshape(tokens.shape),
        input_grad.reshape(tokens.shape),
        ga.reshape(attn),
        gf.reshape(ffn),
        ln_grad,
        ma.reshape(attn),
        mf.reshape(ffn),
        wa.reshape(attn),
        wf.reshape(ffn),
        ca.reshape(attn),
        cf.reshape(ffn),
        first_new,
        second_new,
        ln_new,
    )


def solution(mesh):
    split = P(("wide", "narrow"), None, None)
    rows = P(None, "narrow", None)
    lanes = P(None, "narrow")
    inner = jax.shard_map(
        shards,
        mesh=mesh,
        in_specs=(
            split,
            split,
            P(("wide", "narrow")),
            P(),
            rows,
            rows,
            rows,
            rows,
            P(),
            lanes,
            lanes,
        ),
        out_specs=(
            split,
            split,
            rows,
            rows,
            lanes,
            rows,
            rows,
            rows,
            rows,
            rows,
            rows,
            lanes,
            lanes,
            lanes,
        ),
        check_vma=False,
    )
    return inner
```

```python
import functools
import math

import jax
import jax.numpy as jnp
from jax import lax
from jax.experimental import pallas as pl
from jax.experimental.pallas import tpu as pltpu
from jax.sharding import PartitionSpec as P

D = 512
HEADS = 8
HEAD_DIM = 64
FF = 2048
STEP = 10

norm_epsilon = 1e-05
momentum_keep = 0.5
quintic_lin = 3.4445
quintic_cube = -4.775
quintic_five = 2.0315
muon_rate = 0.7
muon_decay = 0.1
adam_rate = 0.2
beta_first = 0.9
beta_second = 0.999
adam_epsilon = 1e-08

CHUNK = 128
PAIR = 2 * HEAD_DIM
PAIRS = HEADS // 2
VMEM_BYTES = 60 * 1024 * 1024
low_type = jnp.bfloat16
wide_type = jnp.float32


def dot_nn(left, right):
    return lax.dot_general(left, right, (((1,), (0,)), ((), ())), preferred_element_type=wide_type)


def dot_nt(left, right):
    return lax.dot_general(left, right, (((1,), (1,)), ((), ())), preferred_element_type=wide_type)


def dot_tn(left, right):
    return lax.dot_general(left, right, (((0,), (0,)), ((), ())), preferred_element_type=wide_type)


def normalize(rows):
    center = rows - jnp.mean(rows, axis=-1, keepdims=True)
    spread = jnp.mean(center * center, axis=-1, keepdims=True)
    inverse = lax.rsqrt(spread + norm_epsilon)
    return center * inverse, inverse


def norm_back(grad_rows, normed, inverse, gain):
    grad_normed = grad_rows * gain
    mean_grad = jnp.mean(grad_normed, axis=-1, keepdims=True)
    mean_cross = jnp.mean(grad_normed * normed, axis=-1, keepdims=True)
    return inverse * (grad_normed - mean_grad - normed * mean_cross)


def lane_of(shape):
    return lax.broadcasted_iota(jnp.int32, shape, 1)


def row_of(shape):
    return lax.broadcasted_iota(jnp.int32, shape, 0)


def split_pair(pair, first_head):
    zero = jnp.zeros_like(pair)
    return jnp.concatenate(
        [jnp.where(first_head, pair, zero), jnp.where(first_head, zero, pair)], axis=0
    )


def head_reduce(values, first_head, op, neutral):
    left = op(jnp.where(first_head, values, neutral), axis=-1, keepdims=True)
    right = op(jnp.where(first_head, neutral, values), axis=-1, keepdims=True)
    return jnp.where(first_head, left, right)


def attend_back_chunk(refs, state, carry):
    (
        q_ref,
        k_ref,
        v_ref,
        a_ref,
        share_ref,
        logit_ref,
        before_ref,
        datt_ref,
        state_ref,
        dq_ref,
        dk_ref,
        dv_ref,
        de_ref,
    ) = refs
    scaling = HEAD_DIM**-0.5
    first_head = lane_of((CHUNK, PAIR)) < HEAD_DIM
    causal = row_of((CHUNK, 2 * CHUNK)) >= lane_of((CHUNK, 2 * CHUNK)) % CHUNK
    anti = row_of((CHUNK, 2 * CHUNK)) <= lane_of((CHUNK, 2 * CHUNK)) % CHUNK
    same_head = (row_of((PAIR, 2 * PAIR)) // HEAD_DIM) == (
        (lane_of((PAIR, 2 * PAIR)) // HEAD_DIM) % 2
    )
    lower = (row_of((CHUNK, CHUNK)) >= lane_of((CHUNK, CHUNK))).astype(low_type)
    upper = (row_of((CHUNK, CHUNK)) <= lane_of((CHUNK, CHUNK))).astype(low_type)

    def masked(mask, raw):
        return jnp.where(mask, raw, 0.0).astype(low_type)

    items = []
    for seq in range(q_ref.shape[0]):
        total = dot_nn(lower, a_ref[seq]) + before_ref[0, seq]
        inv = 1.0 / total
        for pair in range(PAIRS):
            lanes = slice(pair * PAIR, (pair + 1) * PAIR)
            items.append(
                dict(seq=seq, pair=pair, lanes=lanes, total=total[:, lanes], inv=inv[:, lanes])
            )

    def load(t):
        seq, lanes = t["seq"], t["lanes"]
        t["k"] = k_ref[seq, :, lanes]
        t["v"] = v_ref[seq, :, lanes]
        t["a"] = a_ref[seq, :, lanes]
        t["share"] = share_ref[seq, :, lanes]
        t["datt"] = datt_ref[seq, :, lanes]
        t["q"] = q_ref[seq, :, lanes] * low_type(scaling)
        t["before"] = state_ref[0, seq, t["pair"]]
        t["after"] = jnp.where(same_head, state[seq, t["pair"]], 0.0).astype(low_type)
        t["v_two"] = split_pair(t["v"], first_head)
        t["a_two"] = split_pair(t["a"], first_head)
        t["dmix"] = masked(causal, dot_nt(t["datt"], t["v_two"]))

    def gather(t):
        t["share_two"] = split_pair(t["share"], first_head)
        t["datt_two"] = split_pair(t["datt"], first_head)
        t["dshare"] = dot_nn(t["dmix"], t["a_two"]) + dot_nt(t["datt"], t["before"][:, PAIR:])

    def soften(t):
        logit = logit_ref[t["seq"], :, t["lanes"]].astype(wide_type)
        prob = t["share"].astype(wide_type) * t["total"]
        cross = t["dshare"] * t["inv"] * prob
        dlogit = cross - prob * head_reduce(cross, first_head, jnp.sum, 0.0)
        t["dnumer"] = (dlogit * t["inv"]).astype(low_type)
        t["dtotal"] = -(cross + dlogit * logit) * t["inv"]
        t["mix_t"] = masked(anti, dot_nt(t["a"], t["share_two"]))
        t["dmix_t"] = masked(anti, dot_nt(t["v"], t["datt_two"]))

    def blend(t):
        t["dnumer_two"] = split_pair(t["dnumer"], first_head)
        t["dscores"] = masked(causal, dot_nt(t["dnumer"], t["a_two"]))
        t["dscores_t"] = masked(anti, dot_nt(t["a"], t["dnumer_two"]))
        t["k_two"] = split_pair(t["k"], first_head)
        t["q_two"] = split_pair(t["q"], first_head)
        t["scores_t"] = masked(anti, dot_nt(t["k"], t["q_two"]))
        t["later"] = dot_nn(t["a"], t["after"])

    def finish(t):
        seq, lanes = t["seq"], t["lanes"]
        dq = dot_nn(t["dscores"], t["k_two"]) + dot_nn(t["dnumer"], t["before"][:, :PAIR])
        dq_ref[seq, :, lanes] = (dq * scaling).astype(low_type)
        dv = dot_nn(t["mix_t"], t["datt_two"]) + t["later"][:, PAIR:]
        dv_ref[seq, :, lanes] = dv.astype(low_type)
        dk = dot_nn(t["dscores_t"], t["q_two"]) + t["later"][:, :PAIR]
        dk_ref[seq, :, lanes] = dk.astype(low_type)
        high = t["dtotal"].astype(low_type)
        rest = (t["dtotal"] - high.astype(wide_type)).astype(low_type)
        tail = dot_nn(upper, high) + dot_nn(upper, rest) + carry[seq, :, lanes]
        carry[seq, :, lanes] = tail[0:1, :]
        da = dot_nn(t["dmix_t"], t["share_two"]) + dot_nn(t["scores_t"], t["dnumer_two"])
        da = da + dot_nt(jnp.concatenate([t["k"], t["v"]], axis=1), t["after"]) + tail
        de = da.astype(low_type).astype(wide_type) * t["a"].astype(wide_type)
        de_ref[seq, :, lanes] = de.astype(low_type)
        state[seq, t["pair"], :, :PAIR] += dot_tn(t["dnumer"], t["q"])
        state[seq, t["pair"], :, PAIR:] += dot_tn(t["share"], t["datt"])

    for stage in (load, gather, soften, blend, finish):
        for item in items:
            stage(item)


FF_BLOCK = 256
gelu_root = math.sqrt(2.0 / math.pi)
gelu_cube = 0.044715


def feed_kernel(
    ids_ref,
    weight_ref,
    x_ref,
    att_ref,
    og_ref,
    wo_ref,
    ffn_ref,
    ln_ref,
    out_ref,
    dx_ref,
    datt_ref,
    gffn_ref,
    go_ref,
    gln_ref,
    up_sum,
    down_sum,
    o_sum,
    hidden,
    dinner,
    *,
    per_seq,
):
    step = pl.program_id(0)

    @pl.when(step == 0)
    def _():
        up_sum[...] = jnp.zeros_like(up_sum)
        down_sum[...] = jnp.zeros_like(down_sum)
        o_sum[...] = jnp.zeros_like(o_sum)
        gln_ref[...] = jnp.zeros_like(gln_ref)

    att = att_ref[...]
    mixed = x_ref[...].astype(wide_type) + dot_nn(att, wo_ref[...])
    normed, inverse = normalize(mixed)
    second = (normed * ln_ref[2:3, :] + ln_ref[3:4, :]).astype(low_type)
    mine = lane_of((1, LANES)) == ids_ref[step // per_seq]
    weight = jnp.sum(jnp.where(mine, weight_ref[0:1, :], 0.0), axis=1, keepdims=True)
    dout = og_ref[...].astype(wide_type) * weight
    dy = dout.astype(low_type)
    second_t = second.T
    dy_t = dy.T
    parts = [slice(part * FF_BLOCK, (part + 1) * FF_BLOCK) for part in range(FF // FF_BLOCK)]

    def open_part(part):
        return dot_nt(second, ffn_ref[0, part, :]), dot_nt(dy, ffn_ref[1, part, :])

    ahead = open_part(parts[0])
    for place, part in enumerate(parts):
        inner, dhidden = ahead
        if place + 1 < len(parts):
            ahead = open_part(parts[place + 1])
        square = inner * inner
        bend = jnp.tanh(inner * (gelu_root + (gelu_root * gelu_cube) * square))
        half = 0.5 + 0.5 * bend
        hidden[:, part] = (inner * half).astype(low_type)
        slope = half + (0.5 * inner) * (1.0 - bend * bend) * (
            gelu_root + (3.0 * gelu_root * gelu_cube) * square
        )
        dinner[:, part] = (dhidden * slope).astype(low_type)
    result = mixed + dot_nn(hidden[...], ffn_ref[1])
    dsecond = dot_nn(dinner[...], ffn_ref[0])
    for part in parts:
        down_sum[:, part] += dot_nn(dy_t, hidden[:, part])
        up_sum[:, part] += dot_nn(second_t, dinner[:, part])
    out_ref[...] = result.astype(low_type)
    gln_ref[0:1, :] += jnp.sum(dsecond * normed, axis=0, keepdims=True)
    gln_ref[1:2, :] += jnp.sum(dsecond, axis=0, keepdims=True)
    dmixed = dout + norm_back(dsecond, normed, inverse, ln_ref[2:3, :])
    datt = dmixed.astype(low_type)
    dx_ref[...] = datt
    o_sum[...] += dot_tn(att, datt)
    datt_ref[...] = dot_nt(datt, wo_ref[...]).astype(low_type)

    @pl.when(step == pl.num_programs(0) - 1)
    def _():
        gffn_ref[0] = up_sum[...].astype(low_type)
        gffn_ref[1] = down_sum[...].astype(low_type)
        go_ref[...] = o_sum[...].astype(low_type)


def feed(ids, weights, rows, att, grad, wo, ffn, ln_params, length):
    count = rows.shape[0]
    block = 512
    row_spec = pl.BlockSpec((block, D), lambda i: (i, 0))

    def whole(*shape):
        return pl.BlockSpec(shape, lambda i: (0,) * len(shape))

    return pl.pallas_call(
        functools.partial(feed_kernel, per_seq=length // block),
        grid=(count // block,),
        in_specs=[
            pl.BlockSpec(memory_space=pltpu.SMEM),
            whole(8, LANES),
            row_spec,
            row_spec,
            row_spec,
            whole(D, D),
            whole(2, FF, D),
            whole(4, D),
        ],
        out_specs=[
            row_spec,
            row_spec,
            row_spec,
            whole(2, D, FF),
            whole(D, D),
            whole(2, D),
        ],
        out_shape=[
            jax.ShapeDtypeStruct((count, D), low_type),
            jax.ShapeDtypeStruct((count, D), low_type),
            jax.ShapeDtypeStruct((count, D), low_type),
            jax.ShapeDtypeStruct((2, D, FF), low_type),
            jax.ShapeDtypeStruct((D, D), low_type),
            jax.ShapeDtypeStruct((2, D), wide_type),
        ],
        scratch_shapes=[
            pltpu.VMEM((D, FF), wide_type),
            pltpu.VMEM((D, FF), wide_type),
            pltpu.VMEM((D, D), wide_type),
            pltpu.VMEM((block, FF), low_type),
            pltpu.VMEM((block, FF), low_type),
        ],
        compiler_params=pltpu.CompilerParams(vmem_limit_bytes=VMEM_BYTES),
        name="feed",
    )(ids, weights, rows, att, grad, wo, ffn, ln_params)


def finish_kernel(
    dx_ref,
    dz_ref,
    ga_ref,
    sa_ref,
    wa_ref,
    ma_ref,
    gf_ref,
    sf_ref,
    wf_ref,
    mf_ref,
    ln_ref,
    first_ref,
    second_ref,
    sum_ref,
    grad_ref,
    ga_out,
    ma_out,
    wa_out,
    ca_out,
    gf_out,
    mf_out,
    wf_out,
    cf_out,
    gl_out,
    first_out,
    second_out,
    ln_out,
):
    grad_ref[...] = dx_ref[...].astype(wide_type) + dz_ref[...].astype(wide_type)
    keep = 1.0 - muon_rate * muon_decay
    for refs, size in (
        ((ga_ref, sa_ref, wa_ref, ma_ref, ga_out, ma_out, wa_out, ca_out), D),
        ((gf_ref, sf_ref, wf_ref, mf_ref, gf_out, mf_out, wf_out, cf_out), FF),
    ):
        grad, ortho, weight, moment, grad_out, moment_out, weight_out, copy_out = refs
        grad = grad[...].astype(wide_type)
        grad_out[...] = grad
        moment_out[...] = momentum_keep * moment[...] + grad
        rate = muon_rate * 0.2 * math.sqrt(size)
        new = keep * weight[...] - rate * ortho[...].astype(wide_type)
        weight_out[...] = new
        copy_out[...] = new.astype(low_type)
    width = first_ref.shape[1]
    place = lax.axis_index("narrow")

    def own(ref):
        picked = jnp.zeros((4, width), wide_type)
        for at in range(D // width):
            picked = picked + jnp.where(place == at, ref[0:4, at * width : (at + 1) * width], 0.0)
        return picked

    grad = own(sum_ref)
    first = beta_first * first_ref[...] + (1.0 - beta_first) * grad
    second = beta_second * second_ref[...] + (1.0 - beta_second) * grad * grad
    gl_out[...] = grad
    first_out[...] = first
    second_out[...] = second
    first_fix = 1.0 - beta_first**STEP
    second_fix = 1.0 - beta_second**STEP
    ln_out[...] = own(ln_ref) - adam_rate * (first / first_fix) / (
        jnp.sqrt(second / second_fix) + adam_epsilon
    )


def finish(dx, dz, attn, ffn, ln):
    steps = 4

    def rows(item):
        block = item.shape[0] // steps
        return pl.BlockSpec((block, item.shape[1]), lambda i: (i, 0))

    def whole(item):
        return pl.BlockSpec(item.shape, lambda i: (0, 0))

    def outs(group):
        shape = group[0].shape
        return [jax.ShapeDtypeStruct(shape, wide_type)] * 3 + [
            jax.ShapeDtypeStruct(shape, low_type)
        ]

    row_items = [dx, dz] + list(attn) + list(ffn)
    row_outs = [jax.ShapeDtypeStruct(dx.shape, wide_type)] + outs(attn) + outs(ffn)
    ln_outs = [jax.ShapeDtypeStruct(ln[1].shape, wide_type)] * 4
    return pl.pallas_call(
        finish_kernel,
        grid=(steps,),
        in_specs=[rows(item) for item in row_items] + [whole(item) for item in ln],
        out_specs=[rows(item) for item in row_outs] + [whole(item) for item in ln_outs],
        out_shape=row_outs + ln_outs,
        compiler_params=pltpu.CompilerParams(vmem_limit_bytes=VMEM_BYTES),
        name="finish",
    )(*row_items, *ln)


MESH = pl.DeviceIdType.MESH
LANES = 128


def remote(src, dst, send_sem, recv_sem, device):
    return pltpu.make_async_remote_copy(
        src_ref=src,
        dst_ref=dst,
        send_sem=send_sem,
        recv_sem=recv_sem,
        device_id=device,
        device_id_type=MESH,
    )


def greet(devices):
    barrier = pltpu.get_barrier_semaphore()
    for device in devices:
        pl.semaphore_signal(barrier, inc=1, device_id=device, device_id_type=MESH)
    pl.semaphore_wait(barrier, len(devices))


def attend_chunks(source, refs, seqs, asides):
    att_ref, share_ref, logit_ref, before_ref, state_ref, state, carry = refs
    q_in, k_in, v_in, a_in = source
    first_head = lane_of((CHUNK, PAIR)) < HEAD_DIM
    causal = row_of((CHUNK, 2 * CHUNK)) >= lane_of((CHUNK, 2 * CHUNK)) % CHUNK
    same_head = (row_of((PAIR, 2 * PAIR)) // HEAD_DIM) == (
        (lane_of((PAIR, 2 * PAIR)) // HEAD_DIM) % 2
    )
    lower = (row_of((CHUNK, CHUNK)) >= lane_of((CHUNK, CHUNK))).astype(low_type)
    items = []
    for seq in range(seqs):
        part = slice(seq * CHUNK, (seq + 1) * CHUNK)
        before = carry[seq]
        before_ref[0, seq] = before
        total = dot_nn(lower, a_in[part, :]) + before
        carry[seq] = total[CHUNK - 1 :, :]
        inv = 1.0 / total
        for pair in range(PAIRS):
            lanes = slice(pair * PAIR, (pair + 1) * PAIR)
            items.append(
                dict(
                    seq=seq,
                    pair=pair,
                    lanes=lanes,
                    q=q_in[part, lanes] * low_type(HEAD_DIM**-0.5),
                    k=k_in[part, lanes],
                    v=v_in[part, lanes],
                    a=a_in[part, lanes],
                    inv=inv[:, lanes],
                )
            )

    def score(t):
        t["a_two"] = split_pair(t["a"], first_head)
        t["now"] = jnp.where(same_head, state[t["seq"], t["pair"]], 0.0).astype(low_type)
        state_ref[0, t["seq"], t["pair"]] = t["now"]
        raw = dot_nt(t["q"], split_pair(t["k"], first_head))
        t["scores"] = jnp.where(causal, raw, 0.0).astype(low_type)

    def gather(t):
        numer = dot_nn(t["scores"], t["a_two"]) + dot_nt(t["q"], t["now"][:, :PAIR])
        t["logit"] = numer * t["inv"]
        logit_ref[t["seq"], :, t["lanes"]] = t["logit"].astype(low_type)

    def soften(t):
        expo = jnp.exp(t["logit"] - head_reduce(t["logit"], first_head, jnp.max, -jnp.inf))
        share = expo * (t["inv"] / head_reduce(expo, first_head, jnp.sum, 0.0))
        t["share"] = share.astype(low_type)
        share_ref[t["seq"], :, t["lanes"]] = t["share"]

    def blend(t):
        raw = dot_nt(t["share"], t["a_two"])
        t["mix"] = jnp.where(causal, raw, 0.0).astype(low_type)

    def finish_item(t):
        att = dot_nn(t["mix"], split_pair(t["v"], first_head))
        att = att + dot_nn(t["share"], t["now"][:, PAIR:])
        att_ref[t["seq"], :, t["lanes"]] = att.astype(low_type)
        state[t["seq"], t["pair"]] += dot_tn(t["a"], jnp.concatenate([t["k"], t["v"]], axis=1))

    for stage, aside in zip((score, gather, soften, blend, finish_item), asides):
        for place, item in enumerate(items):
            stage(item)
            if place == len(items) // 2 - 1 and aside is not None:
                aside()


def forward_kernel(
    ids_ref,
    dw_ref,
    x_first_ref,
    x_ref,
    ln_ref,
    attn_hbm,
    ffn_w_hbm,
    q_ref,
    k_ref,
    v_ref,
    a_ref,
    att_ref,
    share_ref,
    logit_ref,
    before_ref,
    state_ref,
    weight_ref,
    in_hbm,
    out_hbm,
    ffn_hbm,
    state,
    carry,
    held,
    in_w,
    piece_ref,
    attn_ref,
    ffn_ref,
    own,
    own_ffn,
    counts,
    counts_z,
    counts_chip,
    counts_mate,
    sems,
    *,
    narrow,
    total_seqs,
    groups,
):
    step = pl.program_id(0)
    steps = pl.num_programs(0)
    seqs = x_ref.shape[0]
    here = Place(narrow)
    copies = Copies(sems)
    z, core, chip = here.z, here.core, here.chip
    rows = attn_ref.shape[1]
    ffn_rows = ffn_ref.shape[1]
    half = rows // 2
    bit = half // 2
    quarter = ffn_rows // 4
    small = rows // 4
    w = lax.axis_index("wide")
    column = range(narrow - 1)
    planes = range(3)
    rounds = range(1, narrow)
    cols = blocks_at(core, D // 2)

    def inside(shard):
        return jnp.clip(shard, 0, narrow - 1)

    def from_z(place):
        return lax.rem(z + narrow - here.hops[place], narrow)

    def in_rows(owner, part):
        return blocks_at(4 * owner + 2 * core + part, bit)

    in_z, in_chip, in_core = [], [], []
    for part in range(2):
        in_z.append(
            [
                copies.remote(
                    own.at[chip, blocks_at(2 * core + part, bit)],
                    in_w.at[chip, in_rows(z, part)],
                    here.column[i],
                )
                for i in column
            ]
        )
        blocks = [in_w.at[chip, in_rows(from_z(i), part)] for i in column]
        in_chip.append(
            [[copies.remote(block, block, here.chips[p]) for p in planes] for block in blocks]
        )
        blocks = [in_w.at[:, in_rows(from_z(i), part)] for i in column]
        in_core.append([copies.remote(block, block, here.mate) for block in blocks])

    side = lax.rem(chip, 2)
    pieces = (side, 2 + chip // 2)
    beside = (w - 2 * chip + 2 * (chip + 1 - 2 * side), z)
    neighbours = (beside, here.chips[1])

    def ffn_block(shard, piece):
        return ffn_hbm.at[core, blocks_at(4 * shard + piece, quarter)]

    def out_block(shard):
        return out_hbm.at[blocks_at(4 * shard + chip, small), cols]

    def sends(way, turn):
        if way == 0:
            return jnp.logical_and(z < narrow - 1, z + 1 - turn >= 0)
        return jnp.logical_and(z > 0, z - 1 + turn <= narrow - 1)

    def gets(way, turn):
        return z - turn >= 0 if way == 0 else z + turn <= narrow - 1

    relay, spread, passed = {}, {}, {}
    for turn in rounds:
        for way in range(2):
            sign = 1 if way == 0 else -1
            there = (w, inside(z + sign))
            shard = inside(z + sign * (1 - turn))
            if turn == 1:
                sources = [own_ffn.at[core, blocks_at(piece, quarter)] for piece in pieces]
                sources.append(own.at[4, blocks_at(chip, small), cols])
            else:
                sources = [ffn_block(shard, piece) for piece in pieces] + [out_block(shard)]
            targets = [ffn_block(shard, piece) for piece in pieces] + [out_block(shard)]
            relay[way, turn] = [
                copies.remote(src, dst, there) for src, dst in zip(sources, targets)
            ]
            got = inside(z - sign * turn)
            spread[way, turn] = []
            for piece, device in zip(pieces, neighbours):
                block = ffn_block(got, piece)
                spread[way, turn].append(copies.remote(block, block, device))
            block = out_block(got)
            spread[way, turn] += [copies.remote(block, block, here.chips[p]) for p in planes]
            passed[way, turn] = [
                copies.remote(block, block, here.mate)
                for block in (
                    ffn_hbm.at[core, blocks_at(got, ffn_rows)],
                    out_hbm.at[blocks_at(got, rows), cols],
                )
            ]

    def relay_send(turn):
        for way in range(2):

            @pl.when(sends(way, turn))
            def _():
                for copy in relay[way, turn]:
                    copy.start()

    def relay_get(turn):
        for way in range(2):

            @pl.when(gets(way, turn))
            def _():
                for copy in relay[way, turn]:
                    copy.wait_recv()
                for copy in spread[way, turn]:
                    copy.start()

        if turn + 1 < narrow:
            relay_send(turn + 1)

    def pass_on(turn):
        for way in range(2):

            @pl.when(gets(way, turn))
            def _():
                for copy in spread[way, turn]:
                    copy.wait_recv()
                for copy in passed[way, turn]:
                    copy.start()

    count_z = [copies.remote(counts, counts_z.at[i], here.column[i]) for i in column]
    count_chip = [copies.remote(counts, counts_chip.at[p], here.chips[p]) for p in planes]
    count_mate = copies.remote(counts, counts_mate, here.mate)
    load_piece = copies.local(attn_hbm.at[chip, blocks_at(core, half)], piece_ref)
    load_attn = copies.local(attn_hbm, attn_ref)
    load_ffn = copies.local(ffn_w_hbm, ffn_ref)
    keep_ffn = copies.local(own_ffn, ffn_hbm.at[:, blocks_at(z, ffn_rows)])
    keep_out = copies.local(own.at[4], out_hbm.at[blocks_at(z, rows)])
    keep_in = copies.local(in_w, in_hbm)

    def normal(ref):
        normed, _ = normalize(ref[...].reshape(seqs * CHUNK, D).astype(wide_type))
        return (normed * ln_ref[0:1, :] + ln_ref[1:2, :]).astype(low_type)

    def product(first, place):
        out = dot_nn(first, in_w[place])
        held[place] = (jnp.exp(out) if place == 3 else out).astype(low_type)

    @pl.when(step == 0)
    def _():
        for copy in (load_piece, load_attn, load_ffn):
            copy.start()
        state[...] = jnp.zeros_like(state)
        carry[...] = jnp.zeros_like(carry)
        greet(here.column + here.chips + [here.mate])
        load_piece.wait()
        own[chip, blocks_at(core, half), :] = piece_ref[...].astype(low_type)
        for part in range(2):
            for i in column:
                in_z[part][i].start()
        load_attn.wait()
        load_ffn.wait()
        for place in range(4):
            in_w[place, blocks_at(z, rows), :] = attn_ref[place].astype(low_type)
        own[4] = attn_ref[4].astype(low_type)
        own_ffn[...] = ffn_ref[...].astype(low_type)
        lanes = lane_of((8, LANES))
        count = jnp.zeros((8, LANES), wide_type)
        for seq in range(ids_ref.shape[0]):
            count = count + (lanes == ids_ref[seq]).astype(wide_type)
        counts[...] = count
        for part in range(2):
            for i in column:
                in_z[part][i].wait_recv()
                for p in planes:
                    in_chip[part][i][p].start()
        relay_send(1)
        for copy in count_z:
            copy.start()
        keep_ffn.start()
        keep_out.start()
        for part in range(2):
            for i in column:
                for p in planes:
                    in_chip[part][i][p].wait_recv()
                in_core[part][i].start()
        relay_get(1)
        for part in range(2):
            for i in column:
                in_core[part][i].wait_recv()
        keep_in.start()
        first = normal(x_first_ref)
        for place in range(4):
            product(first, place)
        if narrow > 2:
            relay_get(2)

    for turn in range(3, narrow):

        @pl.when(step == turn - 1)
        def _():
            relay_get(turn)

    @pl.when(step == 1)
    def _():
        for copy in count_z:
            copy.wait()
        counts[...] = counts[...] + sum(counts_z[i] for i in column)
        for copy in count_chip:
            copy.start()

    @pl.when(step == 2)
    def _():
        for copy in count_chip:
            copy.wait()
        counts[...] = counts[...] + sum(counts_chip[p] for p in planes)
        count_mate.start()

    @pl.when(step == 3)
    def _():
        count_mate.wait()
        total = counts[...] + counts_mate[...]
        lanes = lane_of((8, LANES))
        values = jnp.zeros((8, LANES), wide_type)
        for group in range(groups):
            values = values + jnp.where(lanes == group, dw_ref[group], 0.0)
        weight_ref[...] = values * total_seqs / (groups * jnp.maximum(total, 1.0))

    for turn in rounds:

        @pl.when(step == jnp.minimum(steps - 1, turn + 4))
        def _():
            pass_on(turn)

    source = [held[place] for place in range(4)]
    for ref, item in zip((q_ref, k_ref, v_ref, a_ref), source):
        ref[...] = item.reshape(ref.shape)
    later = {}

    def aside_norm():
        later["first"] = normal(x_ref)

    attend_chunks(
        source,
        (att_ref, share_ref, logit_ref, before_ref, state_ref, state, carry),
        seqs,
        (
            aside_norm,
            lambda: product(later["first"], 0),
            lambda: product(later["first"], 1),
            lambda: product(later["first"], 2),
            lambda: product(later["first"], 3),
        ),
    )

    @pl.when(step == steps - 1)
    def _():
        keep_ffn.wait()
        keep_out.wait()
        keep_in.wait()
        for part in range(2):
            for i in column:
                in_z[part][i].wait_send()
                for p in planes:
                    in_chip[part][i][p].wait_send()
                in_core[part][i].wait_send()
        for turn in rounds:
            for way in range(2):

                @pl.when(sends(way, turn))
                def _():
                    for copy in relay[way, turn]:
                        copy.wait_send()

                @pl.when(gets(way, turn))
                def _():
                    for copy in spread[way, turn]:
                        copy.wait_send()
                    for copy in passed[way, turn]:
                        copy.wait()


def forward(tokens, ids, dw, ln_params, attn_w, ffn_w):
    seqs, length, _ = tokens.shape
    chunks = length // CHUNK
    wide = lax.axis_size("wide")
    narrow = lax.axis_size("narrow")
    if wide > 8:
        sets = [[place + 8 * group for group in range(wide // 8)] for place in range(8)]
        ids = lax.all_gather(ids, "wide", axis_index_groups=sets, tiled=True)
    block = pl.BlockSpec((seqs, CHUNK, D), lambda i: (0, i, 0))
    ahead = pl.BlockSpec((seqs, CHUNK, D), lambda i: (0, jnp.minimum(i + 1, chunks - 1), 0))
    low_out = jax.ShapeDtypeStruct(tokens.shape, low_type)
    any_spec = pl.BlockSpec(memory_space=pl.ANY)

    def whole(*shape):
        return pl.BlockSpec(shape, lambda i: (0,) * len(shape))

    column = narrow - 1
    sems = 6 + 2 * (10 * column + 2 * column * 10 + column + 4)
    return pl.pallas_call(
        functools.partial(
            forward_kernel,
            narrow=narrow,
            total_seqs=seqs * wide * narrow,
            groups=dw.shape[0],
        ),
        grid=(chunks,),
        in_specs=[
            pl.BlockSpec(memory_space=pltpu.SMEM),
            pl.BlockSpec(memory_space=pltpu.SMEM),
            whole(seqs, CHUNK, D),
            ahead,
            whole(4, D),
            any_spec,
            any_spec,
        ],
        out_specs=[block] * 7
        + [
            pl.BlockSpec((1, seqs, 1, D), lambda i: (i, 0, 0, 0)),
            pl.BlockSpec((1, seqs, PAIRS, PAIR, 2 * PAIR), lambda i: (i, 0, 0, 0, 0)),
            whole(8, LANES),
            any_spec,
            any_spec,
            any_spec,
        ],
        out_shape=[low_out] * 7
        + [
            jax.ShapeDtypeStruct((chunks, seqs, 1, D), wide_type),
            jax.ShapeDtypeStruct((chunks, seqs, PAIRS, PAIR, 2 * PAIR), low_type),
            jax.ShapeDtypeStruct((8, LANES), wide_type),
            jax.ShapeDtypeStruct((4, D, D), low_type),
            jax.ShapeDtypeStruct((D, D), low_type),
            jax.ShapeDtypeStruct((2, FF, D), low_type),
        ],
        scratch_shapes=[
            pltpu.VMEM((seqs, PAIRS, PAIR, 2 * PAIR), wide_type),
            pltpu.VMEM((seqs, 1, D), wide_type),
            pltpu.VMEM((4, seqs * CHUNK, D), low_type),
            pltpu.VMEM((4, D, D), low_type),
            pltpu.VMEM((attn_w.shape[1] // 2, D), wide_type),
            pltpu.VMEM(attn_w.shape, wide_type),
            pltpu.VMEM(ffn_w.shape, wide_type),
            pltpu.VMEM(attn_w.shape, low_type),
            pltpu.VMEM(ffn_w.shape, low_type),
            pltpu.VMEM((8, LANES), wide_type),
            pltpu.VMEM((column, 8, LANES), wide_type),
            pltpu.VMEM((3, 8, LANES), wide_type),
            pltpu.VMEM((8, LANES), wide_type),
            pltpu.SemaphoreType.DMA((sems,)),
        ],
        compiler_params=pltpu.CompilerParams(
            vmem_limit_bytes=VMEM_BYTES, collective_id=0, has_side_effects=True
        ),
        name="forward",
    )(ids, dw, tokens, tokens, ln_params, attn_w, ffn_w)


class Place:
    def __init__(self, narrow):
        self.narrow = narrow
        w = lax.axis_index("wide")
        self.z = lax.axis_index("narrow")
        self.core = lax.rem(w, 2)
        self.chip = lax.rem(w // 2, 4)
        self.other = 1 - self.core
        self.hops = list(range(1, narrow))
        self.column_z = [lax.rem(self.z + hop, narrow) for hop in self.hops]
        self.column = [(w, place) for place in self.column_z]
        self.chip_at = [lax.rem(self.chip + hop, 4) for hop in range(1, 4)]
        self.chips = [(w - 2 * self.chip + 2 * chip, self.z) for chip in self.chip_at]
        self.mate = (w + 1 - 2 * self.core, self.z)


class Copies:
    def __init__(self, sems):
        self.sems = sems
        self.used = 0

    def remote(self, src, dst, device):
        at = self.used
        self.used += 2
        return remote(src, dst, self.sems.at[at], self.sems.at[at + 1], device)

    def local(self, src, dst):
        at = self.used
        self.used += 1
        return pltpu.make_async_copy(src, dst, self.sems.at[at])


def blocks_at(owner, size):
    return pl.ds(pl.multiple_of(owner * size, size), size)


def wide_sum(parts):
    total = parts[0].astype(wide_type)
    for part in parts[1:]:
        total = total + part.astype(wide_type)
    return total


def newton_poly(gram):
    size = gram.shape[0]
    eye = row_of((size, size)) == lane_of((size, size))
    trace = jnp.sum(jnp.where(eye, gram, 0.0), axis=1, keepdims=True)
    trace = jnp.sum(trace, axis=0, keepdims=True)
    scale = 1.0 / (jnp.sqrt(trace) + 1e-07)

    def low_dot(left, right):
        return dot_nn(left.astype(low_type), right.astype(low_type))

    def polynomial(one):
        poly = quintic_cube * one + quintic_five * low_dot(one, one)
        return poly + jnp.where(eye, quintic_lin, 0.0)

    gram_one = gram * (scale * scale)
    poly_one = polynomial(gram_one)
    gram_two = low_dot(low_dot(gram_one, poly_one), poly_one)
    poly_two = polynomial(gram_two)
    return low_dot(poly_one, poly_two) * scale


def update_body(
    wsum_ref,
    take_f,
    mom_w_ref,
    mom_hbm,
    mom_f_hbm,
    ln_one_ref,
    ln_two_ref,
    grad_attn,
    step_attn,
    grad_ffn,
    step_ffn,
    ln_ref,
    ln_now,
    ln_mate,
    ln_chips,
    ln_column,
    col_w,
    grad_w,
    moment_w,
    poly_w,
    send_w,
    all_w,
    all_f,
    mom_f,
    mom_o,
    moment_f,
    out_f,
    all_o,
    moment_o,
    step_o,
    cut_gf,
    col_gf,
    strips_gf,
    gram_f,
    cut_go,
    col_go,
    strips_go,
    gram_o,
    *,
    narrow,
    here,
    copies,
    over_groups,
):
    z, core, chip = here.z, here.core, here.chip
    half = D // 2
    quarter = D // 4
    rows = D // narrow
    small = rows // 4
    ffn_rows = FF // narrow
    strip = quarter // narrow
    column = range(narrow - 1)
    planes = range(3)
    own_cols = blocks_at(core, half)
    own_quarter = blocks_at(chip, quarter)
    own_small = blocks_at(chip, small)
    matrix = lax.rem(z, 4)

    def to_plane(src, dst):
        return [copies.remote(src(i), dst(i), here.chips[i]) for i in planes]

    def to_column(src, dst):
        return [copies.remote(src(i), dst(i), here.column[i]) for i in column]

    def same(block):
        return lambda i: block

    keep_f = copies.local(mom_f_hbm.at[core], mom_f)
    keep_o = copies.local(mom_hbm.at[4], mom_o)
    mate_ln = [copies.remote(ln_now, ln_mate, here.mate)]
    plane_ln = to_plane(same(ln_now), lambda i: ln_chips.at[i])
    block = all_f.at[own_quarter]
    plane_f = to_plane(same(block), same(block))
    block = all_o.at[own_small, own_cols]
    plane_f = plane_f + to_plane(same(block), same(block))
    z_sum = to_column(lambda i: wsum_ref.at[lax.rem(here.column_z[i], 4)], lambda i: col_w.at[i])
    z_ln = to_column(same(ln_now), lambda i: ln_column.at[i])
    block = out_f.at[0, core]
    mate_f = [copies.remote(block, block, here.mate)]
    block = all_o.at[:, own_cols]
    mate_o = [copies.remote(block, block, here.mate)]
    z_gf = to_column(
        lambda i: cut_gf.at[blocks_at(here.column_z[i], strip)], lambda i: col_gf.at[i]
    )
    block = grad_w.at[own_quarter, own_cols]
    plane_w = to_plane(same(block), same(block))
    z_go = to_column(
        lambda i: cut_go.at[blocks_at(here.column_z[i], strip)], lambda i: col_go.at[i]
    )
    block = grad_w.at[:, own_cols]
    mate_w = [copies.remote(block, block, here.mate)]
    block = strips_gf.at[blocks_at(z, strip)]
    z_back_f = to_column(same(block), same(block))
    block = strips_go.at[blocks_at(z, strip)]
    z_back_o = to_column(same(block), same(block))
    block = gram_f.at[own_quarter]
    plane_gf = to_plane(same(block), same(block))
    block = gram_o.at[own_quarter, own_cols]
    plane_go = to_plane(same(block), same(block))
    quad = [z - matrix + lax.rem(matrix + hop, 4) for hop in range(1, 4)]

    def hand_back(kind):
        spread = [
            copies.remote(
                send_w.at[kind, there],
                all_w.at[kind, matrix, own_small, own_cols],
                (lax.axis_index("wide"), there),
            )
            for there in quad
        ]
        block = all_w.at[kind, :, own_small, own_cols]
        plane = to_plane(same(block), same(block))
        block = all_w.at[kind, :, :, own_cols]
        return spread, plane, [copies.remote(block, block, here.mate)]

    spread_g, plane_g, mate_g = hand_back(0)
    spread_s, plane_s, mate_s = hand_back(1)
    block = gram_o.at[:, own_cols]
    mate_go = [copies.remote(block, block, here.mate)]
    block = out_f.at[1, core]
    mate_x = [copies.remote(block, block, here.mate)]
    write_f = [copies.local(out_f.at[0], grad_ffn), copies.local(out_f.at[1], step_ffn)]
    write_o = [copies.local(all_o, grad_attn.at[4]), copies.local(step_o, step_attn.at[4])]
    write_w = [
        copies.local(all_w.at[0], grad_attn.at[pl.ds(0, 4)]),
        copies.local(all_w.at[1], step_attn.at[pl.ds(0, 4)]),
    ]
    sent = []

    def start(group):
        for copy in group:
            copy.start()
        sent.extend(group)

    def arrive(group):
        for copy in group:
            copy.wait_recv()

    def begin(group):
        for copy in group:
            copy.start()

    start(z_sum)
    begin([keep_f, keep_o])
    ln_now[...] = jnp.zeros_like(ln_now)
    ln_now[0:2, :] = ln_one_ref[...]
    ln_now[2:4, :] = ln_two_ref[...]
    over_groups(ln_now, 2)
    start(mate_ln)
    grad_f, grad_o = take_f()
    all_f[own_quarter, :] = grad_f
    all_o[own_small, own_cols] = grad_o
    start(plane_f)

    keep_f.wait()
    arrive(plane_f)
    start(mate_o)
    grad = all_f[...].T
    out_f[0, core] = grad
    start(mate_f)
    moment_f[...] = (momentum_keep * mom_f[...] + grad.astype(wide_type)).astype(low_type)
    cut_gf[...] = dot_tn(moment_f[:, own_quarter], moment_f[...]).astype(low_type)
    start(z_gf)

    keep_o.wait()
    arrive(mate_o)
    moment = momentum_keep * mom_o[...] + all_o[...].astype(wide_type)
    moment_o[...] = moment.astype(low_type)
    cut_go[...] = dot_tn(moment_o[:, own_quarter], moment_o[:, own_cols]).astype(low_type)
    start(z_go)

    arrive(z_sum)
    total = wide_sum([wsum_ref[matrix]] + [col_w[i] for i in column])
    grad_w[own_quarter, own_cols] = total.astype(low_type)
    start(plane_w)
    arrive(mate_ln)
    mate_ln[0].wait_send()
    ln_now[...] = ln_now[...] + ln_mate[...]
    start(plane_ln)

    arrive(z_gf)
    total = wide_sum([cut_gf[blocks_at(z, strip), :]] + [col_gf[i] for i in column])
    strips_gf[blocks_at(z, strip), :] = total.astype(low_type)
    start(z_back_f)
    arrive(z_go)
    total = wide_sum([cut_go[blocks_at(z, strip), :]] + [col_go[i] for i in column])
    strips_go[blocks_at(z, strip), :] = total.astype(low_type)
    start(z_back_o)

    arrive(plane_w)
    start(mate_w)
    arrive(plane_ln)
    for copy in plane_ln:
        copy.wait_send()
    ln_now[...] = ln_now[...] + ln_chips[0] + ln_chips[1] + ln_chips[2]
    start(z_ln)

    def small_rows(there):
        return pl.ds(pl.multiple_of(there * rows + chip * small, small), small)

    arrive(mate_w)
    for there in range(narrow):
        send_w[0, there] = grad_w[small_rows(there), own_cols]
    start(spread_g)
    all_w[0, matrix, own_small, own_cols] = send_w[0, z]
    moment = momentum_keep * mom_w_ref[...].astype(wide_type) + grad_w[...].astype(wide_type)
    moment_w[...] = moment.astype(low_type)
    gram = dot_tn(moment_w[...], moment_w[...])
    arrive(z_back_f)
    gram_f[own_quarter, :] = strips_gf[...]
    start(plane_gf)
    arrive(z_back_o)
    gram_o[own_quarter, own_cols] = strips_go[...]
    start(plane_go)

    poly_w[...] = newton_poly(gram).astype(low_type)
    picked = jnp.concatenate([moment_w[small_rows(there), :] for there in range(narrow)], axis=0)
    ortho = dot_nn(picked, poly_w[:, own_cols]).astype(low_type)
    for there in range(narrow):
        send_w[1, there] = ortho[there * small : (there + 1) * small, :]
    start(spread_s)
    all_w[1, matrix, own_small, own_cols] = send_w[1, z]
    arrive(spread_g)
    start(plane_g)

    arrive(plane_gf)
    poly = newton_poly(gram_f[...].astype(wide_type)).astype(low_type)
    out_f[1, core] = dot_nn(moment_f[...], poly).astype(low_type)
    start(mate_x)
    arrive(spread_s)
    start(plane_s)
    arrive(plane_go)
    start(mate_go)
    arrive(plane_g)
    start(mate_g)
    arrive(mate_go)
    poly = newton_poly(gram_o[...].astype(wide_type)).astype(low_type)
    step_o[...] = dot_nn(moment_o[...], poly).astype(low_type)
    arrive(plane_s)
    start(mate_s)
    begin(write_o)
    arrive(mate_f)
    arrive(mate_x)
    begin(write_f)
    arrive(z_ln)
    total = ln_now[...]
    for i in column:
        total = total + ln_column[i]
    ln_ref[...] = total
    arrive(mate_g)
    begin(write_w[:1])
    arrive(mate_s)
    begin(write_w[1:])
    for copy in write_o + write_f + write_w:
        copy.wait()
    settled = [id(copy) for copy in mate_ln + plane_ln]
    for copy in sent:
        if id(copy) not in settled:
            copy.wait_send()


def back_kernel(*refs, narrow, chunks, sets):
    blocks = list(refs[:9])
    xc_ref, x_ref, w_ref, ln_ref, gffn_hbm, go_hbm, mom_hbm, mom_f_hbm, ln_two_ref = refs[9:18]
    dz_ref, grad_attn, step_attn, grad_ffn, step_ffn, ln_sum_ref = refs[18:24]
    state, carry, dq_all, dk_all, dv_all, de_all, first_t = refs[24:31]
    own_f, got_f, far_f, col_f, own_o, got_o, cut_o, far_o, col_o = refs[31:40]
    low_f, low_o, mom_own, mom_low, mom_all = refs[40:45]
    grad_w, got_w, half_w, far_w, staged, gln_ref, wsum_ref = refs[45:52]
    sums = refs[52:54]
    group_w, group_f, group_o, group_ln = refs[54:58]
    *update_refs, sems = refs[58:]
    step = pl.program_id(0)
    steps = pl.num_programs(0)
    here = Place(narrow)
    copies = Copies(sems)
    half = D // 2
    part = D // 4
    rows = D // narrow
    ffn_rows = FF // narrow
    column = range(narrow - 1)
    own_cols = blocks_at(here.core, half)
    mate_cols = blocks_at(here.other, half)
    grads = (dq_all, dk_all, dv_all, de_all)
    w = lax.axis_index("wide")
    peers = [(lax.rem(w + 8 * at, 8 * sets), here.z) for at in range(1, sets)]

    keep_f = copies.local(gffn_hbm.at[here.core], own_f)
    keep_o = copies.local(go_hbm.at[:, own_cols], own_o)
    keep_mom = copies.local(mom_hbm.at[pl.ds(0, 4)], mom_own)
    pieces = [blocks_at(there, part) for there in here.chip_at + [here.chip]]
    mate_f = [
        copies.remote(gffn_hbm.at[here.other, piece], got_f.at[piece], here.mate)
        for piece in pieces
    ]
    mate_o = copies.remote(go_hbm.at[:, mate_cols], got_o, here.mate)
    plane_f = [
        copies.remote(own_f.at[pieces[hop]], far_f.at[hop], here.chips[hop]) for hop in range(3)
    ]
    plane_o = [
        copies.remote(cut_o.at[:, here.chip_at[hop]], far_o.at[hop], here.chips[hop])
        for hop in range(3)
    ]
    z_sum = []
    for i in column:
        there = here.column_z[i]
        z_sum.append(
            copies.remote(low_f.at[:, blocks_at(there, ffn_rows)], col_f.at[i], here.column[i])
        )
        z_sum.append(copies.remote(low_o.at[there], col_o.at[i], here.column[i]))
    z_mom = [
        copies.remote(
            mom_low.at[lax.rem(here.column_z[i], 4), :, own_cols],
            mom_all.at[blocks_at(here.z, rows), own_cols],
            here.column[i],
        )
        for i in column
    ]
    mate_mom = copies.remote(mom_all.at[:, own_cols], mom_all.at[:, own_cols], here.mate)
    mate_w = [
        copies.remote(grad_w.at[m, :, mate_cols], got_w.at[m], here.mate) for m in range(4)
    ]
    plane_w = [
        [
            copies.remote(
                half_w.at[m, blocks_at(here.chip_at[hop], part)],
                far_w.at[hop, m],
                here.chips[hop],
            )
            for hop in range(3)
        ]
        for m in range(4)
    ]

    def gradient(m):
        total = dot_nn(first_t[...], grads[m][...].reshape(-1, D))
        grad_w[m] = total.astype(low_type)
        mate_w[m].start()

    def over_cores(m):
        mate_w[m].wait()
        half_w[m] = wide_sum([grad_w[m, :, own_cols], got_w[m]]).astype(low_type)
        for copy in plane_w[m]:
            copy.start()

    def over_chips(m):
        for copy in plane_w[m]:
            copy.wait()
        mine = half_w[m, blocks_at(here.chip, part), :]
        wsum_ref[m] = wide_sum([mine] + [far_w[hop, m] for hop in range(3)]).astype(low_type)

    @pl.when(step == 0)
    def _():
        state[...] = jnp.zeros_like(state)
        carry[...] = jnp.zeros_like(carry)
        gln_ref[...] = jnp.zeros_like(gln_ref)
        greet(here.column + here.chips + [here.mate] + peers)
        for copy in [keep_f] + mate_f + [keep_o, mate_o, keep_mom]:
            copy.start()

    @pl.when(step == 1)
    def _():
        keep_mom.wait()
        mom_low[...] = mom_own[...].astype(low_type)
        for copy in z_mom:
            copy.start()
        mom_all[blocks_at(here.z, rows), own_cols] = mom_low[lax.rem(here.z, 4), :, own_cols]

    def piece_sum(at):
        mate_f[at].wait()
        piece = pieces[at]
        own_f[piece, :] = wide_sum([own_f[piece, :], got_f[piece, :]]).astype(low_type)
        if at < 3:
            plane_f[at].start()

    @pl.when(step == 1)
    def _():
        keep_f.wait()
        for at in range(2):
            piece_sum(at)

    @pl.when(step == 2)
    def _():
        for at in range(2, 4):
            piece_sum(at)
        keep_o.wait()
        mate_o.wait()
        cut_o[...] = wide_sum([own_o[...], got_o[...]]).astype(low_type).reshape(cut_o.shape)
        for copy in plane_o:
            copy.start()

    @pl.when(step < chunks)
    def _():
        chunk = chunks - 1 - step
        seqs = xc_ref.shape[0]

        for seq in range(seqs):
            normed, _ = normalize(xc_ref[seq].astype(wide_type))
            first = (normed * ln_ref[0:1, :] + ln_ref[1:2, :]).astype(low_type)
            first_t[:, blocks_at(chunk * seqs + seq, CHUNK)] = first.T
        attend_back_chunk(blocks + [staged.at[place] for place in range(4)], state, carry)
        for place in range(4):
            grads[place][chunk] = staged[place]

    @pl.when(step == chunks)
    def _():
        gradient(0)
        gradient(1)
        gradient(2)
        over_cores(0)
        over_cores(1)
        for copy in plane_f + plane_o:
            copy.wait()
        mine = own_f[blocks_at(here.chip, part), :]
        low_f[...] = wide_sum([mine] + [far_f[hop] for hop in range(3)]).astype(low_type)
        mine = cut_o[:, here.chip]
        low_o[...] = wide_sum([mine] + [far_o[hop] for hop in range(3)]).astype(low_type)
        for copy in z_sum:
            copy.start()
        gradient(3)
        over_cores(2)
        over_cores(3)
        for copy in z_mom:
            copy.wait_recv()
        mate_mom.start()

    @pl.when(step >= chunks)
    def _():
        per = chunks // 4
        seqs = x_ref.shape[0]
        parts = [item[pl.ds((step - chunks) * per, per)].reshape(-1, D) for item in grads]
        dfirst = dot_nt(parts[0], w_ref[0])
        for place in range(1, 4):
            dfirst = dfirst + dot_nt(parts[place], w_ref[place])
        spans = [slice(at * CHUNK, (at + 1) * CHUNK) for at in range(per)]
        rows_in = [x_ref[:, span, :].reshape(-1, D) for span in spans]
        normed, inverse = normalize(jnp.concatenate(rows_in, axis=0).astype(wide_type))
        gln_ref[0:1, :] += jnp.sum(dfirst * normed, axis=0, keepdims=True)
        gln_ref[1:2, :] += jnp.sum(dfirst, axis=0, keepdims=True)
        dz = norm_back(dfirst, normed, inverse, ln_ref[0:1, :]).astype(low_type)
        for at, span in enumerate(spans):
            size = seqs * CHUNK
            dz_ref[:, span, :] = dz[at * size : (at + 1) * size].reshape(seqs, CHUNK, D)

    def over_groups(ref, number):
        if sets == 1:
            return
        slots = (group_w, group_f, group_ln, group_o)[number]
        exchange = [
            copies.remote(ref, slots.at[at], peer) for at, peer in enumerate(peers)
        ]
        for copy in exchange:
            copy.start()
        for copy in exchange:
            copy.wait()
        total = wide_sum([ref[...]] + [slots[at] for at in range(len(peers))])
        ref[...] = total.astype(ref.dtype)

    def take_f():
        for copy in z_sum:
            copy.wait()
        sum_f, sum_o = sums
        mine = low_f[:, blocks_at(here.z, ffn_rows)]
        sum_f[...] = wide_sum([mine] + [col_f[i] for i in column]).astype(low_type)
        sum_o[...] = wide_sum([low_o[here.z]] + [col_o[i] for i in column]).astype(low_type)
        over_groups(sum_f, 1)
        over_groups(sum_o, 3)
        return sum_f[...], sum_o[...]

    @pl.when(step == steps - 1)
    def _():
        for m in range(4):
            over_chips(m)
        over_groups(wsum_ref, 0)
        mate_mom.wait()
        for copy in z_mom:
            copy.wait_send()
        update_body(
            wsum_ref,
            take_f,
            mom_all,
            mom_hbm,
            mom_f_hbm,
            gln_ref,
            ln_two_ref,
            grad_attn,
            step_attn,
            grad_ffn,
            step_ffn,
            ln_sum_ref,
            *update_refs,
            narrow=narrow,
            here=here,
            copies=copies,
            over_groups=over_groups,
        )


def back(q, k, v, a, share, logit, before, datt, states, tokens, in_w, ln_params, gffn, go, mom, mom_f, ln_two):
    seqs, length, _ = q.shape
    chunks = length // CHUNK
    narrow = lax.axis_size("narrow")
    small, half, part = D // narrow // 4, D // 2, D // 4
    ffn_rows = FF // narrow

    def chunk_at(i):
        return jnp.maximum(chunks - 1 - i, 0)

    def rows_at(i):
        return (0, jnp.maximum(i - chunks, 0), 0)

    def whole(*shape):
        return pl.BlockSpec(shape, lambda i: (0,) * len(shape))

    block = pl.BlockSpec((seqs, CHUNK, D), lambda i: (0, chunk_at(i), 0))
    row_spec = pl.BlockSpec((seqs, length // 4, D), rows_at)
    any_spec = pl.BlockSpec(memory_space=pl.ANY)
    rows, strip, column = D // narrow, part // narrow, narrow - 1
    sets = lax.axis_size("wide") // 8
    spare = max(sets - 1, 1)
    outs = [(5, rows, D), (5, rows, D), (2, ffn_rows, D), (2, ffn_rows, D)]

    def full(*shape):
        return pltpu.VMEM(shape, wide_type)

    def low(*shape):
        return pltpu.VMEM(shape, low_type)

    return pl.pallas_call(
        functools.partial(back_kernel, narrow=narrow, chunks=chunks, sets=sets),
        grid=(chunks + 4,),
        in_specs=[block] * 6
        + [
            pl.BlockSpec((1, seqs, 1, D), lambda i: (chunk_at(i), 0, 0, 0)),
            block,
            pl.BlockSpec((1, seqs, PAIRS, PAIR, 2 * PAIR), lambda i: (chunk_at(i), 0, 0, 0, 0)),
            block,
            row_spec,
            whole(4, D, D),
            whole(4, D),
            any_spec,
            any_spec,
            any_spec,
            any_spec,
            whole(2, D),
        ],
        out_specs=[row_spec] + [any_spec] * 4 + [whole(8, D)],
        out_shape=[jax.ShapeDtypeStruct(q.shape, low_type)]
        + [jax.ShapeDtypeStruct(shape, low_type) for shape in outs]
        + [jax.ShapeDtypeStruct((8, D), wide_type)],
        scratch_shapes=[
            pltpu.VMEM((seqs, PAIRS, PAIR, 2 * PAIR), wide_type),
            pltpu.VMEM((seqs, 1, D), wide_type),
            low(chunks, seqs, CHUNK, D),
            low(chunks, seqs, CHUNK, D),
            low(chunks, seqs, CHUNK, D),
            low(chunks, seqs, CHUNK, D),
            low(D, seqs * length),
            low(D, FF),
            low(D, FF),
            low(3, part, FF),
            low(narrow - 1, part, ffn_rows),
            low(D, half),
            low(D, half),
            low(narrow, 4, small, half),
            low(3, narrow, small, half),
            low(narrow - 1, small, half),
            low(part, FF),
            low(narrow, small, half),
            pltpu.VMEM((4, D // narrow, D), wide_type),
            low(4, D // narrow, D),
            low(D, D),
            low(4, D, D),
            low(4, D, half),
            low(4, D, half),
            low(3, 4, part, half),
            low(4, seqs, CHUNK, D),
            full(2, D),
            low(4, part, half),
            low(part, ffn_rows),
            low(small, half),
            low(spare, 4, part, half),
            low(spare, part, ffn_rows),
            low(spare, small, half),
            full(spare, 8, D),
            full(8, D),
            full(8, D),
            full(3, 8, D),
            full(column, 8, D),
            low(column, part, half),
            low(D, D),
            low(D, D),
            low(D, D),
            low(2, narrow, small, half),
            low(2, 4, rows, D),
            low(D, ffn_rows),
            full(ffn_rows, D),
            full(rows, D),
            low(ffn_rows, D),
            low(2, 2, ffn_rows, D),
            low(rows, D),
            low(rows, D),
            low(rows, D),
            low(part, D),
            low(column, strip, D),
            low(part, D),
            low(D, D),
            low(part, half),
            low(column, strip, half),
            low(part, half),
            low(D, D),
            pltpu.SemaphoreType.DMA((11 + 2 * (65 + 9 * column + 4 * spare),)),
        ],
        compiler_params=pltpu.CompilerParams(
            vmem_limit_bytes=VMEM_BYTES, collective_id=1, has_side_effects=True
        ),
        name="back",
    )(
        q,
        k,
        v,
        a,
        share,
        logit,
        before,
        datt,
        states,
        tokens,
        tokens,
        in_w,
        ln_params,
        gffn,
        go,
        mom,
        mom_f,
        ln_two,
    )


def shards(
    tokens,
    out_grad,
    group_ids,
    domain_weight,
    attn_w,
    ffn_w,
    attn_mom,
    ffn_mom,
    ln_params,
    ln_first,
    ln_second,
):
    local_seqs, length, _ = tokens.shape
    token_count = local_seqs * length
    rows = tokens.reshape(token_count, D)
    head = (local_seqs, length, D)
    q, k, v, a, att, share, logit, before, states, weights, in_w, out_w, ffn_low = forward(
        tokens, group_ids, domain_weight, ln_params, attn_w, ffn_w
    )
    output, dx, datt, gffn, go, ln_two = feed(
        group_ids,
        weights,
        rows,
        att.reshape(token_count, D),
        out_grad.reshape(token_count, D),
        out_w,
        ffn_low,
        ln_params,
        length,
    )
    dz, attn_grad, attn_step, ffn_grad, ffn_step, ln_sum = back(
        q,
        k,
        v,
        a,
        share,
        logit,
        before,
        datt.reshape(head),
        states,
        tokens,
        in_w,
        ln_params,
        gffn,
        go,
        attn_mom,
        ffn_mom,
        ln_two,
    )

    def flat(*items):
        return [item.reshape(-1, D) for item in items]

    results = finish(
        dx,
        dz.reshape(token_count, D),
        flat(attn_grad, attn_step, attn_w, attn_mom),
        flat(ffn_grad, ffn_step, ffn_w, ffn_mom),
        (ln_params, ln_first, ln_second, ln_sum),
    )
    input_grad, ga, ma, wa, ca, gf, mf, wf, cf, ln_grad, first_new, second_new, ln_new = results
    attn, ffn = attn_w.shape, ffn_w.shape
    return (
        output.reshape(tokens.shape),
        input_grad.reshape(tokens.shape),
        ga.reshape(attn),
        gf.reshape(ffn),
        ln_grad,
        ma.reshape(attn),
        mf.reshape(ffn),
        wa.reshape(attn),
        wf.reshape(ffn),
        ca.reshape(attn),
        cf.reshape(ffn),
        first_new,
        second_new,
        ln_new,
    )


def solution(mesh):
    split = P(("wide", "narrow"), None, None)
    rows = P(None, "narrow", None)
    lanes = P(None, "narrow")
    inner = jax.shard_map(
        shards,
        mesh=mesh,
        in_specs=(
            split,
            split,
            P(("wide", "narrow")),
            P(),
            rows,
            rows,
            rows,
            rows,
            P(),
            lanes,
            lanes,
        ),
        out_specs=(
            split,
            split,
            rows,
            rows,
            lanes,
            rows,
            rows,
            rows,
            rows,
            rows,
            rows,
            lanes,
            lanes,
            lanes,
        ),
        check_vma=False,
    )
    return inner
```

```python
import functools
import math

import jax
import jax.numpy as jnp
from jax import lax
from jax.experimental import pallas as pl
from jax.experimental.pallas import tpu as pltpu
from jax.sharding import PartitionSpec as P

D = 512
HEADS = 8
HEAD_DIM = 64
FF = 2048
STEP = 10

norm_epsilon = 1e-05
momentum_keep = 0.5
quintic_lin = 3.4445
quintic_cube = -4.775
quintic_five = 2.0315
muon_rate = 0.7
muon_decay = 0.1
adam_rate = 0.2
beta_first = 0.9
beta_second = 0.999
adam_epsilon = 1e-08

CHUNK = 128
PAIR = 2 * HEAD_DIM
PAIRS = HEADS // 2
VMEM_BYTES = 60 * 1024 * 1024
low_type = jnp.bfloat16
wide_type = jnp.float32


def dot_nn(left, right):
    return lax.dot_general(left, right, (((1,), (0,)), ((), ())), preferred_element_type=wide_type)


def dot_nt(left, right):
    return lax.dot_general(left, right, (((1,), (1,)), ((), ())), preferred_element_type=wide_type)


def dot_tn(left, right):
    return lax.dot_general(left, right, (((0,), (0,)), ((), ())), preferred_element_type=wide_type)


def normalize(rows):
    center = rows - jnp.mean(rows, axis=-1, keepdims=True)
    spread = jnp.mean(center * center, axis=-1, keepdims=True)
    inverse = lax.rsqrt(spread + norm_epsilon)
    return center * inverse, inverse


def norm_back(grad_rows, normed, inverse, gain):
    grad_normed = grad_rows * gain
    mean_grad = jnp.mean(grad_normed, axis=-1, keepdims=True)
    mean_cross = jnp.mean(grad_normed * normed, axis=-1, keepdims=True)
    return inverse * (grad_normed - mean_grad - normed * mean_cross)


def lane_of(shape):
    return lax.broadcasted_iota(jnp.int32, shape, 1)


def row_of(shape):
    return lax.broadcasted_iota(jnp.int32, shape, 0)


def split_pair(pair, first_head):
    zero = jnp.zeros_like(pair)
    return jnp.concatenate(
        [jnp.where(first_head, pair, zero), jnp.where(first_head, zero, pair)], axis=0
    )


def head_reduce(values, first_head, op, neutral):
    left = op(jnp.where(first_head, values, neutral), axis=-1, keepdims=True)
    right = op(jnp.where(first_head, neutral, values), axis=-1, keepdims=True)
    return jnp.where(first_head, left, right)


def attend_back_chunk(refs, state, carry):
    (
        q_ref,
        k_ref,
        v_ref,
        a_ref,
        share_ref,
        logit_ref,
        before_ref,
        datt_ref,
        state_ref,
        dq_ref,
        dk_ref,
        dv_ref,
        de_ref,
    ) = refs
    scaling = HEAD_DIM**-0.5
    first_head = lane_of((CHUNK, PAIR)) < HEAD_DIM
    causal = row_of((CHUNK, 2 * CHUNK)) >= lane_of((CHUNK, 2 * CHUNK)) % CHUNK
    anti = row_of((CHUNK, 2 * CHUNK)) <= lane_of((CHUNK, 2 * CHUNK)) % CHUNK
    same_head = (row_of((PAIR, 2 * PAIR)) // HEAD_DIM) == (
        (lane_of((PAIR, 2 * PAIR)) // HEAD_DIM) % 2
    )
    lower = (row_of((CHUNK, CHUNK)) >= lane_of((CHUNK, CHUNK))).astype(low_type)
    upper = (row_of((CHUNK, CHUNK)) <= lane_of((CHUNK, CHUNK))).astype(low_type)

    def masked(mask, raw):
        return jnp.where(mask, raw, 0.0).astype(low_type)

    items = []
    for seq in range(q_ref.shape[0]):
        total = dot_nn(lower, a_ref[seq]) + before_ref[0, seq]
        inv = 1.0 / total
        for pair in range(PAIRS):
            lanes = slice(pair * PAIR, (pair + 1) * PAIR)
            items.append(
                dict(seq=seq, pair=pair, lanes=lanes, total=total[:, lanes], inv=inv[:, lanes])
            )

    def load(t):
        seq, lanes = t["seq"], t["lanes"]
        t["k"] = k_ref[seq, :, lanes]
        t["v"] = v_ref[seq, :, lanes]
        t["a"] = a_ref[seq, :, lanes]
        t["share"] = share_ref[seq, :, lanes]
        t["datt"] = datt_ref[seq, :, lanes]
        t["q"] = q_ref[seq, :, lanes] * low_type(scaling)
        t["before"] = state_ref[0, seq, t["pair"]]
        t["after"] = jnp.where(same_head, state[seq, t["pair"]], 0.0).astype(low_type)
        t["v_two"] = split_pair(t["v"], first_head)
        t["a_two"] = split_pair(t["a"], first_head)
        t["dmix"] = masked(causal, dot_nt(t["datt"], t["v_two"]))

    def gather(t):
        t["share_two"] = split_pair(t["share"], first_head)
        t["datt_two"] = split_pair(t["datt"], first_head)
        t["dshare"] = dot_nn(t["dmix"], t["a_two"]) + dot_nt(t["datt"], t["before"][:, PAIR:])

    def soften(t):
        logit = logit_ref[t["seq"], :, t["lanes"]].astype(wide_type)
        prob = t["share"].astype(wide_type) * t["total"]
        cross = t["dshare"] * t["inv"] * prob
        dlogit = cross - prob * head_reduce(cross, first_head, jnp.sum, 0.0)
        t["dnumer"] = (dlogit * t["inv"]).astype(low_type)
        t["dtotal"] = -(cross + dlogit * logit) * t["inv"]
        t["mix_t"] = masked(anti, dot_nt(t["a"], t["share_two"]))
        t["dmix_t"] = masked(anti, dot_nt(t["v"], t["datt_two"]))

    def blend(t):
        t["dnumer_two"] = split_pair(t["dnumer"], first_head)
        t["dscores"] = masked(causal, dot_nt(t["dnumer"], t["a_two"]))
        t["dscores_t"] = masked(anti, dot_nt(t["a"], t["dnumer_two"]))
        t["k_two"] = split_pair(t["k"], first_head)
        t["q_two"] = split_pair(t["q"], first_head)
        t["scores_t"] = masked(anti, dot_nt(t["k"], t["q_two"]))
        t["later"] = dot_nn(t["a"], t["after"])

    def finish(t):
        seq, lanes = t["seq"], t["lanes"]
        dq = dot_nn(t["dscores"], t["k_two"]) + dot_nn(t["dnumer"], t["before"][:, :PAIR])
        dq_ref[seq, :, lanes] = (dq * scaling).astype(low_type)
        dv = dot_nn(t["mix_t"], t["datt_two"]) + t["later"][:, PAIR:]
        dv_ref[seq, :, lanes] = dv.astype(low_type)
        dk = dot_nn(t["dscores_t"], t["q_two"]) + t["later"][:, :PAIR]
        dk_ref[seq, :, lanes] = dk.astype(low_type)
        high = t["dtotal"].astype(low_type)
        rest = (t["dtotal"] - high.astype(wide_type)).astype(low_type)
        tail = dot_nn(upper, high) + dot_nn(upper, rest) + carry[seq, :, lanes]
        carry[seq, :, lanes] = tail[0:1, :]
        da = dot_nn(t["dmix_t"], t["share_two"]) + dot_nn(t["scores_t"], t["dnumer_two"])
        da = da + dot_nt(jnp.concatenate([t["k"], t["v"]], axis=1), t["after"]) + tail
        de = da.astype(low_type).astype(wide_type) * t["a"].astype(wide_type)
        de_ref[seq, :, lanes] = de.astype(low_type)
        state[seq, t["pair"], :, :PAIR] += dot_tn(t["dnumer"], t["q"])
        state[seq, t["pair"], :, PAIR:] += dot_tn(t["share"], t["datt"])

    for stage in (load, gather, soften, blend, finish):
        for item in items:
            stage(item)


FF_BLOCK = 256
gelu_root = math.sqrt(2.0 / math.pi)
gelu_cube = 0.044715


def feed_kernel(
    ids_ref,
    weight_ref,
    x_ref,
    att_ref,
    og_ref,
    wo_ref,
    ffn_ref,
    ln_ref,
    out_ref,
    dx_ref,
    datt_ref,
    gffn_ref,
    go_ref,
    gln_ref,
    up_sum,
    down_sum,
    o_sum,
    hidden,
    dinner,
    *,
    per_seq,
):
    step = pl.program_id(0)

    @pl.when(step == 0)
    def _():
        up_sum[...] = jnp.zeros_like(up_sum)
        down_sum[...] = jnp.zeros_like(down_sum)
        o_sum[...] = jnp.zeros_like(o_sum)
        gln_ref[...] = jnp.zeros_like(gln_ref)

    att = att_ref[...]
    mixed = x_ref[...].astype(wide_type) + dot_nn(att, wo_ref[...])
    normed, inverse = normalize(mixed)
    second = (normed * ln_ref[2:3, :] + ln_ref[3:4, :]).astype(low_type)
    mine = lane_of((1, LANES)) == ids_ref[step // per_seq]
    weight = jnp.sum(jnp.where(mine, weight_ref[0:1, :], 0.0), axis=1, keepdims=True)
    dout = og_ref[...].astype(wide_type) * weight
    dy = dout.astype(low_type)
    second_t = second.T
    dy_t = dy.T
    parts = [slice(part * FF_BLOCK, (part + 1) * FF_BLOCK) for part in range(FF // FF_BLOCK)]

    def open_part(part):
        return dot_nt(second, ffn_ref[0, part, :]), dot_nt(dy, ffn_ref[1, part, :])

    ahead = open_part(parts[0])
    for place, part in enumerate(parts):
        inner, dhidden = ahead
        if place + 1 < len(parts):
            ahead = open_part(parts[place + 1])
        square = inner * inner
        bend = jnp.tanh(inner * (gelu_root + (gelu_root * gelu_cube) * square))
        half = 0.5 + 0.5 * bend
        hidden[:, part] = (inner * half).astype(low_type)
        slope = half + (0.5 * inner) * (1.0 - bend * bend) * (
            gelu_root + (3.0 * gelu_root * gelu_cube) * square
        )
        dinner[:, part] = (dhidden * slope).astype(low_type)
    result = mixed + dot_nn(hidden[...], ffn_ref[1])
    dsecond = dot_nn(dinner[...], ffn_ref[0])
    for part in parts:
        down_sum[:, part] += dot_nn(dy_t, hidden[:, part])
        up_sum[:, part] += dot_nn(second_t, dinner[:, part])
    out_ref[...] = result.astype(low_type)
    gln_ref[0:1, :] += jnp.sum(dsecond * normed, axis=0, keepdims=True)
    gln_ref[1:2, :] += jnp.sum(dsecond, axis=0, keepdims=True)
    dmixed = dout + norm_back(dsecond, normed, inverse, ln_ref[2:3, :])
    datt = dmixed.astype(low_type)
    dx_ref[...] = datt
    o_sum[...] += dot_tn(att, datt)
    datt_ref[...] = dot_nt(datt, wo_ref[...]).astype(low_type)

    @pl.when(step == pl.num_programs(0) - 1)
    def _():
        gffn_ref[0] = up_sum[...].astype(low_type)
        gffn_ref[1] = down_sum[...].astype(low_type)
        go_ref[...] = o_sum[...].astype(low_type)


def feed(ids, weights, rows, att, grad, wo, ffn, ln_params, length):
    count = rows.shape[0]
    block = 512
    row_spec = pl.BlockSpec((block, D), lambda i: (i, 0))

    def whole(*shape):
        return pl.BlockSpec(shape, lambda i: (0,) * len(shape))

    return pl.pallas_call(
        functools.partial(feed_kernel, per_seq=length // block),
        grid=(count // block,),
        in_specs=[
            pl.BlockSpec(memory_space=pltpu.SMEM),
            whole(8, LANES),
            row_spec,
            row_spec,
            row_spec,
            whole(D, D),
            whole(2, FF, D),
            whole(4, D),
        ],
        out_specs=[
            row_spec,
            row_spec,
            row_spec,
            whole(2, D, FF),
            whole(D, D),
            whole(2, D),
        ],
        out_shape=[
            jax.ShapeDtypeStruct((count, D), low_type),
            jax.ShapeDtypeStruct((count, D), low_type),
            jax.ShapeDtypeStruct((count, D), low_type),
            jax.ShapeDtypeStruct((2, D, FF), low_type),
            jax.ShapeDtypeStruct((D, D), low_type),
            jax.ShapeDtypeStruct((2, D), wide_type),
        ],
        scratch_shapes=[
            pltpu.VMEM((D, FF), wide_type),
            pltpu.VMEM((D, FF), wide_type),
            pltpu.VMEM((D, D), wide_type),
            pltpu.VMEM((block, FF), low_type),
            pltpu.VMEM((block, FF), low_type),
        ],
        compiler_params=pltpu.CompilerParams(vmem_limit_bytes=VMEM_BYTES),
        name="feed",
    )(ids, weights, rows, att, grad, wo, ffn, ln_params)


def finish_kernel(
    dx_ref,
    dz_ref,
    ga_ref,
    sa_ref,
    wa_ref,
    ma_ref,
    gf_ref,
    sf_ref,
    wf_ref,
    mf_ref,
    ln_ref,
    first_ref,
    second_ref,
    sum_ref,
    grad_ref,
    ga_out,
    ma_out,
    wa_out,
    ca_out,
    gf_out,
    mf_out,
    wf_out,
    cf_out,
    gl_out,
    first_out,
    second_out,
    ln_out,
):
    grad_ref[...] = dx_ref[...].astype(wide_type) + dz_ref[...].astype(wide_type)
    keep = 1.0 - muon_rate * muon_decay
    for refs, size in (
        ((ga_ref, sa_ref, wa_ref, ma_ref, ga_out, ma_out, wa_out, ca_out), D),
        ((gf_ref, sf_ref, wf_ref, mf_ref, gf_out, mf_out, wf_out, cf_out), FF),
    ):
        grad, ortho, weight, moment, grad_out, moment_out, weight_out, copy_out = refs
        grad = grad[...].astype(wide_type)
        grad_out[...] = grad
        moment_out[...] = momentum_keep * moment[...] + grad
        rate = muon_rate * 0.2 * math.sqrt(size)
        new = keep * weight[...] - rate * ortho[...].astype(wide_type)
        weight_out[...] = new
        copy_out[...] = new.astype(low_type)
    width = first_ref.shape[1]
    place = lax.axis_index("narrow")

    def own(ref):
        picked = jnp.zeros((4, width), wide_type)
        for at in range(D // width):
            picked = picked + jnp.where(place == at, ref[0:4, at * width : (at + 1) * width], 0.0)
        return picked

    grad = own(sum_ref)
    first = beta_first * first_ref[...] + (1.0 - beta_first) * grad
    second = beta_second * second_ref[...] + (1.0 - beta_second) * grad * grad
    gl_out[...] = grad
    first_out[...] = first
    second_out[...] = second
    first_fix = 1.0 - beta_first**STEP
    second_fix = 1.0 - beta_second**STEP
    ln_out[...] = own(ln_ref) - adam_rate * (first / first_fix) / (
        jnp.sqrt(second / second_fix) + adam_epsilon
    )


def finish(dx, dz, attn, ffn, ln):
    steps = 2

    def rows(item):
        block = item.shape[0] // steps
        return pl.BlockSpec((block, item.shape[1]), lambda i: (i, 0))

    def whole(item):
        return pl.BlockSpec(item.shape, lambda i: (0, 0))

    def outs(group):
        shape = group[0].shape
        return [jax.ShapeDtypeStruct(shape, wide_type)] * 3 + [
            jax.ShapeDtypeStruct(shape, low_type)
        ]

    row_items = [dx, dz] + list(attn) + list(ffn)
    row_outs = [jax.ShapeDtypeStruct(dx.shape, wide_type)] + outs(attn) + outs(ffn)
    ln_outs = [jax.ShapeDtypeStruct(ln[1].shape, wide_type)] * 4
    return pl.pallas_call(
        finish_kernel,
        grid=(steps,),
        in_specs=[rows(item) for item in row_items] + [whole(item) for item in ln],
        out_specs=[rows(item) for item in row_outs] + [whole(item) for item in ln_outs],
        out_shape=row_outs + ln_outs,
        compiler_params=pltpu.CompilerParams(vmem_limit_bytes=VMEM_BYTES),
        name="finish",
    )(*row_items, *ln)


MESH = pl.DeviceIdType.MESH
LANES = 128


def remote(src, dst, send_sem, recv_sem, device):
    return pltpu.make_async_remote_copy(
        src_ref=src,
        dst_ref=dst,
        send_sem=send_sem,
        recv_sem=recv_sem,
        device_id=device,
        device_id_type=MESH,
    )


def greet(devices):
    barrier = pltpu.get_barrier_semaphore()
    for device in devices:
        pl.semaphore_signal(barrier, inc=1, device_id=device, device_id_type=MESH)
    pl.semaphore_wait(barrier, len(devices))


def attend_chunks(source, refs, seqs, asides):
    att_ref, share_ref, logit_ref, before_ref, state_ref, state, carry = refs
    q_in, k_in, v_in, a_in = source
    first_head = lane_of((CHUNK, PAIR)) < HEAD_DIM
    causal = row_of((CHUNK, 2 * CHUNK)) >= lane_of((CHUNK, 2 * CHUNK)) % CHUNK
    same_head = (row_of((PAIR, 2 * PAIR)) // HEAD_DIM) == (
        (lane_of((PAIR, 2 * PAIR)) // HEAD_DIM) % 2
    )
    lower = (row_of((CHUNK, CHUNK)) >= lane_of((CHUNK, CHUNK))).astype(low_type)
    items = []
    for seq in range(seqs):
        part = slice(seq * CHUNK, (seq + 1) * CHUNK)
        before = carry[seq]
        before_ref[0, seq] = before
        total = dot_nn(lower, a_in[part, :]) + before
        carry[seq] = total[CHUNK - 1 :, :]
        inv = 1.0 / total
        for pair in range(PAIRS):
            lanes = slice(pair * PAIR, (pair + 1) * PAIR)
            items.append(
                dict(
                    seq=seq,
                    pair=pair,
                    lanes=lanes,
                    q=q_in[part, lanes] * low_type(HEAD_DIM**-0.5),
                    k=k_in[part, lanes],
                    v=v_in[part, lanes],
                    a=a_in[part, lanes],
                    inv=inv[:, lanes],
                )
            )

    def score(t):
        t["a_two"] = split_pair(t["a"], first_head)
        t["now"] = jnp.where(same_head, state[t["seq"], t["pair"]], 0.0).astype(low_type)
        state_ref[0, t["seq"], t["pair"]] = t["now"]
        raw = dot_nt(t["q"], split_pair(t["k"], first_head))
        t["scores"] = jnp.where(causal, raw, 0.0).astype(low_type)

    def gather(t):
        numer = dot_nn(t["scores"], t["a_two"]) + dot_nt(t["q"], t["now"][:, :PAIR])
        t["logit"] = numer * t["inv"]
        logit_ref[t["seq"], :, t["lanes"]] = t["logit"].astype(low_type)

    def soften(t):
        expo = jnp.exp(t["logit"] - head_reduce(t["logit"], first_head, jnp.max, -jnp.inf))
        share = expo * (t["inv"] / head_reduce(expo, first_head, jnp.sum, 0.0))
        t["share"] = share.astype(low_type)
        share_ref[t["seq"], :, t["lanes"]] = t["share"]

    def blend(t):
        raw = dot_nt(t["share"], t["a_two"])
        t["mix"] = jnp.where(causal, raw, 0.0).astype(low_type)

    def finish_item(t):
        att = dot_nn(t["mix"], split_pair(t["v"], first_head))
        att = att + dot_nn(t["share"], t["now"][:, PAIR:])
        att_ref[t["seq"], :, t["lanes"]] = att.astype(low_type)
        state[t["seq"], t["pair"]] += dot_tn(t["a"], jnp.concatenate([t["k"], t["v"]], axis=1))

    for stage, aside in zip((score, gather, soften, blend, finish_item), asides):
        for place, item in enumerate(items):
            stage(item)
            if place == len(items) // 2 - 1 and aside is not None:
                aside()


def forward_kernel(
    ids_ref,
    dw_ref,
    x_first_ref,
    x_ref,
    ln_ref,
    attn_hbm,
    ffn_w_hbm,
    q_ref,
    k_ref,
    v_ref,
    a_ref,
    att_ref,
    share_ref,
    logit_ref,
    before_ref,
    state_ref,
    weight_ref,
    in_hbm,
    out_hbm,
    ffn_hbm,
    state,
    carry,
    held,
    in_w,
    piece_ref,
    attn_ref,
    ffn_ref,
    own,
    own_ffn,
    counts,
    counts_z,
    counts_chip,
    counts_mate,
    sems,
    *,
    narrow,
    total_seqs,
    groups,
):
    step = pl.program_id(0)
    steps = pl.num_programs(0)
    seqs = x_ref.shape[0]
    here = Place(narrow)
    copies = Copies(sems)
    z, core, chip = here.z, here.core, here.chip
    rows = attn_ref.shape[1]
    ffn_rows = ffn_ref.shape[1]
    half = rows // 2
    bit = half // 2
    quarter = ffn_rows // 4
    small = rows // 4
    w = lax.axis_index("wide")
    column = range(narrow - 1)
    planes = range(3)
    rounds = range(1, narrow)
    cols = blocks_at(core, D // 2)

    def inside(shard):
        return jnp.clip(shard, 0, narrow - 1)

    def from_z(place):
        return lax.rem(z + narrow - here.hops[place], narrow)

    def in_rows(owner, part):
        return blocks_at(4 * owner + 2 * core + part, bit)

    in_z, in_chip, in_core = [], [], []
    for part in range(2):
        in_z.append(
            [
                copies.remote(
                    own.at[chip, blocks_at(2 * core + part, bit)],
                    in_w.at[chip, in_rows(z, part)],
                    here.column[i],
                )
                for i in column
            ]
        )
        blocks = [in_w.at[chip, in_rows(from_z(i), part)] for i in column]
        in_chip.append(
            [[copies.remote(block, block, here.chips[p]) for p in planes] for block in blocks]
        )
        blocks = [in_w.at[:, in_rows(from_z(i), part)] for i in column]
        in_core.append([copies.remote(block, block, here.mate) for block in blocks])

    side = lax.rem(chip, 2)
    pieces = (side, 2 + chip // 2)
    beside = (w - 2 * chip + 2 * (chip + 1 - 2 * side), z)
    neighbours = (beside, here.chips[1])

    def ffn_block(shard, piece):
        return ffn_hbm.at[core, blocks_at(4 * shard + piece, quarter)]

    def out_block(shard):
        return out_hbm.at[blocks_at(4 * shard + chip, small), cols]

    def sends(way, turn):
        if way == 0:
            return jnp.logical_and(z < narrow - 1, z + 1 - turn >= 0)
        return jnp.logical_and(z > 0, z - 1 + turn <= narrow - 1)

    def gets(way, turn):
        return z - turn >= 0 if way == 0 else z + turn <= narrow - 1

    relay, spread, passed = {}, {}, {}
    for turn in rounds:
        for way in range(2):
            sign = 1 if way == 0 else -1
            there = (w, inside(z + sign))
            shard = inside(z + sign * (1 - turn))
            if turn == 1:
                sources = [own_ffn.at[core, blocks_at(piece, quarter)] for piece in pieces]
                sources.append(own.at[4, blocks_at(chip, small), cols])
            else:
                sources = [ffn_block(shard, piece) for piece in pieces] + [out_block(shard)]
            targets = [ffn_block(shard, piece) for piece in pieces] + [out_block(shard)]
            relay[way, turn] = [
                copies.remote(src, dst, there) for src, dst in zip(sources, targets)
            ]
            got = inside(z - sign * turn)
            spread[way, turn] = []
            for piece, device in zip(pieces, neighbours):
                block = ffn_block(got, piece)
                spread[way, turn].append(copies.remote(block, block, device))
            block = out_block(got)
            spread[way, turn] += [copies.remote(block, block, here.chips[p]) for p in planes]
            passed[way, turn] = [
                copies.remote(block, block, here.mate)
                for block in (
                    ffn_hbm.at[core, blocks_at(got, ffn_rows)],
                    out_hbm.at[blocks_at(got, rows), cols],
                )
            ]

    def relay_send(turn):
        for way in range(2):

            @pl.when(sends(way, turn))
            def _():
                for copy in relay[way, turn]:
                    copy.start()

    def relay_get(turn):
        for way in range(2):

            @pl.when(gets(way, turn))
            def _():
                for copy in relay[way, turn]:
                    copy.wait_recv()
                for copy in spread[way, turn]:
                    copy.start()

        if turn + 1 < narrow:
            relay_send(turn + 1)

    def pass_on(turn):
        for way in range(2):

            @pl.when(gets(way, turn))
            def _():
                for copy in spread[way, turn]:
                    copy.wait_recv()
                for copy in passed[way, turn]:
                    copy.start()

    count_z = [copies.remote(counts, counts_z.at[i], here.column[i]) for i in column]
    count_chip = [copies.remote(counts, counts_chip.at[p], here.chips[p]) for p in planes]
    count_mate = copies.remote(counts, counts_mate, here.mate)
    load_piece = copies.local(attn_hbm.at[chip, blocks_at(core, half)], piece_ref)
    load_attn = copies.local(attn_hbm, attn_ref)
    load_ffn = copies.local(ffn_w_hbm, ffn_ref)
    keep_ffn = copies.local(own_ffn, ffn_hbm.at[:, blocks_at(z, ffn_rows)])
    keep_out = copies.local(own.at[4], out_hbm.at[blocks_at(z, rows)])
    keep_in = copies.local(in_w, in_hbm)

    def normal(ref):
        normed, _ = normalize(ref[...].reshape(seqs * CHUNK, D).astype(wide_type))
        return (normed * ln_ref[0:1, :] + ln_ref[1:2, :]).astype(low_type)

    def product(first, place):
        out = dot_nn(first, in_w[place])
        held[place] = (jnp.exp(out) if place == 3 else out).astype(low_type)

    @pl.when(step == 0)
    def _():
        for copy in (load_piece, load_attn, load_ffn):
            copy.start()
        state[...] = jnp.zeros_like(state)
        carry[...] = jnp.zeros_like(carry)
        greet(here.column + here.chips + [here.mate])
        load_piece.wait()
        own[chip, blocks_at(core, half), :] = piece_ref[...].astype(low_type)
        for part in range(2):
            for i in column:
                in_z[part][i].start()
        load_attn.wait()
        load_ffn.wait()
        for place in range(4):
            in_w[place, blocks_at(z, rows), :] = attn_ref[place].astype(low_type)
        own[4] = attn_ref[4].astype(low_type)
        own_ffn[...] = ffn_ref[...].astype(low_type)
        lanes = lane_of((8, LANES))
        count = jnp.zeros((8, LANES), wide_type)
        for seq in range(ids_ref.shape[0]):
            count = count + (lanes == ids_ref[seq]).astype(wide_type)
        counts[...] = count
        for part in range(2):
            for i in column:
                in_z[part][i].wait_recv()
                for p in planes:
                    in_chip[part][i][p].start()
        relay_send(1)
        for copy in count_z:
            copy.start()
        keep_ffn.start()
        keep_out.start()
        for part in range(2):
            for i in column:
                for p in planes:
                    in_chip[part][i][p].wait_recv()
                in_core[part][i].start()
        relay_get(1)
        for part in range(2):
            for i in column:
                in_core[part][i].wait_recv()
        keep_in.start()
        first = normal(x_first_ref)
        for place in range(4):
            product(first, place)

    for turn in range(2, narrow):

        @pl.when(step == turn - 1)
        def _():
            relay_get(turn)

    @pl.when(step == 1)
    def _():
        for copy in count_z:
            copy.wait()
        counts[...] = counts[...] + sum(counts_z[i] for i in column)
        for copy in count_chip:
            copy.start()

    @pl.when(step == 2)
    def _():
        for copy in count_chip:
            copy.wait()
        counts[...] = counts[...] + sum(counts_chip[p] for p in planes)
        count_mate.start()

    @pl.when(step == 3)
    def _():
        count_mate.wait()
        total = counts[...] + counts_mate[...]
        lanes = lane_of((8, LANES))
        values = jnp.zeros((8, LANES), wide_type)
        for group in range(groups):
            values = values + jnp.where(lanes == group, dw_ref[group], 0.0)
        weight_ref[...] = values * total_seqs / (groups * jnp.maximum(total, 1.0))

    for turn in rounds:

        @pl.when(step == jnp.minimum(steps - 1, turn + 4))
        def _():
            pass_on(turn)

    source = [held[place] for place in range(4)]
    for ref, item in zip((q_ref, k_ref, v_ref, a_ref), source):
        ref[...] = item.reshape(ref.shape)
    later = {}

    def aside_norm():
        later["first"] = normal(x_ref)

    attend_chunks(
        source,
        (att_ref, share_ref, logit_ref, before_ref, state_ref, state, carry),
        seqs,
        (
            aside_norm,
            lambda: product(later["first"], 0),
            lambda: product(later["first"], 1),
            lambda: product(later["first"], 2),
            lambda: product(later["first"], 3),
        ),
    )

    @pl.when(step == steps - 1)
    def _():
        keep_ffn.wait()
        keep_out.wait()
        keep_in.wait()
        for part in range(2):
            for i in column:
                in_z[part][i].wait_send()
                for p in planes:
                    in_chip[part][i][p].wait_send()
                in_core[part][i].wait_send()
        for turn in rounds:
            for way in range(2):

                @pl.when(sends(way, turn))
                def _():
                    for copy in relay[way, turn]:
                        copy.wait_send()

                @pl.when(gets(way, turn))
                def _():
                    for copy in spread[way, turn]:
                        copy.wait_send()
                    for copy in passed[way, turn]:
                        copy.wait()


def forward(tokens, ids, dw, ln_params, attn_w, ffn_w):
    seqs, length, _ = tokens.shape
    chunks = length // CHUNK
    wide = lax.axis_size("wide")
    narrow = lax.axis_size("narrow")
    if wide > 8:
        sets = [[place + 8 * group for group in range(wide // 8)] for place in range(8)]
        ids = lax.all_gather(ids, "wide", axis_index_groups=sets, tiled=True)
    block = pl.BlockSpec((seqs, CHUNK, D), lambda i: (0, i, 0))
    ahead = pl.BlockSpec((seqs, CHUNK, D), lambda i: (0, jnp.minimum(i + 1, chunks - 1), 0))
    low_out = jax.ShapeDtypeStruct(tokens.shape, low_type)
    any_spec = pl.BlockSpec(memory_space=pl.ANY)

    def whole(*shape):
        return pl.BlockSpec(shape, lambda i: (0,) * len(shape))

    column = narrow - 1
    sems = 6 + 2 * (10 * column + 2 * column * 10 + column + 4)
    return pl.pallas_call(
        functools.partial(
            forward_kernel,
            narrow=narrow,
            total_seqs=seqs * wide * narrow,
            groups=dw.shape[0],
        ),
        grid=(chunks,),
        in_specs=[
            pl.BlockSpec(memory_space=pltpu.SMEM),
            pl.BlockSpec(memory_space=pltpu.SMEM),
            whole(seqs, CHUNK, D),
            ahead,
            whole(4, D),
            any_spec,
            any_spec,
        ],
        out_specs=[block] * 7
        + [
            pl.BlockSpec((1, seqs, 1, D), lambda i: (i, 0, 0, 0)),
            pl.BlockSpec((1, seqs, PAIRS, PAIR, 2 * PAIR), lambda i: (i, 0, 0, 0, 0)),
            whole(8, LANES),
            any_spec,
            any_spec,
            any_spec,
        ],
        out_shape=[low_out] * 7
        + [
            jax.ShapeDtypeStruct((chunks, seqs, 1, D), wide_type),
            jax.ShapeDtypeStruct((chunks, seqs, PAIRS, PAIR, 2 * PAIR), low_type),
            jax.ShapeDtypeStruct((8, LANES), wide_type),
            jax.ShapeDtypeStruct((4, D, D), low_type),
            jax.ShapeDtypeStruct((D, D), low_type),
            jax.ShapeDtypeStruct((2, FF, D), low_type),
        ],
        scratch_shapes=[
            pltpu.VMEM((seqs, PAIRS, PAIR, 2 * PAIR), wide_type),
            pltpu.VMEM((seqs, 1, D), wide_type),
            pltpu.VMEM((4, seqs * CHUNK, D), low_type),
            pltpu.VMEM((4, D, D), low_type),
            pltpu.VMEM((attn_w.shape[1] // 2, D), wide_type),
            pltpu.VMEM(attn_w.shape, wide_type),
            pltpu.VMEM(ffn_w.shape, wide_type),
            pltpu.VMEM(attn_w.shape, low_type),
            pltpu.VMEM(ffn_w.shape, low_type),
            pltpu.VMEM((8, LANES), wide_type),
            pltpu.VMEM((column, 8, LANES), wide_type),
            pltpu.VMEM((3, 8, LANES), wide_type),
            pltpu.VMEM((8, LANES), wide_type),
            pltpu.SemaphoreType.DMA((sems,)),
        ],
        compiler_params=pltpu.CompilerParams(
            vmem_limit_bytes=VMEM_BYTES, collective_id=0, has_side_effects=True
        ),
        name="forward",
    )(ids, dw, tokens, tokens, ln_params, attn_w, ffn_w)


class Place:
    def __init__(self, narrow):
        self.narrow = narrow
        w = lax.axis_index("wide")
        self.z = lax.axis_index("narrow")
        self.core = lax.rem(w, 2)
        self.chip = lax.rem(w // 2, 4)
        self.other = 1 - self.core
        self.hops = list(range(1, narrow))
        self.column_z = [lax.rem(self.z + hop, narrow) for hop in self.hops]
        self.column = [(w, place) for place in self.column_z]
        self.chip_at = [lax.rem(self.chip + hop, 4) for hop in range(1, 4)]
        self.chips = [(w - 2 * self.chip + 2 * chip, self.z) for chip in self.chip_at]
        self.mate = (w + 1 - 2 * self.core, self.z)


class Copies:
    def __init__(self, sems):
        self.sems = sems
        self.used = 0

    def remote(self, src, dst, device):
        at = self.used
        self.used += 2
        return remote(src, dst, self.sems.at[at], self.sems.at[at + 1], device)

    def local(self, src, dst):
        at = self.used
        self.used += 1
        return pltpu.make_async_copy(src, dst, self.sems.at[at])


def blocks_at(owner, size):
    return pl.ds(pl.multiple_of(owner * size, size), size)


def wide_sum(parts):
    total = parts[0].astype(wide_type)
    for part in parts[1:]:
        total = total + part.astype(wide_type)
    return total


def newton_poly(gram):
    size = gram.shape[0]
    eye = row_of((size, size)) == lane_of((size, size))
    trace = jnp.sum(jnp.where(eye, gram, 0.0), axis=1, keepdims=True)
    trace = jnp.sum(trace, axis=0, keepdims=True)
    scale = 1.0 / (jnp.sqrt(trace) + 1e-07)

    def low_dot(left, right):
        return dot_nn(left.astype(low_type), right.astype(low_type))

    def polynomial(one):
        poly = quintic_cube * one + quintic_five * low_dot(one, one)
        return poly + jnp.where(eye, quintic_lin, 0.0)

    gram_one = gram * (scale * scale)
    poly_one = polynomial(gram_one)
    gram_two = low_dot(low_dot(gram_one, poly_one), poly_one)
    poly_two = polynomial(gram_two)
    return poly_one.astype(low_type), (poly_two * scale).astype(low_type)


def newton_step(rows, polys):
    return dot_nn(dot_nn(rows, polys[0]).astype(low_type), polys[1]).astype(low_type)


def update_body(
    wsum_ref,
    take_f,
    mom_w_ref,
    mom_hbm,
    mom_f_hbm,
    ln_one_ref,
    ln_two_ref,
    grad_attn,
    step_attn,
    grad_ffn,
    step_ffn,
    ln_ref,
    ln_now,
    ln_mate,
    ln_chips,
    ln_column,
    col_w,
    grad_w,
    moment_w,
    poly_w,
    send_w,
    all_w,
    all_f,
    mom_f,
    mom_o,
    moment_f,
    out_f,
    all_o,
    moment_o,
    step_o,
    cut_gf,
    col_gf,
    strips_gf,
    gram_f,
    cut_go,
    col_go,
    strips_go,
    gram_o,
    *,
    narrow,
    here,
    copies,
    over_groups,
):
    z, core, chip = here.z, here.core, here.chip
    half = D // 2
    quarter = D // 4
    rows = D // narrow
    small = rows // 4
    ffn_rows = FF // narrow
    strip = quarter // narrow
    column = range(narrow - 1)
    planes = range(3)
    own_cols = blocks_at(core, half)
    own_quarter = blocks_at(chip, quarter)
    own_small = blocks_at(chip, small)
    matrix = lax.rem(z, 4)

    def to_plane(src, dst):
        return [copies.remote(src(i), dst(i), here.chips[i]) for i in planes]

    def to_column(src, dst):
        return [copies.remote(src(i), dst(i), here.column[i]) for i in column]

    def same(block):
        return lambda i: block

    keep_f = copies.local(mom_f_hbm.at[core], mom_f)
    keep_o = copies.local(mom_hbm.at[4], mom_o)
    mate_ln = [copies.remote(ln_now, ln_mate, here.mate)]
    plane_ln = to_plane(same(ln_now), lambda i: ln_chips.at[i])
    block = all_f.at[own_quarter]
    plane_f = to_plane(same(block), same(block))
    block = all_o.at[own_small, own_cols]
    plane_f = plane_f + to_plane(same(block), same(block))
    z_sum = to_column(lambda i: wsum_ref.at[lax.rem(here.column_z[i], 4)], lambda i: col_w.at[i])
    z_ln = to_column(same(ln_now), lambda i: ln_column.at[i])
    block = out_f.at[0, core]
    mate_f = [copies.remote(block, block, here.mate)]
    block = all_o.at[:, own_cols]
    mate_o = [copies.remote(block, block, here.mate)]
    z_gf = to_column(
        lambda i: cut_gf.at[blocks_at(here.column_z[i], strip)], lambda i: col_gf.at[i]
    )
    block = grad_w.at[own_quarter, own_cols]
    plane_w = to_plane(same(block), same(block))
    z_go = to_column(
        lambda i: cut_go.at[blocks_at(here.column_z[i], strip)], lambda i: col_go.at[i]
    )
    block = grad_w.at[:, own_cols]
    mate_w = [copies.remote(block, block, here.mate)]
    block = strips_gf.at[blocks_at(z, strip)]
    z_back_f = to_column(same(block), same(block))
    block = strips_go.at[blocks_at(z, strip)]
    z_back_o = to_column(same(block), same(block))
    block = gram_f.at[own_quarter]
    plane_gf = to_plane(same(block), same(block))
    block = gram_o.at[own_quarter, own_cols]
    plane_go = to_plane(same(block), same(block))
    quad = [z - matrix + lax.rem(matrix + hop, 4) for hop in range(1, 4)]

    def hand_back(kind):
        spread = [
            copies.remote(
                send_w.at[kind, there],
                all_w.at[kind, matrix, own_small, own_cols],
                (lax.axis_index("wide"), there),
            )
            for there in quad
        ]
        block = all_w.at[kind, :, own_small, own_cols]
        plane = to_plane(same(block), same(block))
        block = all_w.at[kind, :, :, own_cols]
        return spread, plane, [copies.remote(block, block, here.mate)]

    spread_g, plane_g, mate_g = hand_back(0)
    spread_s, plane_s, mate_s = hand_back(1)
    block = gram_o.at[:, own_cols]
    mate_go = [copies.remote(block, block, here.mate)]
    block = out_f.at[1, core]
    mate_x = [copies.remote(block, block, here.mate)]
    write_f = [copies.local(out_f.at[0], grad_ffn), copies.local(out_f.at[1], step_ffn)]
    write_o = [copies.local(all_o, grad_attn.at[4]), copies.local(step_o, step_attn.at[4])]
    write_w = [
        copies.local(all_w.at[0], grad_attn.at[pl.ds(0, 4)]),
        copies.local(all_w.at[1], step_attn.at[pl.ds(0, 4)]),
    ]
    sent = []

    def start(group):
        for copy in group:
            copy.start()
        sent.extend(group)

    def arrive(group):
        for copy in group:
            copy.wait_recv()

    def begin(group):
        for copy in group:
            copy.start()

    start(z_sum)
    begin([keep_f, keep_o])
    ln_now[...] = jnp.zeros_like(ln_now)
    ln_now[0:2, :] = ln_one_ref[...]
    ln_now[2:4, :] = ln_two_ref[...]
    over_groups(ln_now, 2)
    start(mate_ln)
    grad_f, grad_o = take_f()
    all_f[own_quarter, :] = grad_f
    all_o[own_small, own_cols] = grad_o
    start(plane_f)

    keep_f.wait()
    arrive(plane_f)
    start(mate_o)
    grad = all_f[...].T
    out_f[0, core] = grad
    start(mate_f)
    moment_f[...] = (momentum_keep * mom_f[...] + grad.astype(wide_type)).astype(low_type)
    cut_gf[...] = dot_tn(moment_f[:, own_quarter], moment_f[...]).astype(low_type)
    start(z_gf)

    keep_o.wait()
    arrive(mate_o)
    moment = momentum_keep * mom_o[...] + all_o[...].astype(wide_type)
    moment_o[...] = moment.astype(low_type)
    cut_go[...] = dot_tn(moment_o[:, own_quarter], moment_o[:, own_cols]).astype(low_type)
    start(z_go)

    arrive(z_sum)
    total = wide_sum([wsum_ref[matrix]] + [col_w[i] for i in column])
    grad_w[own_quarter, own_cols] = total.astype(low_type)
    start(plane_w)
    arrive(mate_ln)
    mate_ln[0].wait_send()
    ln_now[...] = ln_now[...] + ln_mate[...]
    start(plane_ln)

    arrive(z_gf)
    total = wide_sum([cut_gf[blocks_at(z, strip), :]] + [col_gf[i] for i in column])
    strips_gf[blocks_at(z, strip), :] = total.astype(low_type)
    start(z_back_f)
    arrive(z_go)
    total = wide_sum([cut_go[blocks_at(z, strip), :]] + [col_go[i] for i in column])
    strips_go[blocks_at(z, strip), :] = total.astype(low_type)
    start(z_back_o)

    arrive(plane_w)
    start(mate_w)
    arrive(plane_ln)
    for copy in plane_ln:
        copy.wait_send()
    ln_now[...] = ln_now[...] + ln_chips[0] + ln_chips[1] + ln_chips[2]
    start(z_ln)

    def small_rows(there):
        return pl.ds(pl.multiple_of(there * rows + chip * small, small), small)

    arrive(mate_w)
    for there in range(narrow):
        send_w[0, there] = grad_w[small_rows(there), own_cols]
    start(spread_g)
    all_w[0, matrix, own_small, own_cols] = send_w[0, z]
    moment = momentum_keep * mom_w_ref[...].astype(wide_type) + grad_w[...].astype(wide_type)
    moment_w[...] = moment.astype(low_type)
    gram = dot_tn(moment_w[...], moment_w[...])
    arrive(z_back_f)
    gram_f[own_quarter, :] = strips_gf[...]
    start(plane_gf)
    arrive(z_back_o)
    gram_o[own_quarter, own_cols] = strips_go[...]
    start(plane_go)

    poly_one, poly_w[...] = newton_poly(gram)
    picked = jnp.concatenate([moment_w[small_rows(there), :] for there in range(narrow)], axis=0)
    ortho = newton_step(picked, (poly_one, poly_w[:, own_cols]))
    for there in range(narrow):
        send_w[1, there] = ortho[there * small : (there + 1) * small, :]
    start(spread_s)
    all_w[1, matrix, own_small, own_cols] = send_w[1, z]
    arrive(spread_g)
    start(plane_g)

    arrive(plane_gf)
    out_f[1, core] = newton_step(moment_f[...], newton_poly(gram_f[...].astype(wide_type)))
    start(mate_x)
    arrive(spread_s)
    start(plane_s)
    arrive(plane_go)
    start(mate_go)
    arrive(plane_g)
    start(mate_g)
    arrive(mate_go)
    step_o[...] = newton_step(moment_o[...], newton_poly(gram_o[...].astype(wide_type)))
    arrive(plane_s)
    start(mate_s)
    begin(write_o)
    arrive(mate_f)
    arrive(mate_x)
    begin(write_f)
    arrive(z_ln)
    total = ln_now[...]
    for i in column:
        total = total + ln_column[i]
    ln_ref[...] = total
    arrive(mate_g)
    begin(write_w[:1])
    arrive(mate_s)
    begin(write_w[1:])
    for copy in write_o + write_f + write_w:
        copy.wait()
    settled = [id(copy) for copy in mate_ln + plane_ln]
    for copy in sent:
        if id(copy) not in settled:
            copy.wait_send()


def back_kernel(*refs, narrow, chunks, sets):
    blocks = list(refs[:9])
    xc_ref, x_ref, w_ref, ln_ref, gffn_hbm, go_hbm, mom_hbm, mom_f_hbm, ln_two_ref = refs[9:18]
    dz_ref, grad_attn, step_attn, grad_ffn, step_ffn, ln_sum_ref = refs[18:24]
    state, carry, dq_all, dk_all, dv_all, de_all, first_t = refs[24:31]
    own_f, got_f, far_f, col_f, own_o, got_o, cut_o, far_o, col_o = refs[31:40]
    low_f, low_o, mom_own, mom_low, mom_all = refs[40:45]
    grad_w, got_w, half_w, far_w, staged, gln_ref, wsum_ref = refs[45:52]
    sums = refs[52:54]
    group_w, group_f, group_o, group_ln = refs[54:58]
    *update_refs, sems = refs[58:]
    step = pl.program_id(0)
    steps = pl.num_programs(0)
    here = Place(narrow)
    copies = Copies(sems)
    half = D // 2
    part = D // 4
    rows = D // narrow
    ffn_rows = FF // narrow
    column = range(narrow - 1)
    own_cols = blocks_at(here.core, half)
    mate_cols = blocks_at(here.other, half)
    grads = (dq_all, dk_all, dv_all, de_all)
    w = lax.axis_index("wide")
    peers = [(lax.rem(w + 8 * at, 8 * sets), here.z) for at in range(1, sets)]

    keep_f = copies.local(gffn_hbm.at[here.core], own_f)
    keep_o = copies.local(go_hbm.at[:, own_cols], own_o)
    keep_mom = copies.local(mom_hbm.at[pl.ds(0, 4)], mom_own)
    pieces = [blocks_at(there, part) for there in here.chip_at + [here.chip]]
    mate_f = [
        copies.remote(gffn_hbm.at[here.other, piece], got_f.at[piece], here.mate)
        for piece in pieces
    ]
    mate_o = copies.remote(go_hbm.at[:, mate_cols], got_o, here.mate)
    plane_f = [
        copies.remote(own_f.at[pieces[hop]], far_f.at[hop], here.chips[hop]) for hop in range(3)
    ]
    plane_o = [
        copies.remote(cut_o.at[:, here.chip_at[hop]], far_o.at[hop], here.chips[hop])
        for hop in range(3)
    ]
    z_sum = []
    for i in column:
        there = here.column_z[i]
        z_sum.append(
            copies.remote(low_f.at[:, blocks_at(there, ffn_rows)], col_f.at[i], here.column[i])
        )
        z_sum.append(copies.remote(low_o.at[there], col_o.at[i], here.column[i]))
    z_mom = [
        copies.remote(
            mom_low.at[lax.rem(here.column_z[i], 4), :, own_cols],
            mom_all.at[blocks_at(here.z, rows), own_cols],
            here.column[i],
        )
        for i in column
    ]
    mate_mom = copies.remote(mom_all.at[:, own_cols], mom_all.at[:, own_cols], here.mate)
    mate_w = [
        copies.remote(grad_w.at[m, :, mate_cols], got_w.at[m], here.mate) for m in range(4)
    ]
    plane_w = [
        [
            copies.remote(
                half_w.at[m, blocks_at(here.chip_at[hop], part)],
                far_w.at[hop, m],
                here.chips[hop],
            )
            for hop in range(3)
        ]
        for m in range(4)
    ]

    def gradient(m):
        total = dot_nn(first_t[...], grads[m][...].reshape(-1, D))
        grad_w[m] = total.astype(low_type)
        mate_w[m].start()

    def over_cores(m):
        mate_w[m].wait()
        half_w[m] = wide_sum([grad_w[m, :, own_cols], got_w[m]]).astype(low_type)
        for copy in plane_w[m]:
            copy.start()

    def over_chips(m):
        for copy in plane_w[m]:
            copy.wait()
        mine = half_w[m, blocks_at(here.chip, part), :]
        wsum_ref[m] = wide_sum([mine] + [far_w[hop, m] for hop in range(3)]).astype(low_type)

    @pl.when(step == 0)
    def _():
        state[...] = jnp.zeros_like(state)
        carry[...] = jnp.zeros_like(carry)
        gln_ref[...] = jnp.zeros_like(gln_ref)
        greet(here.column + here.chips + [here.mate] + peers)
        for copy in [keep_f] + mate_f + [keep_o, mate_o, keep_mom]:
            copy.start()

    @pl.when(step == 1)
    def _():
        keep_mom.wait()
        mom_low[...] = mom_own[...].astype(low_type)
        for copy in z_mom:
            copy.start()
        mom_all[blocks_at(here.z, rows), own_cols] = mom_low[lax.rem(here.z, 4), :, own_cols]

    def piece_sum(at):
        mate_f[at].wait()
        piece = pieces[at]
        own_f[piece, :] = wide_sum([own_f[piece, :], got_f[piece, :]]).astype(low_type)
        if at < 3:
            plane_f[at].start()

    @pl.when(step == 1)
    def _():
        keep_f.wait()
        for at in range(2):
            piece_sum(at)

    @pl.when(step == 2)
    def _():
        for at in range(2, 4):
            piece_sum(at)
        keep_o.wait()
        mate_o.wait()
        cut_o[...] = wide_sum([own_o[...], got_o[...]]).astype(low_type).reshape(cut_o.shape)
        for copy in plane_o:
            copy.start()

    @pl.when(step < chunks)
    def _():
        chunk = chunks - 1 - step
        seqs = xc_ref.shape[0]

        for seq in range(seqs):
            normed, _ = normalize(xc_ref[seq].astype(wide_type))
            first = (normed * ln_ref[0:1, :] + ln_ref[1:2, :]).astype(low_type)
            first_t[:, blocks_at(chunk * seqs + seq, CHUNK)] = first.T
        attend_back_chunk(blocks + [staged.at[place] for place in range(4)], state, carry)
        for place in range(4):
            grads[place][chunk] = staged[place]

    @pl.when(step == chunks)
    def _():
        gradient(0)
        gradient(1)
        gradient(2)
        over_cores(0)
        over_cores(1)
        for copy in plane_f + plane_o:
            copy.wait()
        mine = own_f[blocks_at(here.chip, part), :]
        low_f[...] = wide_sum([mine] + [far_f[hop] for hop in range(3)]).astype(low_type)
        mine = cut_o[:, here.chip]
        low_o[...] = wide_sum([mine] + [far_o[hop] for hop in range(3)]).astype(low_type)
        for copy in z_sum:
            copy.start()
        gradient(3)
        over_cores(2)
        over_cores(3)
        for copy in z_mom:
            copy.wait_recv()
        mate_mom.start()

    @pl.when(step >= chunks)
    def _():
        per = chunks // 4
        seqs = x_ref.shape[0]
        parts = [item[pl.ds((step - chunks) * per, per)].reshape(-1, D) for item in grads]
        dfirst = dot_nt(parts[0], w_ref[0])
        for place in range(1, 4):
            dfirst = dfirst + dot_nt(parts[place], w_ref[place])
        spans = [slice(at * CHUNK, (at + 1) * CHUNK) for at in range(per)]
        rows_in = [x_ref[:, span, :].reshape(-1, D) for span in spans]
        normed, inverse = normalize(jnp.concatenate(rows_in, axis=0).astype(wide_type))
        gln_ref[0:1, :] += jnp.sum(dfirst * normed, axis=0, keepdims=True)
        gln_ref[1:2, :] += jnp.sum(dfirst, axis=0, keepdims=True)
        dz = norm_back(dfirst, normed, inverse, ln_ref[0:1, :]).astype(low_type)
        for at, span in enumerate(spans):
            size = seqs * CHUNK
            dz_ref[:, span, :] = dz[at * size : (at + 1) * size].reshape(seqs, CHUNK, D)

    def over_groups(ref, number):
        if sets == 1:
            return
        slots = (group_w, group_f, group_ln, group_o)[number]
        exchange = [
            copies.remote(ref, slots.at[at], peer) for at, peer in enumerate(peers)
        ]
        for copy in exchange:
            copy.start()
        for copy in exchange:
            copy.wait()
        total = wide_sum([ref[...]] + [slots[at] for at in range(len(peers))])
        ref[...] = total.astype(ref.dtype)

    def take_f():
        for copy in z_sum:
            copy.wait()
        sum_f, sum_o = sums
        mine = low_f[:, blocks_at(here.z, ffn_rows)]
        sum_f[...] = wide_sum([mine] + [col_f[i] for i in column]).astype(low_type)
        sum_o[...] = wide_sum([low_o[here.z]] + [col_o[i] for i in column]).astype(low_type)
        over_groups(sum_f, 1)
        over_groups(sum_o, 3)
        return sum_f[...], sum_o[...]

    @pl.when(step == steps - 1)
    def _():
        for m in range(4):
            over_chips(m)
        over_groups(wsum_ref, 0)
        mate_mom.wait()
        for copy in z_mom:
            copy.wait_send()
        update_body(
            wsum_ref,
            take_f,
            mom_all,
            mom_hbm,
            mom_f_hbm,
            gln_ref,
            ln_two_ref,
            grad_attn,
            step_attn,
            grad_ffn,
            step_ffn,
            ln_sum_ref,
            *update_refs,
            narrow=narrow,
            here=here,
            copies=copies,
            over_groups=over_groups,
        )


def back(q, k, v, a, share, logit, before, datt, states, tokens, in_w, ln_params, gffn, go, mom, mom_f, ln_two):
    seqs, length, _ = q.shape
    chunks = length // CHUNK
    narrow = lax.axis_size("narrow")
    small, half, part = D // narrow // 4, D // 2, D // 4
    ffn_rows = FF // narrow

    def chunk_at(i):
        return jnp.maximum(chunks - 1 - i, 0)

    def rows_at(i):
        return (0, jnp.maximum(i - chunks, 0), 0)

    def whole(*shape):
        return pl.BlockSpec(shape, lambda i: (0,) * len(shape))

    block = pl.BlockSpec((seqs, CHUNK, D), lambda i: (0, chunk_at(i), 0))
    row_spec = pl.BlockSpec((seqs, length // 4, D), rows_at)
    any_spec = pl.BlockSpec(memory_space=pl.ANY)
    rows, strip, column = D // narrow, part // narrow, narrow - 1
    sets = lax.axis_size("wide") // 8
    spare = max(sets - 1, 1)
    outs = [(5, rows, D), (5, rows, D), (2, ffn_rows, D), (2, ffn_rows, D)]

    def full(*shape):
        return pltpu.VMEM(shape, wide_type)

    def low(*shape):
        return pltpu.VMEM(shape, low_type)

    return pl.pallas_call(
        functools.partial(back_kernel, narrow=narrow, chunks=chunks, sets=sets),
        grid=(chunks + 4,),
        in_specs=[block] * 6
        + [
            pl.BlockSpec((1, seqs, 1, D), lambda i: (chunk_at(i), 0, 0, 0)),
            block,
            pl.BlockSpec((1, seqs, PAIRS, PAIR, 2 * PAIR), lambda i: (chunk_at(i), 0, 0, 0, 0)),
            block,
            row_spec,
            whole(4, D, D),
            whole(4, D),
            any_spec,
            any_spec,
            any_spec,
            any_spec,
            whole(2, D),
        ],
        out_specs=[row_spec] + [any_spec] * 4 + [whole(8, D)],
        out_shape=[jax.ShapeDtypeStruct(q.shape, low_type)]
        + [jax.ShapeDtypeStruct(shape, low_type) for shape in outs]
        + [jax.ShapeDtypeStruct((8, D), wide_type)],
        scratch_shapes=[
            pltpu.VMEM((seqs, PAIRS, PAIR, 2 * PAIR), wide_type),
            pltpu.VMEM((seqs, 1, D), wide_type),
            low(chunks, seqs, CHUNK, D),
            low(chunks, seqs, CHUNK, D),
            low(chunks, seqs, CHUNK, D),
            low(chunks, seqs, CHUNK, D),
            low(D, seqs * length),
            low(D, FF),
            low(D, FF),
            low(3, part, FF),
            low(narrow - 1, part, ffn_rows),
            low(D, half),
            low(D, half),
            low(narrow, 4, small, half),
            low(3, narrow, small, half),
            low(narrow - 1, small, half),
            low(part, FF),
            low(narrow, small, half),
            pltpu.VMEM((4, D // narrow, D), wide_type),
            low(4, D // narrow, D),
            low(D, D),
            low(4, D, D),
            low(4, D, half),
            low(4, D, half),
            low(3, 4, part, half),
            low(4, seqs, CHUNK, D),
            full(2, D),
            low(4, part, half),
            low(part, ffn_rows),
            low(small, half),
            low(spare, 4, part, half),
            low(spare, part, ffn_rows),
            low(spare, small, half),
            full(spare, 8, D),
            full(8, D),
            full(8, D),
            full(3, 8, D),
            full(column, 8, D),
            low(column, part, half),
            low(D, D),
            low(D, D),
            low(D, D),
            low(2, narrow, small, half),
            low(2, 4, rows, D),
            low(D, ffn_rows),
            full(ffn_rows, D),
            full(rows, D),
            low(ffn_rows, D),
            low(2, 2, ffn_rows, D),
            low(rows, D),
            low(rows, D),
            low(rows, D),
            low(part, D),
            low(column, strip, D),
            low(part, D),
            low(D, D),
            low(part, half),
            low(column, strip, half),
            low(part, half),
            low(D, D),
            pltpu.SemaphoreType.DMA((11 + 2 * (65 + 9 * column + 4 * spare),)),
        ],
        compiler_params=pltpu.CompilerParams(
            vmem_limit_bytes=VMEM_BYTES, collective_id=1, has_side_effects=True
        ),
        name="back",
    )(
        q,
        k,
        v,
        a,
        share,
        logit,
        before,
        datt,
        states,
        tokens,
        tokens,
        in_w,
        ln_params,
        gffn,
        go,
        mom,
        mom_f,
        ln_two,
    )


def shards(
    tokens,
    out_grad,
    group_ids,
    domain_weight,
    attn_w,
    ffn_w,
    attn_mom,
    ffn_mom,
    ln_params,
    ln_first,
    ln_second,
):
    local_seqs, length, _ = tokens.shape
    token_count = local_seqs * length
    rows = tokens.reshape(token_count, D)
    head = (local_seqs, length, D)
    q, k, v, a, att, share, logit, before, states, weights, in_w, out_w, ffn_low = forward(
        tokens, group_ids, domain_weight, ln_params, attn_w, ffn_w
    )
    output, dx, datt, gffn, go, ln_two = feed(
        group_ids,
        weights,
        rows,
        att.reshape(token_count, D),
        out_grad.reshape(token_count, D),
        out_w,
        ffn_low,
        ln_params,
        length,
    )
    dz, attn_grad, attn_step, ffn_grad, ffn_step, ln_sum = back(
        q,
        k,
        v,
        a,
        share,
        logit,
        before,
        datt.reshape(head),
        states,
        tokens,
        in_w,
        ln_params,
        gffn,
        go,
        attn_mom,
        ffn_mom,
        ln_two,
    )

    def flat(*items):
        return [item.reshape(-1, D) for item in items]

    results = finish(
        dx,
        dz.reshape(token_count, D),
        flat(attn_grad, attn_step, attn_w, attn_mom),
        flat(ffn_grad, ffn_step, ffn_w, ffn_mom),
        (ln_params, ln_first, ln_second, ln_sum),
    )
    input_grad, ga, ma, wa, ca, gf, mf, wf, cf, ln_grad, first_new, second_new, ln_new = results
    attn, ffn = attn_w.shape, ffn_w.shape
    return (
        output.reshape(tokens.shape),
        input_grad.reshape(tokens.shape),
        ga.reshape(attn),
        gf.reshape(ffn),
        ln_grad,
        ma.reshape(attn),
        mf.reshape(ffn),
        wa.reshape(attn),
        wf.reshape(ffn),
        ca.reshape(attn),
        cf.reshape(ffn),
        first_new,
        second_new,
        ln_new,
    )


def solution(mesh):
    split = P(("wide", "narrow"), None, None)
    rows = P(None, "narrow", None)
    lanes = P(None, "narrow")
    inner = jax.shard_map(
        shards,
        mesh=mesh,
        in_specs=(
            split,
            split,
            P(("wide", "narrow")),
            P(),
            rows,
            rows,
            rows,
            rows,
            P(),
            lanes,
            lanes,
        ),
        out_specs=(
            split,
            split,
            rows,
            rows,
            lanes,
            rows,
            rows,
            rows,
            rows,
            rows,
            rows,
            lanes,
            lanes,
            lanes,
        ),
        check_vma=False,
    )
    return inner
```
